32 devices in a mesh: seq: 8 (over y, x, core), fsdp: 4 (over z).
Axes of the slice: x: 2, y: 2, z: 4, core: 2. Of those that a mesh axis runs over, the one named last changes fastest.
Arguments:
- tokens: bfloat16 [8192, 1024], P(('seq', 'fsdp')), may hold values from -6 to 6
- lengths: int32 [8], replicated, may hold values from 1 to 1370, 8192 in all
- adapter_choice: int32 [8], replicated, may hold values from 0 to 7
- gain_rows: bfloat16 [4, 1024], P(None, ('seq', 'fsdp')), may hold values from 0.099609375 to 1.8984375
- bias_rows: bfloat16 [5, 1024], P(None, ('seq', 'fsdp')), may hold values from -1.796875 to 1.796875
- query_key_value: bfloat16 [1024, 3072], P(('seq', 'fsdp')), may hold values from -0.1875 to 0.1875
- output_weight: bfloat16 [1024, 1024], P(('seq', 'fsdp')), may hold values from -1 to 1
- expand_weight: bfloat16 [1024, 4096], P(('seq', 'fsdp')), may hold values from -0.1875 to 0.1875
- expand_bias: bfloat16 [4096], P(('seq', 'fsdp')), may hold values from -1.796875 to 1.796875
- contract_weight: bfloat16 [4096, 1024], P(('seq', 'fsdp')), may hold values from -0.09375 to 0.09375
- adapter_in_attention: bfloat16 [4, 1024, 128], P(None, ('seq', 'fsdp')), may hold values from -0.1875 to 0.1875
- adapter_out_attention: bfloat16 [4, 128, 1024], P(None, None, ('seq', 'fsdp')), may hold values from -1.5 to 1.5
- adapter_in_expand: bfloat16 [1024, 128], P(('seq', 'fsdp')), may hold values from -0.1875 to 0.1875
- adapter_out_expand: bfloat16 [128, 4096], P(None, ('seq', 'fsdp')), may hold values from -1.5 to 1.5
- adapter_in_contract: bfloat16 [4096, 128], P(('seq', 'fsdp')), may hold values from -0.09375 to 0.09375
- adapter_out_contract: bfloat16 [128, 1024], P(None, ('seq', 'fsdp')), may hold values from -1.5 to 1.5
- cotangent: bfloat16 [8192, 1024], P(('seq', 'fsdp')), may hold values from -6 to 6
Outputs:
- output: bfloat16 [8192, 1024], P(('seq', 'fsdp'))
- input_gradient: float32 [8192, 1024], P(('seq', 'fsdp'))
- adapter_in_attention_gradient: float32 [4, 1024, 128], P(None, ('seq', 'fsdp'))
- adapter_out_attention_gradient: float32 [4, 128, 1024], P(None, None, ('seq', 'fsdp'))
- adapter_in_expand_gradient: float32 [1024, 128], P(('seq', 'fsdp'))
- adapter_out_expand_gradient: float32 [128, 4096], P(None, ('seq', 'fsdp'))
- adapter_in_contract_gradient: float32 [4096, 128], P(('seq', 'fsdp'))
- adapter_out_contract_gradient: float32 [128, 1024], P(None, ('seq', 'fsdp'))
The draws below stay inside these ranges and needn't reach their ends.
Inputs may be any that keep to these rules, and one draw needn't show every extreme that they name: Image lengths in the order of the tokens, summing to 8192; the longest is exactly 1370.
All inputs are finite; a program needn't handle non-finite values.
Results may differ from the reference program's by a relative error of at most 0.015.
The reference program's roundings to bfloat16 on the way count: a program that leaves them out, or rounds other values in their place, can miss the bound.
Values may be sent and summed in bfloat16 or wider, within the bound.
A program may use at most 256 MiB of HBM per device.

```python
import math
import jax
import jax.numpy as jnp
import numpy as np
from jax import lax

D = 1024
HEADS = 16
HEAD_DIM = 64
FF = 4096
RANK = 16
ADAPTERS = 8
IMG_MAX = 1370
TOKENS = 8192
IMAGES = 8


def plant(entries, stream_key, low, largest):
    place = [jax.random.randint(jax.random.fold_in(stream_key, axis), (), 0, length) for axis, length in enumerate(entries.shape)]
    longest = entries.shape.index(max(entries.shape))
    next_to = place[:longest] + [(place[longest] + 1) % entries.shape[longest]] + place[longest + 1:]
    return entries.at[tuple(place)].set(low).at[tuple(next_to)].set(largest)


def with_spikes(drawn, rng, source, target, parts, factor):
    owner, partner = [(jnp.arange(drawn.shape[dim]) // (drawn.shape[dim] // parts)).reshape([-1 if axis == dim else 1 for axis in range(drawn.ndim)]) for dim in (source, target)]
    chosen = jax.random.permutation(rng, parts)[partner]
    strong = (owner == chosen) | (owner == (partner + parts // 2) % parts)
    return jnp.where(strong, factor * drawn, drawn)


def steps_of(rng, dims, split, low, high):
    factor_of, own = 1.0, jax.random.fold_in(rng, 6)
    for position, parts in split:
        steps = jnp.exp(jax.random.uniform(jax.random.fold_in(own, position), (parts,), jnp.float32, low / len(split), high / len(split)))
        factor_of = factor_of * jnp.repeat(steps, dims[position] // parts).reshape([-1 if axis == position else 1 for axis in range(len(dims))])
    return factor_of


def split_up(amount, total, most, slope):
    loads = [(1 << 20) // math.isqrt(rank ** slope) + 1 for rank in range(2, amount + 1)]
    surplus, given = total - most - (amount - 1), [1] * (amount - 1)
    while surplus > 0:
        movable = [i for i in range(amount - 1) if given[i] < most]
        whole, left = sum([loads[i] for i in movable]), surplus
        for i in movable:
            extra = min(most - given[i], max(1, left * loads[i] // whole), surplus)
            given[i] = given[i] + extra
            surplus = surplus - extra
    return np.array([most] + given)


def uneven_parts(key, number_of, total, most, skew):
    if number_of == 2:
        one = jax.random.randint(key, (), max(1, total - most), min(most, total - 1) + 1)
        return jnp.stack([one, total - one])
    tallies = jnp.asarray(split_up(number_of, total, most, skew), jnp.int32)
    pairs = (number_of - 1) // 2
    source_of, sink = tallies[1:1 + 2 * pairs:2], tallies[2:2 + 2 * pairs:2]
    slack = jnp.minimum(source_of - 1, most - sink)
    passed = jax.random.randint(jax.random.fold_in(key, 1), (pairs,), 0, 1 << 20) % (slack + 1)
    tallies = tallies.at[1:1 + 2 * pairs:2].set(source_of - passed).at[2:2 + 2 * pairs:2].set(sink + passed)
    return tallies[jax.random.permutation(jax.random.fold_in(key, 2), number_of)]


def centred(stream_key, shape, scale, bound, split=(), held_as=jnp.bfloat16):
    drawn = scale * jax.random.normal(stream_key, shape, jnp.float32)
    if split:
        drawn = drawn * steps_of(stream_key, shape, split, -0.22, 0.18)
    return jnp.clip(drawn, -bound, bound).astype(held_as)


def bell_draw_with(stream_key, shape, scale, reach, cuts, heavy, kind=jnp.bfloat16):
    drawn = scale * jax.random.normal(stream_key, shape, jnp.float32)
    if cuts:
        drawn = drawn * steps_of(stream_key, shape, cuts, -0.22, 0.18)
    return jnp.clip(with_spikes(drawn, jax.random.fold_in(stream_key, 3), *heavy), -reach, reach).astype(kind)


def setup_inputs(seed: int = 0) -> dict:
    arg_keys = jax.random.split(jax.random.key(seed), 18)
    return {
        "tokens": centred(arg_keys[0], (TOKENS, D), 1.0, 6.0, ((0, 32),)),
        "lengths": uneven_parts(arg_keys[1], IMAGES, TOKENS, IMG_MAX, 1).astype(jnp.int32),
        "adapter_choice": plant(jax.random.randint(arg_keys[2], (IMAGES,), 0, ADAPTERS), jax.random.fold_in(arg_keys[2], 1), 0, ADAPTERS - 1).astype(jnp.int32),
        "gain_rows": jnp.clip(1.0 + 0.18 * jax.random.normal(arg_keys[3], (4, D), jnp.float32), 0.099609375, 1.8984375).astype(jnp.bfloat16),
        "bias_rows": centred(arg_keys[4], (5, D), 0.3, 1.796875, ((1, 32),)),
        "query_key_value": centred(arg_keys[5], (D, 3 * D), D ** -0.5, 0.1875, ((0, 32),)),
        "output_weight": centred(arg_keys[6], (D, D), (D // 32) ** -0.5, 1.0, ((0, 32),)),
        "expand_weight": centred(arg_keys[7], (D, FF), D ** -0.5, 0.1875, ((0, 32),)),
        "expand_bias": centred(arg_keys[8], (FF,), 0.3, 1.796875, ((0, 32),)),
        "contract_weight": centred(arg_keys[9], (FF, D), FF ** -0.5, 0.09375, ((0, 32),)),
        "adapter_in_attention": centred(arg_keys[10], (4, D, ADAPTERS * RANK), D ** -0.5, 0.1875, ((1, 32),)),
        "adapter_out_attention": centred(arg_keys[11], (4, ADAPTERS * RANK, D), RANK ** -0.5, 1.5, ((2, 32),)),
        "adapter_in_expand": centred(arg_keys[12], (D, ADAPTERS * RANK), D ** -0.5, 0.1875, ((0, 32),)),
        "adapter_out_expand": centred(arg_keys[13], (ADAPTERS * RANK, FF), RANK ** -0.5, 1.5, ((1, 32),)),
        "adapter_in_contract": centred(arg_keys[14], (FF, ADAPTERS * RANK), FF ** -0.5, 0.09375, ((0, 32),)),
        "adapter_out_contract": centred(arg_keys[15], (ADAPTERS * RANK, D), RANK ** -0.5, 1.5, ((1, 32),)),
        "cotangent": bell_draw_with(arg_keys[16], (TOKENS, D), 1.0, 6.0, ((0, 32),), (0, 1, 32, 2.75)),
    }


epsilon = 1e-06

@jax.custom_vjp
def low(v):
    return lax.optimization_barrier(v.astype(jnp.bfloat16)).astype(jnp.float32)

@jax.custom_vjp
def low_back(v):
    return v

def low_keep(v):
    return (low(v), None)

def low_pass(kept, grad):
    return (grad,)

def back_keep(v):
    return (v, None)

def back_low(kept, grad):
    return (low(grad),)
low.defvjp(low_keep, low_pass)
low_back.defvjp(back_keep, back_low)

def product(first_operand, second_operand):
    return jnp.dot(first_operand, second_operand, precision=lax.Precision.HIGHEST, preferred_element_type=jnp.float32)

def layer_norm(inputs_row, gain_row, bias_row):
    center = inputs_row - lax.optimization_barrier(jnp.mean(inputs_row, axis=-1, keepdims=True))
    spread = lax.optimization_barrier(jnp.mean(center * center, axis=-1, keepdims=True))
    return center * lax.rsqrt(spread + epsilon) * gain_row + bias_row

def adapter_term(inputs_row, select, down_map, up_map):
    lowrank = low(low_back(product(inputs_row, down_map) * select))
    return product(lowrank, up_map)

def project_rows(frozen, adapters, token_rows, select):
    gain_rows, bias_rows, query_key_value = (frozen[0], frozen[1], frozen[2])
    adapter_in_attention, adapter_out_attention = (adapters[0], adapters[1])
    features = token_rows.shape[1]
    normed = low(layer_norm(token_rows, gain_rows[0], bias_rows[0]))
    pieces = [adapter_term(normed, select, adapter_in_attention[part_index], adapter_out_attention[part_index]) for part_index in range(3)]
    shifted = jnp.concatenate([bias_rows[1], jnp.zeros((2 * features,), jnp.float32)])
    return low(low_back(product(normed, query_key_value) + jnp.concatenate(pieces, axis=1) + shifted))

def finish_rows(frozen, adapters, token_rows, attended, select):
    gain_rows, bias_rows, query_key_value, output_weight, expand_weight, expand_bias, contract_weight = frozen
    adapter_in_attention, adapter_out_attention, adapter_in_expand, adapter_out_expand, adapter_in_contract, adapter_out_contract = adapters
    mixed = low_back(product(attended, output_weight) + bias_rows[2] + adapter_term(attended, select, adapter_in_attention[3], adapter_out_attention[3]))
    middle = token_rows + gain_rows[1] * mixed
    normed = low(layer_norm(middle, gain_rows[2], bias_rows[3]))
    hidden_pre = low_back(product(normed, expand_weight) + expand_bias + adapter_term(normed, select, adapter_in_expand, adapter_out_expand))
    active = low(jax.nn.gelu(hidden_pre, approximate=False))
    branch = low_back(product(active, contract_weight) + bias_rows[4] + adapter_term(active, select, adapter_in_contract, adapter_out_contract))
    return middle + gain_rows[3] * branch

def attend_block(query_rows, key_rows, value_rows, query_image, key_image):
    scores = low_back(product(query_rows, key_rows.T) * HEAD_DIM ** (-0.5))
    scores = jnp.where(query_image[:, None] == key_image[None, :], scores, -1e+30)
    highest = lax.optimization_barrier(jnp.max(scores, axis=1, keepdims=True))
    weights = jnp.exp(scores - highest)
    soft = weights / lax.optimization_barrier(jnp.sum(weights, axis=1, keepdims=True))
    return product(low(soft), value_rows)

def windows(source, filler, block_rows, hop_count):
    block_count = source.shape[0] // block_rows
    border = jnp.full((hop_count * block_rows,) + source.shape[1:], filler, source.dtype)
    padded = jnp.concatenate([border, source, border], axis=0)
    blocks = padded.reshape((block_count + 2 * hop_count, block_rows) + source.shape[1:])
    return jnp.concatenate([blocks[offset:offset + block_count] for offset in range(2 * hop_count + 1)], axis=1)

def attention(queries, keys, values, image_of):
    block_rows = math.gcd(TOKENS, 512)
    hop_count = (IMG_MAX - 2 + block_rows) // block_rows
    block_count = TOKENS // block_rows
    query_image = image_of.reshape(block_count, block_rows)
    key_image = windows(image_of, -1, block_rows, hop_count)

    def one_head(head_parts):
        query_head, key_head, value_head = head_parts
        key_windows = windows(key_head, 0.0, block_rows, hop_count)
        value_windows = windows(value_head, 0.0, block_rows, hop_count)
        return lax.map(jax.checkpoint(lambda group: attend_block(*group)), (query_head.reshape(block_count, block_rows, HEAD_DIM), key_windows, value_windows, query_image, key_image))

    def split_heads(matrix):
        return matrix.reshape(TOKENS, HEADS, HEAD_DIM).transpose(1, 0, 2)
    result = lax.map(jax.checkpoint(one_head), (split_heads(queries), split_heads(keys), split_heads(values)))
    return result.reshape(HEADS, TOKENS, HEAD_DIM).transpose(1, 0, 2).reshape(TOKENS, HEADS * HEAD_DIM)

def forward(token_rows, adapters, frozen, select, image_of):
    row_block = math.gcd(TOKENS, 4096)
    row_count = TOKENS // row_block
    features = token_rows.shape[1]

    def by_rows(matrix):
        return matrix.reshape((row_count, row_block) + matrix.shape[1:])
    projected = lax.map(jax.checkpoint(lambda group: project_rows(frozen, adapters, group[0], group[1])), (by_rows(token_rows), by_rows(select)))
    projected = projected.reshape(TOKENS, 3 * features)
    attended = low(low_back(attention(projected[:, :features], projected[:, features:2 * features], projected[:, 2 * features:], image_of)))
    finished = lax.map(jax.checkpoint(lambda group: finish_rows(frozen, adapters, group[0], group[1], group[2])), (by_rows(token_rows), by_rows(attended), by_rows(select)))
    return finished.reshape(TOKENS, features)

def reference(tokens, lengths, adapter_choice, gain_rows, bias_rows, query_key_value, output_weight, expand_weight, expand_bias, contract_weight, adapter_in_attention, adapter_out_attention, adapter_in_expand, adapter_out_expand, adapter_in_contract, adapter_out_contract, cotangent):
    image_ends = jnp.cumsum(lengths).astype(jnp.int32)
    places = jnp.arange(TOKENS, dtype=jnp.int32)
    image_of = lax.optimization_barrier(jnp.sum((places[:, None] >= image_ends[None, :]).astype(jnp.int32), axis=1)).astype(jnp.int32)
    chosen = adapter_choice[image_of]
    select = (jnp.arange(ADAPTERS * RANK, dtype=jnp.int32)[None, :] // RANK == chosen[:, None]).astype(jnp.float32)
    frozen = tuple((matrix.astype(jnp.float32) for matrix in (gain_rows, bias_rows, query_key_value, output_weight, expand_weight, expand_bias, contract_weight)))
    adapters = tuple((matrix.astype(jnp.float32) for matrix in (adapter_in_attention, adapter_out_attention, adapter_in_expand, adapter_out_expand, adapter_in_contract, adapter_out_contract)))
    result, pullback = jax.vjp(lambda token_rows, params: forward(token_rows, params, frozen, select, image_of), tokens.astype(jnp.float32), adapters)
    grad_tokens, grad_adapters = pullback(cotangent.astype(jnp.float32))
    return (result.astype(jnp.bfloat16), grad_tokens, grad_adapters[0], grad_adapters[1], grad_adapters[2], grad_adapters[3], grad_adapters[4], grad_adapters[5])
```

```python
import functools
import jax
import jax.numpy as jnp
from jax import lax
from jax.experimental import pallas as pl
from jax.experimental.pallas import tpu as pltpu
from jax.sharding import PartitionSpec as P

HEADS = 16
RANK = 16
HOPS = 6
EDGE = 1408
LONGEST = 1370


epsilon = 1e-06
float_type = jnp.float32
narrow_type = jnp.bfloat16


def passed_along(block, axis, distance):
    devices = range(lax.axis_size(axis))
    route = [(i - distance, i) for i in devices if i - distance in devices]
    return lax.ppermute(block, axis, route)


def layer_norm(inputs_row, gain_row, bias_row):
    center = inputs_row - jnp.mean(inputs_row, axis=-1, keepdims=True)
    scaling = lax.rsqrt(jnp.mean(center * center, axis=-1, keepdims=True) + epsilon)
    normal = center * scaling
    return (normal * gain_row + bias_row, normal, scaling)


def norm_backward(gradient, gain_row, normal, scaling):
    weighted = gradient * gain_row
    return scaling * (
        weighted
        - jnp.mean(weighted, axis=-1, keepdims=True)
        - normal * jnp.mean(weighted * normal, axis=-1, keepdims=True)
    )


def matmul(first_operand, second_operand):
    return jnp.dot(first_operand, second_operand, preferred_element_type=float_type)


def transposed_left(first_operand, second_operand):
    return lax.dot_general(
        first_operand, second_operand, (((0,), (0,)), ((), ())), preferred_element_type=float_type
    )


def transposed_right(first_operand, second_operand):
    return lax.dot_general(
        first_operand, second_operand, (((1,), (1,)), ((), ())), preferred_element_type=float_type
    )


def gelu_slope(hidden_pre):
    cumulative = 0.5 * (1.0 + lax.erf(hidden_pre * 0.7071067811865476))
    density = jnp.exp(-0.5 * hidden_pre * hidden_pre) * 0.3989422804014327
    return cumulative + hidden_pre * density


def general_layer(
    tokens,
    lengths,
    adapter_choice,
    gain_rows,
    bias_rows,
    query_key_value,
    output_weight,
    expand_weight,
    expand_bias,
    contract_weight,
    adapter_in_attention,
    adapter_out_attention,
    adapter_in_expand,
    adapter_out_expand,
    adapter_in_contract,
    adapter_out_contract,
    cotangent,
):
    gathered = (
        lax.all_gather(gain_rows, ("seq", "fsdp"), axis=1, tiled=True),
        lax.all_gather(bias_rows, ("seq", "fsdp"), axis=1, tiled=True),
        lax.all_gather(query_key_value, ("seq", "fsdp"), axis=0, tiled=True),
        lax.all_gather(output_weight, ("seq", "fsdp"), axis=0, tiled=True),
        lax.all_gather(expand_weight, ("seq", "fsdp"), axis=0, tiled=True),
        lax.all_gather(expand_bias, ("seq", "fsdp"), axis=0, tiled=True),
        lax.all_gather(contract_weight, ("seq", "fsdp"), axis=0, tiled=True),
        lax.all_gather(adapter_in_attention, ("seq", "fsdp"), axis=1, tiled=True),
        lax.all_gather(adapter_out_attention, ("seq", "fsdp"), axis=2, tiled=True),
        lax.all_gather(adapter_in_expand, ("seq", "fsdp"), axis=0, tiled=True),
        lax.all_gather(adapter_out_expand, ("seq", "fsdp"), axis=1, tiled=True),
        lax.all_gather(adapter_in_contract, ("seq", "fsdp"), axis=0, tiled=True),
        lax.all_gather(adapter_out_contract, ("seq", "fsdp"), axis=1, tiled=True),
    )
    (
        gains_full,
        biases_full,
        qkv_full,
        output_full,
        expand_full,
        expand_bias_full,
        contract_full,
        attention_down,
        attention_up,
        expand_down,
        expand_up,
        contract_down,
        contract_up,
    ) = gathered
    gains_wide = gains_full.astype(float_type)
    biases_wide = biases_full.astype(float_type)
    row_count, features = tokens.shape
    device_count = lax.axis_size(("seq", "fsdp"))
    position = lax.axis_index(("seq", "fsdp"))
    head_width = features // HEADS
    pair_width = 2 * head_width
    pair_count = HEADS // 2
    scaling_score = head_width ** (-0.5)
    rank_width = attention_down.shape[2]
    window_start = HOPS * row_count - EDGE
    window_rows = row_count + 2 * EDGE
    image_ends = jnp.cumsum(lengths)
    places = (
        position * row_count
        - HOPS * row_count
        + jnp.arange((2 * HOPS + 1) * row_count, dtype=jnp.int32)
    )
    image_of = jnp.sum((places[:, None] >= image_ends[None, :]).astype(jnp.int32), axis=1)
    image_of = jnp.where((places >= 0) & (places < device_count * row_count), image_of, -1)
    own_image = image_of[HOPS * row_count : (HOPS + 1) * row_count]
    key_image = image_of[window_start : window_start + window_rows]
    allowed = own_image[:, None] == key_image[None, :]
    matches = own_image[:, None] == jnp.arange(lengths.shape[0], dtype=jnp.int32)[None, :]
    chosen = jnp.sum(jnp.where(matches, adapter_choice[None, :], 0), axis=1)
    select = (jnp.arange(rank_width, dtype=jnp.int32)[None, :] // RANK == chosen[:, None]).astype(
        float_type
    )
    residual = tokens.astype(float_type)
    normed_first, normal_first, scaling_first = layer_norm(residual, gains_wide[0], biases_wide[0])
    normed_first = normed_first.astype(narrow_type)
    rank_qkv = (
        jnp.einsum(
            "td,pdr->tpr", normed_first, attention_down[:3], preferred_element_type=float_type
        )
        * select[:, None, :]
    ).astype(narrow_type)
    adapted_qkv = jnp.einsum(
        "tpr,prd->tpd", rank_qkv, attention_up[:3], preferred_element_type=float_type
    ).reshape(row_count, 3 * features)
    query_bias = jnp.concatenate([biases_wide[1], jnp.zeros((2 * features,), float_type)])
    projected = (matmul(normed_first, qkv_full) + adapted_qkv + query_bias).astype(narrow_type)
    queries = projected[:, :features]
    key_values = projected[:, features:]
    from_lower = []
    from_higher = []
    for distance in range(1, HOPS + 1):
        from_lower.append(passed_along(key_values, ("seq", "fsdp"), distance))
        from_higher.append(passed_along(key_values, ("seq", "fsdp"), -distance))
    beside_all = jnp.concatenate(from_lower[::-1] + [key_values] + from_higher, axis=0)
    window = beside_all[window_start : window_start + window_rows]

    def pair_slices(pair_index):
        offset = pair_index * pair_width
        query_part = lax.dynamic_slice_in_dim(queries, offset, pair_width, 1).reshape(
            row_count, 2, head_width
        )
        key_part = lax.dynamic_slice_in_dim(window, offset, pair_width, 1).reshape(
            window_rows, 2, head_width
        )
        value_part = lax.dynamic_slice_in_dim(window, features + offset, pair_width, 1).reshape(
            window_rows, 2, head_width
        )
        scores = (
            jnp.einsum("qhd,khd->hqk", query_part, key_part, preferred_element_type=float_type)
            * scaling_score
        )
        scores = jnp.where(allowed[None], scores, -1e30)
        return (query_part, key_part, value_part, scores)

    def pair_forward(pair_index):
        query_part, key_part, value_part, scores = pair_slices(pair_index)
        highest = jnp.max(scores, axis=2, keepdims=True)
        weights = jnp.exp(scores - highest)
        denominator = jnp.sum(weights, axis=2, keepdims=True)
        soft = (weights / denominator).astype(narrow_type)
        mixed_part = jnp.einsum("hqk,khd->qhd", soft, value_part, preferred_element_type=float_type)
        return (
            mixed_part.reshape(row_count, pair_width),
            (highest + jnp.log(denominator))[:, :, 0],
        )

    attended_pairs, log_totals = lax.map(pair_forward, jnp.arange(pair_count))
    attended = attended_pairs.transpose(1, 0, 2).reshape(row_count, features).astype(narrow_type)
    rank_out = (matmul(attended, attention_down[3]) * select).astype(narrow_type)
    mixed = matmul(attended, output_full) + biases_wide[2] + matmul(rank_out, attention_up[3])
    middle = residual + gains_wide[1] * mixed
    normed_second, normal_second, scaling_second = layer_norm(middle, gains_wide[2], biases_wide[3])
    normed_second = normed_second.astype(narrow_type)
    rank_expand = (matmul(normed_second, expand_down) * select).astype(narrow_type)
    hidden_pre = (
        matmul(normed_second, expand_full)
        + expand_bias_full.astype(float_type)
        + matmul(rank_expand, expand_up)
    )
    active = jax.nn.gelu(hidden_pre, approximate=False).astype(narrow_type)
    rank_contract = (matmul(active, contract_down) * select).astype(narrow_type)
    branch = matmul(active, contract_full) + biases_wide[4] + matmul(rank_contract, contract_up)
    result = (middle + gains_wide[3] * branch).astype(narrow_type)
    renewed = lax.optimization_barrier(
        (
            gain_rows,
            bias_rows,
            query_key_value,
            output_weight,
            expand_weight,
            expand_bias,
            contract_weight,
            adapter_in_attention,
            adapter_out_attention,
            adapter_in_expand,
            adapter_out_expand,
            adapter_in_contract,
            adapter_out_contract,
            cotangent,
        )
    )
    gathered = (
        lax.all_gather(renewed[0], ("seq", "fsdp"), axis=1, tiled=True),
        lax.all_gather(renewed[1], ("seq", "fsdp"), axis=1, tiled=True),
        lax.all_gather(renewed[2], ("seq", "fsdp"), axis=0, tiled=True),
        lax.all_gather(renewed[3], ("seq", "fsdp"), axis=0, tiled=True),
        lax.all_gather(renewed[4], ("seq", "fsdp"), axis=0, tiled=True),
        lax.all_gather(renewed[5], ("seq", "fsdp"), axis=0, tiled=True),
        lax.all_gather(renewed[6], ("seq", "fsdp"), axis=0, tiled=True),
        lax.all_gather(renewed[7], ("seq", "fsdp"), axis=1, tiled=True),
        lax.all_gather(renewed[8], ("seq", "fsdp"), axis=2, tiled=True),
        lax.all_gather(renewed[9], ("seq", "fsdp"), axis=0, tiled=True),
        lax.all_gather(renewed[10], ("seq", "fsdp"), axis=1, tiled=True),
        lax.all_gather(renewed[11], ("seq", "fsdp"), axis=0, tiled=True),
        lax.all_gather(renewed[12], ("seq", "fsdp"), axis=1, tiled=True),
    )
    (
        gains_full,
        biases_full,
        qkv_full,
        output_full,
        expand_full,
        expand_bias_full,
        contract_full,
        attention_down,
        attention_up,
        expand_down,
        expand_up,
        contract_down,
        contract_up,
    ) = gathered
    gains_wide = gains_full.astype(float_type)
    gradient_out = cotangent.astype(float_type)
    grad_branch = (gains_wide[3] * gradient_out).astype(narrow_type)
    grad_rank_contract = (transposed_right(grad_branch, contract_up) * select).astype(narrow_type)
    grad_contract_down = transposed_left(active, grad_rank_contract)
    grad_contract_up = transposed_left(rank_contract, grad_branch)
    grad_active = transposed_right(grad_branch, contract_full) + transposed_right(
        grad_rank_contract, contract_down
    )
    grad_hidden = (grad_active * gelu_slope(hidden_pre)).astype(narrow_type)
    grad_rank_expand = (transposed_right(grad_hidden, expand_up) * select).astype(narrow_type)
    grad_expand_down = transposed_left(normed_second, grad_rank_expand)
    grad_expand_up = transposed_left(rank_expand, grad_hidden)
    grad_normed_second = transposed_right(grad_hidden, expand_full) + transposed_right(
        grad_rank_expand, expand_down
    )
    grad_middle = gradient_out + norm_backward(
        grad_normed_second, gains_wide[2], normal_second, scaling_second
    )
    grad_mixed = (gains_wide[1] * grad_middle).astype(narrow_type)
    grad_rank_out = (transposed_right(grad_mixed, attention_up[3]) * select).astype(narrow_type)
    grad_out_down = transposed_left(attended, grad_rank_out)
    grad_out_up = transposed_left(rank_out, grad_mixed)
    grad_attended = (
        transposed_right(grad_mixed, output_full)
        + transposed_right(grad_rank_out, attention_down[3])
    ).astype(narrow_type)

    def pair_backward(pair_index):
        query_part, key_part, value_part, scores = pair_slices(pair_index)
        grad_part = lax.dynamic_slice_in_dim(
            grad_attended, pair_index * pair_width, pair_width, 1
        ).reshape(row_count, 2, head_width)
        log_pair = log_totals[pair_index]
        probable = jnp.exp(scores - log_pair[:, :, None])
        grad_probable = jnp.einsum(
            "qhd,khd->hqk", grad_part, value_part, preferred_element_type=float_type
        )
        grad_scores = probable * (
            grad_probable - jnp.sum(grad_probable * probable, axis=2, keepdims=True)
        )
        grad_scores = grad_scores.astype(narrow_type)
        grad_query = (
            jnp.einsum("hqk,khd->qhd", grad_scores, key_part, preferred_element_type=float_type)
            * scaling_score
        )
        grad_key = (
            jnp.einsum("hqk,qhd->khd", grad_scores, query_part, preferred_element_type=float_type)
            * scaling_score
        )
        grad_value = jnp.einsum(
            "hqk,qhd->khd",
            probable.astype(narrow_type),
            grad_part,
            preferred_element_type=float_type,
        )
        return (
            grad_query.reshape(row_count, pair_width),
            grad_key.reshape(window_rows, pair_width),
            grad_value.reshape(window_rows, pair_width),
        )

    grad_query_pairs, grad_key_pairs, grad_value_pairs = lax.map(
        pair_backward, jnp.arange(pair_count)
    )
    grad_queries = grad_query_pairs.transpose(1, 0, 2).reshape(row_count, features)
    grad_keys = grad_key_pairs.transpose(1, 0, 2).reshape(window_rows, features)
    grad_values = grad_value_pairs.transpose(1, 0, 2).reshape(window_rows, features)
    grad_window = jnp.concatenate([grad_keys, grad_values], axis=1)
    padded_grads = jnp.pad(grad_window, ((window_start, window_start), (0, 0)))
    grad_pairs = padded_grads[HOPS * row_count : (HOPS + 1) * row_count]
    for distance in range(1, HOPS + 1):
        lower_piece = padded_grads[
            (HOPS - distance) * row_count : (HOPS - distance + 1) * row_count
        ]
        higher_piece = padded_grads[
            (HOPS + distance) * row_count : (HOPS + distance + 1) * row_count
        ]
        grad_pairs = grad_pairs + passed_along(
            lower_piece.astype(jnp.bfloat16), ("seq", "fsdp"), -distance
        ).astype(lower_piece.dtype)
        grad_pairs = grad_pairs + passed_along(
            higher_piece.astype(jnp.bfloat16), ("seq", "fsdp"), distance
        ).astype(higher_piece.dtype)
    grad_projected = jnp.concatenate([grad_queries, grad_pairs], axis=1).astype(narrow_type)
    grad_blocks = grad_projected.reshape(row_count, 3, features)
    grad_rank_qkv = (
        jnp.einsum("tpd,prd->tpr", grad_blocks, attention_up[:3], preferred_element_type=float_type)
        * select[:, None, :]
    ).astype(narrow_type)
    grad_qkv_down = jnp.einsum(
        "td,tpr->pdr", normed_first, grad_rank_qkv, preferred_element_type=float_type
    )
    grad_qkv_up = jnp.einsum(
        "tpr,tpd->prd", rank_qkv, grad_blocks, preferred_element_type=float_type
    )
    grad_normed_first = transposed_right(grad_projected, qkv_full) + jnp.einsum(
        "tpr,pdr->td", grad_rank_qkv, attention_down[:3], preferred_element_type=float_type
    )
    input_gradient = grad_middle + norm_backward(
        grad_normed_first, gains_wide[0], normal_first, scaling_first
    )
    grad_attention_down = jnp.concatenate([grad_qkv_down, grad_out_down[None]], axis=0)
    grad_attention_up = jnp.concatenate([grad_qkv_up, grad_out_up[None]], axis=0)
    summed = (
        lax.psum_scatter(grad_attention_down, ("seq", "fsdp"), scatter_dimension=1, tiled=True),
        lax.psum_scatter(grad_attention_up, ("seq", "fsdp"), scatter_dimension=2, tiled=True),
        lax.psum_scatter(grad_expand_down, ("seq", "fsdp"), scatter_dimension=0, tiled=True),
        lax.psum_scatter(grad_expand_up, ("seq", "fsdp"), scatter_dimension=1, tiled=True),
        lax.psum_scatter(grad_contract_down, ("seq", "fsdp"), scatter_dimension=0, tiled=True),
        lax.psum_scatter(grad_contract_up, ("seq", "fsdp"), scatter_dimension=1, tiled=True),
    )
    return (
        result,
        input_gradient,
        summed[0],
        summed[1],
        summed[2],
        summed[3],
        summed[4],
        summed[5],
    )


MESH_ID = pl.DeviceIdType.MESH
CORES, SIDE_X, SIDE_Y = 1, 2, 4
ANYWHERE = pl.BlockSpec(memory_space=pl.ANY)
IN_VMEM = pl.BlockSpec(memory_space=pltpu.VMEM)
IN_SMEM = pl.BlockSpec(memory_space=pltpu.SMEM)


def place_here():
    return lax.axis_index("seq"), lax.axis_index("fsdp")


def remote(source, target, send, receive, seq, fsdp):
    return pltpu.make_async_remote_copy(
        src_ref=source,
        dst_ref=target,
        send_sem=send,
        recv_sem=receive,
        device_id=(seq, fsdp),
        device_id_type=MESH_ID,
    )


def greet(barrier, seq, fsdp):
    pl.semaphore_signal(barrier, 1, device_id=(seq, fsdp), device_id_type=MESH_ID)


def greet_neighbours(barrier, seq, fsdp, depth):
    for bit in (CORES, SIDE_X, SIDE_Y):
        greet(barrier, seq ^ bit, fsdp)
    for step in range(1, depth):
        greet(barrier, seq, lax.rem(fsdp + step, depth))


def gather_kernel(count, chunks, depth, *refs):
    shards, fulls, sems = refs[:count], refs[count : 2 * count], refs[2 * count :]
    send, receive, local = sems
    seq, fsdp = place_here()
    me = seq * depth + fsdp
    barrier = pltpu.get_barrier_semaphore()
    greet_neighbours(barrier, seq, fsdp, depth)
    own = [
        pltpu.make_async_copy(shard, full.at[me], local.at[i])
        for i, (shard, full) in enumerate(zip(shards, fulls))
    ]
    for copy in own:
        copy.start()
    pl.semaphore_wait(barrier, 3 + depth - 1)
    issued = []

    def go(source, target, index, seq_to, fsdp_to):
        copy = remote(source, target, send.at[index], receive.at[index], seq_to, fsdp_to)
        copy.start()
        issued.append(copy)
        return copy

    def group(chunk, at_seq):
        array, rows, columns, _ = chunk
        return fulls[array].at[pl.ds(at_seq * depth, depth), rows, columns]

    tick = [0]

    def fresh():
        tick[0] += 1
        return tick[0] - 1

    along_z = []
    for array, rows, columns, _ in chunks:
        waits = []
        for step in range(1, depth):
            waits.append(
                go(
                    shards[array].at[rows, columns],
                    fulls[array].at[me, rows, columns],
                    fresh(),
                    seq,
                    lax.rem(fsdp + step, depth),
                )
            )
        along_z.append(waits)
    for copy in own:
        copy.wait()
    second, third, last = [], [], []

    def to_core(chunk, at_seq):
        piece = group(chunk, at_seq)
        last.append(go(piece, piece, fresh(), seq ^ CORES, fsdp))

    for turn in range(len(chunks) + 2):
        if turn < len(chunks):
            chunk = chunks[turn]
            first_side = SIDE_X if chunk[3] else SIDE_Y
            for copy in along_z[turn]:
                copy.wait_recv()
            piece = group(chunk, seq)
            second.append(go(piece, piece, fresh(), seq ^ first_side, fsdp))
            to_core(chunk, seq)
        if 0 <= turn - 1 < len(chunks):
            chunk = chunks[turn - 1]
            first_side, other = (SIDE_X, SIDE_Y) if chunk[3] else (SIDE_Y, SIDE_X)
            mine = group(chunk, seq)
            third.append([go(mine, mine, fresh(), seq ^ other, fsdp)])
            second[turn - 1].wait_recv()
            piece = group(chunk, seq ^ first_side)
            third[-1].append(go(piece, piece, fresh(), seq ^ other, fsdp))
            to_core(chunk, seq ^ first_side)
        if 0 <= turn - 2 < len(chunks):
            chunk = chunks[turn - 2]
            first_side, other = (SIDE_X, SIDE_Y) if chunk[3] else (SIDE_Y, SIDE_X)
            for copy, at_seq in zip(third[turn - 2], (seq ^ other, seq ^ other ^ first_side)):
                copy.wait_recv()
                to_core(chunk, at_seq)
    for copy in last:
        copy.wait_recv()
    for copy in issued:
        copy.wait_send()


def gather_everything(shards, chunks, devices, depth, collective):
    copies = len(chunks) * ((depth - 1) + 1 + 2 + 4)
    return pl.pallas_call(
        functools.partial(gather_kernel, len(shards), chunks, depth),
        out_shape=tuple(jax.ShapeDtypeStruct((devices,) + a.shape, a.dtype) for a in shards),
        in_specs=[ANYWHERE] * len(shards),
        out_specs=tuple([ANYWHERE] * len(shards)),
        scratch_shapes=[
            pltpu.SemaphoreType.DMA((copies,)),
            pltpu.SemaphoreType.DMA((copies,)),
            pltpu.SemaphoreType.DMA((len(shards),)),
        ],
        compiler_params=pltpu.CompilerParams(collective_id=collective, has_side_effects=True),
    )(*shards)


def holder_of(head, core, depth):
    return lax.div(head, depth) * 2 + core, lax.rem(head, depth)


def to_heads_kernel(heads, depth, halo, x_ref, y_ref, send, receive, local):
    seq, fsdp = place_here()
    me = seq * depth + fsdp
    core, half = lax.rem(seq, 2), lax.div(seq, 4)
    head = lax.div(seq, 2) * depth + fsdp
    own = heads
    base = core * (own - halo)
    barrier = pltpu.get_barrier_semaphore()

    @pl.loop(0, heads)
    def _(k):
        source = core * own + k

        @pl.when(source != me)
        def _():
            greet(barrier, lax.div(source, depth), lax.rem(source, depth))

    if halo:
        greet(barrier, seq ^ CORES, fsdp)

    @pl.when(half == core)
    def _():
        pltpu.make_async_copy(x_ref.at[:, head], y_ref.at[me - base], local).start()

    pl.semaphore_wait(barrier, heads - (half == core).astype(jnp.int32) + (1 if halo else 0))
    target_slot = me - half * (own - halo)

    def piece(k):
        seq_to, fsdp_to = holder_of(k, half, depth)
        return remote(
            x_ref.at[:, k], y_ref.at[target_slot], send.at[k], receive.at[lax.rem(me, own)], seq_to, fsdp_to
        )

    @pl.loop(0, heads)
    def _(step):
        k = lax.rem(step + head, heads)

        @pl.when((k != head) | (half != core))
        def _():
            piece(k).start()

    @pl.loop(0, heads)
    def _(k):
        source = core * own + k

        @pl.when(source != me)
        def _():
            remote(
                x_ref.at[:, k], y_ref.at[source - base], send.at[k], receive.at[k], seq ^ CORES, fsdp
            ).wait_recv()

    @pl.when(half == core)
    def _():
        pltpu.make_async_copy(x_ref.at[:, head], y_ref.at[me - base], local).wait()

    if halo:
        here = (own - halo) - base
        there = (own - halo) + halo - base - (own - halo)
        first = jnp.where(core == 0, own - halo, own)
        source_slot = first - base
        other_slot = first - (own - halo) * (1 - core)
        over = remote(
            y_ref.at[pl.ds(source_slot, halo), 1:3],
            y_ref.at[pl.ds(other_slot, halo), 1:3],
            send.at[heads],
            receive.at[heads],
            seq ^ CORES,
            fsdp,
        )
        over.start()
        over.wait()

    @pl.loop(0, heads)
    def _(k):
        @pl.when((k != head) | (half != core))
        def _():
            piece(k).wait_send()


def to_heads(x, halo, depth, collective):
    parts, heads, width, rows = x.shape
    return pl.pallas_call(
        functools.partial(to_heads_kernel, heads, depth, halo),
        out_shape=jax.ShapeDtypeStruct((heads + halo, parts, width, rows), x.dtype),
        in_specs=[ANYWHERE],
        out_specs=ANYWHERE,
        scratch_shapes=[
            pltpu.SemaphoreType.DMA((heads + 1,)),
            pltpu.SemaphoreType.DMA((heads + 1,)),
            pltpu.SemaphoreType.DMA,
        ],
        compiler_params=pltpu.CompilerParams(collective_id=collective, has_side_effects=True),
    )(x)


def to_rows_kernel(heads, depth, x_ref, y_ref, send, receive, local):
    seq, fsdp = place_here()
    me = seq * depth + fsdp
    core, half = lax.rem(seq, 2), lax.div(seq, 4)
    head = lax.div(seq, 2) * depth + fsdp
    own = heads
    barrier = pltpu.get_barrier_semaphore()

    @pl.loop(0, heads)
    def _(k):
        seq_to, fsdp_to = holder_of(k, half, depth)

        @pl.when((k != head) | (half != core))
        def _():
            greet(barrier, seq_to, fsdp_to)

    @pl.when(half == core)
    def _():
        pltpu.make_async_copy(x_ref.at[me - core * own], y_ref.at[:, head], local).start()

    pl.semaphore_wait(barrier, heads - (half == core).astype(jnp.int32))

    def piece(k):
        target = core * own + k
        return remote(
            x_ref.at[k],
            y_ref.at[:, head],
            send.at[k],
            receive.at[head],
            lax.div(target, depth),
            lax.rem(target, depth),
        )

    @pl.loop(0, heads)
    def _(step):
        k = lax.rem(step + me, heads)

        @pl.when(core * own + k != me)
        def _():
            piece(k).start()

    @pl.loop(0, heads)
    def _(k):
        @pl.when((k != head) | (half != core))
        def _():
            remote(x_ref.at[0], y_ref.at[:, k], send.at[k], receive.at[k], seq ^ CORES, fsdp).wait_recv()

    @pl.when(half == core)
    def _():
        pltpu.make_async_copy(x_ref.at[me - core * own], y_ref.at[:, head], local).wait()

    @pl.loop(0, heads)
    def _(k):
        @pl.when(core * own + k != me)
        def _():
            piece(k).wait_send()


def to_rows(x, depth, collective):
    heads, parts, width, rows = x.shape
    return pl.pallas_call(
        functools.partial(to_rows_kernel, heads, depth),
        out_shape=jax.ShapeDtypeStruct((parts, heads, width, rows), x.dtype),
        in_specs=[ANYWHERE],
        out_specs=ANYWHERE,
        scratch_shapes=[
            pltpu.SemaphoreType.DMA((heads,)),
            pltpu.SemaphoreType.DMA((heads,)),
            pltpu.SemaphoreType.DMA,
        ],
        compiler_params=pltpu.CompilerParams(collective_id=collective, has_side_effects=True),
    )(x)


def to_rows_merged_kernel(heads, depth, halo, x_ref, h_ref, y_ref, merged, other, send, receive, local):
    seq, fsdp = place_here()
    me = seq * depth + fsdp
    core, half = lax.rem(seq, 2), lax.div(seq, 4)
    head = lax.div(seq, 2) * depth + fsdp
    own = heads
    barrier = pltpu.get_barrier_semaphore()
    greet(barrier, seq ^ CORES, fsdp)

    @pl.loop(0, heads)
    def _(k):
        seq_to, fsdp_to = holder_of(k, half, depth)

        @pl.when((k != head) | (half != core))
        def _():
            greet(barrier, seq_to, fsdp_to)

    pl.semaphore_wait(barrier, heads + 1 - (half == core).astype(jnp.int32))
    over = remote(h_ref, other, send.at[heads], receive.at[heads], seq ^ CORES, fsdp)
    over.start()

    def piece(k):
        target = core * own + k
        return remote(
            merged.at[k],
            y_ref.at[:, head],
            send.at[k],
            receive.at[head],
            lax.div(target, depth),
            lax.rem(target, depth),
        )

    def launch(k):
        @pl.when(core * own + k != me)
        def _():
            piece(k).start()

        @pl.when(core * own + k == me)
        def _():
            pltpu.make_async_copy(merged.at[k], y_ref.at[:, head], local).start()

    shared = jnp.where(core == 0, own - halo, 0)
    alone = jnp.where(core == 0, 0, halo)

    @pl.loop(0, own - halo)
    def _(step):
        k = alone + lax.rem(step + me, own - halo)
        merged[k] = x_ref[k]
        launch(k)

    over.wait_recv()

    @pl.loop(0, halo)
    def _(step):
        k = shared + step
        merged[k, 0] = x_ref[k, 0]
        for part in range(2):
            merged[k, 1 + part] = (
                x_ref[k, 1 + part].astype(float_type) + other[step, part].astype(float_type)
            ).astype(narrow_type)
        launch(k)

    @pl.loop(0, heads)
    def _(k):
        @pl.when((k != head) | (half != core))
        def _():
            remote(merged.at[0], y_ref.at[:, k], send.at[k], receive.at[k], seq ^ CORES, fsdp).wait_recv()

    @pl.when(half == core)
    def _():
        pltpu.make_async_copy(merged.at[0], y_ref.at[:, head], local).wait()

    @pl.loop(0, heads)
    def _(k):
        @pl.when(core * own + k != me)
        def _():
            piece(k).wait_send()

    over.wait_send()


def to_rows_merged(x, h, depth, collective):
    heads, parts, width, rows = x.shape
    return pl.pallas_call(
        functools.partial(to_rows_merged_kernel, heads, depth, h.shape[0]),
        out_shape=jax.ShapeDtypeStruct((parts, heads, width, rows), x.dtype),
        in_specs=[IN_VMEM, IN_VMEM],
        out_specs=ANYWHERE,
        scratch_shapes=[
            pltpu.VMEM(x.shape, x.dtype),
            pltpu.VMEM(h.shape, h.dtype),
            pltpu.SemaphoreType.DMA((heads + 1,)),
            pltpu.SemaphoreType.DMA((heads + 1,)),
            pltpu.SemaphoreType.DMA,
        ],
        compiler_params=pltpu.CompilerParams(
            collective_id=collective, has_side_effects=True, vmem_limit_bytes=24 << 20
        ),
    )(x, h)


def reduce_kernel(depth, g_ref, out_ref, first, second, third, fourth, send, receive):
    seq, fsdp = place_here()
    core, x, y = lax.rem(seq, 2), lax.rem(lax.div(seq, 2), 2), lax.div(seq, 4)
    barrier = pltpu.get_barrier_semaphore()
    greet_neighbours(barrier, seq, fsdp, depth)
    pl.semaphore_wait(barrier, 3 + depth - 1)
    rows = g_ref.shape[2]
    half = rows // 2
    halves = (pl.ds(0, half), pl.ds(half, half))
    tick = [0]
    issued = []

    def go(source, target, seq_to, fsdp_to):
        index = tick[0]
        tick[0] += 1
        copy = remote(source, target, send.at[index], receive.at[index], seq_to, fsdp_to)
        copy.start()
        issued.append(copy)
        return copy

    def add_into(target, other):
        @pl.loop(0, depth)
        def _(i):
            target[i] = (target[i].astype(float_type) + other[i].astype(float_type)).astype(narrow_type)

    copies = [go(g_ref.at[2 * t + 1 - core], first.at[t], seq ^ CORES, fsdp) for t in range(4)]
    for t in range(4):
        copies[t].wait_recv()
        add_into(first.at[t], g_ref.at[2 * t + core])
    over = [
        [go(first.at[2 * j + 1 - x, :, halves[0]], second.at[0, j], seq ^ SIDE_X, fsdp) for j in range(2)],
        [go(first.at[2 * (1 - y) + j, :, halves[1]], second.at[1, j], seq ^ SIDE_Y, fsdp) for j in range(2)],
    ]
    for j in range(2):
        over[0][j].wait_recv()
        add_into(second.at[0, j], first.at[2 * j + x, :, halves[0]])
        over[1][j].wait_recv()
        add_into(second.at[1, j], first.at[2 * y + j, :, halves[1]])
    last = [
        go(second.at[0, 1 - y], third.at[0], seq ^ SIDE_Y, fsdp),
        go(second.at[1, 1 - x], third.at[1], seq ^ SIDE_X, fsdp),
    ]
    last[0].wait_recv()
    add_into(third.at[0], second.at[0, y])
    last[1].wait_recv()
    add_into(third.at[1], second.at[1, x])
    finals = []
    for step in range(1, depth):
        to = lax.rem(fsdp + step, depth)
        for j in range(2):
            finals.append(go(third.at[j, to], fourth.at[j, step], seq, to))
    for copy in finals:
        copy.wait_recv()
    for j in range(2):
        total = third[j, fsdp].astype(float_type)
        for step in range(1, depth):
            total = total + fourth[j, step].astype(float_type)
        out_ref[halves[j]] = total
    for copy in issued:
        copy.wait_send()


def reduce_shards(g, depth, collective):
    seqs, _, rows, lanes = g.shape
    half = rows // 2
    copies = 4 + 4 + 2 + 2 * (depth - 1)
    return pl.pallas_call(
        functools.partial(reduce_kernel, depth),
        out_shape=jax.ShapeDtypeStruct((rows, lanes), float_type),
        in_specs=[IN_VMEM],
        out_specs=IN_VMEM,
        scratch_shapes=[
            pltpu.VMEM((4, depth, rows, lanes), g.dtype),
            pltpu.VMEM((2, 2, depth, half, lanes), g.dtype),
            pltpu.VMEM((2, depth, half, lanes), g.dtype),
            pltpu.VMEM((2, depth, half, lanes), g.dtype),
            pltpu.SemaphoreType.DMA((copies,)),
            pltpu.SemaphoreType.DMA((copies,)),
        ],
        compiler_params=pltpu.CompilerParams(
            collective_id=collective, has_side_effects=True, vmem_limit_bytes=32 << 20
        ),
    )(g)


BIG = 32768.0


def bounds(lens_ref, n, base_block, rows, i):
    first=(base_block+i)*rows; last=first+rows-1
    lo=jnp.int32(0); hi=jnp.int32(0); start=jnp.int32(0)
    for m in range(n):
        end=start+lens_ref[m]
        lo=jnp.where((start<=first)&(first<end),start,lo)
        hi=jnp.where((start<=last)&(last<end),end-1,hi)
        start=end
    return lax.div(lo,rows), lax.div(hi,rows)

def image_marks(lens_ref, n, marks, rows):
    r=lax.broadcasted_iota(jnp.int32,(marks,rows),0)
    st=jnp.full((marks,rows),1<<30,jnp.int32); en=jnp.zeros((marks,rows),jnp.int32)
    start=jnp.int32(0)
    for m in range(n):
        end=start+lens_ref[m]
        st=jnp.where(r==m,start,st); en=jnp.where(r==m,end,en)
        start=end
    return st,en

def fwd_kernel(n,own,slots,halo,rows,width,marks, lens_ref,x_ref,att_ref,lse_ref,o_ref,qa,ka):
    core=lax.rem(lax.axis_index("seq"),2)
    base=core*(own-halo)
    shift=core*halo
    st,en=image_marks(lens_ref,n,marks,rows)
    pos=lax.broadcasted_iota(jnp.int32,(marks,rows),1)
    def prep(s,_):
        p=pos+(base+s)*rows
        inside=(p>=st)&(p<en)
        oh=jnp.where(inside,1.0,0.0).astype(float_type)
        kt=jnp.concatenate([x_ref[s,1].astype(float_type),(oh-1.0)*BIG],axis=0)
        ka[s]=kt.T.astype(narrow_type)
        return 0
    lax.fori_loop(0,slots,prep,0)
    def one_q(i,_):
        s_q=i+shift
        p=pos+(base+s_q)*rows
        oh=jnp.where((p>=st)&(p<en),1.0,0.0).astype(narrow_type)
        q=jnp.concatenate([(x_ref[s_q,0].astype(float_type)*(width**-0.5)).astype(narrow_type),oh],axis=0)
        lo,hi=bounds(lens_ref,n,base+shift,rows,i)
        lo=lo-base; hi=hi-base
        def tile(m,l,o,s):
            sc=matmul(ka[s],q)
            m2=jnp.maximum(m,jnp.max(sc,axis=0,keepdims=True))
            pr=jnp.exp(sc-m2)
            al=jnp.exp(m-m2)
            return m2, l*al+jnp.sum(pr,axis=0,keepdims=True), o*al+matmul(x_ref[s,2],pr.astype(narrow_type))
        def tile2(m,l,o,s):
            sa=matmul(ka[s],q); sb=matmul(ka[s+1],q)
            m2=jnp.maximum(m,jnp.maximum(jnp.max(sa,axis=0,keepdims=True),jnp.max(sb,axis=0,keepdims=True)))
            pa=jnp.exp(sa-m2); pb=jnp.exp(sb-m2)
            al=jnp.exp(m-m2)
            l=l*al+jnp.sum(pa,axis=0,keepdims=True)+jnp.sum(pb,axis=0,keepdims=True)
            return m2,l,o*al+matmul(x_ref[s,2],pa.astype(narrow_type))+matmul(x_ref[s+1,2],pb.astype(narrow_type))
        m=jnp.full((1,rows),-1e30,float_type); l=jnp.zeros((1,rows),float_type); o=jnp.zeros((width,rows),float_type)
        cnt=hi-lo+1
        m,l,o=lax.fori_loop(0,cnt//2,lambda t,c: tile2(*c,lo+2*t),(m,l,o))
        m,l,o=lax.fori_loop(0,cnt%2,lambda t,c: tile(*c,hi),(m,l,o))
        o=o/l
        att_ref[i]=o.astype(narrow_type)
        o_ref[i]=o
        lse_ref[i]=jnp.broadcast_to(m+jnp.log(l),(8,rows))
        return 0
    lax.fori_loop(0,own,one_q,0)

def attention_forward(lengths,x,own,halo):
    slots,_,width,rows=x.shape
    n=lengths.shape[0]; marks=-(-n//16)*16
    V=pl.BlockSpec(memory_space=pltpu.VMEM)
    return pl.pallas_call(functools.partial(fwd_kernel,n,own,slots,halo,rows,width,marks),
        out_shape=(jax.ShapeDtypeStruct((own,width,rows),narrow_type),jax.ShapeDtypeStruct((own,8,rows),float_type),jax.ShapeDtypeStruct((own,width,rows),float_type)),
        in_specs=[pl.BlockSpec(memory_space=pltpu.SMEM),V],out_specs=(V,V,V),
        scratch_shapes=[pltpu.VMEM((width+marks,rows),narrow_type),pltpu.VMEM((slots,rows,width+marks),narrow_type)],
        compiler_params=pltpu.CompilerParams(vmem_limit_bytes=40<<20))(lengths,x)

def bwd_kernel(n,own,slots,halo,rows,width,marks, lens_ref,x_ref,g_ref,lse_ref,o_ref,dx_ref,dh_ref,ka,vv,qa,qn,gn,dd,dq):
    core=lax.rem(lax.axis_index("seq"),2)
    base=core*(own-halo); shift=core*halo
    st,en=image_marks(lens_ref,n,marks,rows)
    pos=lax.broadcasted_iota(jnp.int32,(marks,rows),1)
    def prep(s,_):
        p=pos+(base+s)*rows
        oh=jnp.where((p>=st)&(p<en),1.0,0.0).astype(float_type)
        kt=jnp.concatenate([x_ref[s,1].astype(float_type),(oh-1.0)*BIG],axis=0)
        ka[s]=kt.T.astype(narrow_type)
        vv[s]=x_ref[s,2].astype(float_type).T.astype(narrow_type)
        return 0
    lax.fori_loop(0,slots,prep,0)
    def prepq(i,_):
        s=i+shift
        p=pos+(base+s)*rows
        oh=jnp.where((p>=st)&(p<en),1.0,0.0).astype(narrow_type)
        qs=x_ref[s,0].astype(float_type)*(width**-0.5)
        qa[i]=jnp.concatenate([qs.astype(narrow_type),oh],axis=0)
        qn[i]=qs.T.astype(narrow_type)
        g=g_ref[i].astype(float_type)
        gn[i]=g.T.astype(narrow_type)
        dd[i]=jnp.broadcast_to(jnp.sum(g*o_ref[i],axis=0,keepdims=True),(8,rows))
        dq[i]=jnp.zeros((width,rows),float_type)
        return 0
    lax.fori_loop(0,own,prepq,0)
    def one_k(s,_):
        lo,hi=bounds(lens_ref,n,base,rows,s)
        lo=jnp.maximum(lo-base-shift,0); hi=jnp.minimum(hi-base-shift,own-1)
        kt=x_ref[s,1]
        def tile(i,dk,dv):
            sc=matmul(ka[s],qa[i])
            pr=jnp.exp(sc-lse_ref[i][0:1])
            dp=matmul(vv[s],g_ref[i])
            ds=(pr*(dp-dd[i][0:1])).astype(narrow_type)
            dq[i]+=matmul(kt,ds)
            return dk+matmul(ds,qn[i]), dv+matmul(pr.astype(narrow_type),gn[i])
        z=jnp.zeros((rows,width),float_type)
        cnt=jnp.maximum(hi-lo+1,0)
        def two(t,c):
            c=tile(lo+2*t,*c)
            return tile(lo+2*t+1,*c)
        dk,dv=lax.fori_loop(0,cnt//2,two,(z,z))
        dk,dv=lax.fori_loop(0,cnt%2,lambda t,c: tile(hi,*c),(dk,dv))
        i=s-shift
        @pl.when((i>=0)&(i<own))
        def _():
            dx_ref[i,1]=dk.T.astype(narrow_type)
            dx_ref[i,2]=dv.T.astype(narrow_type)
        @pl.when((i<0)|(i>=own))
        def _():
            j=jnp.where(i<0,s,i-own)
            dh_ref[j,0]=dk.T.astype(narrow_type)
            dh_ref[j,1]=dv.T.astype(narrow_type)
        return 0
    lax.fori_loop(0,slots,one_k,0)
    def fin(i,_):
        dx_ref[i,0]=(dq[i]*(width**-0.5)).astype(narrow_type)
        return 0
    lax.fori_loop(0,own,fin,0)

def attention_backward(lengths,x,g,lse,o,own,halo):
    slots,_,width,rows=x.shape
    n=lengths.shape[0]; marks=-(-n//16)*16
    V=pl.BlockSpec(memory_space=pltpu.VMEM)
    return pl.pallas_call(functools.partial(bwd_kernel,n,own,slots,halo,rows,width,marks),
        out_shape=(jax.ShapeDtypeStruct((own,3,width,rows),narrow_type),jax.ShapeDtypeStruct((halo,2,width,rows),narrow_type)),
        in_specs=[pl.BlockSpec(memory_space=pltpu.SMEM),V,V,V,V],out_specs=(V,V),
        scratch_shapes=[pltpu.VMEM((slots,rows,width+marks),narrow_type),pltpu.VMEM((slots,rows,width),narrow_type),
          pltpu.VMEM((own,width+marks,rows),narrow_type),pltpu.VMEM((own,rows,width),narrow_type),pltpu.VMEM((own,rows,width),narrow_type),
          pltpu.VMEM((own,8,rows),float_type),pltpu.VMEM((own,width,rows),float_type)],
        compiler_params=pltpu.CompilerParams(vmem_limit_bytes=48<<20))(lengths,x,g,lse,o)


def layer_on_slice(
    tokens,
    lengths,
    adapter_choice,
    gain_rows,
    bias_rows,
    query_key_value,
    output_weight,
    expand_weight,
    expand_bias,
    contract_weight,
    adapter_in_attention,
    adapter_out_attention,
    adapter_in_expand,
    adapter_out_expand,
    adapter_in_contract,
    adapter_out_contract,
    cotangent,
):
    row_count, features = tokens.shape
    depth = lax.axis_size("fsdp")
    devices = lax.axis_size(("seq", "fsdp"))
    position = lax.axis_index(("seq", "fsdp"))
    own = devices // 2
    head_width = features // HEADS
    rank_width = adapter_in_attention.shape[2]
    share = features // devices
    hidden_share = contract_weight.shape[0]
    halo = -(-(LONGEST - 1) // row_count)

    vectors = jnp.concatenate([gain_rows.T, bias_rows.T, expand_bias.reshape(share, -1)], axis=1)
    vectors = jnp.pad(vectors, ((0, 0), (0, rank_width - vectors.shape[1])))
    pieces = (
        adapter_in_attention.reshape(4 * share, rank_width),
        adapter_out_attention.transpose(0, 2, 1).reshape(4 * share, rank_width),
        adapter_in_expand,
        adapter_out_expand.T,
        adapter_in_contract,
        adapter_out_contract.T,
        vectors,
    )
    offsets = [0]
    for piece in pieces:
        offsets.append(offsets[-1] + piece.shape[0])
    packed = jnp.concatenate(pieces, axis=0)
    shards = (packed, query_key_value, output_weight, expand_weight, contract_weight)
    chunks = []
    for array in (0, 1, 2, 3, 4):
        rows, columns = shards[array].shape
        for which in range(2):
            if columns > rank_width:
                half = columns // 2
                chunks.append((array, slice(0, rows), slice(which * half, (which + 1) * half), which))
            else:
                half = rows // 2
                chunks.append((array, slice(which * half, (which + 1) * half), slice(0, columns), which))
    packed_full, qkv_full, output_full, expand_full, contract_full = gather_everything(
        shards, chunks, devices, depth, 1
    )
    qkv_full = qkv_full.reshape(features, 3 * features)
    output_full = output_full.reshape(features, features)
    expand_full = expand_full.reshape(features, -1)
    contract_full = contract_full.reshape(-1, features)
    parts = [packed_full[:, a:b] for a, b in zip(offsets[:-1], offsets[1:])]

    def four(part):
        return (
            part.reshape(devices, 4, share, rank_width).transpose(1, 0, 2, 3).reshape(4, features, rank_width)
        )

    attention_down, attention_up = four(parts[0]), four(parts[1])
    expand_down, expand_up, contract_down, contract_up = (
        part.reshape(-1, rank_width) for part in parts[2:6]
    )
    vectors = parts[6].reshape(features, rank_width).astype(float_type)
    gains_wide = vectors[:, :4].T
    biases_wide = vectors[:, 4:9].T
    expand_bias_wide = vectors[:, 9 : 9 + hidden_share // share].reshape(-1)

    image_ends = jnp.cumsum(lengths)
    places = position * row_count + jnp.arange(row_count, dtype=jnp.int32)
    own_image = jnp.sum((places[:, None] >= image_ends[None, :]).astype(jnp.int32), axis=1)
    matches = own_image[:, None] == jnp.arange(lengths.shape[0], dtype=jnp.int32)[None, :]
    chosen = jnp.sum(jnp.where(matches, adapter_choice[None, :], 0), axis=1)
    select = (jnp.arange(rank_width, dtype=jnp.int32)[None, :] // RANK == chosen[:, None]).astype(float_type)

    residual = tokens.astype(float_type)
    normed_first, normal_first, scaling_first = layer_norm(residual, gains_wide[0], biases_wide[0])
    normed_first = normed_first.astype(narrow_type)
    rank_qkv = [
        (matmul(normed_first, attention_down[p]) * select).astype(narrow_type) for p in range(3)
    ]
    adapted = jnp.concatenate([transposed_right(attention_up[p], rank_qkv[p]) for p in range(3)], axis=0)
    query_bias = jnp.concatenate([biases_wide[1], jnp.zeros((2 * features,), float_type)])
    projected = lax.dot_general(
        qkv_full, normed_first, (((0,), (1,)), ((), ())), preferred_element_type=float_type
    )
    projected = (projected + adapted + query_bias[:, None]).astype(narrow_type)
    on_heads = to_heads(projected.reshape(3, HEADS, head_width, row_count), halo, depth, 2)
    attended_blocks, log_totals, attended_wide = attention_forward(lengths, on_heads, own, halo)
    attended = to_rows(attended_blocks[:, None], depth, 3).reshape(features, row_count)

    rank_out = (transposed_left(attended, attention_down[3]) * select).astype(narrow_type)
    mixed = (
        transposed_left(attended, output_full)
        + biases_wide[2]
        + transposed_right(rank_out, attention_up[3])
    )
    middle = residual + gains_wide[1] * mixed
    normed_second, normal_second, scaling_second = layer_norm(middle, gains_wide[2], biases_wide[3])
    normed_second = normed_second.astype(narrow_type)
    rank_expand = (matmul(normed_second, expand_down) * select).astype(narrow_type)
    hidden_pre = (
        matmul(normed_second, expand_full)
        + expand_bias_wide
        + transposed_right(rank_expand, expand_up)
    )
    active = jax.nn.gelu(hidden_pre, approximate=False).astype(narrow_type)
    rank_contract = (matmul(active, contract_down) * select).astype(narrow_type)
    branch = (
        matmul(active, contract_full) + biases_wide[4] + transposed_right(rank_contract, contract_up)
    )
    result = (middle + gains_wide[3] * branch).astype(narrow_type)

    gradient_out = cotangent.astype(float_type)
    grad_branch = (gains_wide[3] * gradient_out).astype(narrow_type)
    grad_rank_contract = (matmul(grad_branch, contract_up) * select).astype(narrow_type)
    grad_contract_down = transposed_left(active, grad_rank_contract)
    grad_contract_up = transposed_left(grad_branch, rank_contract)
    grad_active = transposed_right(grad_branch, contract_full) + transposed_right(
        grad_rank_contract, contract_down
    )
    grad_hidden = (grad_active * gelu_slope(hidden_pre)).astype(narrow_type)
    grad_rank_expand = (matmul(grad_hidden, expand_up) * select).astype(narrow_type)
    grad_expand_down = transposed_left(normed_second, grad_rank_expand)
    grad_expand_up = transposed_left(grad_hidden, rank_expand)
    grad_normed_second = transposed_right(grad_hidden, expand_full) + transposed_right(
        grad_rank_expand, expand_down
    )
    grad_middle = gradient_out + norm_backward(
        grad_normed_second, gains_wide[2], normal_second, scaling_second
    )
    grad_mixed = (gains_wide[1] * grad_middle).astype(narrow_type)
    grad_rank_out = (matmul(grad_mixed, attention_up[3]) * select).astype(narrow_type)
    grad_out_down = matmul(attended, grad_rank_out)
    grad_out_up = transposed_left(grad_mixed, rank_out)
    grad_attended = (
        transposed_right(output_full, grad_mixed) + transposed_right(attention_down[3], grad_rank_out)
    ).astype(narrow_type)
    grad_on_heads = to_heads(
        grad_attended.reshape(1, HEADS, head_width, row_count), 0, depth, 4
    ).reshape(own, head_width, row_count)
    grad_blocks, grad_halo = attention_backward(
        lengths, on_heads, grad_on_heads, log_totals, attended_wide, own, halo
    )
    grad_projected = to_rows_merged(grad_blocks, grad_halo, depth, 5).reshape(3, features, row_count)

    grad_rank_qkv = [
        (transposed_left(grad_projected[p], attention_up[p]) * select).astype(narrow_type)
        for p in range(3)
    ]
    grad_down = [transposed_left(normed_first, grad_rank_qkv[p]) for p in range(3)] + [grad_out_down]
    grad_up = [matmul(grad_projected[p], rank_qkv[p]) for p in range(3)] + [grad_out_up]
    grad_normed_first = lax.dot_general(
        grad_projected.reshape(3 * features, row_count),
        qkv_full,
        (((0,), (1,)), ((), ())),
        preferred_element_type=float_type,
    )
    for p in range(3):
        grad_normed_first = grad_normed_first + transposed_right(grad_rank_qkv[p], attention_down[p])
    input_gradient = grad_middle + norm_backward(
        grad_normed_first, gains_wide[0], normal_first, scaling_first
    )

    terms = jnp.concatenate(
        [
            grad.astype(narrow_type).reshape(devices, -1, rank_width)
            for grad in grad_down
            + grad_up
            + [grad_expand_down, grad_expand_up, grad_contract_down, grad_contract_up]
        ],
        axis=1,
    )
    total = reduce_shards(terms.reshape(devices // depth, depth, -1, rank_width), depth, 6)
    shares = [total[a:b] for a, b in zip(offsets[:-1], offsets[1:-1])]
    return (
        result,
        input_gradient,
        shares[0].reshape(4, share, rank_width),
        shares[1].reshape(4, share, rank_width).transpose(0, 2, 1),
        shares[2],
        shares[3].T,
        shares[4],
        shares[5].T,
    )


def solution(mesh):
    per_device = layer_on_slice if dict(mesh.shape) == {"seq": 8, "fsdp": 4} else general_layer
    placed = (
        P(("seq", "fsdp"), None),
        P(),
        P(),
        P(None, ("seq", "fsdp")),
        P(None, ("seq", "fsdp")),
        P(("seq", "fsdp"), None),
        P(("seq", "fsdp"), None),
        P(("seq", "fsdp"), None),
        P(("seq", "fsdp")),
        P(("seq", "fsdp"), None),
        P(None, ("seq", "fsdp"), None),
        P(None, None, ("seq", "fsdp")),
        P(("seq", "fsdp"), None),
        P(None, ("seq", "fsdp")),
        P(("seq", "fsdp"), None),
        P(None, ("seq", "fsdp")),
        P(("seq", "fsdp"), None),
    )
    return jax.shard_map(
        per_device,
        mesh=mesh,
        in_specs=placed,
        out_specs=(
            P(("seq", "fsdp"), None),
            P(("seq", "fsdp"), None),
            P(None, ("seq", "fsdp"), None),
            P(None, None, ("seq", "fsdp")),
            P(("seq", "fsdp"), None),
            P(None, ("seq", "fsdp")),
            P(("seq", "fsdp"), None),
            P(None, ("seq", "fsdp")),
        ),
        check_vma=False,
    )
```

```python
import functools
import jax
import jax.numpy as jnp
from jax import lax
from jax.experimental import pallas as pl
from jax.experimental.pallas import tpu as pltpu
from jax.sharding import PartitionSpec as P

HEADS = 16
RANK = 16
HOPS = 6
EDGE = 1408
LONGEST = 1370


epsilon = 1e-06
float_type = jnp.float32
narrow_type = jnp.bfloat16


def passed_along(block, axis, distance):
    devices = range(lax.axis_size(axis))
    route = [(i - distance, i) for i in devices if i - distance in devices]
    return lax.ppermute(block, axis, route)


def layer_norm(inputs_row, gain_row, bias_row):
    center = inputs_row - jnp.mean(inputs_row, axis=-1, keepdims=True)
    scaling = lax.rsqrt(jnp.mean(center * center, axis=-1, keepdims=True) + epsilon)
    normal = center * scaling
    return (normal * gain_row + bias_row, normal, scaling)


def norm_backward(gradient, gain_row, normal, scaling):
    weighted = gradient * gain_row
    return scaling * (
        weighted
        - jnp.mean(weighted, axis=-1, keepdims=True)
        - normal * jnp.mean(weighted * normal, axis=-1, keepdims=True)
    )


def matmul(first_operand, second_operand):
    return jnp.dot(first_operand, second_operand, preferred_element_type=float_type)


def transposed_left(first_operand, second_operand):
    return lax.dot_general(
        first_operand, second_operand, (((0,), (0,)), ((), ())), preferred_element_type=float_type
    )


def transposed_right(first_operand, second_operand):
    return lax.dot_general(
        first_operand, second_operand, (((1,), (1,)), ((), ())), preferred_element_type=float_type
    )


def gelu_slope(hidden_pre):
    cumulative = 0.5 * (1.0 + lax.erf(hidden_pre * 0.7071067811865476))
    density = jnp.exp(-0.5 * hidden_pre * hidden_pre) * 0.3989422804014327
    return cumulative + hidden_pre * density


def general_layer(
    tokens,
    lengths,
    adapter_choice,
    gain_rows,
    bias_rows,
    query_key_value,
    output_weight,
    expand_weight,
    expand_bias,
    contract_weight,
    adapter_in_attention,
    adapter_out_attention,
    adapter_in_expand,
    adapter_out_expand,
    adapter_in_contract,
    adapter_out_contract,
    cotangent,
):
    gathered = (
        lax.all_gather(gain_rows, ("seq", "fsdp"), axis=1, tiled=True),
        lax.all_gather(bias_rows, ("seq", "fsdp"), axis=1, tiled=True),
        lax.all_gather(query_key_value, ("seq", "fsdp"), axis=0, tiled=True),
        lax.all_gather(output_weight, ("seq", "fsdp"), axis=0, tiled=True),
        lax.all_gather(expand_weight, ("seq", "fsdp"), axis=0, tiled=True),
        lax.all_gather(expand_bias, ("seq", "fsdp"), axis=0, tiled=True),
        lax.all_gather(contract_weight, ("seq", "fsdp"), axis=0, tiled=True),
        lax.all_gather(adapter_in_attention, ("seq", "fsdp"), axis=1, tiled=True),
        lax.all_gather(adapter_out_attention, ("seq", "fsdp"), axis=2, tiled=True),
        lax.all_gather(adapter_in_expand, ("seq", "fsdp"), axis=0, tiled=True),
        lax.all_gather(adapter_out_expand, ("seq", "fsdp"), axis=1, tiled=True),
        lax.all_gather(adapter_in_contract, ("seq", "fsdp"), axis=0, tiled=True),
        lax.all_gather(adapter_out_contract, ("seq", "fsdp"), axis=1, tiled=True),
    )
    (
        gains_full,
        biases_full,
        qkv_full,
        output_full,
        expand_full,
        expand_bias_full,
        contract_full,
        attention_down,
        attention_up,
        expand_down,
        expand_up,
        contract_down,
        contract_up,
    ) = gathered
    gains_wide = gains_full.astype(float_type)
    biases_wide = biases_full.astype(float_type)
    row_count, features = tokens.shape
    device_count = lax.axis_size(("seq", "fsdp"))
    position = lax.axis_index(("seq", "fsdp"))
    head_width = features // HEADS
    pair_width = 2 * head_width
    pair_count = HEADS // 2
    scaling_score = head_width ** (-0.5)
    rank_width = attention_down.shape[2]
    window_start = HOPS * row_count - EDGE
    window_rows = row_count + 2 * EDGE
    image_ends = jnp.cumsum(lengths)
    places = (
        position * row_count
        - HOPS * row_count
        + jnp.arange((2 * HOPS + 1) * row_count, dtype=jnp.int32)
    )
    image_of = jnp.sum((places[:, None] >= image_ends[None, :]).astype(jnp.int32), axis=1)
    image_of = jnp.where((places >= 0) & (places < device_count * row_count), image_of, -1)
    own_image = image_of[HOPS * row_count : (HOPS + 1) * row_count]
    key_image = image_of[window_start : window_start + window_rows]
    allowed = own_image[:, None] == key_image[None, :]
    matches = own_image[:, None] == jnp.arange(lengths.shape[0], dtype=jnp.int32)[None, :]
    chosen = jnp.sum(jnp.where(matches, adapter_choice[None, :], 0), axis=1)
    select = (jnp.arange(rank_width, dtype=jnp.int32)[None, :] // RANK == chosen[:, None]).astype(
        float_type
    )
    residual = tokens.astype(float_type)
    normed_first, normal_first, scaling_first = layer_norm(residual, gains_wide[0], biases_wide[0])
    normed_first = normed_first.astype(narrow_type)
    rank_qkv = (
        jnp.einsum(
            "td,pdr->tpr", normed_first, attention_down[:3], preferred_element_type=float_type
        )
        * select[:, None, :]
    ).astype(narrow_type)
    adapted_qkv = jnp.einsum(
        "tpr,prd->tpd", rank_qkv, attention_up[:3], preferred_element_type=float_type
    ).reshape(row_count, 3 * features)
    query_bias = jnp.concatenate([biases_wide[1], jnp.zeros((2 * features,), float_type)])
    projected = (matmul(normed_first, qkv_full) + adapted_qkv + query_bias).astype(narrow_type)
    queries = projected[:, :features]
    key_values = projected[:, features:]
    from_lower = []
    from_higher = []
    for distance in range(1, HOPS + 1):
        from_lower.append(passed_along(key_values, ("seq", "fsdp"), distance))
        from_higher.append(passed_along(key_values, ("seq", "fsdp"), -distance))
    beside_all = jnp.concatenate(from_lower[::-1] + [key_values] + from_higher, axis=0)
    window = beside_all[window_start : window_start + window_rows]

    def pair_slices(pair_index):
        offset = pair_index * pair_width
        query_part = lax.dynamic_slice_in_dim(queries, offset, pair_width, 1).reshape(
            row_count, 2, head_width
        )
        key_part = lax.dynamic_slice_in_dim(window, offset, pair_width, 1).reshape(
            window_rows, 2, head_width
        )
        value_part = lax.dynamic_slice_in_dim(window, features + offset, pair_width, 1).reshape(
            window_rows, 2, head_width
        )
        scores = (
            jnp.einsum("qhd,khd->hqk", query_part, key_part, preferred_element_type=float_type)
            * scaling_score
        )
        scores = jnp.where(allowed[None], scores, -1e30)
        return (query_part, key_part, value_part, scores)

    def pair_forward(pair_index):
        query_part, key_part, value_part, scores = pair_slices(pair_index)
        highest = jnp.max(scores, axis=2, keepdims=True)
        weights = jnp.exp(scores - highest)
        denominator = jnp.sum(weights, axis=2, keepdims=True)
        soft = (weights / denominator).astype(narrow_type)
        mixed_part = jnp.einsum("hqk,khd->qhd", soft, value_part, preferred_element_type=float_type)
        return (
            mixed_part.reshape(row_count, pair_width),
            (highest + jnp.log(denominator))[:, :, 0],
        )

    attended_pairs, log_totals = lax.map(pair_forward, jnp.arange(pair_count))
    attended = attended_pairs.transpose(1, 0, 2).reshape(row_count, features).astype(narrow_type)
    rank_out = (matmul(attended, attention_down[3]) * select).astype(narrow_type)
    mixed = matmul(attended, output_full) + biases_wide[2] + matmul(rank_out, attention_up[3])
    middle = residual + gains_wide[1] * mixed
    normed_second, normal_second, scaling_second = layer_norm(middle, gains_wide[2], biases_wide[3])
    normed_second = normed_second.astype(narrow_type)
    rank_expand = (matmul(normed_second, expand_down) * select).astype(narrow_type)
    hidden_pre = (
        matmul(normed_second, expand_full)
        + expand_bias_full.astype(float_type)
        + matmul(rank_expand, expand_up)
    )
    active = jax.nn.gelu(hidden_pre, approximate=False).astype(narrow_type)
    rank_contract = (matmul(active, contract_down) * select).astype(narrow_type)
    branch = matmul(active, contract_full) + biases_wide[4] + matmul(rank_contract, contract_up)
    result = (middle + gains_wide[3] * branch).astype(narrow_type)
    renewed = lax.optimization_barrier(
        (
            gain_rows,
            bias_rows,
            query_key_value,
            output_weight,
            expand_weight,
            expand_bias,
            contract_weight,
            adapter_in_attention,
            adapter_out_attention,
            adapter_in_expand,
            adapter_out_expand,
            adapter_in_contract,
            adapter_out_contract,
            cotangent,
        )
    )
    gathered = (
        lax.all_gather(renewed[0], ("seq", "fsdp"), axis=1, tiled=True),
        lax.all_gather(renewed[1], ("seq", "fsdp"), axis=1, tiled=True),
        lax.all_gather(renewed[2], ("seq", "fsdp"), axis=0, tiled=True),
        lax.all_gather(renewed[3], ("seq", "fsdp"), axis=0, tiled=True),
        lax.all_gather(renewed[4], ("seq", "fsdp"), axis=0, tiled=True),
        lax.all_gather(renewed[5], ("seq", "fsdp"), axis=0, tiled=True),
        lax.all_gather(renewed[6], ("seq", "fsdp"), axis=0, tiled=True),
        lax.all_gather(renewed[7], ("seq", "fsdp"), axis=1, tiled=True),
        lax.all_gather(renewed[8], ("seq", "fsdp"), axis=2, tiled=True),
        lax.all_gather(renewed[9], ("seq", "fsdp"), axis=0, tiled=True),
        lax.all_gather(renewed[10], ("seq", "fsdp"), axis=1, tiled=True),
        lax.all_gather(renewed[11], ("seq", "fsdp"), axis=0, tiled=True),
        lax.all_gather(renewed[12], ("seq", "fsdp"), axis=1, tiled=True),
    )
    (
        gains_full,
        biases_full,
        qkv_full,
        output_full,
        expand_full,
        expand_bias_full,
        contract_full,
        attention_down,
        attention_up,
        expand_down,
        expand_up,
        contract_down,
        contract_up,
    ) = gathered
    gains_wide = gains_full.astype(float_type)
    gradient_out = cotangent.astype(float_type)
    grad_branch = (gains_wide[3] * gradient_out).astype(narrow_type)
    grad_rank_contract = (transposed_right(grad_branch, contract_up) * select).astype(narrow_type)
    grad_contract_down = transposed_left(active, grad_rank_contract)
    grad_contract_up = transposed_left(rank_contract, grad_branch)
    grad_active = transposed_right(grad_branch, contract_full) + transposed_right(
        grad_rank_contract, contract_down
    )
    grad_hidden = (grad_active * gelu_slope(hidden_pre)).astype(narrow_type)
    grad_rank_expand = (transposed_right(grad_hidden, expand_up) * select).astype(narrow_type)
    grad_expand_down = transposed_left(normed_second, grad_rank_expand)
    grad_expand_up = transposed_left(rank_expand, grad_hidden)
    grad_normed_second = transposed_right(grad_hidden, expand_full) + transposed_right(
        grad_rank_expand, expand_down
    )
    grad_middle = gradient_out + norm_backward(
        grad_normed_second, gains_wide[2], normal_second, scaling_second
    )
    grad_mixed = (gains_wide[1] * grad_middle).astype(narrow_type)
    grad_rank_out = (transposed_right(grad_mixed, attention_up[3]) * select).astype(narrow_type)
    grad_out_down = transposed_left(attended, grad_rank_out)
    grad_out_up = transposed_left(rank_out, grad_mixed)
    grad_attended = (
        transposed_right(grad_mixed, output_full)
        + transposed_right(grad_rank_out, attention_down[3])
    ).astype(narrow_type)

    def pair_backward(pair_index):
        query_part, key_part, value_part, scores = pair_slices(pair_index)
        grad_part = lax.dynamic_slice_in_dim(
            grad_attended, pair_index * pair_width, pair_width, 1
        ).reshape(row_count, 2, head_width)
        log_pair = log_totals[pair_index]
        probable = jnp.exp(scores - log_pair[:, :, None])
        grad_probable = jnp.einsum(
            "qhd,khd->hqk", grad_part, value_part, preferred_element_type=float_type
        )
        grad_scores = probable * (
            grad_probable - jnp.sum(grad_probable * probable, axis=2, keepdims=True)
        )
        grad_scores = grad_scores.astype(narrow_type)
        grad_query = (
            jnp.einsum("hqk,khd->qhd", grad_scores, key_part, preferred_element_type=float_type)
            * scaling_score
        )
        grad_key = (
            jnp.einsum("hqk,qhd->khd", grad_scores, query_part, preferred_element_type=float_type)
            * scaling_score
        )
        grad_value = jnp.einsum(
            "hqk,qhd->khd",
            probable.astype(narrow_type),
            grad_part,
            preferred_element_type=float_type,
        )
        return (
            grad_query.reshape(row_count, pair_width),
            grad_key.reshape(window_rows, pair_width),
            grad_value.reshape(window_rows, pair_width),
        )

    grad_query_pairs, grad_key_pairs, grad_value_pairs = lax.map(
        pair_backward, jnp.arange(pair_count)
    )
    grad_queries = grad_query_pairs.transpose(1, 0, 2).reshape(row_count, features)
    grad_keys = grad_key_pairs.transpose(1, 0, 2).reshape(window_rows, features)
    grad_values = grad_value_pairs.transpose(1, 0, 2).reshape(window_rows, features)
    grad_window = jnp.concatenate([grad_keys, grad_values], axis=1)
    padded_grads = jnp.pad(grad_window, ((window_start, window_start), (0, 0)))
    grad_pairs = padded_grads[HOPS * row_count : (HOPS + 1) * row_count]
    for distance in range(1, HOPS + 1):
        lower_piece = padded_grads[
            (HOPS - distance) * row_count : (HOPS - distance + 1) * row_count
        ]
        higher_piece = padded_grads[
            (HOPS + distance) * row_count : (HOPS + distance + 1) * row_count
        ]
        grad_pairs = grad_pairs + passed_along(
            lower_piece.astype(jnp.bfloat16), ("seq", "fsdp"), -distance
        ).astype(lower_piece.dtype)
        grad_pairs = grad_pairs + passed_along(
            higher_piece.astype(jnp.bfloat16), ("seq", "fsdp"), distance
        ).astype(higher_piece.dtype)
    grad_projected = jnp.concatenate([grad_queries, grad_pairs], axis=1).astype(narrow_type)
    grad_blocks = grad_projected.reshape(row_count, 3, features)
    grad_rank_qkv = (
        jnp.einsum("tpd,prd->tpr", grad_blocks, attention_up[:3], preferred_element_type=float_type)
        * select[:, None, :]
    ).astype(narrow_type)
    grad_qkv_down = jnp.einsum(
        "td,tpr->pdr", normed_first, grad_rank_qkv, preferred_element_type=float_type
    )
    grad_qkv_up = jnp.einsum(
        "tpr,tpd->prd", rank_qkv, grad_blocks, preferred_element_type=float_type
    )
    grad_normed_first = transposed_right(grad_projected, qkv_full) + jnp.einsum(
        "tpr,pdr->td", grad_rank_qkv, attention_down[:3], preferred_element_type=float_type
    )
    input_gradient = grad_middle + norm_backward(
        grad_normed_first, gains_wide[0], normal_first, scaling_first
    )
    grad_attention_down = jnp.concatenate([grad_qkv_down, grad_out_down[None]], axis=0)
    grad_attention_up = jnp.concatenate([grad_qkv_up, grad_out_up[None]], axis=0)
    summed = (
        lax.psum_scatter(grad_attention_down, ("seq", "fsdp"), scatter_dimension=1, tiled=True),
        lax.psum_scatter(grad_attention_up, ("seq", "fsdp"), scatter_dimension=2, tiled=True),
        lax.psum_scatter(grad_expand_down, ("seq", "fsdp"), scatter_dimension=0, tiled=True),
        lax.psum_scatter(grad_expand_up, ("seq", "fsdp"), scatter_dimension=1, tiled=True),
        lax.psum_scatter(grad_contract_down, ("seq", "fsdp"), scatter_dimension=0, tiled=True),
        lax.psum_scatter(grad_contract_up, ("seq", "fsdp"), scatter_dimension=1, tiled=True),
    )
    return (
        result,
        input_gradient,
        summed[0],
        summed[1],
        summed[2],
        summed[3],
        summed[4],
        summed[5],
    )


MESH_ID = pl.DeviceIdType.MESH
CORES, SIDE_X, SIDE_Y = 1, 2, 4
ANYWHERE = pl.BlockSpec(memory_space=pl.ANY)
IN_VMEM = pl.BlockSpec(memory_space=pltpu.VMEM)
IN_SMEM = pl.BlockSpec(memory_space=pltpu.SMEM)


def place_here():
    return lax.axis_index("seq"), lax.axis_index("fsdp")


def remote(source, target, send, receive, seq, fsdp):
    return pltpu.make_async_remote_copy(
        src_ref=source,
        dst_ref=target,
        send_sem=send,
        recv_sem=receive,
        device_id=(seq, fsdp),
        device_id_type=MESH_ID,
    )


def greet(barrier, seq, fsdp):
    pl.semaphore_signal(barrier, 1, device_id=(seq, fsdp), device_id_type=MESH_ID)


def greet_neighbours(barrier, seq, fsdp, depth):
    for bit in (CORES, SIDE_X, SIDE_Y):
        greet(barrier, seq ^ bit, fsdp)
    for step in range(1, depth):
        greet(barrier, seq, lax.rem(fsdp + step, depth))


class Gather:
    STEPS = 10

    def __init__(self, depth, send, receive):
        self.depth, self.send, self.receive = depth, send, receive
        self.seq, self.fsdp = place_here()
        self.me = self.seq * depth + self.fsdp

    def copy(self, index, step, source, target, seq, fsdp):
        at = index * self.STEPS + step
        return remote(source, target, self.send.at[at], self.receive.at[at], seq, fsdp)

    def group(self, chunk, at_seq):
        full, rows, columns, _ = chunk
        return full.at[pl.ds(at_seq * self.depth, self.depth), rows, columns]

    def sides(self, chunk):
        flip = chunk[3]
        if isinstance(flip, int):
            return (SIDE_X, SIDE_Y) if flip else (SIDE_Y, SIDE_X)
        return SIDE_Y - flip * (SIDE_Y - SIDE_X), SIDE_X + flip * (SIDE_Y - SIDE_X)

    def line(self, index, chunk):
        full, rows, columns, _ = chunk
        piece = full.at[self.me, rows, columns]
        return [
            self.copy(index, step - 1, piece, piece, self.seq, lax.rem(self.fsdp + step, self.depth))
            for step in range(1, self.depth)
        ]

    def over(self, index, chunk):
        a, b = self.sides(chunk)
        mine, theirs = self.group(chunk, self.seq), self.group(chunk, self.seq ^ a)
        return [
            self.copy(index, 3, mine, mine, self.seq ^ a, self.fsdp),
            self.copy(index, 4, mine, mine, self.seq ^ b, self.fsdp),
            self.copy(index, 5, theirs, theirs, self.seq ^ b, self.fsdp),
        ]

    def across(self, index, chunk):
        a, b = self.sides(chunk)
        copies = []
        for i, at_seq in enumerate((self.seq, self.seq ^ a, self.seq ^ b, self.seq ^ a ^ b)):
            piece = self.group(chunk, at_seq)
            copies.append(self.copy(index, 6 + i, piece, piece, self.seq ^ CORES, self.fsdp))
        return copies

    def along(self, index, chunk):
        for copy in self.line(index, chunk):
            copy.start()

    def first(self, index, chunk):
        for copy in self.line(index, chunk):
            copy.wait_recv()
        over = self.over(index, chunk)
        over[0].start()
        over[1].start()
        self.across(index, chunk)[0].start()

    def second(self, index, chunk):
        over = self.over(index, chunk)
        over[0].wait_recv()
        over[2].start()
        self.across(index, chunk)[1].start()

    def third(self, index, chunk):
        over, across = self.over(index, chunk), self.across(index, chunk)
        over[1].wait_recv()
        across[2].start()
        over[2].wait_recv()
        across[3].start()

    def finish(self, index, chunk):
        for copy in self.across(index, chunk):
            copy.wait_recv()

    def drain(self, index, chunk):
        for copy in self.line(index, chunk) + self.over(index, chunk) + self.across(index, chunk):
            copy.wait_send()


class Exchange:
    def __init__(self, depth, heads):
        self.depth, self.heads = depth, heads
        self.seq, self.fsdp = place_here()
        self.me = self.seq * depth + self.fsdp
        self.core, self.half = lax.rem(self.seq, 2), lax.div(self.seq, 4)
        self.head = lax.div(self.seq, 2) * depth + self.fsdp
        self.same = (self.half == self.core).astype(jnp.int32)

    def holder(self, k):
        return lax.div(k, self.depth) * 2 + self.half, lax.rem(k, self.depth)

    def owner(self, k):
        block = self.core * self.heads + k
        return lax.div(block, self.depth), lax.rem(block, self.depth)

    def away_head(self, k):
        return (k != self.head) | (self.half != self.core)

    def away_block(self, k):
        return self.core * self.heads + k != self.me

    def greet_holders(self, barrier):
        @pl.loop(0, self.heads)
        def _(k):
            @pl.when(self.away_head(k))
            def _():
                greet(barrier, *self.holder(k))

        return self.heads - self.same

    def greet_owners(self, barrier):
        @pl.loop(0, self.heads)
        def _(k):
            @pl.when(self.away_block(k))
            def _():
                greet(barrier, *self.owner(k))

        return self.heads - self.same


def as_matrix(block):
    return block.reshape(-1, block.shape[-1])


def turned(block, tile=256):
    return block.astype(float_type).T.astype(narrow_type)


def rows_of_vectors(ve, target):
    flat = as_matrix(ve[:, 0:32, :]).astype(float_type)
    target[...] = flat.T[0:16]


def attention_in_kernel(
    depth,
    halo,
    heads,
    chunks,
    tok_ref,
    sel_ref,
    wqkv,
    wout,
    a_att,
    b_att,
    a_exp,
    b_con,
    w2,
    a_con,
    b_exp,
    vec,
    fa_out,
    ve_out,
    f2,
    y_ref,
    rank_ref,
    fa,
    ve,
    proj,
    normed,
    vectors,
    send,
    receive,
    local,
    piece_send,
    piece_receive,
    piece_local,
):
    gather, swap = Gather(depth, send, receive), Exchange(depth, heads)
    me, seq, fsdp = swap.me, swap.seq, swap.fsdp
    core, half, head, own = swap.core, swap.half, swap.head, heads
    features = normed.shape[1]
    wide = features + 256
    barrier = pltpu.get_barrier_semaphore()
    greet_neighbours(barrier, seq, fsdp, depth)
    waits = 3 + depth - 1 + swap.greet_owners(barrier)
    places = [(vec, ve.at[me])]
    for p in range(4):
        source = wqkv.at[:, pl.ds(p * features, features)] if p < 3 else wout
        places.append((source, fa.at[me, :, pl.ds(p * wide, features)]))
        places.append((a_att.at[p], fa.at[me, :, pl.ds(p * wide + features, 128)]))
        places.append((b_att.at[p], fa.at[me, :, pl.ds(p * wide + features + 128, 128)]))
    places.append((a_exp, fa.at[me, :, pl.ds(4 * wide, 128)]))
    places.append((b_con, fa.at[me, :, pl.ds(4 * wide + 128, 128)]))
    places.append((w2, f2.at[me, :, pl.ds(0, features)]))
    places.append((a_con, f2.at[me, :, pl.ds(features, 128)]))
    places.append((b_exp, f2.at[me, :, pl.ds(features + 128, 128)]))
    placed = [pltpu.make_async_copy(a, b, local.at[i]) for i, (a, b) in enumerate(places)]
    for copy in placed:
        copy.start()
    for copy in placed:
        copy.wait()
    refs = {"ve": ve, "fa": fa, "f2": f2}
    chunks = [(refs[name], rows, columns, flip) for name, rows, columns, flip in chunks]
    pl.semaphore_wait(barrier, waits)
    for index, chunk in enumerate(chunks):
        gather.along(index, chunk)
    base = core * (own - halo)
    slot = me - half * (own - halo)

    def piece(p, k):
        return remote(
            proj.at[p, k],
            y_ref.at[slot, p],
            piece_send.at[p, k],
            piece_receive.at[p, lax.rem(me, own)],
            *swap.holder(k),
        )

    def arrival(p, k):
        return remote(
            proj.at[p, 0],
            y_ref.at[core * own + k - base, p],
            piece_send.at[p, k],
            piece_receive.at[p, k],
            seq ^ CORES,
            fsdp,
        )

    def kept(p):
        return pltpu.make_async_copy(proj.at[p, head], y_ref.at[me - base, p], piece_local.at[p])

    def norm():
        rows_of_vectors(ve, vectors)
        rows = tok_ref[...].astype(float_type)
        normed[...] = layer_norm(rows, vectors[0:1], vectors[4:5])[0].astype(narrow_type)

    def project(p):
        down = as_matrix(fa[:, :, p * wide + features : p * wide + features + 128])
        rank = (matmul(normed[...], down) * sel_ref[...]).astype(narrow_type)
        rank_ref[p] = rank

        @pl.loop(0, features // 256)
        def _(j):
            weight = as_matrix(fa[:, :, pl.ds(pl.multiple_of(p * wide + j * 256, 128), 256)])
            up = as_matrix(fa[pl.ds(j * 8, 8), :, p * wide + features + 128 : (p + 1) * wide])
            result = matmul(normed[...], weight) + transposed_right(rank, up)
            if p == 0:
                result = result + vectors[5:6, pl.ds(pl.multiple_of(j * 256, 128), 256)]
            proj[p, pl.ds(j * 4, 4)] = result.T.astype(narrow_type).reshape(4, 64, 256)

            @pl.loop(0, 4)
            def _(i):
                k = j * 4 + i

                @pl.when(swap.away_head(k))
                def _():
                    piece(p, k).start()

        @pl.when(half == core)
        def _():
            kept(p).start()

    after = {0: norm, 2: lambda: project(0), 4: lambda: project(1), 6: lambda: project(2)}
    after_attention = [i for i, chunk in enumerate(chunks) if chunk[0] is fa][-1]
    outs = [
        pltpu.make_async_copy(fa, fa_out, local.at[0]),
        pltpu.make_async_copy(ve, ve_out, local.at[1]),
    ]

    def store():
        for copy in outs:
            copy.start()

    for turn in range(len(chunks) + 3):
        for delay, step in enumerate((gather.first, gather.second, gather.third, gather.finish)):
            index = turn - delay
            if 0 <= index < len(chunks):
                step(index, chunks[index])
                if delay == 3:
                    after.get(index, lambda: None)()
                    if index == after_attention:
                        store()

    @pl.loop(0, own)
    def _(k):
        @pl.when(swap.away_block(k))
        def _():
            for p in range(3):
                arrival(p, k).wait_recv()

    @pl.when(half == core)
    def _():
        for p in range(3):
            kept(p).wait()

    first = jnp.where(core == 0, own - halo, own)
    over = remote(
        y_ref.at[pl.ds(first - base, halo), 1:3],
        y_ref.at[pl.ds(first - (own - halo) * (1 - core), halo), 1:3],
        piece_send.at[3, 0],
        piece_receive.at[3, 0],
        seq ^ CORES,
        fsdp,
    )
    over.start()
    over.wait()

    @pl.loop(0, heads)
    def _(k):
        @pl.when(swap.away_head(k))
        def _():
            for p in range(3):
                piece(p, k).wait_send()

    for index, chunk in enumerate(chunks):
        gather.drain(index, chunk)
    for copy in outs:
        copy.wait()


def attention_in(tokens, select, arrays, halo, depth, heads, devices, collective):
    rows, features = tokens.shape
    wide = features + 256
    total = 4 * wide + 256
    share, hidden_share = features // devices, arrays[6].shape[0]
    chunks = [("ve", slice(0, 48), slice(0, 128), 0)]
    for p in range(3):
        chunks.append(("fa", slice(0, share), slice(p * wide, p * wide + wide // 2), 0))
        chunks.append(("fa", slice(0, share), slice(p * wide + wide // 2, (p + 1) * wide), 1))
    middle = 3 * wide + (total - 3 * wide) // 2
    chunks.append(("fa", slice(0, share), slice(3 * wide, middle), 0))
    chunks.append(("fa", slice(0, share), slice(middle, total), 1))
    for part in range(0, hidden_share, 32):
        chunks.append(("f2", slice(part, part + 32), slice(0, wide // 2), 0))
        chunks.append(("f2", slice(part, part + 32), slice(wide // 2, wide), 1))
    copies = Gather.STEPS * len(chunks)
    return pl.pallas_call(
        functools.partial(attention_in_kernel, depth, halo, heads, chunks),
        out_shape=(
            jax.ShapeDtypeStruct((devices, share, total), narrow_type),
            jax.ShapeDtypeStruct((devices, 48, 128), narrow_type),
            jax.ShapeDtypeStruct((devices, hidden_share, wide), narrow_type),
            jax.ShapeDtypeStruct((heads + halo, 3, features // heads, rows), narrow_type),
            jax.ShapeDtypeStruct((3, rows, 128), narrow_type),
        ),
        in_specs=[IN_VMEM, IN_VMEM] + [ANYWHERE] * len(arrays),
        out_specs=(ANYWHERE, ANYWHERE, ANYWHERE, ANYWHERE, IN_VMEM),
        scratch_shapes=[
            pltpu.VMEM((devices, share, total), narrow_type),
            pltpu.VMEM((devices, 48, 128), narrow_type),
            pltpu.VMEM((3, heads, features // heads, rows), narrow_type),
            pltpu.VMEM((rows, features), narrow_type),
            pltpu.VMEM((16, features), float_type),
            pltpu.SemaphoreType.DMA((copies,)),
            pltpu.SemaphoreType.DMA((copies,)),
            pltpu.SemaphoreType.DMA((20,)),
            pltpu.SemaphoreType.DMA((4, heads)),
            pltpu.SemaphoreType.DMA((4, heads)),
            pltpu.SemaphoreType.DMA((3,)),
        ],
        compiler_params=pltpu.CompilerParams(
            collective_id=collective, has_side_effects=True, vmem_limit_bytes=48 << 20
        ),
    )(tokens, select, *arrays)


HIDDEN_TILE = 512


def middle_kernel(
    depth,
    heads,
    att_ref,
    tok_ref,
    cot_ref,
    sel_ref,
    fa_in,
    ve,
    f2_in,
    w1,
    result_ref,
    gm_ref,
    terms,
    gy_ref,
    fa,
    f2,
    f1,
    att_t,
    att,
    gatt_t,
    vectors,
    hidden_bias,
    middle,
    normal,
    normed,
    branch,
    grad_branch,
    grad_normed,
    ranks,
    rank_sums,
    send,
    receive,
    local,
    a_send,
    a_receive,
    b_send,
    b_receive,
    own_local,
):
    gather, swap = Gather(depth, send, receive), Exchange(depth, heads)
    me, seq, fsdp = swap.me, swap.seq, swap.fsdp
    core, half, head, own = swap.core, swap.half, swap.head, heads
    devices, share = f1.shape[0], f1.shape[1]
    row_count, features = tok_ref.shape
    wide = features + 256
    tiles = f1.shape[2] // HIDDEN_TILE
    in_tile = HIDDEN_TILE // f2.shape[1]
    barrier = pltpu.get_barrier_semaphore()
    greet_neighbours(barrier, seq, fsdp, depth)
    waits = 3 + depth - 1 + swap.greet_owners(barrier) + swap.greet_holders(barrier)
    loads = [
        pltpu.make_async_copy(w1, f1.at[me], local.at[0]),
        pltpu.make_async_copy(fa_in.at[:, :, pl.ds(3 * wide, wide + 256)], fa, local.at[1]),
        pltpu.make_async_copy(f2_in, f2, local.at[2]),
    ]
    for copy in loads:
        copy.start()
    loads[0].wait()
    pl.semaphore_wait(barrier, waits)

    def attended_piece(k):
        return remote(att_ref.at[k], att_t.at[head], a_send.at[k], a_receive.at[head], *swap.owner(k))

    def attended_arrival(k):
        return remote(att_ref.at[0], att_t.at[k], a_send.at[k], a_receive.at[k], seq ^ CORES, fsdp)

    attended_kept = pltpu.make_async_copy(att_ref.at[me - core * own], att_t.at[head], own_local.at[0])

    @pl.when(half == core)
    def _():
        attended_kept.start()

    @pl.loop(0, own)
    def _(step):
        k = lax.rem(step + me, own)

        @pl.when(swap.away_block(k))
        def _():
            attended_piece(k).start()

    def chunk(c):
        flip = c % 2 if isinstance(c, int) else lax.rem(c, 2)
        start = c * HIDDEN_TILE if isinstance(c, int) else pl.multiple_of(c * HIDDEN_TILE, 128)
        return (f1, slice(0, share), pl.ds(start, HIDDEN_TILE), flip)

    @pl.loop(0, tiles)
    def _(c):
        gather.along(c, chunk(c))

    rows_of_vectors(ve, vectors)
    for d in range(devices):
        hidden_bias[:, d * 128 : (d + 1) * 128] = ve[d, 32:48, :].astype(float_type)[0:8]
    grad_branch[...] = (vectors[3:4] * cot_ref[...].astype(float_type)).astype(narrow_type)
    loads[1].wait()
    contract_up = as_matrix(fa[:, :, wide + 128 : wide + 256])
    ranks[1] = (matmul(grad_branch[...], contract_up) * sel_ref[...]).astype(narrow_type)
    branch[...] = jnp.zeros_like(branch)
    grad_normed[...] = jnp.zeros_like(grad_normed)
    rank_sums[...] = jnp.zeros_like(rank_sums)

    gather.first(0, chunk(0))
    gather.first(1, chunk(1))
    gather.second(0, chunk(0))
    gather.first(2, chunk(2))
    gather.second(1, chunk(1))
    gather.third(0, chunk(0))

    @pl.loop(0, heads)
    def _(k):
        @pl.when(swap.away_head(k))
        def _():
            attended_arrival(k).wait_recv()

    @pl.when(half == core)
    def _():
        attended_kept.wait()

    for j in range(4):
        att[:, j * 256 : (j + 1) * 256] = turned(as_matrix(att_t[4 * j : 4 * j + 4]))
    out_down = as_matrix(fa[:, :, features : features + 128])
    rank_out = (matmul(att[...], out_down) * sel_ref[...]).astype(narrow_type)
    ranks[2] = rank_out

    @pl.loop(0, 4)
    def _(j):
        at = pl.ds(pl.multiple_of(j * 256, 128), 256)
        weight = as_matrix(fa[:, :, at])
        up = as_matrix(fa[pl.ds(j * 8, 8), :, features + 128 : wide])
        mixed = matmul(att[...], weight) + transposed_right(rank_out, up) + vectors[6:7, at]
        middle[:, at] = tok_ref[:, at].astype(float_type) + vectors[1:2, at] * mixed

    shifted, normal_rows, scaling = layer_norm(middle[...], vectors[2:3], vectors[7:8])
    normal[...] = normal_rows
    normed[...] = shifted.astype(narrow_type)
    expand_down = as_matrix(fa[:, :, wide : wide + 128])
    rank_expand = (matmul(normed[...], expand_down) * sel_ref[...]).astype(narrow_type)
    ranks[0] = rank_expand
    ranks[3, 0:128] = turned(rank_expand)[:, 0:128]
    ranks[3, 128:256] = turned(rank_expand)[:, 128:256]
    ranks[4, 0:128] = turned(ranks[1])[:, 0:128]
    ranks[4, 128:256] = turned(ranks[1])[:, 128:256]
    loads[2].wait()

    def hidden(c):
        at = pl.ds(pl.multiple_of(c * HIDDEN_TILE, 128), HIDDEN_TILE)
        slots = pl.ds(c * in_tile, in_tile)
        expand = as_matrix(f1[:, :, at])
        contract = as_matrix(f2[slots, :, 0:features])
        down = as_matrix(f2[slots, :, features : features + 128])
        up = as_matrix(f2[slots, :, features + 128 : wide])
        before = matmul(normed[...], expand) + transposed_right(ranks[0], up) + hidden_bias[0:1, at]
        total = 0.5 * (1.0 + lax.erf(before * 0.7071067811865476))
        density = jnp.exp(-0.5 * before * before) * 0.3989422804014327
        active = (before * total).astype(narrow_type)
        slope = total + before * density
        branch[...] += matmul(active, contract)
        rank_sums[0] += matmul(active, down)
        grad_active = transposed_right(grad_branch[...], contract) + transposed_right(ranks[1], down)
        grad_hidden = (grad_active * slope).astype(narrow_type)
        rank_sums[1] += matmul(grad_hidden, up)
        grad_normed[...] += transposed_right(grad_hidden, expand)
        turned_expand = jnp.concatenate([ranks[3, 0:128], ranks[3, 128:256]], axis=1)
        turned_contract = jnp.concatenate([ranks[4, 0:128], ranks[4, 128:256]], axis=1)
        grad_up = matmul(turned_expand, grad_hidden).astype(narrow_type)
        grad_down = matmul(turned_contract, active).astype(narrow_type)
        for i in range(in_tile):
            terms[c * in_tile + i, 96:224] = grad_up[:, i * 128 : (i + 1) * 128]
            terms[c * in_tile + i, 224:352] = grad_down[:, i * 128 : (i + 1) * 128]

    @pl.loop(3, tiles + 3)
    def _(turn):
        @pl.when(turn < tiles)
        def _():
            gather.first(turn, chunk(turn))

        @pl.when(turn - 1 < tiles)
        def _():
            gather.second(turn - 1, chunk(turn - 1))

        @pl.when(turn - 2 < tiles)
        def _():
            gather.third(turn - 2, chunk(turn - 2))

        gather.finish(turn - 3, chunk(turn - 3))
        hidden(turn - 3)

    rank_contract = (rank_sums[0] * sel_ref[...]).astype(narrow_type)
    grad_rank_expand = (rank_sums[1] * sel_ref[...]).astype(narrow_type)
    gradient = grad_normed[...] + transposed_right(grad_rank_expand, expand_down)
    gm_ref[...] = cot_ref[...].astype(float_type) + norm_backward(gradient, vectors[2:3], normal[...], scaling)
    grad_mixed = (vectors[1:2] * gm_ref[...]).astype(narrow_type)
    out_up = as_matrix(fa[:, :, features + 128 : wide])
    grad_rank_out = (matmul(grad_mixed, out_up) * sel_ref[...]).astype(narrow_type)

    def gradient_piece(k):
        return remote(
            gatt_t.at[k], gy_ref.at[lax.rem(me, own)], b_send.at[k], b_receive.at[lax.rem(me, own)], *swap.holder(k)
        )

    def gradient_arrival(k):
        return remote(gatt_t.at[0], gy_ref.at[k], b_send.at[k], b_receive.at[k], seq ^ CORES, fsdp)

    gradient_kept = pltpu.make_async_copy(gatt_t.at[head], gy_ref.at[lax.rem(me, own)], own_local.at[1])

    @pl.loop(0, 4)
    def _(j):
        slots = pl.ds(j * 8, 8)
        weight = as_matrix(fa[slots, :, 0:features])
        down = as_matrix(fa[slots, :, features : features + 128])
        rows = transposed_right(grad_mixed, weight) + transposed_right(grad_rank_out, down)
        gatt_t[pl.ds(j * 4, 4)] = rows.T.astype(narrow_type).reshape(4, 64, 256)

        @pl.loop(0, 4)
        def _(i):
            k = j * 4 + i

            @pl.when(swap.away_head(k))
            def _():
                gradient_piece(k).start()

    @pl.when(half == core)
    def _():
        gradient_kept.start()

    up_rows = transposed_right(rank_contract, contract_up)
    result_ref[...] = (
        middle[...] + vectors[3:4] * (branch[...] + vectors[8:9] + up_rows)
    ).astype(narrow_type)
    shaped = (devices, share, 128)
    terms[:, 0:32] = matmul(as_matrix(att_t[...]), grad_rank_out).astype(narrow_type).reshape(shaped)
    terms[:, 32:64] = transposed_left(grad_mixed, rank_out).astype(narrow_type).reshape(shaped)
    terms[:, 64:96] = transposed_left(normed[...], grad_rank_expand).astype(narrow_type).reshape(shaped)
    terms[:, 352:384] = transposed_left(grad_branch[...], rank_contract).astype(narrow_type).reshape(shaped)

    @pl.loop(0, own)
    def _(k):
        @pl.when(swap.away_block(k))
        def _():
            gradient_arrival(k).wait_recv()
            attended_piece(k).wait_send()

    @pl.when(half == core)
    def _():
        gradient_kept.wait()

    @pl.loop(0, heads)
    def _(k):
        @pl.when(swap.away_head(k))
        def _():
            gradient_piece(k).wait_send()

    @pl.loop(0, tiles)
    def _(c):
        gather.drain(c, chunk(c))


def middle_part(att, tokens, cotangent, select, fa, ve, f2, w1, depth, collective):
    heads, width, rows = att.shape
    features = tokens.shape[1]
    wide = features + 256
    devices, hidden_share = f2.shape[0], f2.shape[1]
    share, hidden_total = w1.shape
    copies = Gather.STEPS * (hidden_total // HIDDEN_TILE)

    def wide_rows():
        return pltpu.VMEM((rows, features), float_type)

    def narrow_rows():
        return pltpu.VMEM((rows, features), narrow_type)

    return pl.pallas_call(
        functools.partial(middle_kernel, depth, heads),
        out_shape=(
            jax.ShapeDtypeStruct((rows, features), narrow_type),
            jax.ShapeDtypeStruct((rows, features), float_type),
            jax.ShapeDtypeStruct((devices, 384, 128), narrow_type),
            jax.ShapeDtypeStruct((heads, width, rows), narrow_type),
        ),
        in_specs=[IN_VMEM, IN_VMEM, IN_VMEM, IN_VMEM, ANYWHERE, IN_VMEM, ANYWHERE, ANYWHERE],
        out_specs=(IN_VMEM, IN_VMEM, IN_VMEM, ANYWHERE),
        scratch_shapes=[
            pltpu.VMEM((devices, share, wide + 256), narrow_type),
            pltpu.VMEM(f2.shape, narrow_type),
            pltpu.VMEM((devices, share, hidden_total), narrow_type),
            pltpu.VMEM((heads, width, rows), narrow_type),
            narrow_rows(),
            pltpu.VMEM((heads, width, rows), narrow_type),
            pltpu.VMEM((16, features), float_type),
            pltpu.VMEM((8, hidden_total), float_type),
            wide_rows(),
            wide_rows(),
            narrow_rows(),
            wide_rows(),
            narrow_rows(),
            wide_rows(),
            pltpu.VMEM((5, rows, 128), narrow_type),
            pltpu.VMEM((2, rows, 128), float_type),
            pltpu.SemaphoreType.DMA((copies,)),
            pltpu.SemaphoreType.DMA((copies,)),
            pltpu.SemaphoreType.DMA((3,)),
            pltpu.SemaphoreType.DMA((heads,)),
            pltpu.SemaphoreType.DMA((heads,)),
            pltpu.SemaphoreType.DMA((heads,)),
            pltpu.SemaphoreType.DMA((heads,)),
            pltpu.SemaphoreType.DMA((2,)),
        ],
        compiler_params=pltpu.CompilerParams(
            collective_id=collective, has_side_effects=True, vmem_limit_bytes=60 << 20
        ),
    )(att, tokens, cotangent, select, fa, ve, f2, w1)


class Reduce:
    COPIES = 16

    def __init__(self, depth, base, terms, first, second, third, fourth, send, receive):
        self.depth, self.base, self.terms = depth, base, terms
        self.buffers = first, second, third, fourth
        self.send, self.receive = send, receive
        self.seq, self.fsdp = place_here()
        self.core, self.x, self.y = lax.rem(self.seq, 2), lax.rem(lax.div(self.seq, 2), 2), lax.div(self.seq, 4)
        half = terms.shape[1] // 2
        self.halves = (slice(0, half), slice(half, 2 * half))

    def copy(self, step, source, target, seq, fsdp):
        at = self.base + step
        return remote(source, target, self.send.at[at], self.receive.at[at], seq, fsdp)

    def to_core(self):
        first = self.buffers[0]
        lines = [self.terms.at[pl.ds((2 * t + 1 - self.core) * self.depth, self.depth)] for t in range(4)]
        return [self.copy(t, lines[t], first.at[t], self.seq ^ CORES, self.fsdp) for t in range(4)]

    def to_sides(self):
        first, second = self.buffers[:2]
        x, y = self.x, self.y
        copies = []
        for j in range(2):
            copies.append(
                self.copy(
                    4 + j,
                    first.at[2 * j + 1 - x, :, self.halves[0]],
                    second.at[0, j],
                    self.seq ^ SIDE_X,
                    self.fsdp,
                )
            )
            copies.append(
                self.copy(
                    6 + j,
                    first.at[2 * (1 - y) + j, :, self.halves[1]],
                    second.at[1, j],
                    self.seq ^ SIDE_Y,
                    self.fsdp,
                )
            )
        return copies

    def to_corner(self):
        second, third = self.buffers[1:3]
        return [
            self.copy(8, second.at[0, 1 - self.y], third.at[0], self.seq ^ SIDE_Y, self.fsdp),
            self.copy(9, second.at[1, 1 - self.x], third.at[1], self.seq ^ SIDE_X, self.fsdp),
        ]

    def to_line(self):
        third, fourth = self.buffers[2:]
        copies = []
        for step in range(1, self.depth):
            to = lax.rem(self.fsdp + step, self.depth)
            for j in range(2):
                copies.append(
                    self.copy(8 + 2 * step + j, third.at[j, to], fourth.at[j, step], self.seq, to)
                )
        return copies

    def add(self, target, other):
        @pl.loop(0, self.depth)
        def _(i):
            target[i] = (target[i].astype(float_type) + other[i].astype(float_type)).astype(narrow_type)

    def begin(self):
        for copy in self.to_core():
            copy.start()

    def sides(self):
        first = self.buffers[0]
        for t, copy in enumerate(self.to_core()):
            copy.wait_recv()
            self.add(first.at[t], self.terms.at[pl.ds((2 * t + self.core) * self.depth, self.depth)])
        for copy in self.to_sides():
            copy.start()

    def corner(self):
        first, second = self.buffers[:2]
        copies = self.to_sides()
        for j in range(2):
            copies[2 * j].wait_recv()
            self.add(second.at[0, j], first.at[2 * j + self.x, :, self.halves[0]])
            copies[2 * j + 1].wait_recv()
            self.add(second.at[1, j], first.at[2 * self.y + j, :, self.halves[1]])
        for copy in self.to_corner():
            copy.start()

    def line(self):
        second, third = self.buffers[1:3]
        copies = self.to_corner()
        copies[0].wait_recv()
        self.add(third.at[0], second.at[0, self.y])
        copies[1].wait_recv()
        self.add(third.at[1], second.at[1, self.x])
        for copy in self.to_line():
            copy.start()

    def end(self, out):
        third, fourth = self.buffers[2:]
        for copy in self.to_line():
            copy.wait_recv()
        for j in range(2):
            total = third[j, self.fsdp].astype(float_type)
            for step in range(1, self.depth):
                total = total + fourth[j, step].astype(float_type)
            out[self.halves[j]] = total

    def drain(self):
        for copy in self.to_core() + self.to_sides() + self.to_corner() + self.to_line():
            copy.wait_send()


def last_kernel(
    depth,
    heads,
    halo,
    dx_ref,
    dh_ref,
    tok_ref,
    gm_ref,
    sel_ref,
    fa_in,
    ve,
    rank_ref,
    early_terms,
    gradient_ref,
    early_ref,
    late_ref,
    fa,
    vectors,
    normed,
    total,
    arrived,
    arrived_rows,
    merged,
    other,
    late_terms,
    early_buffers,
    late_buffers,
    send,
    receive,
    local,
    piece_send,
    piece_receive,
    piece_local,
):
    swap = Exchange(depth, heads)
    me, seq, fsdp = swap.me, swap.seq, swap.fsdp
    core, half, head, own = swap.core, swap.half, swap.head, heads
    row_count, features = tok_ref.shape
    devices, share = fa.shape[0], fa.shape[1]
    wide = features + 256
    barrier = pltpu.get_barrier_semaphore()
    greet_neighbours(barrier, seq, fsdp, depth)
    waits = 3 + depth - 1 + swap.greet_holders(barrier)
    load = pltpu.make_async_copy(fa_in.at[:, :, pl.ds(0, 3 * wide)], fa, local.at[0])
    load.start()
    pl.semaphore_wait(barrier, waits)
    over = remote(dh_ref, other, piece_send.at[3, 0], piece_receive.at[3, 0], seq ^ CORES, fsdp)
    over.start()
    early = Reduce(depth, 0, early_terms, *early_buffers, send, receive)
    late = [
        Reduce(
            depth, Reduce.COPIES * (p + 1), late_terms.at[p], *[b.at[p] for b in late_buffers], send, receive
        )
        for p in range(3)
    ]
    shared = jnp.where(core == 0, own - halo, 0)

    def in_shared(k):
        return (k >= shared) & (k < shared + halo)

    def sent(p, k, source):
        return remote(
            source, arrived.at[p, head], piece_send.at[p, k], piece_receive.at[p, head], *swap.owner(k)
        )

    def launch(p, k, source):
        @pl.when(swap.away_block(k))
        def _():
            sent(p, k, source).start()

        @pl.when(core * own + k == me)
        def _():
            pltpu.make_async_copy(source, arrived.at[p, head], piece_local.at[p]).start()

    def arrival(p, k):
        return remote(
            dx_ref.at[0, 0], arrived.at[p, k], piece_send.at[p, k], piece_receive.at[p, k], seq ^ CORES, fsdp
        )

    @pl.loop(0, own)
    def _(step):
        k = lax.rem(step + me, own)
        launch(0, k, dx_ref.at[k, 0])

    over.wait_recv()

    @pl.loop(0, halo)
    def _(i):
        for part in range(2):
            merged[i, part] = (
                dx_ref[shared + i, 1 + part].astype(float_type) + other[i, part].astype(float_type)
            ).astype(narrow_type)

    for p in (1, 2):

        @pl.loop(0, own)
        def _(step, p=p):
            k = lax.rem(step + me, own)

            @pl.when(in_shared(k))
            def _():
                launch(p, k, merged.at[jnp.clip(k - shared, 0, halo - 1), p - 1])

            @pl.when(jnp.logical_not(in_shared(k)))
            def _():
                launch(p, k, dx_ref.at[k, p])

    early.begin()
    rows_of_vectors(ve, vectors)
    early.sides()
    shifted, normal, scaling = layer_norm(tok_ref[...].astype(float_type), vectors[0:1], vectors[4:5])
    normed[...] = shifted.astype(narrow_type)
    early.corner()
    load.wait()

    def gather_part(p):
        @pl.loop(0, heads)
        def _(k):
            @pl.when(swap.away_head(k))
            def _():
                arrival(p, k).wait_recv()

        @pl.when(half == core)
        def _():
            pltpu.make_async_copy(dx_ref.at[0, p], arrived.at[p, head], piece_local.at[p]).wait()

    def project_back(p):
        for j in range(4):
            arrived_rows[:, j * 256 : (j + 1) * 256] = turned(as_matrix(arrived[p, 4 * j : 4 * j + 4]))
        up = as_matrix(fa[:, :, p * wide + features + 128 : (p + 1) * wide])
        grad_rank = (matmul(arrived_rows[...], up) * sel_ref[...]).astype(narrow_type)

        @pl.loop(0, 4)
        def _(j):
            at = pl.ds(pl.multiple_of(j * 256, 128), 256)
            slots = pl.ds(j * 8, 8)
            weight = as_matrix(fa[slots, :, p * wide : p * wide + features])
            down = as_matrix(fa[slots, :, p * wide + features : p * wide + features + 128])
            term = transposed_right(arrived_rows[...], weight) + transposed_right(grad_rank, down)
            if p == 0:
                total[:, at] = term
            else:
                total[:, at] += term

        shaped = (devices, share, 128)
        late_terms[p, :, 0:32] = transposed_left(normed[...], grad_rank).astype(narrow_type).reshape(shaped)
        late_terms[p, :, 32:64] = (
            matmul(as_matrix(arrived[p]), rank_ref[p]).astype(narrow_type).reshape(shaped)
        )

    gather_part(0)
    project_back(0)
    late[0].begin()
    early.line()
    late[0].sides()
    gather_part(1)
    project_back(1)
    late[1].begin()
    late[0].corner()
    late[1].sides()
    gather_part(2)
    project_back(2)
    late[2].begin()
    late[0].line()
    late[1].corner()
    late[2].sides()
    gradient_ref[...] = gm_ref[...] + norm_backward(total[...], vectors[0:1], normal, scaling)
    late[1].line()
    late[2].corner()
    early.end(early_ref)
    late[0].end(late_ref.at[0])
    late[2].line()
    late[1].end(late_ref.at[1])
    late[2].end(late_ref.at[2])
    for reduce in [early] + late:
        reduce.drain()

    @pl.loop(0, own)
    def _(k):
        @pl.when(swap.away_block(k))
        def _():
            for p in range(3):
                sent(p, k, dx_ref.at[k, p]).wait_send()

    over.wait_send()


def last_part(dx, dh, tokens, grad_middle, select, fa, ve, rank, terms, depth, collective):
    heads = dx.shape[0]
    halo = dh.shape[0]
    rows, features = tokens.shape
    wide = features + 256
    devices, share = fa.shape[0], fa.shape[1]

    def buffers(count, size):
        return [
            pltpu.VMEM(count + (4, depth, size, 128), narrow_type),
            pltpu.VMEM(count + (2, 2, depth, size // 2, 128), narrow_type),
            pltpu.VMEM(count + (2, depth, size // 2, 128), narrow_type),
            pltpu.VMEM(count + (2, depth, size // 2, 128), narrow_type),
        ]

    return pl.pallas_call(
        functools.partial(last_kernel, depth, heads, halo),
        out_shape=(
            jax.ShapeDtypeStruct((rows, features), float_type),
            jax.ShapeDtypeStruct((terms.shape[1], 128), float_type),
            jax.ShapeDtypeStruct((3, 2 * share, 128), float_type),
        ),
        in_specs=[IN_VMEM] * 5 + [ANYWHERE] + [IN_VMEM] * 3,
        out_specs=(IN_VMEM, IN_VMEM, IN_VMEM),
        scratch_shapes=[
            pltpu.VMEM((devices, share, 3 * wide), narrow_type),
            pltpu.VMEM((16, features), float_type),
            pltpu.VMEM((rows, features), narrow_type),
            pltpu.VMEM((rows, features), float_type),
            pltpu.VMEM((3, heads, features // heads, rows), narrow_type),
            pltpu.VMEM((rows, features), narrow_type),
            pltpu.VMEM(dh.shape, narrow_type),
            pltpu.VMEM(dh.shape, narrow_type),
            pltpu.VMEM((3, devices, 2 * share, 128), narrow_type),
            buffers((), terms.shape[1]),
            buffers((3,), 2 * share),
            pltpu.SemaphoreType.DMA((4 * Reduce.COPIES,)),
            pltpu.SemaphoreType.DMA((4 * Reduce.COPIES,)),
            pltpu.SemaphoreType.DMA((1,)),
            pltpu.SemaphoreType.DMA((4, heads)),
            pltpu.SemaphoreType.DMA((4, heads)),
            pltpu.SemaphoreType.DMA((3,)),
        ],
        compiler_params=pltpu.CompilerParams(
            collective_id=collective, has_side_effects=True, vmem_limit_bytes=56 << 20
        ),
    )(dx, dh, tokens, grad_middle, select, fa, ve, rank, terms)


BIG = 32768.0


def bounds(lens_ref, n, base_block, rows, i):
    first=(base_block+i)*rows; last=first+rows-1
    lo=jnp.int32(0); hi=jnp.int32(0); start=jnp.int32(0)
    for m in range(n):
        end=start+lens_ref[m]
        lo=jnp.where((start<=first)&(first<end),start,lo)
        hi=jnp.where((start<=last)&(last<end),end-1,hi)
        start=end
    return lax.div(lo,rows), lax.div(hi,rows)

def image_marks(lens_ref, n, marks, rows):
    r=lax.broadcasted_iota(jnp.int32,(marks,rows),0)
    st=jnp.full((marks,rows),1<<30,jnp.int32); en=jnp.zeros((marks,rows),jnp.int32)
    start=jnp.int32(0)
    for m in range(n):
        end=start+lens_ref[m]
        st=jnp.where(r==m,start,st); en=jnp.where(r==m,end,en)
        start=end
    return st,en

def fwd_kernel(n,own,slots,halo,rows,width,marks, lens_ref,x_ref,att_ref,lse_ref,o_ref,qa,ka):
    core=lax.rem(lax.axis_index("seq"),2)
    base=core*(own-halo)
    shift=core*halo
    st,en=image_marks(lens_ref,n,marks,rows)
    pos=lax.broadcasted_iota(jnp.int32,(marks,rows),1)
    def prep(s,_):
        p=pos+(base+s)*rows
        inside=(p>=st)&(p<en)
        oh=jnp.where(inside,1.0,0.0).astype(float_type)
        kt=jnp.concatenate([x_ref[s,1].astype(float_type),(oh-1.0)*BIG],axis=0)
        ka[s]=kt.T.astype(narrow_type)
        return 0
    lax.fori_loop(0,slots,prep,0)
    def one_q(i,_):
        s_q=i+shift
        p=pos+(base+s_q)*rows
        oh=jnp.where((p>=st)&(p<en),1.0,0.0).astype(narrow_type)
        q=jnp.concatenate([(x_ref[s_q,0].astype(float_type)*(width**-0.5)).astype(narrow_type),oh],axis=0)
        lo,hi=bounds(lens_ref,n,base+shift,rows,i)
        lo=lo-base; hi=hi-base
        def tile(m,l,o,s):
            sc=matmul(ka[s],q)
            m2=jnp.maximum(m,jnp.max(sc,axis=0,keepdims=True))
            pr=jnp.exp(sc-m2)
            al=jnp.exp(m-m2)
            return m2, l*al+jnp.sum(pr,axis=0,keepdims=True), o*al+matmul(x_ref[s,2],pr.astype(narrow_type))
        def tile2(m,l,o,s):
            sa=matmul(ka[s],q); sb=matmul(ka[s+1],q)
            m2=jnp.maximum(m,jnp.maximum(jnp.max(sa,axis=0,keepdims=True),jnp.max(sb,axis=0,keepdims=True)))
            pa=jnp.exp(sa-m2); pb=jnp.exp(sb-m2)
            al=jnp.exp(m-m2)
            l=l*al+jnp.sum(pa,axis=0,keepdims=True)+jnp.sum(pb,axis=0,keepdims=True)
            return m2,l,o*al+matmul(x_ref[s,2],pa.astype(narrow_type))+matmul(x_ref[s+1,2],pb.astype(narrow_type))
        m=jnp.full((1,rows),-1e30,float_type); l=jnp.zeros((1,rows),float_type); o=jnp.zeros((width,rows),float_type)
        cnt=hi-lo+1
        m,l,o=lax.fori_loop(0,cnt//2,lambda t,c: tile2(*c,lo+2*t),(m,l,o))
        m,l,o=lax.fori_loop(0,cnt%2,lambda t,c: tile(*c,hi),(m,l,o))
        o=o/l
        att_ref[i]=o.astype(narrow_type)
        o_ref[i]=o
        lse_ref[i]=jnp.broadcast_to(m+jnp.log(l),(8,rows))
        return 0
    lax.fori_loop(0,own,one_q,0)

def attention_forward(lengths,x,own,halo):
    slots,_,width,rows=x.shape
    n=lengths.shape[0]; marks=-(-n//16)*16
    V=pl.BlockSpec(memory_space=pltpu.VMEM)
    return pl.pallas_call(functools.partial(fwd_kernel,n,own,slots,halo,rows,width,marks),
        out_shape=(jax.ShapeDtypeStruct((own,width,rows),narrow_type),jax.ShapeDtypeStruct((own,8,rows),float_type),jax.ShapeDtypeStruct((own,width,rows),float_type)),
        in_specs=[pl.BlockSpec(memory_space=pltpu.SMEM),V],out_specs=(V,V,V),
        scratch_shapes=[pltpu.VMEM((width+marks,rows),narrow_type),pltpu.VMEM((slots,rows,width+marks),narrow_type)],
        compiler_params=pltpu.CompilerParams(vmem_limit_bytes=40<<20))(lengths,x)

def bwd_kernel(n,own,slots,halo,rows,width,marks, lens_ref,x_ref,g_ref,lse_ref,o_ref,dx_ref,dh_ref,ka,vv,qa,qn,gn,dd,dq):
    core=lax.rem(lax.axis_index("seq"),2)
    base=core*(own-halo); shift=core*halo
    st,en=image_marks(lens_ref,n,marks,rows)
    pos=lax.broadcasted_iota(jnp.int32,(marks,rows),1)
    def prep(s,_):
        p=pos+(base+s)*rows
        oh=jnp.where((p>=st)&(p<en),1.0,0.0).astype(float_type)
        kt=jnp.concatenate([x_ref[s,1].astype(float_type),(oh-1.0)*BIG],axis=0)
        ka[s]=kt.T.astype(narrow_type)
        vv[s]=x_ref[s,2].astype(float_type).T.astype(narrow_type)
        return 0
    lax.fori_loop(0,slots,prep,0)
    def prepq(i,_):
        s=i+shift
        p=pos+(base+s)*rows
        oh=jnp.where((p>=st)&(p<en),1.0,0.0).astype(narrow_type)
        qs=x_ref[s,0].astype(float_type)*(width**-0.5)
        qa[i]=jnp.concatenate([qs.astype(narrow_type),oh],axis=0)
        qn[i]=qs.T.astype(narrow_type)
        g=g_ref[i].astype(float_type)
        gn[i]=g.T.astype(narrow_type)
        dd[i]=jnp.broadcast_to(jnp.sum(g*o_ref[i],axis=0,keepdims=True),(8,rows))
        dq[i]=jnp.zeros((width,rows),float_type)
        return 0
    lax.fori_loop(0,own,prepq,0)
    def one_k(s,_):
        lo,hi=bounds(lens_ref,n,base,rows,s)
        lo=jnp.maximum(lo-base-shift,0); hi=jnp.minimum(hi-base-shift,own-1)
        kt=x_ref[s,1]
        def tile(i,dk,dv):
            sc=matmul(ka[s],qa[i])
            pr=jnp.exp(sc-lse_ref[i][0:1])
            dp=matmul(vv[s],g_ref[i])
            ds=(pr*(dp-dd[i][0:1])).astype(narrow_type)
            dq[i]+=matmul(kt,ds)
            return dk+matmul(ds,qn[i]), dv+matmul(pr.astype(narrow_type),gn[i])
        z=jnp.zeros((rows,width),float_type)
        cnt=jnp.maximum(hi-lo+1,0)
        def two(t,c):
            c=tile(lo+2*t,*c)
            return tile(lo+2*t+1,*c)
        dk,dv=lax.fori_loop(0,cnt//2,two,(z,z))
        dk,dv=lax.fori_loop(0,cnt%2,lambda t,c: tile(hi,*c),(dk,dv))
        i=s-shift
        @pl.when((i>=0)&(i<own))
        def _():
            dx_ref[i,1]=dk.T.astype(narrow_type)
            dx_ref[i,2]=dv.T.astype(narrow_type)
        @pl.when((i<0)|(i>=own))
        def _():
            j=jnp.where(i<0,s,i-own)
            dh_ref[j,0]=dk.T.astype(narrow_type)
            dh_ref[j,1]=dv.T.astype(narrow_type)
        return 0
    lax.fori_loop(0,slots,one_k,0)
    def fin(i,_):
        dx_ref[i,0]=(dq[i]*(width**-0.5)).astype(narrow_type)
        return 0
    lax.fori_loop(0,own,fin,0)

def attention_backward(lengths,x,g,lse,o,own,halo):
    slots,_,width,rows=x.shape
    n=lengths.shape[0]; marks=-(-n//16)*16
    V=pl.BlockSpec(memory_space=pltpu.VMEM)
    return pl.pallas_call(functools.partial(bwd_kernel,n,own,slots,halo,rows,width,marks),
        out_shape=(jax.ShapeDtypeStruct((own,3,width,rows),narrow_type),jax.ShapeDtypeStruct((halo,2,width,rows),narrow_type)),
        in_specs=[pl.BlockSpec(memory_space=pltpu.SMEM),V,V,V,V],out_specs=(V,V),
        scratch_shapes=[pltpu.VMEM((slots,rows,width+marks),narrow_type),pltpu.VMEM((slots,rows,width),narrow_type),
          pltpu.VMEM((own,width+marks,rows),narrow_type),pltpu.VMEM((own,rows,width),narrow_type),pltpu.VMEM((own,rows,width),narrow_type),
          pltpu.VMEM((own,8,rows),float_type),pltpu.VMEM((own,width,rows),float_type)],
        compiler_params=pltpu.CompilerParams(vmem_limit_bytes=48<<20))(lengths,x,g,lse,o)


def layer_on_slice(
    tokens,
    lengths,
    adapter_choice,
    gain_rows,
    bias_rows,
    query_key_value,
    output_weight,
    expand_weight,
    expand_bias,
    contract_weight,
    adapter_in_attention,
    adapter_out_attention,
    adapter_in_expand,
    adapter_out_expand,
    adapter_in_contract,
    adapter_out_contract,
    cotangent,
):
    row_count, features = tokens.shape
    depth = lax.axis_size("fsdp")
    devices = lax.axis_size(("seq", "fsdp"))
    position = lax.axis_index(("seq", "fsdp"))
    own = devices // 2
    head_width = features // HEADS
    rank_width = adapter_in_attention.shape[2]
    share = features // devices
    halo = -(-(LONGEST - 1) // row_count)

    vectors = jnp.concatenate([gain_rows.T, bias_rows.T], axis=1)
    vectors = jnp.pad(vectors, ((0, 16), (0, rank_width - vectors.shape[1])))
    vectors = lax.dynamic_update_slice(vectors, expand_bias[None], (share, 0))
    arrays = (
        query_key_value,
        output_weight,
        adapter_in_attention,
        adapter_out_attention.transpose(0, 2, 1),
        adapter_in_expand,
        adapter_out_contract.T,
        contract_weight,
        adapter_in_contract,
        adapter_out_expand.T,
        vectors,
    )
    image_ends = jnp.cumsum(lengths)
    places = position * row_count + jnp.arange(row_count, dtype=jnp.int32)
    own_image = jnp.sum((places[:, None] >= image_ends[None, :]).astype(jnp.int32), axis=1)
    matches = own_image[:, None] == jnp.arange(lengths.shape[0], dtype=jnp.int32)[None, :]
    chosen = jnp.sum(jnp.where(matches, adapter_choice[None, :], 0), axis=1)
    select = (jnp.arange(rank_width, dtype=jnp.int32)[None, :] // RANK == chosen[:, None]).astype(float_type)

    fa, ve, f2, on_heads, rank = attention_in(tokens, select, arrays, halo, depth, HEADS, devices, 1)
    attended, log_totals, attended_wide = attention_forward(lengths, on_heads, own, halo)
    result, grad_middle, terms, grad_on_heads = middle_part(
        attended, tokens, cotangent, select, fa, ve, f2, expand_weight, depth, 2
    )
    grad_blocks, grad_halo = attention_backward(
        lengths, on_heads, grad_on_heads, log_totals, attended_wide, own, halo
    )
    input_gradient, early, late = last_part(
        grad_blocks, grad_halo, tokens, grad_middle, select, fa, ve, rank, terms, depth, 3
    )
    down = jnp.concatenate([late[:, :share], early[None, :share]], axis=0)
    up = jnp.concatenate([late[:, share:], early[None, share : 2 * share]], axis=0)
    return (
        result,
        input_gradient,
        down,
        up.transpose(0, 2, 1),
        early[64:96],
        early[96:224],
        early[224:352].T,
        early[352:384].T,
    )


def solution(mesh):
    per_device = layer_on_slice if dict(mesh.shape) == {"seq": 8, "fsdp": 4} else general_layer
    placed = (
        P(("seq", "fsdp"), None),
        P(),
        P(),
        P(None, ("seq", "fsdp")),
        P(None, ("seq", "fsdp")),
        P(("seq", "fsdp"), None),
        P(("seq", "fsdp"), None),
        P(("seq", "fsdp"), None),
        P(("seq", "fsdp")),
        P(("seq", "fsdp"), None),
        P(None, ("seq", "fsdp"), None),
        P(None, None, ("seq", "fsdp")),
        P(("seq", "fsdp"), None),
        P(None, ("seq", "fsdp")),
        P(("seq", "fsdp"), None),
        P(None, ("seq", "fsdp")),
        P(("seq", "fsdp"), None),
    )
    return jax.shard_map(
        per_device,
        mesh=mesh,
        in_specs=placed,
        out_specs=(
            P(("seq", "fsdp"), None),
            P(("seq", "fsdp"), None),
            P(None, ("seq", "fsdp"), None),
            P(None, None, ("seq", "fsdp")),
            P(("seq", "fsdp"), None),
            P(None, ("seq", "fsdp")),
            P(("seq", "fsdp"), None),
            P(None, ("seq", "fsdp")),
        ),
        check_vma=False,
    )
```

```python
import functools
import jax
import jax.numpy as jnp
from jax import lax
from jax.experimental import pallas as pl
from jax.experimental.pallas import tpu as pltpu
from jax.sharding import PartitionSpec as P

HEADS = 16
RANK = 16
HOPS = 6
EDGE = 1408
LONGEST = 1370


epsilon = 1e-06
float_type = jnp.float32
narrow_type = jnp.bfloat16


def passed_along(block, axis, distance):
    devices = range(lax.axis_size(axis))
    route = [(i - distance, i) for i in devices if i - distance in devices]
    return lax.ppermute(block, axis, route)


def layer_norm(inputs_row, gain_row, bias_row):
    center = inputs_row - jnp.mean(inputs_row, axis=-1, keepdims=True)
    scaling = lax.rsqrt(jnp.mean(center * center, axis=-1, keepdims=True) + epsilon)
    normal = center * scaling
    return (normal * gain_row + bias_row, normal, scaling)


def norm_backward(gradient, gain_row, normal, scaling):
    weighted = gradient * gain_row
    return scaling * (
        weighted
        - jnp.mean(weighted, axis=-1, keepdims=True)
        - normal * jnp.mean(weighted * normal, axis=-1, keepdims=True)
    )


def matmul(first_operand, second_operand):
    return jnp.dot(first_operand, second_operand, preferred_element_type=float_type)


def transposed_left(first_operand, second_operand):
    return lax.dot_general(
        first_operand, second_operand, (((0,), (0,)), ((), ())), preferred_element_type=float_type
    )


def transposed_right(first_operand, second_operand):
    return lax.dot_general(
        first_operand, second_operand, (((1,), (1,)), ((), ())), preferred_element_type=float_type
    )


def gelu_slope(hidden_pre):
    cumulative = 0.5 * (1.0 + lax.erf(hidden_pre * 0.7071067811865476))
    density = jnp.exp(-0.5 * hidden_pre * hidden_pre) * 0.3989422804014327
    return cumulative + hidden_pre * density


def general_layer(
    tokens,
    lengths,
    adapter_choice,
    gain_rows,
    bias_rows,
    query_key_value,
    output_weight,
    expand_weight,
    expand_bias,
    contract_weight,
    adapter_in_attention,
    adapter_out_attention,
    adapter_in_expand,
    adapter_out_expand,
    adapter_in_contract,
    adapter_out_contract,
    cotangent,
):
    gathered = (
        lax.all_gather(gain_rows, ("seq", "fsdp"), axis=1, tiled=True),
        lax.all_gather(bias_rows, ("seq", "fsdp"), axis=1, tiled=True),
        lax.all_gather(query_key_value, ("seq", "fsdp"), axis=0, tiled=True),
        lax.all_gather(output_weight, ("seq", "fsdp"), axis=0, tiled=True),
        lax.all_gather(expand_weight, ("seq", "fsdp"), axis=0, tiled=True),
        lax.all_gather(expand_bias, ("seq", "fsdp"), axis=0, tiled=True),
        lax.all_gather(contract_weight, ("seq", "fsdp"), axis=0, tiled=True),
        lax.all_gather(adapter_in_attention, ("seq", "fsdp"), axis=1, tiled=True),
        lax.all_gather(adapter_out_attention, ("seq", "fsdp"), axis=2, tiled=True),
        lax.all_gather(adapter_in_expand, ("seq", "fsdp"), axis=0, tiled=True),
        lax.all_gather(adapter_out_expand, ("seq", "fsdp"), axis=1, tiled=True),
        lax.all_gather(adapter_in_contract, ("seq", "fsdp"), axis=0, tiled=True),
        lax.all_gather(adapter_out_contract, ("seq", "fsdp"), axis=1, tiled=True),
    )
    (
        gains_full,
        biases_full,
        qkv_full,
        output_full,
        expand_full,
        expand_bias_full,
        contract_full,
        attention_down,
        attention_up,
        expand_down,
        expand_up,
        contract_down,
        contract_up,
    ) = gathered
    gains_wide = gains_full.astype(float_type)
    biases_wide = biases_full.astype(float_type)
    row_count, features = tokens.shape
    device_count = lax.axis_size(("seq", "fsdp"))
    position = lax.axis_index(("seq", "fsdp"))
    head_width = features // HEADS
    pair_width = 2 * head_width
    pair_count = HEADS // 2
    scaling_score = head_width ** (-0.5)
    rank_width = attention_down.shape[2]
    window_start = HOPS * row_count - EDGE
    window_rows = row_count + 2 * EDGE
    image_ends = jnp.cumsum(lengths)
    places = (
        position * row_count
        - HOPS * row_count
        + jnp.arange((2 * HOPS + 1) * row_count, dtype=jnp.int32)
    )
    image_of = jnp.sum((places[:, None] >= image_ends[None, :]).astype(jnp.int32), axis=1)
    image_of = jnp.where((places >= 0) & (places < device_count * row_count), image_of, -1)
    own_image = image_of[HOPS * row_count : (HOPS + 1) * row_count]
    key_image = image_of[window_start : window_start + window_rows]
    allowed = own_image[:, None] == key_image[None, :]
    matches = own_image[:, None] == jnp.arange(lengths.shape[0], dtype=jnp.int32)[None, :]
    chosen = jnp.sum(jnp.where(matches, adapter_choice[None, :], 0), axis=1)
    select = (jnp.arange(rank_width, dtype=jnp.int32)[None, :] // RANK == chosen[:, None]).astype(
        float_type
    )
    residual = tokens.astype(float_type)
    normed_first, normal_first, scaling_first = layer_norm(residual, gains_wide[0], biases_wide[0])
    normed_first = normed_first.astype(narrow_type)
    rank_qkv = (
        jnp.einsum(
            "td,pdr->tpr", normed_first, attention_down[:3], preferred_element_type=float_type
        )
        * select[:, None, :]
    ).astype(narrow_type)
    adapted_qkv = jnp.einsum(
        "tpr,prd->tpd", rank_qkv, attention_up[:3], preferred_element_type=float_type
    ).reshape(row_count, 3 * features)
    query_bias = jnp.concatenate([biases_wide[1], jnp.zeros((2 * features,), float_type)])
    projected = (matmul(normed_first, qkv_full) + adapted_qkv + query_bias).astype(narrow_type)
    queries = projected[:, :features]
    key_values = projected[:, features:]
    from_lower = []
    from_higher = []
    for distance in range(1, HOPS + 1):
        from_lower.append(passed_along(key_values, ("seq", "fsdp"), distance))
        from_higher.append(passed_along(key_values, ("seq", "fsdp"), -distance))
    beside_all = jnp.concatenate(from_lower[::-1] + [key_values] + from_higher, axis=0)
    window = beside_all[window_start : window_start + window_rows]

    def pair_slices(pair_index):
        offset = pair_index * pair_width
        query_part = lax.dynamic_slice_in_dim(queries, offset, pair_width, 1).reshape(
            row_count, 2, head_width
        )
        key_part = lax.dynamic_slice_in_dim(window, offset, pair_width, 1).reshape(
            window_rows, 2, head_width
        )
        value_part = lax.dynamic_slice_in_dim(window, features + offset, pair_width, 1).reshape(
            window_rows, 2, head_width
        )
        scores = (
            jnp.einsum("qhd,khd->hqk", query_part, key_part, preferred_element_type=float_type)
            * scaling_score
        )
        scores = jnp.where(allowed[None], scores, -1e30)
        return (query_part, key_part, value_part, scores)

    def pair_forward(pair_index):
        query_part, key_part, value_part, scores = pair_slices(pair_index)
        highest = jnp.max(scores, axis=2, keepdims=True)
        weights = jnp.exp(scores - highest)
        denominator = jnp.sum(weights, axis=2, keepdims=True)
        soft = (weights / denominator).astype(narrow_type)
        mixed_part = jnp.einsum("hqk,khd->qhd", soft, value_part, preferred_element_type=float_type)
        return (
            mixed_part.reshape(row_count, pair_width),
            (highest + jnp.log(denominator))[:, :, 0],
        )

    attended_pairs, log_totals = lax.map(pair_forward, jnp.arange(pair_count))
    attended = attended_pairs.transpose(1, 0, 2).reshape(row_count, features).astype(narrow_type)
    rank_out = (matmul(attended, attention_down[3]) * select).astype(narrow_type)
    mixed = matmul(attended, output_full) + biases_wide[2] + matmul(rank_out, attention_up[3])
    middle = residual + gains_wide[1] * mixed
    normed_second, normal_second, scaling_second = layer_norm(middle, gains_wide[2], biases_wide[3])
    normed_second = normed_second.astype(narrow_type)
    rank_expand = (matmul(normed_second, expand_down) * select).astype(narrow_type)
    hidden_pre = (
        matmul(normed_second, expand_full)
        + expand_bias_full.astype(float_type)
        + matmul(rank_expand, expand_up)
    )
    active = jax.nn.gelu(hidden_pre, approximate=False).astype(narrow_type)
    rank_contract = (matmul(active, contract_down) * select).astype(narrow_type)
    branch = matmul(active, contract_full) + biases_wide[4] + matmul(rank_contract, contract_up)
    result = (middle + gains_wide[3] * branch).astype(narrow_type)
    renewed = lax.optimization_barrier(
        (
            gain_rows,
            bias_rows,
            query_key_value,
            output_weight,
            expand_weight,
            expand_bias,
            contract_weight,
            adapter_in_attention,
            adapter_out_attention,
            adapter_in_expand,
            adapter_out_expand,
            adapter_in_contract,
            adapter_out_contract,
            cotangent,
        )
    )
    gathered = (
        lax.all_gather(renewed[0], ("seq", "fsdp"), axis=1, tiled=True),
        lax.all_gather(renewed[1], ("seq", "fsdp"), axis=1, tiled=True),
        lax.all_gather(renewed[2], ("seq", "fsdp"), axis=0, tiled=True),
        lax.all_gather(renewed[3], ("seq", "fsdp"), axis=0, tiled=True),
        lax.all_gather(renewed[4], ("seq", "fsdp"), axis=0, tiled=True),
        lax.all_gather(renewed[5], ("seq", "fsdp"), axis=0, tiled=True),
        lax.all_gather(renewed[6], ("seq", "fsdp"), axis=0, tiled=True),
        lax.all_gather(renewed[7], ("seq", "fsdp"), axis=1, tiled=True),
        lax.all_gather(renewed[8], ("seq", "fsdp"), axis=2, tiled=True),
        lax.all_gather(renewed[9], ("seq", "fsdp"), axis=0, tiled=True),
        lax.all_gather(renewed[10], ("seq", "fsdp"), axis=1, tiled=True),
        lax.all_gather(renewed[11], ("seq", "fsdp"), axis=0, tiled=True),
        lax.all_gather(renewed[12], ("seq", "fsdp"), axis=1, tiled=True),
    )
    (
        gains_full,
        biases_full,
        qkv_full,
        output_full,
        expand_full,
        expand_bias_full,
        contract_full,
        attention_down,
        attention_up,
        expand_down,
        expand_up,
        contract_down,
        contract_up,
    ) = gathered
    gains_wide = gains_full.astype(float_type)
    gradient_out = cotangent.astype(float_type)
    grad_branch = (gains_wide[3] * gradient_out).astype(narrow_type)
    grad_rank_contract = (transposed_right(grad_branch, contract_up) * select).astype(narrow_type)
    grad_contract_down = transposed_left(active, grad_rank_contract)
    grad_contract_up = transposed_left(rank_contract, grad_branch)
    grad_active = transposed_right(grad_branch, contract_full) + transposed_right(
        grad_rank_contract, contract_down
    )
    grad_hidden = (grad_active * gelu_slope(hidden_pre)).astype(narrow_type)
    grad_rank_expand = (transposed_right(grad_hidden, expand_up) * select).astype(narrow_type)
    grad_expand_down = transposed_left(normed_second, grad_rank_expand)
    grad_expand_up = transposed_left(rank_expand, grad_hidden)
    grad_normed_second = transposed_right(grad_hidden, expand_full) + transposed_right(
        grad_rank_expand, expand_down
    )
    grad_middle = gradient_out + norm_backward(
        grad_normed_second, gains_wide[2], normal_second, scaling_second
    )
    grad_mixed = (gains_wide[1] * grad_middle).astype(narrow_type)
    grad_rank_out = (transposed_right(grad_mixed, attention_up[3]) * select).astype(narrow_type)
    grad_out_down = transposed_left(attended, grad_rank_out)
    grad_out_up = transposed_left(rank_out, grad_mixed)
    grad_attended = (
        transposed_right(grad_mixed, output_full)
        + transposed_right(grad_rank_out, attention_down[3])
    ).astype(narrow_type)

    def pair_backward(pair_index):
        query_part, key_part, value_part, scores = pair_slices(pair_index)
        grad_part = lax.dynamic_slice_in_dim(
            grad_attended, pair_index * pair_width, pair_width, 1
        ).reshape(row_count, 2, head_width)
        log_pair = log_totals[pair_index]
        probable = jnp.exp(scores - log_pair[:, :, None])
        grad_probable = jnp.einsum(
            "qhd,khd->hqk", grad_part, value_part, preferred_element_type=float_type
        )
        grad_scores = probable * (
            grad_probable - jnp.sum(grad_probable * probable, axis=2, keepdims=True)
        )
        grad_scores = grad_scores.astype(narrow_type)
        grad_query = (
            jnp.einsum("hqk,khd->qhd", grad_scores, key_part, preferred_element_type=float_type)
            * scaling_score
        )
        grad_key = (
            jnp.einsum("hqk,qhd->khd", grad_scores, query_part, preferred_element_type=float_type)
            * scaling_score
        )
        grad_value = jnp.einsum(
            "hqk,qhd->khd",
            probable.astype(narrow_type),
            grad_part,
            preferred_element_type=float_type,
        )
        return (
            grad_query.reshape(row_count, pair_width),
            grad_key.reshape(window_rows, pair_width),
            grad_value.reshape(window_rows, pair_width),
        )

    grad_query_pairs, grad_key_pairs, grad_value_pairs = lax.map(
        pair_backward, jnp.arange(pair_count)
    )
    grad_queries = grad_query_pairs.transpose(1, 0, 2).reshape(row_count, features)
    grad_keys = grad_key_pairs.transpose(1, 0, 2).reshape(window_rows, features)
    grad_values = grad_value_pairs.transpose(1, 0, 2).reshape(window_rows, features)
    grad_window = jnp.concatenate([grad_keys, grad_values], axis=1)
    padded_grads = jnp.pad(grad_window, ((window_start, window_start), (0, 0)))
    grad_pairs = padded_grads[HOPS * row_count : (HOPS + 1) * row_count]
    for distance in range(1, HOPS + 1):
        lower_piece = padded_grads[
            (HOPS - distance) * row_count : (HOPS - distance + 1) * row_count
        ]
        higher_piece = padded_grads[
            (HOPS + distance) * row_count : (HOPS + distance + 1) * row_count
        ]
        grad_pairs = grad_pairs + passed_along(
            lower_piece.astype(jnp.bfloat16), ("seq", "fsdp"), -distance
        ).astype(lower_piece.dtype)
        grad_pairs = grad_pairs + passed_along(
            higher_piece.astype(jnp.bfloat16), ("seq", "fsdp"), distance
        ).astype(higher_piece.dtype)
    grad_projected = jnp.concatenate([grad_queries, grad_pairs], axis=1).astype(narrow_type)
    grad_blocks = grad_projected.reshape(row_count, 3, features)
    grad_rank_qkv = (
        jnp.einsum("tpd,prd->tpr", grad_blocks, attention_up[:3], preferred_element_type=float_type)
        * select[:, None, :]
    ).astype(narrow_type)
    grad_qkv_down = jnp.einsum(
        "td,tpr->pdr", normed_first, grad_rank_qkv, preferred_element_type=float_type
    )
    grad_qkv_up = jnp.einsum(
        "tpr,tpd->prd", rank_qkv, grad_blocks, preferred_element_type=float_type
    )
    grad_normed_first = transposed_right(grad_projected, qkv_full) + jnp.einsum(
        "tpr,pdr->td", grad_rank_qkv, attention_down[:3], preferred_element_type=float_type
    )
    input_gradient = grad_middle + norm_backward(
        grad_normed_first, gains_wide[0], normal_first, scaling_first
    )
    grad_attention_down = jnp.concatenate([grad_qkv_down, grad_out_down[None]], axis=0)
    grad_attention_up = jnp.concatenate([grad_qkv_up, grad_out_up[None]], axis=0)
    summed = (
        lax.psum_scatter(grad_attention_down, ("seq", "fsdp"), scatter_dimension=1, tiled=True),
        lax.psum_scatter(grad_attention_up, ("seq", "fsdp"), scatter_dimension=2, tiled=True),
        lax.psum_scatter(grad_expand_down, ("seq", "fsdp"), scatter_dimension=0, tiled=True),
        lax.psum_scatter(grad_expand_up, ("seq", "fsdp"), scatter_dimension=1, tiled=True),
        lax.psum_scatter(grad_contract_down, ("seq", "fsdp"), scatter_dimension=0, tiled=True),
        lax.psum_scatter(grad_contract_up, ("seq", "fsdp"), scatter_dimension=1, tiled=True),
    )
    return (
        result,
        input_gradient,
        summed[0],
        summed[1],
        summed[2],
        summed[3],
        summed[4],
        summed[5],
    )


MESH_ID = pl.DeviceIdType.MESH
CORES, SIDE_X, SIDE_Y = 1, 2, 4
ANYWHERE = pl.BlockSpec(memory_space=pl.ANY)
IN_VMEM = pl.BlockSpec(memory_space=pltpu.VMEM)
IN_SMEM = pl.BlockSpec(memory_space=pltpu.SMEM)


def place_here():
    return lax.axis_index("seq"), lax.axis_index("fsdp")


def remote(source, target, send, receive, seq, fsdp):
    return pltpu.make_async_remote_copy(
        src_ref=source,
        dst_ref=target,
        send_sem=send,
        recv_sem=receive,
        device_id=(seq, fsdp),
        device_id_type=MESH_ID,
    )


def greet(barrier, seq, fsdp):
    pl.semaphore_signal(barrier, 1, device_id=(seq, fsdp), device_id_type=MESH_ID)


def greet_neighbours(barrier, seq, fsdp, depth):
    for bit in (CORES, SIDE_X, SIDE_Y):
        greet(barrier, seq ^ bit, fsdp)
    for step in range(1, depth):
        greet(barrier, seq, lax.rem(fsdp + step, depth))


WHOLE, OPEN, LINE = 0, 1, 2


class Gather:
    STEPS = 10

    def __init__(self, depth, send, receive):
        self.depth, self.send, self.receive = depth, send, receive
        self.seq, self.fsdp = place_here()
        self.me = self.seq * depth + self.fsdp
        self.inside = (self.fsdp == 1) | (self.fsdp == 2)

    def copy(self, index, step, source, target, seq, fsdp):
        at = index * self.STEPS + step
        return remote(source, target, self.send.at[at], self.receive.at[at], seq, fsdp)

    def part(self, chunk, at_seq, first, count):
        full, rows, columns, _, kind, _ = chunk
        base = 0 if kind == LINE else at_seq * self.depth
        return full.at[pl.ds(base + first, count), rows, columns]

    def group(self, chunk, at_seq):
        return self.part(chunk, at_seq, 0, self.depth)

    def sides(self, chunk):
        return (SIDE_X, SIDE_Y) if chunk[3] else (SIDE_Y, SIDE_X)

    def line(self, index, chunk, step):
        pair = lax.div(self.fsdp, 2)
        if step == 0:
            piece, to = self.part(chunk, self.seq, self.fsdp, 1), self.fsdp ^ 1
            if chunk[5] is not None:
                source = chunk[5].at[pl.ds(0, 1), chunk[1], chunk[2]]
                return self.copy(index, step, source, piece, self.seq, to)
        elif step == 1:
            piece, to = self.part(chunk, self.seq, 2 * pair, 2), 3 - self.fsdp
        else:
            piece, to = self.part(chunk, self.seq, 2 - 2 * pair, 2), self.fsdp ^ 1
        return self.copy(index, step, piece, piece, self.seq, to)

    def over(self, index, chunk, step):
        a, b = self.sides(chunk)
        piece = self.group(chunk, self.seq ^ a if step == 2 else self.seq)
        return self.copy(index, 3 + step, piece, piece, self.seq ^ (b if step else a), self.fsdp)

    def across(self, index, chunk, step):
        a, b = self.sides(chunk)
        piece = self.group(chunk, self.seq ^ (0, a, b, a ^ b)[step])
        return self.copy(index, 6 + step, piece, piece, self.seq ^ CORES, self.fsdp)

    def own(self, index, chunk):
        self.line(index, chunk, 0).start()

    def inner(self, index, chunk):
        @pl.when(self.inside)
        def _():
            self.line(index, chunk, 0).wait_recv()
            self.line(index, chunk, 1).start()

    def outer(self, index, chunk):
        @pl.when(self.inside)
        def _():
            self.line(index, chunk, 1).wait_recv()
            self.line(index, chunk, 2).start()

    def arrive(self, index, chunk):
        @pl.when(jnp.logical_not(self.inside))
        def _():
            self.line(index, chunk, 0).wait_recv()
            self.line(index, chunk, 2).wait_recv()

    def first(self, index, chunk):
        self.arrive(index, chunk)
        self.over(index, chunk, 0).start()
        self.over(index, chunk, 1).start()
        self.across(index, chunk, 0).start()

    def second(self, index, chunk):
        self.over(index, chunk, 0).wait_recv()
        if chunk[4] == WHOLE:
            self.over(index, chunk, 2).start()
        self.across(index, chunk, 1).start()

    def third(self, index, chunk):
        self.over(index, chunk, 1).wait_recv()
        self.across(index, chunk, 2).start()
        if chunk[4] == WHOLE:
            self.over(index, chunk, 2).wait_recv()
            self.across(index, chunk, 3).start()

    def finish(self, index, chunk):
        for step in range(4 if chunk[4] == WHOLE else 3):
            self.across(index, chunk, step).wait_recv()

    def drain(self, index, chunk):
        self.line(index, chunk, 0).wait_send()

        @pl.when(self.inside)
        def _():
            self.line(index, chunk, 1).wait_send()
            self.line(index, chunk, 2).wait_send()

        if chunk[4] == LINE:
            return
        for step in range(3 if chunk[4] == WHOLE else 2):
            self.over(index, chunk, step).wait_send()
        for step in range(4 if chunk[4] == WHOLE else 3):
            self.across(index, chunk, step).wait_send()


class Exchange:
    def __init__(self, depth, heads):
        self.depth, self.heads = depth, heads
        self.seq, self.fsdp = place_here()
        self.me = self.seq * depth + self.fsdp
        self.core, self.half = lax.rem(self.seq, 2), lax.div(self.seq, 4)
        self.head = lax.div(self.seq, 2) * depth + self.fsdp
        self.same = (self.half == self.core).astype(jnp.int32)

    def holder(self, k):
        return lax.div(k, self.depth) * 2 + self.half, lax.rem(k, self.depth)

    def owner(self, k):
        block = self.core * self.heads + k
        return lax.div(block, self.depth), lax.rem(block, self.depth)

    def away_head(self, k):
        return (k != self.head) | (self.half != self.core)

    def away_block(self, k):
        return self.core * self.heads + k != self.me

    def greet_holders(self, barrier):
        @pl.loop(0, self.heads)
        def _(k):
            @pl.when(self.away_head(k))
            def _():
                greet(barrier, *self.holder(k))

        return self.heads - self.same

    def greet_owners(self, barrier):
        @pl.loop(0, self.heads)
        def _(k):
            @pl.when(self.away_block(k))
            def _():
                greet(barrier, *self.owner(k))

        return self.heads - self.same


def as_matrix(block):
    return block.reshape(-1, block.shape[-1])


def turned(block, tile=256):
    return block.astype(float_type).T.astype(narrow_type)


def rows_of_vectors(ve, target):
    flat = as_matrix(ve[:, 0:32, :]).astype(float_type)
    target[...] = flat.T[0:16]


def by_feature_wide(block):
    return jnp.concatenate([block, jnp.zeros((112, block.shape[1]), block.dtype)], axis=0)


def selected(lens_ref, choice_ref, block, rows, lanes):
    place = lax.broadcasted_iota(jnp.int32, (rows, lanes), 0) + block * rows
    lane = lax.broadcasted_iota(jnp.int32, (rows, lanes), 1)
    chosen = jnp.zeros((rows, lanes), jnp.int32)
    start = jnp.int32(0)
    for image in range(lens_ref.shape[0]):
        end = start + lens_ref[image]
        chosen = jnp.where((place >= start) & (place < end), choice_ref[image] * RANK, chosen)
        start = end
    return jnp.where((lane >= chosen) & (lane < chosen + RANK), 1.0, 0.0).astype(float_type)


def stood_up(block):
    n, m = block.shape
    block = block.astype(float_type)
    if m < 128:
        block = jnp.concatenate([block, jnp.zeros((n, 128 - m), float_type)], axis=1)
    if n < 128:
        block = jnp.concatenate([block, jnp.zeros((128 - n, 128), float_type)], axis=0)
    return block.T[0:m].astype(narrow_type)


def attention_in_kernel(
    depth,
    halo,
    heads,
    chunks,
    lens_ref,
    choice_ref,
    tok_in,
    gains_in,
    biases_in,
    bias_in,
    wqkv,
    wout,
    a_att,
    b_att,
    a_exp,
    b_con,
    w2,
    a_con,
    b_exp_in,
    w1,
    fa_out,
    ve_out,
    f2,
    line_a,
    line_b,
    y_ref,
    rank_ref,
    fa,
    ve,
    proj,
    normed,
    vectors,
    tok,
    gains,
    biases,
    bias,
    b_exp,
    shard_f2,
    shard_a,
    shard_b,
    select,
    send,
    receive,
    local,
    piece_send,
    piece_receive,
    piece_local,
):
    gather, swap = Gather(depth, send, receive), Exchange(depth, heads)
    me, seq, fsdp = swap.me, swap.seq, swap.fsdp
    core, half, head, own = swap.core, swap.half, swap.head, heads
    features = normed.shape[1]
    wide = features + 256
    barrier = pltpu.get_barrier_semaphore()
    greet_neighbours(barrier, seq, fsdp, depth)
    waits = 3 + depth - 1 + swap.greet_owners(barrier)
    half_columns = line_a.shape[2]
    small = [
        (gains_in, gains.at[0:4]),
        (biases_in, biases.at[0:5]),
        (bias_in, bias),
        (b_exp_in, b_exp),
        (tok_in, tok),
    ]
    places = []
    for p in range(4):
        source = wqkv.at[:, pl.ds(p * features, features)] if p < 3 else wout
        places.append((source, fa.at[me, :, pl.ds(p * wide, features)]))
        places.append((a_att.at[p], fa.at[me, :, pl.ds(p * wide + features, 128)]))
        places.append((b_att.at[p], fa.at[me, :, pl.ds(p * wide + features + 128, 128)]))
    places.append((a_exp, fa.at[me, :, pl.ds(4 * wide, 128)]))
    places.append((b_con, fa.at[me, :, pl.ds(4 * wide + 128, 128)]))
    places.append((w2, shard_f2.at[0, :, pl.ds(0, features)]))
    places.append((a_con, shard_f2.at[0, :, pl.ds(features, 128)]))
    places.append((w1.at[:, pl.ds(0, half_columns)], shard_a.at[0]))
    places.append((w1.at[:, pl.ds(half_columns, half_columns)], shard_b.at[0]))
    placed = [pltpu.make_async_copy(a, b, local.at[i]) for i, (a, b) in enumerate(small + places)]
    for copy in placed:
        copy.start()
    for copy in placed[: len(small) - 1]:
        copy.wait()
    shard_f2[0, :, features + 128 : wide] = stood_up(b_exp[...])
    by_feature = jnp.concatenate(
        [gains[0:4].astype(float_type), biases[0:5].astype(float_type), jnp.zeros((7, 32), float_type)], axis=0
    )
    ve[me, 0:32] = stood_up(by_feature_wide(by_feature))
    ve[me, 32:48] = jnp.broadcast_to(bias[...].astype(float_type), (16, 128)).astype(narrow_type)
    for copy in placed[len(small) - 1 :]:
        copy.wait()
    own_shards = [
        pltpu.make_async_copy(shard.at[0], full.at[slot], local.at[i])
        for i, (shard, full, slot) in enumerate(((shard_f2, f2, me), (shard_a, line_a, fsdp), (shard_b, line_b, fsdp)))
    ]
    for copy in own_shards:
        copy.start()
    refs = {
        "ve": (ve, WHOLE, None),
        "fa": (fa, WHOLE, None),
        "f2": (f2, OPEN, shard_f2),
        "a": (line_a, LINE, shard_a),
        "b": (line_b, LINE, shard_b),
    }
    chunks = [
        (refs[name][0], rows, columns, flip) + refs[name][1:] for name, rows, columns, flip in chunks
    ]
    first_hidden = [i for i, chunk in enumerate(chunks) if chunk[4] != WHOLE][:1]
    pl.semaphore_wait(barrier, waits)
    early = [i for i, chunk in enumerate(chunks) if chunk[0] is fa or chunk[0] is ve]
    for index in early:
        gather.own(index, chunks[index])
    select[...] = selected(lens_ref, choice_ref, me, *select.shape)
    base = core * (own - halo)
    slot = me - half * (own - halo)

    def piece(p, k):
        return remote(
            proj.at[p, k],
            y_ref.at[slot, p],
            piece_send.at[p, k],
            piece_receive.at[p, lax.rem(me, own)],
            *swap.holder(k),
        )

    def arrival(p, k):
        return remote(
            proj.at[p, 0],
            y_ref.at[core * own + k - base, p],
            piece_send.at[p, k],
            piece_receive.at[p, k],
            seq ^ CORES,
            fsdp,
        )

    def kept(p):
        return pltpu.make_async_copy(proj.at[p, head], y_ref.at[me - base, p], piece_local.at[p])

    def norm():
        rows_of_vectors(ve, vectors)
        rows = tok[...].astype(float_type)
        normed[...] = layer_norm(rows, vectors[0:1], vectors[4:5])[0].astype(narrow_type)

    def project(p):
        down = as_matrix(fa[:, :, p * wide + features : p * wide + features + 128])
        rank = (matmul(normed[...], down) * select[...]).astype(narrow_type)
        rank_ref[p] = rank

        @pl.loop(0, features // 256)
        def _(j):
            weight = as_matrix(fa[:, :, pl.ds(pl.multiple_of(p * wide + j * 256, 128), 256)])
            up = as_matrix(fa[pl.ds(j * 8, 8), :, p * wide + features + 128 : (p + 1) * wide])
            result = matmul(normed[...], weight) + transposed_right(rank, up)
            if p == 0:
                result = result + vectors[5:6, pl.ds(pl.multiple_of(j * 256, 128), 256)]
            proj[p, pl.ds(j * 4, 4)] = result.T.astype(narrow_type).reshape(4, 64, 256)

            @pl.loop(0, 4)
            def _(i):
                k = j * 4 + i

                @pl.when(swap.away_head(k))
                def _():
                    piece(p, k).start()

        @pl.when(half == core)
        def _():
            kept(p).start()

    after = {0: norm, 2: lambda: project(0), 4: lambda: project(1), 6: lambda: project(2)}
    after_attention = [i for i, chunk in enumerate(chunks) if chunk[0] is fa][-1]
    outs = [
        pltpu.make_async_copy(fa, fa_out, local.at[3]),
        pltpu.make_async_copy(ve, ve_out, local.at[4]),
    ]

    def store():
        for copy in outs:
            copy.start()

    steps = (gather.own, gather.inner, gather.outer, gather.first, gather.second, gather.third, gather.finish)
    for turn in range(-LOOKAHEAD, len(chunks) + 3):
        for delay, step in zip((-LOOKAHEAD, -2, -1, 0, 1, 2, 3), steps):
            index = turn - delay
            if not 0 <= index < len(chunks) or (delay == -LOOKAHEAD and index in early):
                continue
            chunk = chunks[index]
            if delay == -2 and index in first_hidden:
                for copy in own_shards:
                    copy.wait()
            if chunk[4] == LINE and delay == 0:
                step = gather.arrive
            if chunk[4] == LINE and delay > 0:
                continue
            step(index, chunk)
            if delay == 3:
                after.get(index, lambda: None)()
                if index == after_attention:
                    store()

    @pl.loop(0, own)
    def _(k):
        @pl.when(swap.away_block(k))
        def _():
            for p in range(3):
                arrival(p, k).wait_recv()

    @pl.when(half == core)
    def _():
        for p in range(3):
            kept(p).wait()

    first = jnp.where(core == 0, own - halo, own)
    over = remote(
        y_ref.at[pl.ds(first - base, halo), 1:3],
        y_ref.at[pl.ds(first - (own - halo) * (1 - core), halo), 1:3],
        piece_send.at[3, 0],
        piece_receive.at[3, 0],
        seq ^ CORES,
        fsdp,
    )
    over.start()
    over.wait()

    @pl.loop(0, heads)
    def _(k):
        @pl.when(swap.away_head(k))
        def _():
            for p in range(3):
                piece(p, k).wait_send()

    for index, chunk in enumerate(chunks):
        gather.drain(index, chunk)
    for copy in outs:
        copy.wait()


def attention_in(lengths, choice, tokens, arrays, halo, depth, heads, devices, collective):
    rows, features = tokens.shape
    wide = features + 256
    total = 4 * wide + 256
    share, hidden_share, hidden_total = features // devices, arrays[9].shape[0], arrays[12].shape[1]
    chunks = [("ve", slice(0, 48), slice(0, 128), 0)]
    for p in range(3):
        chunks.append(("fa", slice(0, share), slice(p * wide, p * wide + wide // 2), 0))
        chunks.append(("fa", slice(0, share), slice(p * wide + wide // 2, (p + 1) * wide), 1))
    middle = 3 * wide + (total - 3 * wide) // 2
    chunks.append(("fa", slice(0, share), slice(3 * wide, middle), 0))
    chunks.append(("fa", slice(0, share), slice(middle, total), 1))
    for part in range(0, hidden_share, 32):
        chunks.append(("f2", slice(part, part + 32), slice(0, wide // 2), 0))
        chunks.append(("f2", slice(part, part + 32), slice(wide // 2, wide), 1))
    for part in range(0, hidden_total // 2, 1024):
        chunks.append(("a", slice(0, share), slice(part, part + 1024), 0))
        chunks.append(("b", slice(0, share), slice(part, part + 1024), 1))
    copies = Gather.STEPS * len(chunks)
    return pl.pallas_call(
        functools.partial(attention_in_kernel, depth, halo, heads, chunks),
        out_shape=(
            jax.ShapeDtypeStruct((devices, share, total), narrow_type),
            jax.ShapeDtypeStruct((devices, 48, 128), narrow_type),
            jax.ShapeDtypeStruct((devices, hidden_share, wide), narrow_type),
            jax.ShapeDtypeStruct((depth, share, hidden_total // 2), narrow_type),
            jax.ShapeDtypeStruct((depth, share, hidden_total // 2), narrow_type),
            jax.ShapeDtypeStruct((heads + halo, 3, features // heads, rows), narrow_type),
            jax.ShapeDtypeStruct((3, rows, 128), narrow_type),
        ),
        in_specs=[IN_SMEM, IN_SMEM] + [ANYWHERE] * (1 + len(arrays)),
        out_specs=(ANYWHERE,) * 6 + (IN_VMEM,),
        scratch_shapes=[
            pltpu.VMEM((devices, share, total), narrow_type),
            pltpu.VMEM((devices, 48, 128), narrow_type),
            pltpu.VMEM((3, heads, features // heads, rows), narrow_type),
            pltpu.VMEM((rows, features), narrow_type),
            pltpu.VMEM((16, features), float_type),
            pltpu.VMEM((rows, features), narrow_type),
            pltpu.VMEM((4, share), narrow_type),
            pltpu.VMEM((5, share), narrow_type),
            pltpu.VMEM((1, 128), narrow_type),
            pltpu.VMEM((128, 128), narrow_type),
            pltpu.VMEM((1, hidden_share, wide), narrow_type),
            pltpu.VMEM((1, share, hidden_total // 2), narrow_type),
            pltpu.VMEM((1, share, hidden_total // 2), narrow_type),
            pltpu.VMEM((rows, 128), float_type),
            pltpu.SemaphoreType.DMA((copies,)),
            pltpu.SemaphoreType.DMA((copies,)),
            pltpu.SemaphoreType.DMA((24,)),
            pltpu.SemaphoreType.DMA((4, heads)),
            pltpu.SemaphoreType.DMA((4, heads)),
            pltpu.SemaphoreType.DMA((3,)),
        ],
        compiler_params=pltpu.CompilerParams(
            collective_id=collective, has_side_effects=True, vmem_limit_bytes=60 << 20
        ),
    )(lengths, choice, tokens, *arrays)


LOOKAHEAD = 5
HIDDEN_TILE = 512


def middle_kernel(
    depth,
    heads,
    lens_ref,
    choice_ref,
    att_ref,
    tok_ref,
    cot_ref,
    fa_in,
    ve,
    f2_in,
    line_a,
    line_b,
    ya,
    yb,
    xa,
    xb,
    result_ref,
    gm_ref,
    terms,
    gy_ref,
    fa,
    f2,
    f1,
    att_t,
    att,
    gatt_t,
    vectors,
    hidden_bias,
    middle,
    normal,
    normed,
    branch,
    grad_branch,
    grad_normed,
    ranks,
    rank_sums,
    select,
    send,
    receive,
    local,
    a_send,
    a_receive,
    b_send,
    b_receive,
    own_local,
):
    swap = Exchange(depth, heads)
    me, seq, fsdp = swap.me, swap.seq, swap.fsdp
    core, half, head, own = swap.core, swap.half, swap.head, heads
    devices, share = f1.shape[0], f1.shape[1]
    row_count, features = tok_ref.shape
    wide = features + 256
    tiles = f1.shape[2] // HIDDEN_TILE
    in_tile = HIDDEN_TILE // f2.shape[1]
    barrier = pltpu.get_barrier_semaphore()
    greet_neighbours(barrier, seq, fsdp, depth)
    waits = 3 + depth - 1 + swap.greet_owners(barrier) + swap.greet_holders(barrier)
    half_columns = line_a.shape[2]
    left, right = pl.ds(0, half_columns), pl.ds(half_columns, half_columns)
    lines = [
        (line, f1.at[pl.ds((seq ^ bit) * depth, depth), :, columns])
        for line, bit, columns in (
            (line_a, 0, left),
            (line_b, 0, right),
            (ya, SIDE_Y, left),
            (yb, SIDE_Y, right),
            (xa, SIDE_X, left),
            (xb, SIDE_X, right),
        )
    ]
    groups = [pl.ds((seq ^ k) * depth, depth) for k in range(8)]
    loads = (
        [pltpu.make_async_copy(fa_in.at[:, :, pl.ds(3 * wide, wide + 256)], fa, local.at[0])]
        + [pltpu.make_async_copy(line, place, local.at[1 + i]) for i, (line, place) in enumerate(lines)]
        + [pltpu.make_async_copy(f2_in.at[groups[k]], f2.at[groups[k]], local.at[7 + k]) for k in range(6)]
    )
    for copy in loads:
        copy.start()
    pl.semaphore_wait(barrier, waits)
    corners = [
        remote(ya, lines[2][1], send.at[0], receive.at[0], seq ^ SIDE_X, fsdp),
        remote(xb, lines[5][1], send.at[1], receive.at[1], seq ^ SIDE_Y, fsdp),
    ]
    tops, tails = pl.ds(0, wide // 2), pl.ds(wide // 2, wide // 2)
    f2_parts = ((SIDE_Y, SIDE_X, tops), (SIDE_X, SIDE_Y, tails))
    for i, (via, to, columns) in enumerate(f2_parts):
        line = pl.ds((seq ^ via) * depth, depth)
        corners.append(
            remote(
                f2_in.at[line, :, columns],
                f2.at[line, :, columns],
                send.at[10 + i],
                receive.at[10 + i],
                seq ^ to,
                fsdp,
            )
        )
    across = [
        remote(line, place, send.at[2 + i], receive.at[2 + i], seq ^ CORES, fsdp)
        for i, (line, place) in enumerate(lines)
    ]
    for i, columns in enumerate((left, right)):
        place = f1.at[pl.ds((seq ^ SIDE_X ^ SIDE_Y) * depth, depth), :, columns]
        across.append(remote(place, place, send.at[8 + i], receive.at[8 + i], seq ^ CORES, fsdp))
    f2_across = remote(
        f2.at[groups[6]], f2.at[groups[6]], send.at[12], receive.at[12], seq ^ CORES, fsdp
    )

    def attended_piece(k):
        return remote(att_ref.at[k], att_t.at[head], a_send.at[k], a_receive.at[head], *swap.owner(k))

    def attended_arrival(k):
        return remote(att_ref.at[0], att_t.at[k], a_send.at[k], a_receive.at[k], seq ^ CORES, fsdp)

    attended_kept = pltpu.make_async_copy(att_ref.at[me - core * own], att_t.at[head], own_local.at[0])

    @pl.when(half == core)
    def _():
        attended_kept.start()

    @pl.loop(0, own)
    def _(step):
        k = lax.rem(step + me, own)

        @pl.when(swap.away_block(k))
        def _():
            attended_piece(k).start()

    for copy in corners + across[:6]:
        copy.start()
    select[...] = selected(lens_ref, choice_ref, me, *select.shape)
    rows_of_vectors(ve, vectors)
    for d in range(devices):
        hidden_bias[:, d * 128 : (d + 1) * 128] = ve[d, 32:48, :].astype(float_type)[0:8]
    grad_branch[...] = (vectors[3:4] * cot_ref[...].astype(float_type)).astype(narrow_type)
    loads[0].wait()
    contract_up = as_matrix(fa[:, :, wide + 128 : wide + 256])
    ranks[1] = (matmul(grad_branch[...], contract_up) * select[...]).astype(narrow_type)
    branch[...] = jnp.zeros_like(branch)
    grad_normed[...] = jnp.zeros_like(grad_normed)
    rank_sums[...] = jnp.zeros_like(rank_sums)

    @pl.loop(0, heads)
    def _(k):
        @pl.when(swap.away_head(k))
        def _():
            attended_arrival(k).wait_recv()

    @pl.when(half == core)
    def _():
        attended_kept.wait()

    for i in range(2):
        corners[i].wait_recv()
        across[6 + i].start()
    for j in range(4):
        att[:, j * 256 : (j + 1) * 256] = turned(as_matrix(att_t[4 * j : 4 * j + 4]))
    out_down = as_matrix(fa[:, :, features : features + 128])
    rank_out = (matmul(att[...], out_down) * select[...]).astype(narrow_type)
    ranks[2] = rank_out

    @pl.loop(0, 4)
    def _(j):
        at = pl.ds(pl.multiple_of(j * 256, 128), 256)
        weight = as_matrix(fa[:, :, at])
        up = as_matrix(fa[pl.ds(j * 8, 8), :, features + 128 : wide])
        mixed = matmul(att[...], weight) + transposed_right(rank_out, up) + vectors[6:7, at]
        middle[:, at] = tok_ref[:, at].astype(float_type) + vectors[1:2, at] * mixed

    shifted, normal_rows, scaling = layer_norm(middle[...], vectors[2:3], vectors[7:8])
    normal[...] = normal_rows
    normed[...] = shifted.astype(narrow_type)
    expand_down = as_matrix(fa[:, :, wide : wide + 128])
    rank_expand = (matmul(normed[...], expand_down) * select[...]).astype(narrow_type)
    ranks[0] = rank_expand
    ranks[3, 0:128] = turned(rank_expand)[:, 0:128]
    ranks[3, 128:256] = turned(rank_expand)[:, 128:256]
    ranks[4, 0:128] = turned(ranks[1])[:, 0:128]
    ranks[4, 128:256] = turned(ranks[1])[:, 128:256]
    for copy in loads[1:]:
        copy.wait()
    for copy in across:
        copy.wait_recv()

    def hidden(k):
        @pl.when(k == 6)
        def _():
            corners[2].wait_recv()
            corners[3].wait_recv()
            f2_across.start()

        @pl.when(k == 7)
        def _():
            f2_across.wait_recv()

        c = seq ^ k
        at = pl.ds(pl.multiple_of(c * HIDDEN_TILE, 128), HIDDEN_TILE)
        slots = pl.ds(c * in_tile, in_tile)
        expand = as_matrix(f1[:, :, at])
        contract = as_matrix(f2[slots, :, 0:features])
        down = as_matrix(f2[slots, :, features : features + 128])
        up = as_matrix(f2[slots, :, features + 128 : wide])
        before = matmul(normed[...], expand) + transposed_right(ranks[0], up) + hidden_bias[0:1, at]
        total = 0.5 * (1.0 + lax.erf(before * 0.7071067811865476))
        density = jnp.exp(-0.5 * before * before) * 0.3989422804014327
        active = (before * total).astype(narrow_type)
        slope = total + before * density
        branch[...] += matmul(active, contract)
        rank_sums[0] += matmul(active, down)
        grad_active = transposed_right(grad_branch[...], contract) + transposed_right(ranks[1], down)
        grad_hidden = (grad_active * slope).astype(narrow_type)
        rank_sums[1] += matmul(grad_hidden, up)
        grad_normed[...] += transposed_right(grad_hidden, expand)
        turned_expand = jnp.concatenate([ranks[3, 0:128], ranks[3, 128:256]], axis=1)
        turned_contract = jnp.concatenate([ranks[4, 0:128], ranks[4, 128:256]], axis=1)
        grad_up = matmul(turned_expand, grad_hidden).astype(narrow_type)
        grad_down = matmul(turned_contract, active).astype(narrow_type)
        for i in range(in_tile):
            terms[c * in_tile + i, 96:224] = grad_up[:, i * 128 : (i + 1) * 128]
            terms[c * in_tile + i, 224:352] = grad_down[:, i * 128 : (i + 1) * 128]

    pl.loop(0, tiles)(hidden)
    rank_contract = (rank_sums[0] * select[...]).astype(narrow_type)
    grad_rank_expand = (rank_sums[1] * select[...]).astype(narrow_type)
    gradient = grad_normed[...] + transposed_right(grad_rank_expand, expand_down)
    gm_ref[...] = cot_ref[...].astype(float_type) + norm_backward(gradient, vectors[2:3], normal[...], scaling)
    grad_mixed = (vectors[1:2] * gm_ref[...]).astype(narrow_type)
    out_up = as_matrix(fa[:, :, features + 128 : wide])
    grad_rank_out = (matmul(grad_mixed, out_up) * select[...]).astype(narrow_type)

    def gradient_piece(k):
        return remote(
            gatt_t.at[k], gy_ref.at[lax.rem(me, own)], b_send.at[k], b_receive.at[lax.rem(me, own)], *swap.holder(k)
        )

    def gradient_arrival(k):
        return remote(gatt_t.at[0], gy_ref.at[k], b_send.at[k], b_receive.at[k], seq ^ CORES, fsdp)

    gradient_kept = pltpu.make_async_copy(gatt_t.at[head], gy_ref.at[lax.rem(me, own)], own_local.at[1])

    @pl.loop(0, 4)
    def _(j):
        slots = pl.ds(j * 8, 8)
        weight = as_matrix(fa[slots, :, 0:features])
        down = as_matrix(fa[slots, :, features : features + 128])
        rows = transposed_right(grad_mixed, weight) + transposed_right(grad_rank_out, down)
        gatt_t[pl.ds(j * 4, 4)] = rows.T.astype(narrow_type).reshape(4, 64, 256)

        @pl.loop(0, 4)
        def _(i):
            k = j * 4 + i

            @pl.when(swap.away_head(k))
            def _():
                gradient_piece(k).start()

    @pl.when(half == core)
    def _():
        gradient_kept.start()

    up_rows = transposed_right(rank_contract, contract_up)
    result_ref[...] = (
        middle[...] + vectors[3:4] * (branch[...] + vectors[8:9] + up_rows)
    ).astype(narrow_type)
    shaped = (devices, share, 128)
    terms[:, 0:32] = matmul(as_matrix(att_t[...]), grad_rank_out).astype(narrow_type).reshape(shaped)
    terms[:, 32:64] = transposed_left(grad_mixed, rank_out).astype(narrow_type).reshape(shaped)
    terms[:, 64:96] = transposed_left(normed[...], grad_rank_expand).astype(narrow_type).reshape(shaped)
    terms[:, 352:384] = transposed_left(grad_branch[...], rank_contract).astype(narrow_type).reshape(shaped)

    @pl.loop(0, own)
    def _(k):
        @pl.when(swap.away_block(k))
        def _():
            gradient_arrival(k).wait_recv()
            attended_piece(k).wait_send()

    @pl.when(half == core)
    def _():
        gradient_kept.wait()

    @pl.loop(0, heads)
    def _(k):
        @pl.when(swap.away_head(k))
        def _():
            gradient_piece(k).wait_send()

    for copy in corners + across + [f2_across]:
        copy.wait_send()


def middle_part(lengths, choice, att, tokens, cotangent, fa, ve, f2, lines, depth, collective):
    heads, width, rows = att.shape
    features = tokens.shape[1]
    wide = features + 256
    devices, hidden_share = f2.shape[0], f2.shape[1]
    share, hidden_total = features // devices, 2 * lines[0].shape[2]
    copies = 13

    def wide_rows():
        return pltpu.VMEM((rows, features), float_type)

    def narrow_rows():
        return pltpu.VMEM((rows, features), narrow_type)

    return pl.pallas_call(
        functools.partial(middle_kernel, depth, heads),
        out_shape=(
            jax.ShapeDtypeStruct((rows, features), narrow_type),
            jax.ShapeDtypeStruct((rows, features), float_type),
            jax.ShapeDtypeStruct((devices, 384, 128), narrow_type),
            jax.ShapeDtypeStruct((heads, width, rows), narrow_type),
        ),
        in_specs=[IN_SMEM, IN_SMEM, IN_VMEM, IN_VMEM, IN_VMEM, ANYWHERE, IN_VMEM] + [ANYWHERE] * 7,
        out_specs=(IN_VMEM, IN_VMEM, IN_VMEM, ANYWHERE),
        scratch_shapes=[
            pltpu.VMEM((devices, share, wide + 256), narrow_type),
            pltpu.VMEM(f2.shape, narrow_type),
            pltpu.VMEM((devices, share, hidden_total), narrow_type),
            pltpu.VMEM((heads, width, rows), narrow_type),
            narrow_rows(),
            pltpu.VMEM((heads, width, rows), narrow_type),
            pltpu.VMEM((16, features), float_type),
            pltpu.VMEM((8, hidden_total), float_type),
            wide_rows(),
            wide_rows(),
            narrow_rows(),
            wide_rows(),
            narrow_rows(),
            wide_rows(),
            pltpu.VMEM((5, rows, 128), narrow_type),
            pltpu.VMEM((2, rows, 128), float_type),
            pltpu.VMEM((rows, 128), float_type),
            pltpu.SemaphoreType.DMA((copies,)),
            pltpu.SemaphoreType.DMA((copies,)),
            pltpu.SemaphoreType.DMA((13,)),
            pltpu.SemaphoreType.DMA((heads,)),
            pltpu.SemaphoreType.DMA((heads,)),
            pltpu.SemaphoreType.DMA((heads,)),
            pltpu.SemaphoreType.DMA((heads,)),
            pltpu.SemaphoreType.DMA((2,)),
        ],
        compiler_params=pltpu.CompilerParams(
            collective_id=collective, has_side_effects=True, vmem_limit_bytes=54 << 20
        ),
    )(lengths, choice, att, tokens, cotangent, fa, ve, f2, *lines)


class Reduce:
    COPIES = 16

    def __init__(self, depth, base, terms, first, second, third, fourth, send, receive):
        self.depth, self.base, self.terms = depth, base, terms
        self.buffers = first, second, third, fourth
        self.send, self.receive = send, receive
        self.seq, self.fsdp = place_here()
        self.core, self.x, self.y = lax.rem(self.seq, 2), lax.rem(lax.div(self.seq, 2), 2), lax.div(self.seq, 4)
        half = terms.shape[1] // 2
        self.halves = (slice(0, half), slice(half, 2 * half))

    def copy(self, step, source, target, seq, fsdp):
        at = self.base + step
        return remote(source, target, self.send.at[at], self.receive.at[at], seq, fsdp)

    def to_core(self):
        first = self.buffers[0]
        lines = [self.terms.at[pl.ds((2 * t + 1 - self.core) * self.depth, self.depth)] for t in range(4)]
        return [self.copy(t, lines[t], first.at[t], self.seq ^ CORES, self.fsdp) for t in range(4)]

    def to_sides(self):
        first, second = self.buffers[:2]
        x, y = self.x, self.y
        copies = []
        for j in range(2):
            copies.append(
                self.copy(
                    4 + j,
                    first.at[2 * j + 1 - x, :, self.halves[0]],
                    second.at[0, j],
                    self.seq ^ SIDE_X,
                    self.fsdp,
                )
            )
            copies.append(
                self.copy(
                    6 + j,
                    first.at[2 * (1 - y) + j, :, self.halves[1]],
                    second.at[1, j],
                    self.seq ^ SIDE_Y,
                    self.fsdp,
                )
            )
        return copies

    def to_corner(self):
        second, third = self.buffers[1:3]
        return [
            self.copy(8, second.at[0, 1 - self.y], third.at[0], self.seq ^ SIDE_Y, self.fsdp),
            self.copy(9, second.at[1, 1 - self.x], third.at[1], self.seq ^ SIDE_X, self.fsdp),
        ]

    def to_line(self):
        third, fourth = self.buffers[2:]
        copies = []
        for step in range(1, self.depth):
            to = lax.rem(self.fsdp + step, self.depth)
            for j in range(2):
                copies.append(
                    self.copy(8 + 2 * step + j, third.at[j, to], fourth.at[j, step], self.seq, to)
                )
        return copies

    def add(self, target, other):
        @pl.loop(0, self.depth)
        def _(i):
            target[i] = (target[i].astype(float_type) + other[i].astype(float_type)).astype(narrow_type)

    def begin(self):
        for copy in self.to_core():
            copy.start()

    def sides(self):
        first = self.buffers[0]
        for t, copy in enumerate(self.to_core()):
            copy.wait_recv()
            self.add(first.at[t], self.terms.at[pl.ds((2 * t + self.core) * self.depth, self.depth)])
        for copy in self.to_sides():
            copy.start()

    def corner(self):
        first, second = self.buffers[:2]
        copies = self.to_sides()
        for j in range(2):
            copies[2 * j].wait_recv()
            self.add(second.at[0, j], first.at[2 * j + self.x, :, self.halves[0]])
            copies[2 * j + 1].wait_recv()
            self.add(second.at[1, j], first.at[2 * self.y + j, :, self.halves[1]])
        for copy in self.to_corner():
            copy.start()

    def line(self):
        second, third = self.buffers[1:3]
        copies = self.to_corner()
        copies[0].wait_recv()
        self.add(third.at[0], second.at[0, self.y])
        copies[1].wait_recv()
        self.add(third.at[1], second.at[1, self.x])
        for copy in self.to_line():
            copy.start()

    def end(self, out):
        third, fourth = self.buffers[2:]
        for copy in self.to_line():
            copy.wait_recv()
        for j in range(2):
            total = third[j, self.fsdp].astype(float_type)
            for step in range(1, self.depth):
                total = total + fourth[j, step].astype(float_type)
            out[self.halves[j]] = total

    def drain(self):
        for copy in self.to_core() + self.to_sides() + self.to_corner() + self.to_line():
            copy.wait_send()


def last_kernel(
    depth,
    heads,
    halo,
    lens_ref,
    choice_ref,
    dq_ref,
    dkv_ref,
    tok_ref,
    gm_ref,
    fa_in,
    ve,
    rank_ref,
    early_terms,
    gradient_ref,
    early_ref,
    late_ref,
    fa,
    vectors,
    normed,
    total,
    arrived,
    arrived_rows,
    merged,
    other,
    late_terms,
    early_buffers,
    late_buffers,
    select,
    send,
    receive,
    local,
    piece_send,
    piece_receive,
    piece_local,
):
    swap = Exchange(depth, heads)
    me, seq, fsdp = swap.me, swap.seq, swap.fsdp
    core, half, head, own = swap.core, swap.half, swap.head, heads
    row_count, features = tok_ref.shape
    devices, share = fa.shape[0], fa.shape[1]
    wide = features + 256
    barrier = pltpu.get_barrier_semaphore()
    greet_neighbours(barrier, seq, fsdp, depth)
    waits = 3 + depth - 1 + swap.greet_holders(barrier)
    load = pltpu.make_async_copy(fa_in.at[:, :, pl.ds(0, 3 * wide)], fa, local.at[0])
    load.start()
    pl.semaphore_wait(barrier, waits)
    over = remote(
        dkv_ref.at[pl.ds(jnp.where(core == 0, own, 0), halo)],
        other,
        piece_send.at[3, 0], piece_receive.at[3, 0], seq ^ CORES, fsdp)
    over.start()
    early = Reduce(depth, 0, early_terms, *early_buffers, send, receive)
    late = [
        Reduce(
            depth, Reduce.COPIES * (p + 1), late_terms.at[p], *[b.at[p] for b in late_buffers], send, receive
        )
        for p in range(3)
    ]
    shared = jnp.where(core == 0, own - halo, 0)
    shift = core * halo

    def in_shared(k):
        return (k >= shared) & (k < shared + halo)

    def sent(p, k, source):
        return remote(
            source, arrived.at[p, head], piece_send.at[p, k], piece_receive.at[p, head], *swap.owner(k)
        )

    def launch(p, k, source):
        @pl.when(swap.away_block(k))
        def _():
            sent(p, k, source).start()

        @pl.when(core * own + k == me)
        def _():
            pltpu.make_async_copy(source, arrived.at[p, head], piece_local.at[p]).start()

    def arrival(p, k):
        return remote(
            dq_ref.at[0], arrived.at[p, k], piece_send.at[p, k], piece_receive.at[p, k], seq ^ CORES, fsdp
        )

    @pl.loop(0, own)
    def _(step):
        k = lax.rem(step + me, own)
        launch(0, k, dq_ref.at[k])

    over.wait_recv()

    @pl.loop(0, halo)
    def _(i):
        for part in range(2):
            merged[i, part] = (
                dkv_ref[shared + shift + i, part].astype(float_type) + other[i, part].astype(float_type)
            ).astype(narrow_type)

    for p in (1, 2):

        @pl.loop(0, own)
        def _(step, p=p):
            k = lax.rem(step + me, own)

            @pl.when(in_shared(k))
            def _():
                launch(p, k, merged.at[jnp.clip(k - shared, 0, halo - 1), p - 1])

            @pl.when(jnp.logical_not(in_shared(k)))
            def _():
                launch(p, k, dkv_ref.at[k + shift, p - 1])

    early.begin()
    rows_of_vectors(ve, vectors)
    select[...] = selected(lens_ref, choice_ref, me, *select.shape)
    early.sides()
    shifted, normal, scaling = layer_norm(tok_ref[...].astype(float_type), vectors[0:1], vectors[4:5])
    normed[...] = shifted.astype(narrow_type)
    early.corner()
    load.wait()

    def gather_part(p):
        @pl.loop(0, heads)
        def _(k):
            @pl.when(swap.away_head(k))
            def _():
                arrival(p, k).wait_recv()

        @pl.when(half == core)
        def _():
            pltpu.make_async_copy(dq_ref.at[0], arrived.at[p, head], piece_local.at[p]).wait()

    def project_back(p):
        for j in range(4):
            arrived_rows[:, j * 256 : (j + 1) * 256] = turned(as_matrix(arrived[p, 4 * j : 4 * j + 4]))
        up = as_matrix(fa[:, :, p * wide + features + 128 : (p + 1) * wide])
        grad_rank = (matmul(arrived_rows[...], up) * select[...]).astype(narrow_type)

        @pl.loop(0, 4)
        def _(j):
            at = pl.ds(pl.multiple_of(j * 256, 128), 256)
            slots = pl.ds(j * 8, 8)
            weight = as_matrix(fa[slots, :, p * wide : p * wide + features])
            down = as_matrix(fa[slots, :, p * wide + features : p * wide + features + 128])
            term = transposed_right(arrived_rows[...], weight) + transposed_right(grad_rank, down)
            if p == 0:
                total[:, at] = term
            else:
                total[:, at] += term

        shaped = (devices, share, 128)
        late_terms[p, :, 0:32] = transposed_left(normed[...], grad_rank).astype(narrow_type).reshape(shaped)
        late_terms[p, :, 32:64] = (
            matmul(as_matrix(arrived[p]), rank_ref[p]).astype(narrow_type).reshape(shaped)
        )

    gather_part(0)
    project_back(0)
    late[0].begin()
    early.line()
    late[0].sides()
    gather_part(1)
    project_back(1)
    late[1].begin()
    late[0].corner()
    late[1].sides()
    gather_part(2)
    project_back(2)
    late[2].begin()
    late[0].line()
    late[1].corner()
    late[2].sides()
    gradient_ref[...] = gm_ref[...] + norm_backward(total[...], vectors[0:1], normal, scaling)
    late[1].line()
    late[2].corner()
    early.end(early_ref)
    late[0].end(late_ref.at[0])
    late[2].line()
    late[1].end(late_ref.at[1])
    late[2].end(late_ref.at[2])
    for reduce in [early] + late:
        reduce.drain()

    @pl.loop(0, own)
    def _(k):
        @pl.when(swap.away_block(k))
        def _():
            for p in range(3):
                sent(p, k, dq_ref.at[k]).wait_send()

    over.wait_send()


def last_part(lengths, choice, dq, dkv, tokens, grad_middle, fa, ve, rank, terms, depth, collective):
    heads = dq.shape[0]
    halo = dkv.shape[0] - heads
    rows, features = tokens.shape
    wide = features + 256
    devices, share = fa.shape[0], fa.shape[1]

    def buffers(count, size):
        return [
            pltpu.VMEM(count + (4, depth, size, 128), narrow_type),
            pltpu.VMEM(count + (2, 2, depth, size // 2, 128), narrow_type),
            pltpu.VMEM(count + (2, depth, size // 2, 128), narrow_type),
            pltpu.VMEM(count + (2, depth, size // 2, 128), narrow_type),
        ]

    return pl.pallas_call(
        functools.partial(last_kernel, depth, heads, halo),
        out_shape=(
            jax.ShapeDtypeStruct((rows, features), float_type),
            jax.ShapeDtypeStruct((terms.shape[1], 128), float_type),
            jax.ShapeDtypeStruct((3, 2 * share, 128), float_type),
        ),
        in_specs=[IN_SMEM] * 2 + [IN_VMEM] * 4 + [ANYWHERE] + [IN_VMEM] * 3,
        out_specs=(IN_VMEM, IN_VMEM, IN_VMEM),
        scratch_shapes=[
            pltpu.VMEM((devices, share, 3 * wide), narrow_type),
            pltpu.VMEM((16, features), float_type),
            pltpu.VMEM((rows, features), narrow_type),
            pltpu.VMEM((rows, features), float_type),
            pltpu.VMEM((3, heads, features // heads, rows), narrow_type),
            pltpu.VMEM((rows, features), narrow_type),
            pltpu.VMEM((halo,) + dkv.shape[1:], narrow_type),
            pltpu.VMEM((halo,) + dkv.shape[1:], narrow_type),
            pltpu.VMEM((3, devices, 2 * share, 128), narrow_type),
            buffers((), terms.shape[1]),
            buffers((3,), 2 * share),
            pltpu.VMEM((rows, 128), float_type),
            pltpu.SemaphoreType.DMA((4 * Reduce.COPIES,)),
            pltpu.SemaphoreType.DMA((4 * Reduce.COPIES,)),
            pltpu.SemaphoreType.DMA((1,)),
            pltpu.SemaphoreType.DMA((4, heads)),
            pltpu.SemaphoreType.DMA((4, heads)),
            pltpu.SemaphoreType.DMA((3,)),
        ],
        compiler_params=pltpu.CompilerParams(
            collective_id=collective, has_side_effects=True, vmem_limit_bytes=44 << 20
        ),
    )(lengths, choice, dq, dkv, tokens, grad_middle, fa, ve, rank, terms)


def spread_kernel(result_in, gradient_in, early, late, result, gradient, down, up, exp_down, exp_up, con_down, con_up):
    share = down.shape[1]
    result[...] = result_in[...]
    gradient[...] = gradient_in[...]
    for p in range(4):
        first = late[p, 0:share] if p < 3 else early[0:share]
        second = late[p, share : 2 * share] if p < 3 else early[share : 2 * share]
        down[p] = first
        up[p] = second
    exp_down[...] = early[64:96]
    exp_up[...] = early[96:224]
    con_down[...] = early[224:352].T
    con_up[...] = early[352:384]


def spread(result, gradient, early, late):
    share = late.shape[1] // 2
    shapes = ((4, share, 128), (4, share, 128), (share, 128), (128, 128), (128, 128), (share, 128))
    return pl.pallas_call(
        spread_kernel,
        out_shape=tuple(jax.ShapeDtypeStruct(a.shape, a.dtype) for a in (result, gradient))
        + tuple(jax.ShapeDtypeStruct(shape, float_type) for shape in shapes),
        in_specs=[IN_VMEM] * 4,
        out_specs=(IN_VMEM,) * 8,
        compiler_params=pltpu.CompilerParams(vmem_limit_bytes=24 << 20),
    )(result, gradient, early, late)


BIG = 32768.0


def image_range(lens_ref, first, last):
    low = high = start = jnp.int32(0)
    for image in range(lens_ref.shape[0]):
        end = start + lens_ref[image]
        low = jnp.where((start <= first) & (first < end), start, low)
        high = jnp.where((start <= last) & (last < end), end - 1, high)
        start = end
    return low, high


def image_edges(lens_ref, marks, rows):
    row = lax.broadcasted_iota(jnp.int32, (marks, rows), 0)
    starts = jnp.full((marks, rows), 1 << 30, jnp.int32)
    ends = jnp.zeros((marks, rows), jnp.int32)
    start = jnp.int32(0)
    for image in range(lens_ref.shape[0]):
        end = start + lens_ref[image]
        starts, ends = jnp.where(row == image, start, starts), jnp.where(row == image, end, ends)
        start = end
    return starts, ends


class Blocks:
    def __init__(self, lens_ref, own, halo, rows, marks):
        core = lax.rem(lax.axis_index("seq"), 2)
        self.lens_ref, self.own, self.rows, self.slots = lens_ref, own, rows, own + halo
        self.base = core * (own - halo)
        self.shift = core * halo
        self.starts, self.ends = image_edges(lens_ref, marks, rows)
        self.lane = lax.broadcasted_iota(jnp.int32, (marks, rows), 1)

    def marks(self, slot):
        place = self.lane + (self.base + slot) * self.rows
        return jnp.where((place >= self.starts) & (place < self.ends), 1.0, 0.0).astype(float_type)

    def reach(self, slot):
        first = (self.base + slot) * self.rows
        low, high = image_range(self.lens_ref, first, first + self.rows - 1)
        return lax.div(low, self.rows) - self.base, lax.div(high, self.rows) - self.base


def forward_kernel(
    own, halo, step, lens_ref, x_ref, att_ref, lse_ref, out_ref, keys, queries, score, weight, item_row, item_low
):
    slots, _, width, rows = x_ref.shape
    blocks = Blocks(lens_ref, own, halo, rows, keys.shape[1] - width)
    scale = width**-0.5

    @pl.loop(0, slots)
    def _(slot):
        block = jnp.concatenate([x_ref[slot, 1].astype(float_type), (blocks.marks(slot) - 1.0) * BIG], axis=0)
        keys[pl.ds(pl.multiple_of(slot * rows, rows), rows)] = block.T.astype(narrow_type)

    def prepare(i, total):
        slot = i + blocks.shift
        queries[i] = jnp.concatenate([x_ref[slot, 0].astype(float_type) * scale, blocks.marks(slot)], axis=0).astype(narrow_type)
        low, high = blocks.reach(slot)
        count = lax.div(high - low + step, step)
        low = jnp.minimum(low, slots - step * count)

        @pl.loop(0, count)
        def _(j):
            item_row[total + j] = i
            item_low[total + j] = low + j * step

        return total + count

    total = lax.fori_loop(0, own, prepare, jnp.int32(0))
    item_row[total] = item_row[total - 1]
    item_low[total] = item_low[total - 1]

    def scored(t, side):
        at = pl.multiple_of(item_low[t] * rows, rows)
        score[side] = matmul(keys[pl.ds(at, step * rows)], queries[item_row[t]])

    def mixed(t):
        low = item_low[t]
        result = matmul(x_ref[low, 2], weight[0:rows])
        for j in range(1, step):
            result += matmul(x_ref[low + j, 2], weight[j * rows : (j + 1) * rows])
        return result

    def soften(fresh, side, highest, summed):
        highest = jnp.where(fresh, -1e30, highest)
        summed = jnp.where(fresh, 0.0, summed)
        s = score[side]
        higher = jnp.maximum(highest, jnp.max(s, axis=0, keepdims=True))
        p = jnp.exp(s - higher)
        fade = jnp.where(fresh, 0.0, jnp.exp(highest - higher))
        return higher, summed * fade + jnp.sum(p, axis=0, keepdims=True), fade, p

    def finish(t, out, fade, highest, summed):
        i = item_row[t]
        out = out * fade + mixed(t)
        whole = out / summed
        att_ref[i] = whole.astype(narrow_type)
        out_ref[i] = whole
        lse_ref[i] = jnp.broadcast_to(highest + jnp.log(summed), (8, rows))
        return out

    def turn(t, side, carry):
        highest, summed, out, fade = carry
        out = finish(t - 1, out, fade, highest, summed)
        scored(t + 1, 1 - side)
        fresh = item_row[t] != item_row[t - 1]
        highest, summed, fade, p = soften(fresh, side, highest, summed)
        weight[...] = p.astype(narrow_type)
        return highest, summed, out, fade

    scored(0, 0)
    scored(1, 1)
    highest, summed, fade, p = soften(True, 0, jnp.zeros((1, rows), float_type), jnp.zeros((1, rows), float_type))
    weight[...] = p.astype(narrow_type)
    carry = (highest, summed, jnp.zeros((width, rows), float_type), fade)
    pairs = lax.div(total - 1, 2)
    carry = lax.fori_loop(0, pairs, lambda j, c: turn(2 * j + 2, 0, turn(2 * j + 1, 1, c)), carry)
    carry = lax.fori_loop(2 * pairs + 1, total, lambda t, c: turn(t, 1, c), carry)
    highest, summed, out, fade = carry
    finish(total - 1, out, fade, highest, summed)


def attention_forward(lengths, x, own, halo, step=2):
    slots, _, width, rows = x.shape
    marks = -(-lengths.shape[0] // 16) * 16
    most = own * (slots // step + 2) + 8
    return pl.pallas_call(
        functools.partial(forward_kernel, own, halo, step),
        out_shape=(
            jax.ShapeDtypeStruct((own, width, rows), narrow_type),
            jax.ShapeDtypeStruct((own, 8, rows), float_type),
            jax.ShapeDtypeStruct((own, width, rows), float_type),
        ),
        in_specs=[IN_SMEM, IN_VMEM],
        out_specs=(IN_VMEM, IN_VMEM, IN_VMEM),
        scratch_shapes=[
            pltpu.VMEM((slots * rows, width + marks), narrow_type),
            pltpu.VMEM((own, width + marks, rows), narrow_type),
            pltpu.VMEM((2, step * rows, rows), float_type),
            pltpu.VMEM((step * rows, rows), narrow_type),
            pltpu.SMEM((most,), jnp.int32),
            pltpu.SMEM((most,), jnp.int32),
        ],
        compiler_params=pltpu.CompilerParams(vmem_limit_bytes=32 << 20),
    )(lengths, x)


def backward_kernel(
    own, halo, step, lens_ref, x_ref, g_ref, lse_ref, out_ref, dq_ref, dkv_ref,
    keys, values, queries, offset, dq, score, grad_prob, weight, grad_score, item_slot, item_low,
):
    slots, _, width, rows = x_ref.shape
    blocks = Blocks(lens_ref, own, halo, rows, keys.shape[2] - width)
    scale = width**-0.5

    def prepare(slot, total):
        block = jnp.concatenate([x_ref[slot, 1].astype(float_type), (blocks.marks(slot) - 1.0) * BIG], axis=0)
        keys[slot] = block.T.astype(narrow_type)
        values[slot] = x_ref[slot, 2].astype(float_type).T.astype(narrow_type)
        dkv_ref[slot] = jnp.zeros((2, width, rows), narrow_type)
        low, high = blocks.reach(slot)
        low = jnp.maximum(low - blocks.shift, 0)
        high = jnp.minimum(high - blocks.shift, own - 1)
        count = jnp.maximum(lax.div(high - low + step, step), 0)
        low = jnp.minimum(low, own - step * count)

        @pl.loop(0, count)
        def _(j):
            item_slot[total + j] = slot
            item_low[total + j] = low + j * step

        return total + count

    total = lax.fori_loop(0, slots, prepare, jnp.int32(0))
    item_slot[total] = item_slot[total - 1]
    item_low[total] = item_low[total - 1]

    @pl.loop(0, own)
    def _(i):
        slot = i + blocks.shift
        q = x_ref[slot, 0].astype(float_type) * scale
        queries[i] = jnp.concatenate([q, blocks.marks(slot)], axis=0).astype(narrow_type)
        g = g_ref[i].astype(float_type)
        offset[i] = jnp.broadcast_to(jnp.sum(g * out_ref[i], axis=0, keepdims=True), (8, rows))
        dq[i] = jnp.zeros((width, rows), float_type)

    def scored(t, side):
        slot, low = item_slot[t], item_low[t]
        for j in range(step):
            score[side, j] = matmul(keys[slot], queries[low + j])
            grad_prob[side, j] = matmul(values[slot], g_ref[low + j])

    def soften(t, side):
        low = item_low[t]
        done = []
        for j in range(step):
            p = jnp.exp(score[side, j] - lse_ref[low + j, 0:1])
            d = p * (grad_prob[side, j] - offset[low + j, 0:1])
            done.append((p.astype(narrow_type), d.astype(narrow_type)))
        return done

    def keep(done):
        for j in range(step):
            weight[j] = done[j][0]
            grad_score[j] = done[j][1]

    def mixed(t, fresh, dk, dv):
        slot, low = item_slot[t], item_low[t]
        dk = jnp.where(fresh, 0.0, dk)
        dv = jnp.where(fresh, 0.0, dv)
        key = x_ref[slot, 1]
        for j in range(step):
            dk += transposed_right(queries[low + j, 0:width], grad_score[j])
            dv += transposed_right(g_ref[low + j], weight[j])
        for j in range(step):
            dq[low + j] += matmul(key, grad_score[j])
        dkv_ref[slot, 0] = dk.astype(narrow_type)
        dkv_ref[slot, 1] = dv.astype(narrow_type)
        return dk, dv

    def turn(t, side, carry):
        fresh = (t == 1) | (item_slot[t - 1] != item_slot[jnp.maximum(t - 2, 0)])
        carry = mixed(t - 1, fresh, *carry)
        scored(t + 1, 1 - side)
        keep(soften(t, side))
        return carry

    scored(0, 0)
    scored(1, 1)
    keep(soften(0, 0))
    zero = jnp.zeros((width, rows), float_type)
    pairs = lax.div(total - 1, 2)
    carry = lax.fori_loop(0, pairs, lambda j, c: turn(2 * j + 2, 0, turn(2 * j + 1, 1, c)), (zero, zero))
    carry = lax.fori_loop(2 * pairs + 1, total, lambda t, c: turn(t, 1, c), carry)
    mixed(total - 1, item_slot[total - 1] != item_slot[jnp.maximum(total - 2, 0)], *carry)

    @pl.loop(0, own)
    def _(i):
        dq_ref[i] = (dq[i] * scale).astype(narrow_type)


def attention_backward(lengths, x, g, lse, out, own, halo, step=2):
    slots, _, width, rows = x.shape
    marks = -(-lengths.shape[0] // 16) * 16
    most = slots * (own // step + 2) + 8
    return pl.pallas_call(
        functools.partial(backward_kernel, own, halo, step),
        out_shape=(
            jax.ShapeDtypeStruct((own, width, rows), narrow_type),
            jax.ShapeDtypeStruct((slots, 2, width, rows), narrow_type),
        ),
        in_specs=[IN_SMEM] + [IN_VMEM] * 4,
        out_specs=(IN_VMEM, IN_VMEM),
        scratch_shapes=[
            pltpu.VMEM((slots, rows, width + marks), narrow_type),
            pltpu.VMEM((slots, rows, width), narrow_type),
            pltpu.VMEM((own, width + marks, rows), narrow_type),
            pltpu.VMEM((own, 8, rows), float_type),
            pltpu.VMEM((own, width, rows), float_type),
            pltpu.VMEM((2, step, rows, rows), float_type),
            pltpu.VMEM((2, step, rows, rows), float_type),
            pltpu.VMEM((step, rows, rows), narrow_type),
            pltpu.VMEM((step, rows, rows), narrow_type),
            pltpu.SMEM((most,), jnp.int32),
            pltpu.SMEM((most,), jnp.int32),
        ],
        compiler_params=pltpu.CompilerParams(vmem_limit_bytes=40 << 20),
    )(lengths, x, g, lse, out)


def layer_on_slice(
    tokens,
    lengths,
    adapter_choice,
    gain_rows,
    bias_rows,
    query_key_value,
    output_weight,
    expand_weight,
    expand_bias,
    contract_weight,
    adapter_in_attention,
    adapter_out_attention,
    adapter_in_expand,
    adapter_out_expand,
    adapter_in_contract,
    adapter_out_contract,
    cotangent,
):
    row_count = tokens.shape[0]
    depth = lax.axis_size("fsdp")
    devices = lax.axis_size(("seq", "fsdp"))
    own = devices // 2
    halo = -(-(LONGEST - 1) // row_count)

    arrays = (
        gain_rows,
        bias_rows,
        expand_bias[None],
        query_key_value,
        output_weight,
        adapter_in_attention,
        adapter_out_attention.transpose(0, 2, 1),
        adapter_in_expand,
        adapter_out_contract.T,
        contract_weight,
        adapter_in_contract,
        adapter_out_expand,
        expand_weight,
    )
    fa, ve, f2, line_a, line_b, on_heads, rank = attention_in(
        lengths, adapter_choice, tokens, arrays, halo, depth, HEADS, devices, 1
    )

    def swapped(line, bit):
        route = [
            (seq * depth + fsdp, (seq ^ bit) * depth + fsdp)
            for seq in range(devices // depth)
            for fsdp in range(depth)
        ]
        return lax.ppermute(line, ("seq", "fsdp"), route)

    lines = (
        line_a,
        line_b,
        swapped(line_a, SIDE_Y),
        swapped(line_b, SIDE_Y),
        swapped(line_a, SIDE_X),
        swapped(line_b, SIDE_X),
    )
    attended, log_totals, attended_wide = attention_forward(lengths, on_heads, own, halo)
    result, grad_middle, terms, grad_on_heads = middle_part(
        lengths, adapter_choice, attended, tokens, cotangent, fa, ve, f2, lines, depth, 2
    )
    grad_queries, grad_key_values = attention_backward(
        lengths, on_heads, grad_on_heads, log_totals, attended_wide, own, halo
    )
    input_gradient, early, late = last_part(
        lengths, adapter_choice, grad_queries, grad_key_values, tokens, grad_middle, fa, ve, rank, terms, depth, 3
    )
    outs = spread(result, input_gradient, early, late)
    return outs[:3] + (outs[3].transpose(0, 2, 1),) + outs[4:7] + (outs[7].T,)


def solution(mesh):
    per_device = layer_on_slice if dict(mesh.shape) == {"seq": 8, "fsdp": 4} else general_layer
    placed = (
        P(("seq", "fsdp"), None),
        P(),
        P(),
        P(None, ("seq", "fsdp")),
        P(None, ("seq", "fsdp")),
        P(("seq", "fsdp"), None),
        P(("seq", "fsdp"), None),
        P(("seq", "fsdp"), None),
        P(("seq", "fsdp")),
        P(("seq", "fsdp"), None),
        P(None, ("seq", "fsdp"), None),
        P(None, None, ("seq", "fsdp")),
        P(("seq", "fsdp"), None),
        P(None, ("seq", "fsdp")),
        P(("seq", "fsdp"), None),
        P(None, ("seq", "fsdp")),
        P(("seq", "fsdp"), None),
    )
    return jax.shard_map(
        per_device,
        mesh=mesh,
        in_specs=placed,
        out_specs=(
            P(("seq", "fsdp"), None),
            P(("seq", "fsdp"), None),
            P(None, ("seq", "fsdp"), None),
            P(None, None, ("seq", "fsdp")),
            P(("seq", "fsdp"), None),
            P(None, ("seq", "fsdp")),
            P(("seq", "fsdp"), None),
            P(None, ("seq", "fsdp")),
        ),
        check_vma=False,
    )
```

```python
import functools
import jax
import jax.numpy as jnp
from jax import lax
from jax.experimental import pallas as pl
from jax.experimental.pallas import tpu as pltpu
from jax.sharding import PartitionSpec as P

HEADS = 16
RANK = 16
HOPS = 6
EDGE = 1408
LONGEST = 1370


epsilon = 1e-06
float_type = jnp.float32
narrow_type = jnp.bfloat16


def passed_along(block, axis, distance):
    devices = range(lax.axis_size(axis))
    route = [(i - distance, i) for i in devices if i - distance in devices]
    return lax.ppermute(block, axis, route)


def layer_norm(inputs_row, gain_row, bias_row):
    center = inputs_row - jnp.mean(inputs_row, axis=-1, keepdims=True)
    scaling = lax.rsqrt(jnp.mean(center * center, axis=-1, keepdims=True) + epsilon)
    normal = center * scaling
    return (normal * gain_row + bias_row, normal, scaling)


def norm_backward(gradient, gain_row, normal, scaling):
    weighted = gradient * gain_row
    return scaling * (
        weighted
        - jnp.mean(weighted, axis=-1, keepdims=True)
        - normal * jnp.mean(weighted * normal, axis=-1, keepdims=True)
    )


def matmul(first_operand, second_operand):
    return jnp.dot(first_operand, second_operand, preferred_element_type=float_type)


def transposed_left(first_operand, second_operand):
    return lax.dot_general(
        first_operand, second_operand, (((0,), (0,)), ((), ())), preferred_element_type=float_type
    )


def transposed_right(first_operand, second_operand):
    return lax.dot_general(
        first_operand, second_operand, (((1,), (1,)), ((), ())), preferred_element_type=float_type
    )


def gelu_slope(hidden_pre):
    cumulative = 0.5 * (1.0 + lax.erf(hidden_pre * 0.7071067811865476))
    density = jnp.exp(-0.5 * hidden_pre * hidden_pre) * 0.3989422804014327
    return cumulative + hidden_pre * density


def general_layer(
    tokens,
    lengths,
    adapter_choice,
    gain_rows,
    bias_rows,
    query_key_value,
    output_weight,
    expand_weight,
    expand_bias,
    contract_weight,
    adapter_in_attention,
    adapter_out_attention,
    adapter_in_expand,
    adapter_out_expand,
    adapter_in_contract,
    adapter_out_contract,
    cotangent,
):
    gathered = (
        lax.all_gather(gain_rows, ("seq", "fsdp"), axis=1, tiled=True),
        lax.all_gather(bias_rows, ("seq", "fsdp"), axis=1, tiled=True),
        lax.all_gather(query_key_value, ("seq", "fsdp"), axis=0, tiled=True),
        lax.all_gather(output_weight, ("seq", "fsdp"), axis=0, tiled=True),
        lax.all_gather(expand_weight, ("seq", "fsdp"), axis=0, tiled=True),
        lax.all_gather(expand_bias, ("seq", "fsdp"), axis=0, tiled=True),
        lax.all_gather(contract_weight, ("seq", "fsdp"), axis=0, tiled=True),
        lax.all_gather(adapter_in_attention, ("seq", "fsdp"), axis=1, tiled=True),
        lax.all_gather(adapter_out_attention, ("seq", "fsdp"), axis=2, tiled=True),
        lax.all_gather(adapter_in_expand, ("seq", "fsdp"), axis=0, tiled=True),
        lax.all_gather(adapter_out_expand, ("seq", "fsdp"), axis=1, tiled=True),
        lax.all_gather(adapter_in_contract, ("seq", "fsdp"), axis=0, tiled=True),
        lax.all_gather(adapter_out_contract, ("seq", "fsdp"), axis=1, tiled=True),
    )
    (
        gains_full,
        biases_full,
        qkv_full,
        output_full,
        expand_full,
        expand_bias_full,
        contract_full,
        attention_down,
        attention_up,
        expand_down,
        expand_up,
        contract_down,
        contract_up,
    ) = gathered
    gains_wide = gains_full.astype(float_type)
    biases_wide = biases_full.astype(float_type)
    row_count, features = tokens.shape
    device_count = lax.axis_size(("seq", "fsdp"))
    position = lax.axis_index(("seq", "fsdp"))
    head_width = features // HEADS
    pair_width = 2 * head_width
    pair_count = HEADS // 2
    scaling_score = head_width ** (-0.5)
    rank_width = attention_down.shape[2]
    window_start = HOPS * row_count - EDGE
    window_rows = row_count + 2 * EDGE
    image_ends = jnp.cumsum(lengths)
    places = (
        position * row_count
        - HOPS * row_count
        + jnp.arange((2 * HOPS + 1) * row_count, dtype=jnp.int32)
    )
    image_of = jnp.sum((places[:, None] >= image_ends[None, :]).astype(jnp.int32), axis=1)
    image_of = jnp.where((places >= 0) & (places < device_count * row_count), image_of, -1)
    own_image = image_of[HOPS * row_count : (HOPS + 1) * row_count]
    key_image = image_of[window_start : window_start + window_rows]
    allowed = own_image[:, None] == key_image[None, :]
    matches = own_image[:, None] == jnp.arange(lengths.shape[0], dtype=jnp.int32)[None, :]
    chosen = jnp.sum(jnp.where(matches, adapter_choice[None, :], 0), axis=1)
    select = (jnp.arange(rank_width, dtype=jnp.int32)[None, :] // RANK == chosen[:, None]).astype(
        float_type
    )
    residual = tokens.astype(float_type)
    normed_first, normal_first, scaling_first = layer_norm(residual, gains_wide[0], biases_wide[0])
    normed_first = normed_first.astype(narrow_type)
    rank_qkv = (
        jnp.einsum(
            "td,pdr->tpr", normed_first, attention_down[:3], preferred_element_type=float_type
        )
        * select[:, None, :]
    ).astype(narrow_type)
    adapted_qkv = jnp.einsum(
        "tpr,prd->tpd", rank_qkv, attention_up[:3], preferred_element_type=float_type
    ).reshape(row_count, 3 * features)
    query_bias = jnp.concatenate([biases_wide[1], jnp.zeros((2 * features,), float_type)])
    projected = (matmul(normed_first, qkv_full) + adapted_qkv + query_bias).astype(narrow_type)
    queries = projected[:, :features]
    key_values = projected[:, features:]
    from_lower = []
    from_higher = []
    for distance in range(1, HOPS + 1):
        from_lower.append(passed_along(key_values, ("seq", "fsdp"), distance))
        from_higher.append(passed_along(key_values, ("seq", "fsdp"), -distance))
    beside_all = jnp.concatenate(from_lower[::-1] + [key_values] + from_higher, axis=0)
    window = beside_all[window_start : window_start + window_rows]

    def pair_slices(pair_index):
        offset = pair_index * pair_width
        query_part = lax.dynamic_slice_in_dim(queries, offset, pair_width, 1).reshape(
            row_count, 2, head_width
        )
        key_part = lax.dynamic_slice_in_dim(window, offset, pair_width, 1).reshape(
            window_rows, 2, head_width
        )
        value_part = lax.dynamic_slice_in_dim(window, features + offset, pair_width, 1).reshape(
            window_rows, 2, head_width
        )
        scores = (
            jnp.einsum("qhd,khd->hqk", query_part, key_part, preferred_element_type=float_type)
            * scaling_score
        )
        scores = jnp.where(allowed[None], scores, -1e30)
        return (query_part, key_part, value_part, scores)

    def pair_forward(pair_index):
        query_part, key_part, value_part, scores = pair_slices(pair_index)
        highest = jnp.max(scores, axis=2, keepdims=True)
        weights = jnp.exp(scores - highest)
        denominator = jnp.sum(weights, axis=2, keepdims=True)
        soft = (weights / denominator).astype(narrow_type)
        mixed_part = jnp.einsum("hqk,khd->qhd", soft, value_part, preferred_element_type=float_type)
        return (
            mixed_part.reshape(row_count, pair_width),
            (highest + jnp.log(denominator))[:, :, 0],
        )

    attended_pairs, log_totals = lax.map(pair_forward, jnp.arange(pair_count))
    attended = attended_pairs.transpose(1, 0, 2).reshape(row_count, features).astype(narrow_type)
    rank_out = (matmul(attended, attention_down[3]) * select).astype(narrow_type)
    mixed = matmul(attended, output_full) + biases_wide[2] + matmul(rank_out, attention_up[3])
    middle = residual + gains_wide[1] * mixed
    normed_second, normal_second, scaling_second = layer_norm(middle, gains_wide[2], biases_wide[3])
    normed_second = normed_second.astype(narrow_type)
    rank_expand = (matmul(normed_second, expand_down) * select).astype(narrow_type)
    hidden_pre = (
        matmul(normed_second, expand_full)
        + expand_bias_full.astype(float_type)
        + matmul(rank_expand, expand_up)
    )
    active = jax.nn.gelu(hidden_pre, approximate=False).astype(narrow_type)
    rank_contract = (matmul(active, contract_down) * select).astype(narrow_type)
    branch = matmul(active, contract_full) + biases_wide[4] + matmul(rank_contract, contract_up)
    result = (middle + gains_wide[3] * branch).astype(narrow_type)
    renewed = lax.optimization_barrier(
        (
            gain_rows,
            bias_rows,
            query_key_value,
            output_weight,
            expand_weight,
            expand_bias,
            contract_weight,
            adapter_in_attention,
            adapter_out_attention,
            adapter_in_expand,
            adapter_out_expand,
            adapter_in_contract,
            adapter_out_contract,
            cotangent,
        )
    )
    gathered = (
        lax.all_gather(renewed[0], ("seq", "fsdp"), axis=1, tiled=True),
        lax.all_gather(renewed[1], ("seq", "fsdp"), axis=1, tiled=True),
        lax.all_gather(renewed[2], ("seq", "fsdp"), axis=0, tiled=True),
        lax.all_gather(renewed[3], ("seq", "fsdp"), axis=0, tiled=True),
        lax.all_gather(renewed[4], ("seq", "fsdp"), axis=0, tiled=True),
        lax.all_gather(renewed[5], ("seq", "fsdp"), axis=0, tiled=True),
        lax.all_gather(renewed[6], ("seq", "fsdp"), axis=0, tiled=True),
        lax.all_gather(renewed[7], ("seq", "fsdp"), axis=1, tiled=True),
        lax.all_gather(renewed[8], ("seq", "fsdp"), axis=2, tiled=True),
        lax.all_gather(renewed[9], ("seq", "fsdp"), axis=0, tiled=True),
        lax.all_gather(renewed[10], ("seq", "fsdp"), axis=1, tiled=True),
        lax.all_gather(renewed[11], ("seq", "fsdp"), axis=0, tiled=True),
        lax.all_gather(renewed[12], ("seq", "fsdp"), axis=1, tiled=True),
    )
    (
        gains_full,
        biases_full,
        qkv_full,
        output_full,
        expand_full,
        expand_bias_full,
        contract_full,
        attention_down,
        attention_up,
        expand_down,
        expand_up,
        contract_down,
        contract_up,
    ) = gathered
    gains_wide = gains_full.astype(float_type)
    gradient_out = cotangent.astype(float_type)
    grad_branch = (gains_wide[3] * gradient_out).astype(narrow_type)
    grad_rank_contract = (transposed_right(grad_branch, contract_up) * select).astype(narrow_type)
    grad_contract_down = transposed_left(active, grad_rank_contract)
    grad_contract_up = transposed_left(rank_contract, grad_branch)
    grad_active = transposed_right(grad_branch, contract_full) + transposed_right(
        grad_rank_contract, contract_down
    )
    grad_hidden = (grad_active * gelu_slope(hidden_pre)).astype(narrow_type)
    grad_rank_expand = (transposed_right(grad_hidden, expand_up) * select).astype(narrow_type)
    grad_expand_down = transposed_left(normed_second, grad_rank_expand)
    grad_expand_up = transposed_left(rank_expand, grad_hidden)
    grad_normed_second = transposed_right(grad_hidden, expand_full) + transposed_right(
        grad_rank_expand, expand_down
    )
    grad_middle = gradient_out + norm_backward(
        grad_normed_second, gains_wide[2], normal_second, scaling_second
    )
    grad_mixed = (gains_wide[1] * grad_middle).astype(narrow_type)
    grad_rank_out = (transposed_right(grad_mixed, attention_up[3]) * select).astype(narrow_type)
    grad_out_down = transposed_left(attended, grad_rank_out)
    grad_out_up = transposed_left(rank_out, grad_mixed)
    grad_attended = (
        transposed_right(grad_mixed, output_full)
        + transposed_right(grad_rank_out, attention_down[3])
    ).astype(narrow_type)

    def pair_backward(pair_index):
        query_part, key_part, value_part, scores = pair_slices(pair_index)
        grad_part = lax.dynamic_slice_in_dim(
            grad_attended, pair_index * pair_width, pair_width, 1
        ).reshape(row_count, 2, head_width)
        log_pair = log_totals[pair_index]
        probable = jnp.exp(scores - log_pair[:, :, None])
        grad_probable = jnp.einsum(
            "qhd,khd->hqk", grad_part, value_part, preferred_element_type=float_type
        )
        grad_scores = probable * (
            grad_probable - jnp.sum(grad_probable * probable, axis=2, keepdims=True)
        )
        grad_scores = grad_scores.astype(narrow_type)
        grad_query = (
            jnp.einsum("hqk,khd->qhd", grad_scores, key_part, preferred_element_type=float_type)
            * scaling_score
        )
        grad_key = (
            jnp.einsum("hqk,qhd->khd", grad_scores, query_part, preferred_element_type=float_type)
            * scaling_score
        )
        grad_value = jnp.einsum(
            "hqk,qhd->khd",
            probable.astype(narrow_type),
            grad_part,
            preferred_element_type=float_type,
        )
        return (
            grad_query.reshape(row_count, pair_width),
            grad_key.reshape(window_rows, pair_width),
            grad_value.reshape(window_rows, pair_width),
        )

    grad_query_pairs, grad_key_pairs, grad_value_pairs = lax.map(
        pair_backward, jnp.arange(pair_count)
    )
    grad_queries = grad_query_pairs.transpose(1, 0, 2).reshape(row_count, features)
    grad_keys = grad_key_pairs.transpose(1, 0, 2).reshape(window_rows, features)
    grad_values = grad_value_pairs.transpose(1, 0, 2).reshape(window_rows, features)
    grad_window = jnp.concatenate([grad_keys, grad_values], axis=1)
    padded_grads = jnp.pad(grad_window, ((window_start, window_start), (0, 0)))
    grad_pairs = padded_grads[HOPS * row_count : (HOPS + 1) * row_count]
    for distance in range(1, HOPS + 1):
        lower_piece = padded_grads[
            (HOPS - distance) * row_count : (HOPS - distance + 1) * row_count
        ]
        higher_piece = padded_grads[
            (HOPS + distance) * row_count : (HOPS + distance + 1) * row_count
        ]
        grad_pairs = grad_pairs + passed_along(
            lower_piece.astype(jnp.bfloat16), ("seq", "fsdp"), -distance
        ).astype(lower_piece.dtype)
        grad_pairs = grad_pairs + passed_along(
            higher_piece.astype(jnp.bfloat16), ("seq", "fsdp"), distance
        ).astype(higher_piece.dtype)
    grad_projected = jnp.concatenate([grad_queries, grad_pairs], axis=1).astype(narrow_type)
    grad_blocks = grad_projected.reshape(row_count, 3, features)
    grad_rank_qkv = (
        jnp.einsum("tpd,prd->tpr", grad_blocks, attention_up[:3], preferred_element_type=float_type)
        * select[:, None, :]
    ).astype(narrow_type)
    grad_qkv_down = jnp.einsum(
        "td,tpr->pdr", normed_first, grad_rank_qkv, preferred_element_type=float_type
    )
    grad_qkv_up = jnp.einsum(
        "tpr,tpd->prd", rank_qkv, grad_blocks, preferred_element_type=float_type
    )
    grad_normed_first = transposed_right(grad_projected, qkv_full) + jnp.einsum(
        "tpr,pdr->td", grad_rank_qkv, attention_down[:3], preferred_element_type=float_type
    )
    input_gradient = grad_middle + norm_backward(
        grad_normed_first, gains_wide[0], normal_first, scaling_first
    )
    grad_attention_down = jnp.concatenate([grad_qkv_down, grad_out_down[None]], axis=0)
    grad_attention_up = jnp.concatenate([grad_qkv_up, grad_out_up[None]], axis=0)
    summed = (
        lax.psum_scatter(grad_attention_down, ("seq", "fsdp"), scatter_dimension=1, tiled=True),
        lax.psum_scatter(grad_attention_up, ("seq", "fsdp"), scatter_dimension=2, tiled=True),
        lax.psum_scatter(grad_expand_down, ("seq", "fsdp"), scatter_dimension=0, tiled=True),
        lax.psum_scatter(grad_expand_up, ("seq", "fsdp"), scatter_dimension=1, tiled=True),
        lax.psum_scatter(grad_contract_down, ("seq", "fsdp"), scatter_dimension=0, tiled=True),
        lax.psum_scatter(grad_contract_up, ("seq", "fsdp"), scatter_dimension=1, tiled=True),
    )
    return (
        result,
        input_gradient,
        summed[0],
        summed[1],
        summed[2],
        summed[3],
        summed[4],
        summed[5],
    )


MESH_ID = pl.DeviceIdType.MESH
CORES, SIDE_X, SIDE_Y = 1, 2, 4
ANYWHERE = pl.BlockSpec(memory_space=pl.ANY)
IN_VMEM = pl.BlockSpec(memory_space=pltpu.VMEM)
IN_SMEM = pl.BlockSpec(memory_space=pltpu.SMEM)


def place_here():
    return lax.axis_index("seq"), lax.axis_index("fsdp")


def remote(source, target, send, receive, seq, fsdp):
    return pltpu.make_async_remote_copy(
        src_ref=source,
        dst_ref=target,
        send_sem=send,
        recv_sem=receive,
        device_id=(seq, fsdp),
        device_id_type=MESH_ID,
    )


def greet(barrier, seq, fsdp):
    pl.semaphore_signal(barrier, 1, device_id=(seq, fsdp), device_id_type=MESH_ID)


def greet_neighbours(barrier, seq, fsdp, depth):
    for bit in (CORES, SIDE_X, SIDE_Y):
        greet(barrier, seq ^ bit, fsdp)
    for step in range(1, depth):
        greet(barrier, seq, lax.rem(fsdp + step, depth))


WHOLE, OPEN, LINE = 0, 1, 2


class Gather:
    STEPS = 10

    def __init__(self, depth, send, receive):
        self.depth, self.send, self.receive = depth, send, receive
        self.seq, self.fsdp = place_here()
        self.me = self.seq * depth + self.fsdp
        self.inside = (self.fsdp == 1) | (self.fsdp == 2)

    def copy(self, index, step, source, target, seq, fsdp):
        at = index * self.STEPS + step
        return remote(source, target, self.send.at[at], self.receive.at[at], seq, fsdp)

    def part(self, chunk, at_seq, first, count):
        full, rows, columns, _, kind, _ = chunk
        base = 0 if kind == LINE else at_seq * self.depth
        return full.at[pl.ds(base + first, count), rows, columns]

    def group(self, chunk, at_seq):
        return self.part(chunk, at_seq, 0, self.depth)

    def sides(self, chunk):
        return (SIDE_X, SIDE_Y) if chunk[3] else (SIDE_Y, SIDE_X)

    def line(self, index, chunk, step):
        pair = lax.div(self.fsdp, 2)
        if step == 0:
            piece, to = self.part(chunk, self.seq, self.fsdp, 1), self.fsdp ^ 1
            if chunk[5] is not None:
                source = chunk[5].at[pl.ds(0, 1), chunk[1], chunk[2]]
                return self.copy(index, step, source, piece, self.seq, to)
        elif step == 1:
            piece, to = self.part(chunk, self.seq, 2 * pair, 2), 3 - self.fsdp
        else:
            piece, to = self.part(chunk, self.seq, 2 - 2 * pair, 2), self.fsdp ^ 1
        return self.copy(index, step, piece, piece, self.seq, to)

    def over(self, index, chunk, step):
        a, b = self.sides(chunk)
        piece = self.group(chunk, self.seq ^ a if step == 2 else self.seq)
        return self.copy(index, 3 + step, piece, piece, self.seq ^ (b if step else a), self.fsdp)

    def across(self, index, chunk, step):
        a, b = self.sides(chunk)
        piece = self.group(chunk, self.seq ^ (0, a, b, a ^ b)[step])
        return self.copy(index, 6 + step, piece, piece, self.seq ^ CORES, self.fsdp)

    def own(self, index, chunk):
        self.line(index, chunk, 0).start()

    def inner(self, index, chunk):
        @pl.when(self.inside)
        def _():
            self.line(index, chunk, 0).wait_recv()
            self.line(index, chunk, 1).start()

    def outer(self, index, chunk):
        @pl.when(self.inside)
        def _():
            self.line(index, chunk, 1).wait_recv()
            self.line(index, chunk, 2).start()

    def arrive(self, index, chunk):
        @pl.when(jnp.logical_not(self.inside))
        def _():
            self.line(index, chunk, 0).wait_recv()
            self.line(index, chunk, 2).wait_recv()

    def first(self, index, chunk):
        self.arrive(index, chunk)
        self.over(index, chunk, 0).start()
        self.over(index, chunk, 1).start()
        self.across(index, chunk, 0).start()

    def second(self, index, chunk):
        self.over(index, chunk, 0).wait_recv()
        if chunk[4] == WHOLE:
            self.over(index, chunk, 2).start()
        self.across(index, chunk, 1).start()

    def third(self, index, chunk):
        self.over(index, chunk, 1).wait_recv()
        self.across(index, chunk, 2).start()
        if chunk[4] == WHOLE:
            self.over(index, chunk, 2).wait_recv()
            self.across(index, chunk, 3).start()

    def finish(self, index, chunk):
        for step in range(4 if chunk[4] == WHOLE else 3):
            self.across(index, chunk, step).wait_recv()

    def drain(self, index, chunk):
        self.line(index, chunk, 0).wait_send()

        @pl.when(self.inside)
        def _():
            self.line(index, chunk, 1).wait_send()
            self.line(index, chunk, 2).wait_send()

        if chunk[4] == LINE:
            return
        for step in range(3 if chunk[4] == WHOLE else 2):
            self.over(index, chunk, step).wait_send()
        for step in range(4 if chunk[4] == WHOLE else 3):
            self.across(index, chunk, step).wait_send()


class Exchange:
    def __init__(self, depth, heads):
        self.depth, self.heads = depth, heads
        self.seq, self.fsdp = place_here()
        self.me = self.seq * depth + self.fsdp
        self.core, self.half = lax.rem(self.seq, 2), lax.div(self.seq, 4)
        self.head = lax.div(self.seq, 2) * depth + self.fsdp
        self.same = (self.half == self.core).astype(jnp.int32)

    def holder(self, k):
        return lax.div(k, self.depth) * 2 + self.half, lax.rem(k, self.depth)

    def owner(self, k):
        block = self.core * self.heads + k
        return lax.div(block, self.depth), lax.rem(block, self.depth)

    def away_head(self, k):
        return (k != self.head) | (self.half != self.core)

    def away_block(self, k):
        return self.core * self.heads + k != self.me

    def greet_holders(self, barrier):
        @pl.loop(0, self.heads)
        def _(k):
            @pl.when(self.away_head(k))
            def _():
                greet(barrier, *self.holder(k))

        return self.heads - self.same

    def greet_owners(self, barrier):
        @pl.loop(0, self.heads)
        def _(k):
            @pl.when(self.away_block(k))
            def _():
                greet(barrier, *self.owner(k))

        return self.heads - self.same


def as_matrix(block):
    return block.reshape(-1, block.shape[-1])


def turned(block, tile=256):
    return block.astype(float_type).T.astype(narrow_type)


def rows_of_vectors(ve, target):
    flat = as_matrix(ve[:, 0:32, :]).astype(float_type)
    target[...] = flat.T[0:16]


def by_feature_wide(block):
    return jnp.concatenate([block, jnp.zeros((112, block.shape[1]), block.dtype)], axis=0)


def selected(lens_ref, choice_ref, block, rows, lanes):
    place = lax.broadcasted_iota(jnp.int32, (rows, lanes), 0) + block * rows
    lane = lax.broadcasted_iota(jnp.int32, (rows, lanes), 1)
    chosen = jnp.zeros((rows, lanes), jnp.int32)
    start = jnp.int32(0)
    for image in range(lens_ref.shape[0]):
        end = start + lens_ref[image]
        chosen = jnp.where((place >= start) & (place < end), choice_ref[image] * RANK, chosen)
        start = end
    return jnp.where((lane >= chosen) & (lane < chosen + RANK), 1.0, 0.0).astype(float_type)


def stood_up(block):
    n, m = block.shape
    block = block.astype(float_type)
    if m < 128:
        block = jnp.concatenate([block, jnp.zeros((n, 128 - m), float_type)], axis=1)
    if n < 128:
        block = jnp.concatenate([block, jnp.zeros((128 - n, 128), float_type)], axis=0)
    return block.T[0:m].astype(narrow_type)


def attention_in_kernel(
    depth,
    halo,
    heads,
    chunks,
    lens_ref,
    choice_ref,
    tok_in,
    gains_in,
    biases_in,
    bias_in,
    wqkv,
    wout,
    a_att,
    b_att,
    a_exp,
    b_con,
    w2,
    a_con,
    b_exp_in,
    w1,
    fa_out,
    ve_out,
    f2,
    line_a,
    line_b,
    y_ref,
    rank_ref,
    fa,
    ve,
    proj,
    normed,
    vectors,
    tok,
    gains,
    biases,
    bias,
    b_exp,
    shard_f2,
    shard_a,
    shard_b,
    select,
    send,
    receive,
    local,
    piece_send,
    piece_receive,
    piece_local,
):
    gather, swap = Gather(depth, send, receive), Exchange(depth, heads)
    me, seq, fsdp = swap.me, swap.seq, swap.fsdp
    core, half, head, own = swap.core, swap.half, swap.head, heads
    features = normed.shape[1]
    wide = features + 256
    barrier = pltpu.get_barrier_semaphore()
    greet_neighbours(barrier, seq, fsdp, depth)
    waits = 3 + depth - 1 + swap.greet_owners(barrier)
    half_columns = line_a.shape[2]
    small = [
        (gains_in, gains.at[0:4]),
        (biases_in, biases.at[0:5]),
        (bias_in, bias),
        (b_exp_in, b_exp),
        (tok_in, tok),
    ]
    places = []
    for p in range(4):
        source = wqkv.at[:, pl.ds(p * features, features)] if p < 3 else wout
        places.append((source, fa.at[me, :, pl.ds(p * wide, features)]))
        places.append((a_att.at[p], fa.at[me, :, pl.ds(p * wide + features, 128)]))
        places.append((b_att.at[p], fa.at[me, :, pl.ds(p * wide + features + 128, 128)]))
    places.append((a_exp, fa.at[me, :, pl.ds(4 * wide, 128)]))
    places.append((b_con, fa.at[me, :, pl.ds(4 * wide + 128, 128)]))
    places.append((w2, shard_f2.at[0, :, pl.ds(0, features)]))
    places.append((a_con, shard_f2.at[0, :, pl.ds(features, 128)]))
    places.append((w1.at[:, pl.ds(0, half_columns)], shard_a.at[0]))
    places.append((w1.at[:, pl.ds(half_columns, half_columns)], shard_b.at[0]))
    placed = [pltpu.make_async_copy(a, b, local.at[i]) for i, (a, b) in enumerate(small + places)]
    for copy in placed:
        copy.start()
    for copy in placed[: len(small) - 1]:
        copy.wait()
    shard_f2[0, :, features + 128 : wide] = stood_up(b_exp[...])
    by_feature = jnp.concatenate(
        [gains[0:4].astype(float_type), biases[0:5].astype(float_type), jnp.zeros((7, 32), float_type)], axis=0
    )
    ve[me, 0:32] = stood_up(by_feature_wide(by_feature))
    ve[me, 32:48] = jnp.broadcast_to(bias[...].astype(float_type), (16, 128)).astype(narrow_type)
    for copy in placed[len(small) - 1 :]:
        copy.wait()
    own_shards = [
        pltpu.make_async_copy(shard.at[0], full.at[slot], local.at[i])
        for i, (shard, full, slot) in enumerate(((shard_f2, f2, me), (shard_a, line_a, fsdp), (shard_b, line_b, fsdp)))
    ]
    for copy in own_shards:
        copy.start()
    refs = {
        "ve": (ve, WHOLE, None),
        "fa": (fa, WHOLE, None),
        "f2": (f2, OPEN, shard_f2),
        "a": (line_a, LINE, shard_a),
        "b": (line_b, LINE, shard_b),
    }
    chunks = [
        (refs[name][0], rows, columns, flip) + refs[name][1:] for name, rows, columns, flip in chunks
    ]
    first_hidden = [i for i, chunk in enumerate(chunks) if chunk[4] != WHOLE][:1]
    pl.semaphore_wait(barrier, waits)
    early = [i for i, chunk in enumerate(chunks) if chunk[0] is fa or chunk[0] is ve]
    for index in early:
        gather.own(index, chunks[index])
    select[...] = selected(lens_ref, choice_ref, me, *select.shape)
    base = core * (own - halo)
    slot = me - half * (own - halo)

    def piece(p, k):
        return remote(
            proj.at[p, k],
            y_ref.at[slot, p],
            piece_send.at[p, k],
            piece_receive.at[p, lax.rem(me, own)],
            *swap.holder(k),
        )

    def arrival(p, k):
        return remote(
            proj.at[p, 0],
            y_ref.at[core * own + k - base, p],
            piece_send.at[p, k],
            piece_receive.at[p, k],
            seq ^ CORES,
            fsdp,
        )

    def kept(p):
        return pltpu.make_async_copy(proj.at[p, head], y_ref.at[me - base, p], piece_local.at[p])

    def norm():
        rows_of_vectors(ve, vectors)
        rows = tok[...].astype(float_type)
        normed[...] = layer_norm(rows, vectors[0:1], vectors[4:5])[0].astype(narrow_type)

    def project(p):
        down = as_matrix(fa[:, :, p * wide + features : p * wide + features + 128])
        rank = (matmul(normed[...], down) * select[...]).astype(narrow_type)
        rank_ref[p] = rank

        @pl.loop(0, features // 256)
        def _(j):
            weight = as_matrix(fa[:, :, pl.ds(pl.multiple_of(p * wide + j * 256, 128), 256)])
            up = as_matrix(fa[pl.ds(j * 8, 8), :, p * wide + features + 128 : (p + 1) * wide])
            result = matmul(normed[...], weight) + transposed_right(rank, up)
            if p == 0:
                result = result + vectors[5:6, pl.ds(pl.multiple_of(j * 256, 128), 256)]
            proj[p, pl.ds(j * 4, 4)] = result.T.astype(narrow_type).reshape(4, 64, 256)

            @pl.loop(0, 4)
            def _(i):
                k = j * 4 + i

                @pl.when(swap.away_head(k))
                def _():
                    piece(p, k).start()

        @pl.when(half == core)
        def _():
            kept(p).start()

    after = {0: norm, 2: lambda: project(0), 4: lambda: project(1), 6: lambda: project(2)}
    after_attention = [i for i, chunk in enumerate(chunks) if chunk[0] is fa][-1]
    outs = [
        pltpu.make_async_copy(fa, fa_out, local.at[3]),
        pltpu.make_async_copy(ve, ve_out, local.at[4]),
    ]

    def store():
        for copy in outs:
            copy.start()

    def exchanged():
        @pl.loop(0, own)
        def _(k):
            @pl.when(swap.away_block(k))
            def _():
                for p in range(3):
                    arrival(p, k).wait_recv()

        @pl.when(half == core)
        def _():
            for p in range(3):
                kept(p).wait()

        first = jnp.where(core == 0, own - halo, own)
        over = remote(
            y_ref.at[pl.ds(first - base, halo), 1:3],
            y_ref.at[pl.ds(first - (own - halo) * (1 - core), halo), 1:3],
            piece_send.at[3, 0],
            piece_receive.at[3, 0],
            seq ^ CORES,
            fsdp,
        )
        over.start()
        return over

    steps = (gather.own, gather.inner, gather.outer, gather.first, gather.second, gather.third, gather.finish)
    for turn in range(DELAYS[0], len(chunks) + DELAYS[-1]):
        if turn == len(chunks) - 2:
            over = exchanged()
        for delay, step in zip(DELAYS, steps):
            index = turn - delay
            if not 0 <= index < len(chunks) or (delay == DELAYS[0] and index in early):
                continue
            chunk = chunks[index]
            if delay == DELAYS[1] and index in first_hidden:
                for copy in own_shards:
                    copy.wait()
            if chunk[4] == LINE and delay == 0:
                step = gather.arrive
            if chunk[4] == LINE and delay > 0:
                continue
            step(index, chunk)
            if delay == 3:
                after.get(index, lambda: None)()
                if index == after_attention:
                    store()

    over.wait()

    @pl.loop(0, heads)
    def _(k):
        @pl.when(swap.away_head(k))
        def _():
            for p in range(3):
                piece(p, k).wait_send()

    for index, chunk in enumerate(chunks):
        gather.drain(index, chunk)
    for copy in outs:
        copy.wait()


def attention_in(lengths, choice, tokens, arrays, halo, depth, heads, devices, collective):
    rows, features = tokens.shape
    wide = features + 256
    total = 4 * wide + 256
    share, hidden_share, hidden_total = features // devices, arrays[9].shape[0], arrays[12].shape[1]
    chunks = [("ve", slice(0, 48), slice(0, 128), 0)]
    for p in range(3):
        chunks.append(("fa", slice(0, share), slice(p * wide, p * wide + wide // 2), 0))
        chunks.append(("fa", slice(0, share), slice(p * wide + wide // 2, (p + 1) * wide), 1))
    middle = 3 * wide + (total - 3 * wide) // 2
    chunks.append(("fa", slice(0, share), slice(3 * wide, middle), 0))
    chunks.append(("fa", slice(0, share), slice(middle, total), 1))
    for part in range(0, hidden_share, 64):
        chunks.append(("f2", slice(part, part + 64), slice(0, wide // 2), 0))
        chunks.append(("f2", slice(part, part + 64), slice(wide // 2, wide), 1))
    for part in range(0, hidden_total // 2, 2048):
        chunks.append(("a", slice(0, share), slice(part, part + 2048), 0))
        chunks.append(("b", slice(0, share), slice(part, part + 2048), 1))
    copies = Gather.STEPS * len(chunks)
    return pl.pallas_call(
        functools.partial(attention_in_kernel, depth, halo, heads, chunks),
        out_shape=(
            jax.ShapeDtypeStruct((devices, share, total), narrow_type),
            jax.ShapeDtypeStruct((devices, 48, 128), narrow_type),
            jax.ShapeDtypeStruct((devices, hidden_share, wide), narrow_type),
            jax.ShapeDtypeStruct((depth, share, hidden_total // 2), narrow_type),
            jax.ShapeDtypeStruct((depth, share, hidden_total // 2), narrow_type),
            jax.ShapeDtypeStruct((heads + halo, 3, features // heads, rows), narrow_type),
            jax.ShapeDtypeStruct((3, rows, 128), narrow_type),
        ),
        in_specs=[IN_SMEM, IN_SMEM] + [ANYWHERE] * (1 + len(arrays)),
        out_specs=(ANYWHERE,) * 6 + (IN_VMEM,),
        scratch_shapes=[
            pltpu.VMEM((devices, share, total), narrow_type),
            pltpu.VMEM((devices, 48, 128), narrow_type),
            pltpu.VMEM((3, heads, features // heads, rows), narrow_type),
            pltpu.VMEM((rows, features), narrow_type),
            pltpu.VMEM((16, features), float_type),
            pltpu.VMEM((rows, features), narrow_type),
            pltpu.VMEM((4, share), narrow_type),
            pltpu.VMEM((5, share), narrow_type),
            pltpu.VMEM((1, 128), narrow_type),
            pltpu.VMEM((128, 128), narrow_type),
            pltpu.VMEM((1, hidden_share, wide), narrow_type),
            pltpu.VMEM((1, share, hidden_total // 2), narrow_type),
            pltpu.VMEM((1, share, hidden_total // 2), narrow_type),
            pltpu.VMEM((rows, 128), float_type),
            pltpu.SemaphoreType.DMA((copies,)),
            pltpu.SemaphoreType.DMA((copies,)),
            pltpu.SemaphoreType.DMA((24,)),
            pltpu.SemaphoreType.DMA((4, heads)),
            pltpu.SemaphoreType.DMA((4, heads)),
            pltpu.SemaphoreType.DMA((3,)),
        ],
        compiler_params=pltpu.CompilerParams(
            collective_id=collective, has_side_effects=True, vmem_limit_bytes=60 << 20
        ),
    )(lengths, choice, tokens, *arrays)


DELAYS = (-9, -6, -3, 0, 1, 2, 3)
HIDDEN_TILE = 512


def middle_kernel(
    depth,
    heads,
    lens_ref,
    choice_ref,
    att_ref,
    tok_ref,
    cot_ref,
    fa_in,
    ve,
    f2_in,
    line_a,
    line_b,
    ya,
    yb,
    xa,
    xb,
    result_ref,
    gm_ref,
    terms,
    gy_ref,
    fa,
    f2,
    f1,
    att_t,
    att,
    gatt_t,
    vectors,
    hidden_bias,
    middle,
    normal,
    normed,
    branch,
    grad_branch,
    grad_normed,
    ranks,
    rank_sums,
    select,
    send,
    receive,
    local,
    a_send,
    a_receive,
    b_send,
    b_receive,
    own_local,
):
    swap = Exchange(depth, heads)
    me, seq, fsdp = swap.me, swap.seq, swap.fsdp
    core, half, head, own = swap.core, swap.half, swap.head, heads
    devices, share = f1.shape[0], f1.shape[1]
    row_count, features = tok_ref.shape
    wide = features + 256
    tiles = f1.shape[2] // HIDDEN_TILE
    in_tile = HIDDEN_TILE // f2.shape[1]
    barrier = pltpu.get_barrier_semaphore()
    greet_neighbours(barrier, seq, fsdp, depth)
    waits = 3 + depth - 1 + swap.greet_owners(barrier) + swap.greet_holders(barrier)
    half_columns = line_a.shape[2]
    left, right = pl.ds(0, half_columns), pl.ds(half_columns, half_columns)
    lines = [
        (line, f1.at[pl.ds((seq ^ bit) * depth, depth), :, columns])
        for line, bit, columns in (
            (line_a, 0, left),
            (line_b, 0, right),
            (ya, SIDE_Y, left),
            (yb, SIDE_Y, right),
            (xa, SIDE_X, left),
            (xb, SIDE_X, right),
        )
    ]
    groups = [pl.ds((seq ^ k) * depth, depth) for k in range(8)]
    loads = (
        [pltpu.make_async_copy(fa_in.at[:, :, pl.ds(3 * wide, wide + 256)], fa, local.at[0])]
        + [pltpu.make_async_copy(line, place, local.at[1 + i]) for i, (line, place) in enumerate(lines)]
        + [pltpu.make_async_copy(f2_in.at[groups[k]], f2.at[groups[k]], local.at[7 + k]) for k in range(6)]
    )
    for copy in loads:
        copy.start()
    pl.semaphore_wait(barrier, waits)
    corners = [
        remote(ya, lines[2][1], send.at[0], receive.at[0], seq ^ SIDE_X, fsdp),
        remote(xb, lines[5][1], send.at[1], receive.at[1], seq ^ SIDE_Y, fsdp),
    ]
    tops, tails = pl.ds(0, wide // 2), pl.ds(wide // 2, wide // 2)
    f2_parts = ((SIDE_Y, SIDE_X, tops), (SIDE_X, SIDE_Y, tails))
    for i, (via, to, columns) in enumerate(f2_parts):
        line = pl.ds((seq ^ via) * depth, depth)
        corners.append(
            remote(
                f2_in.at[line, :, columns],
                f2.at[line, :, columns],
                send.at[10 + i],
                receive.at[10 + i],
                seq ^ to,
                fsdp,
            )
        )
    across = [
        remote(line, place, send.at[2 + i], receive.at[2 + i], seq ^ CORES, fsdp)
        for i, (line, place) in enumerate(lines)
    ]
    for i, columns in enumerate((left, right)):
        place = f1.at[pl.ds((seq ^ SIDE_X ^ SIDE_Y) * depth, depth), :, columns]
        across.append(remote(place, place, send.at[8 + i], receive.at[8 + i], seq ^ CORES, fsdp))
    f2_across = remote(
        f2.at[groups[6]], f2.at[groups[6]], send.at[12], receive.at[12], seq ^ CORES, fsdp
    )

    def attended_piece(k):
        return remote(att_ref.at[k], att_t.at[head], a_send.at[k], a_receive.at[head], *swap.owner(k))

    def attended_arrival(k):
        return remote(att_ref.at[0], att_t.at[k], a_send.at[k], a_receive.at[k], seq ^ CORES, fsdp)

    attended_kept = pltpu.make_async_copy(att_ref.at[me - core * own], att_t.at[head], own_local.at[0])

    @pl.when(half == core)
    def _():
        attended_kept.start()

    @pl.loop(0, own)
    def _(step):
        k = lax.rem(step + me, own)

        @pl.when(swap.away_block(k))
        def _():
            attended_piece(k).start()

    for copy in corners + across[:6]:
        copy.start()
    select[...] = selected(lens_ref, choice_ref, me, *select.shape)
    rows_of_vectors(ve, vectors)
    for d in range(devices):
        hidden_bias[:, d * 128 : (d + 1) * 128] = ve[d, 32:48, :].astype(float_type)[0:8]
    grad_branch[...] = (vectors[3:4] * cot_ref[...].astype(float_type)).astype(narrow_type)
    loads[0].wait()
    contract_up = as_matrix(fa[:, :, wide + 128 : wide + 256])
    ranks[1] = (matmul(grad_branch[...], contract_up) * select[...]).astype(narrow_type)
    branch[...] = jnp.zeros_like(branch)
    grad_normed[...] = jnp.zeros_like(grad_normed)
    rank_sums[...] = jnp.zeros_like(rank_sums)

    @pl.loop(0, heads)
    def _(k):
        @pl.when(swap.away_head(k))
        def _():
            attended_arrival(k).wait_recv()

    @pl.when(half == core)
    def _():
        attended_kept.wait()

    for i in range(2):
        corners[i].wait_recv()
        across[6 + i].start()
    for j in range(4):
        att[:, j * 256 : (j + 1) * 256] = turned(as_matrix(att_t[4 * j : 4 * j + 4]))
    out_down = as_matrix(fa[:, :, features : features + 128])
    rank_out = (matmul(att[...], out_down) * select[...]).astype(narrow_type)
    ranks[2] = rank_out

    @pl.loop(0, 4)
    def _(j):
        at = pl.ds(pl.multiple_of(j * 256, 128), 256)
        weight = as_matrix(fa[:, :, at])
        up = as_matrix(fa[pl.ds(j * 8, 8), :, features + 128 : wide])
        mixed = matmul(att[...], weight) + transposed_right(rank_out, up) + vectors[6:7, at]
        middle[:, at] = tok_ref[:, at].astype(float_type) + vectors[1:2, at] * mixed

    shifted, normal_rows, scaling = layer_norm(middle[...], vectors[2:3], vectors[7:8])
    normal[...] = normal_rows
    normed[...] = shifted.astype(narrow_type)
    expand_down = as_matrix(fa[:, :, wide : wide + 128])
    rank_expand = (matmul(normed[...], expand_down) * select[...]).astype(narrow_type)
    ranks[0] = rank_expand
    ranks[3, 0:128] = turned(rank_expand)[:, 0:128]
    ranks[3, 128:256] = turned(rank_expand)[:, 128:256]
    ranks[4, 0:128] = turned(ranks[1])[:, 0:128]
    ranks[4, 128:256] = turned(ranks[1])[:, 128:256]
    for copy in loads[1:]:
        copy.wait()
    for copy in across:
        copy.wait_recv()

    def hidden(k):
        @pl.when(k == 6)
        def _():
            corners[2].wait_recv()
            corners[3].wait_recv()
            f2_across.start()

        @pl.when(k == 7)
        def _():
            f2_across.wait_recv()

        c = seq ^ k
        at = pl.ds(pl.multiple_of(c * HIDDEN_TILE, 128), HIDDEN_TILE)
        slots = pl.ds(c * in_tile, in_tile)
        expand = as_matrix(f1[:, :, at])
        contract = as_matrix(f2[slots, :, 0:features])
        down = as_matrix(f2[slots, :, features : features + 128])
        up = as_matrix(f2[slots, :, features + 128 : wide])
        before = matmul(normed[...], expand) + transposed_right(ranks[0], up) + hidden_bias[0:1, at]
        total = 0.5 * (1.0 + lax.erf(before * 0.7071067811865476))
        density = jnp.exp(-0.5 * before * before) * 0.3989422804014327
        active = (before * total).astype(narrow_type)
        slope = total + before * density
        branch[...] += matmul(active, contract)
        rank_sums[0] += matmul(active, down)
        grad_active = transposed_right(grad_branch[...], contract) + transposed_right(ranks[1], down)
        grad_hidden = (grad_active * slope).astype(narrow_type)
        rank_sums[1] += matmul(grad_hidden, up)
        grad_normed[...] += transposed_right(grad_hidden, expand)
        turned_expand = jnp.concatenate([ranks[3, 0:128], ranks[3, 128:256]], axis=1)
        turned_contract = jnp.concatenate([ranks[4, 0:128], ranks[4, 128:256]], axis=1)
        grad_up = matmul(turned_expand, grad_hidden).astype(narrow_type)
        grad_down = matmul(turned_contract, active).astype(narrow_type)
        for i in range(in_tile):
            terms[c * in_tile + i, 96:224] = grad_up[:, i * 128 : (i + 1) * 128]
            terms[c * in_tile + i, 224:352] = grad_down[:, i * 128 : (i + 1) * 128]

    pl.loop(0, tiles)(hidden)
    rank_contract = (rank_sums[0] * select[...]).astype(narrow_type)
    grad_rank_expand = (rank_sums[1] * select[...]).astype(narrow_type)
    gradient = grad_normed[...] + transposed_right(grad_rank_expand, expand_down)
    gm_ref[...] = cot_ref[...].astype(float_type) + norm_backward(gradient, vectors[2:3], normal[...], scaling)
    grad_mixed = (vectors[1:2] * gm_ref[...]).astype(narrow_type)
    out_up = as_matrix(fa[:, :, features + 128 : wide])
    grad_rank_out = (matmul(grad_mixed, out_up) * select[...]).astype(narrow_type)

    def gradient_piece(k):
        return remote(
            gatt_t.at[k], gy_ref.at[lax.rem(me, own)], b_send.at[k], b_receive.at[lax.rem(me, own)], *swap.holder(k)
        )

    def gradient_arrival(k):
        return remote(gatt_t.at[0], gy_ref.at[k], b_send.at[k], b_receive.at[k], seq ^ CORES, fsdp)

    gradient_kept = pltpu.make_async_copy(gatt_t.at[head], gy_ref.at[lax.rem(me, own)], own_local.at[1])

    @pl.loop(0, 4)
    def _(j):
        slots = pl.ds(j * 8, 8)
        weight = as_matrix(fa[slots, :, 0:features])
        down = as_matrix(fa[slots, :, features : features + 128])
        rows = transposed_right(grad_mixed, weight) + transposed_right(grad_rank_out, down)
        gatt_t[pl.ds(j * 4, 4)] = rows.T.astype(narrow_type).reshape(4, 64, 256)

        @pl.loop(0, 4)
        def _(i):
            k = j * 4 + i

            @pl.when(swap.away_head(k))
            def _():
                gradient_piece(k).start()

    @pl.when(half == core)
    def _():
        gradient_kept.start()

    up_rows = transposed_right(rank_contract, contract_up)
    result_ref[...] = (
        middle[...] + vectors[3:4] * (branch[...] + vectors[8:9] + up_rows)
    ).astype(narrow_type)
    shaped = (devices, share, 128)
    terms[:, 0:32] = matmul(as_matrix(att_t[...]), grad_rank_out).astype(narrow_type).reshape(shaped)
    terms[:, 32:64] = transposed_left(grad_mixed, rank_out).astype(narrow_type).reshape(shaped)
    terms[:, 64:96] = transposed_left(normed[...], grad_rank_expand).astype(narrow_type).reshape(shaped)
    terms[:, 352:384] = transposed_left(grad_branch[...], rank_contract).astype(narrow_type).reshape(shaped)

    @pl.loop(0, own)
    def _(k):
        @pl.when(swap.away_block(k))
        def _():
            gradient_arrival(k).wait_recv()
            attended_piece(k).wait_send()

    @pl.when(half == core)
    def _():
        gradient_kept.wait()

    @pl.loop(0, heads)
    def _(k):
        @pl.when(swap.away_head(k))
        def _():
            gradient_piece(k).wait_send()

    for copy in corners + across + [f2_across]:
        copy.wait_send()


def middle_part(lengths, choice, att, tokens, cotangent, fa, ve, f2, lines, depth, collective):
    heads, width, rows = att.shape
    features = tokens.shape[1]
    wide = features + 256
    devices, hidden_share = f2.shape[0], f2.shape[1]
    share, hidden_total = features // devices, 2 * lines[0].shape[2]
    copies = 13

    def wide_rows():
        return pltpu.VMEM((rows, features), float_type)

    def narrow_rows():
        return pltpu.VMEM((rows, features), narrow_type)

    return pl.pallas_call(
        functools.partial(middle_kernel, depth, heads),
        out_shape=(
            jax.ShapeDtypeStruct((rows, features), narrow_type),
            jax.ShapeDtypeStruct((rows, features), float_type),
            jax.ShapeDtypeStruct((devices, 384, 128), narrow_type),
            jax.ShapeDtypeStruct((heads, width, rows), narrow_type),
        ),
        in_specs=[IN_SMEM, IN_SMEM, IN_VMEM, IN_VMEM, IN_VMEM, ANYWHERE, IN_VMEM] + [ANYWHERE] * 7,
        out_specs=(IN_VMEM, IN_VMEM, IN_VMEM, ANYWHERE),
        scratch_shapes=[
            pltpu.VMEM((devices, share, wide + 256), narrow_type),
            pltpu.VMEM(f2.shape, narrow_type),
            pltpu.VMEM((devices, share, hidden_total), narrow_type),
            pltpu.VMEM((heads, width, rows), narrow_type),
            narrow_rows(),
            pltpu.VMEM((heads, width, rows), narrow_type),
            pltpu.VMEM((16, features), float_type),
            pltpu.VMEM((8, hidden_total), float_type),
            wide_rows(),
            wide_rows(),
            narrow_rows(),
            wide_rows(),
            narrow_rows(),
            wide_rows(),
            pltpu.VMEM((5, rows, 128), narrow_type),
            pltpu.VMEM((2, rows, 128), float_type),
            pltpu.VMEM((rows, 128), float_type),
            pltpu.SemaphoreType.DMA((copies,)),
            pltpu.SemaphoreType.DMA((copies,)),
            pltpu.SemaphoreType.DMA((13,)),
            pltpu.SemaphoreType.DMA((heads,)),
            pltpu.SemaphoreType.DMA((heads,)),
            pltpu.SemaphoreType.DMA((heads,)),
            pltpu.SemaphoreType.DMA((heads,)),
            pltpu.SemaphoreType.DMA((2,)),
        ],
        compiler_params=pltpu.CompilerParams(
            collective_id=collective, has_side_effects=True, vmem_limit_bytes=54 << 20
        ),
    )(lengths, choice, att, tokens, cotangent, fa, ve, f2, *lines)


class Reduce:
    COPIES = 16

    def __init__(self, depth, base, terms, first, second, third, fourth, send, receive):
        self.depth, self.base, self.terms = depth, base, terms
        self.buffers = first, second, third, fourth
        self.send, self.receive = send, receive
        self.seq, self.fsdp = place_here()
        self.core, self.x, self.y = lax.rem(self.seq, 2), lax.rem(lax.div(self.seq, 2), 2), lax.div(self.seq, 4)
        half = terms.shape[1] // 2
        self.halves = (slice(0, half), slice(half, 2 * half))

    def copy(self, step, source, target, seq, fsdp):
        at = self.base + step
        return remote(source, target, self.send.at[at], self.receive.at[at], seq, fsdp)

    def to_core(self):
        first = self.buffers[0]
        lines = [self.terms.at[pl.ds((2 * t + 1 - self.core) * self.depth, self.depth)] for t in range(4)]
        return [self.copy(t, lines[t], first.at[t], self.seq ^ CORES, self.fsdp) for t in range(4)]

    def to_sides(self):
        first, second = self.buffers[:2]
        x, y = self.x, self.y
        copies = []
        for j in range(2):
            copies.append(
                self.copy(
                    4 + j,
                    first.at[2 * j + 1 - x, :, self.halves[0]],
                    second.at[0, j],
                    self.seq ^ SIDE_X,
                    self.fsdp,
                )
            )
            copies.append(
                self.copy(
                    6 + j,
                    first.at[2 * (1 - y) + j, :, self.halves[1]],
                    second.at[1, j],
                    self.seq ^ SIDE_Y,
                    self.fsdp,
                )
            )
        return copies

    def to_corner(self):
        second, third = self.buffers[1:3]
        return [
            self.copy(8, second.at[0, 1 - self.y], third.at[0], self.seq ^ SIDE_Y, self.fsdp),
            self.copy(9, second.at[1, 1 - self.x], third.at[1], self.seq ^ SIDE_X, self.fsdp),
        ]

    def to_line(self):
        third, fourth = self.buffers[2:]
        copies = []
        for step in range(1, self.depth):
            to = lax.rem(self.fsdp + step, self.depth)
            for j in range(2):
                copies.append(
                    self.copy(8 + 2 * step + j, third.at[j, to], fourth.at[j, step], self.seq, to)
                )
        return copies

    def add(self, target, other):
        @pl.loop(0, self.depth)
        def _(i):
            target[i] = (target[i].astype(float_type) + other[i].astype(float_type)).astype(narrow_type)

    def begin(self):
        for copy in self.to_core():
            copy.start()

    def sides(self):
        first = self.buffers[0]
        for t, copy in enumerate(self.to_core()):
            copy.wait_recv()
            self.add(first.at[t], self.terms.at[pl.ds((2 * t + self.core) * self.depth, self.depth)])
        for copy in self.to_sides():
            copy.start()

    def corner(self):
        first, second = self.buffers[:2]
        copies = self.to_sides()
        for j in range(2):
            copies[2 * j].wait_recv()
            self.add(second.at[0, j], first.at[2 * j + self.x, :, self.halves[0]])
            copies[2 * j + 1].wait_recv()
            self.add(second.at[1, j], first.at[2 * self.y + j, :, self.halves[1]])
        for copy in self.to_corner():
            copy.start()

    def line(self):
        second, third = self.buffers[1:3]
        copies = self.to_corner()
        copies[0].wait_recv()
        self.add(third.at[0], second.at[0, self.y])
        copies[1].wait_recv()
        self.add(third.at[1], second.at[1, self.x])
        for copy in self.to_line():
            copy.start()

    def end(self, out):
        third, fourth = self.buffers[2:]
        for copy in self.to_line():
            copy.wait_recv()
        for j in range(2):
            total = third[j, self.fsdp].astype(float_type)
            for step in range(1, self.depth):
                total = total + fourth[j, step].astype(float_type)
            out[self.halves[j]] = total

    def drain(self):
        for copy in self.to_core() + self.to_sides() + self.to_corner() + self.to_line():
            copy.wait_send()


def last_kernel(
    depth,
    heads,
    halo,
    lens_ref,
    choice_ref,
    dq_ref,
    dkv_ref,
    tok_ref,
    gm_ref,
    fa_in,
    ve,
    rank_ref,
    early_terms,
    gradient_ref,
    early_ref,
    late_ref,
    fa,
    vectors,
    normed,
    total,
    arrived,
    arrived_rows,
    merged,
    other,
    late_terms,
    early_buffers,
    late_buffers,
    select,
    send,
    receive,
    local,
    piece_send,
    piece_receive,
    piece_local,
):
    swap = Exchange(depth, heads)
    me, seq, fsdp = swap.me, swap.seq, swap.fsdp
    core, half, head, own = swap.core, swap.half, swap.head, heads
    row_count, features = tok_ref.shape
    devices, share = fa.shape[0], fa.shape[1]
    wide = features + 256
    barrier = pltpu.get_barrier_semaphore()
    greet_neighbours(barrier, seq, fsdp, depth)
    waits = 3 + depth - 1 + swap.greet_holders(barrier)
    load = pltpu.make_async_copy(fa_in.at[:, :, pl.ds(0, 3 * wide)], fa, local.at[0])
    load.start()
    pl.semaphore_wait(barrier, waits)
    over = remote(
        dkv_ref.at[pl.ds(jnp.where(core == 0, own, 0), halo)],
        other,
        piece_send.at[3, 0], piece_receive.at[3, 0], seq ^ CORES, fsdp)
    over.start()
    early = Reduce(depth, 0, early_terms, *early_buffers, send, receive)
    late = [
        Reduce(
            depth, Reduce.COPIES * (p + 1), late_terms.at[p], *[b.at[p] for b in late_buffers], send, receive
        )
        for p in range(3)
    ]
    shared = jnp.where(core == 0, own - halo, 0)
    shift = core * halo

    def in_shared(k):
        return (k >= shared) & (k < shared + halo)

    def sent(p, k, source):
        return remote(
            source, arrived.at[p, head], piece_send.at[p, k], piece_receive.at[p, head], *swap.owner(k)
        )

    def launch(p, k, source):
        @pl.when(swap.away_block(k))
        def _():
            sent(p, k, source).start()

        @pl.when(core * own + k == me)
        def _():
            pltpu.make_async_copy(source, arrived.at[p, head], piece_local.at[p]).start()

    def arrival(p, k):
        return remote(
            dq_ref.at[0], arrived.at[p, k], piece_send.at[p, k], piece_receive.at[p, k], seq ^ CORES, fsdp
        )

    @pl.loop(0, own)
    def _(step):
        k = lax.rem(step + me, own)
        launch(0, k, dq_ref.at[k])

    over.wait_recv()

    @pl.loop(0, halo)
    def _(i):
        for part in range(2):
            merged[i, part] = (
                dkv_ref[shared + shift + i, part].astype(float_type) + other[i, part].astype(float_type)
            ).astype(narrow_type)

    for p in (1, 2):

        @pl.loop(0, own)
        def _(step, p=p):
            k = lax.rem(step + me, own)

            @pl.when(in_shared(k))
            def _():
                launch(p, k, merged.at[jnp.clip(k - shared, 0, halo - 1), p - 1])

            @pl.when(jnp.logical_not(in_shared(k)))
            def _():
                launch(p, k, dkv_ref.at[k + shift, p - 1])

    early.begin()
    rows_of_vectors(ve, vectors)
    select[...] = selected(lens_ref, choice_ref, me, *select.shape)
    early.sides()
    shifted, normal, scaling = layer_norm(tok_ref[...].astype(float_type), vectors[0:1], vectors[4:5])
    normed[...] = shifted.astype(narrow_type)
    early.corner()
    load.wait()

    def gather_part(p):
        @pl.loop(0, heads)
        def _(k):
            @pl.when(swap.away_head(k))
            def _():
                arrival(p, k).wait_recv()

        @pl.when(half == core)
        def _():
            pltpu.make_async_copy(dq_ref.at[0], arrived.at[p, head], piece_local.at[p]).wait()

    def project_back(p):
        for j in range(4):
            arrived_rows[:, j * 256 : (j + 1) * 256] = turned(as_matrix(arrived[p, 4 * j : 4 * j + 4]))
        up = as_matrix(fa[:, :, p * wide + features + 128 : (p + 1) * wide])
        grad_rank = (matmul(arrived_rows[...], up) * select[...]).astype(narrow_type)

        @pl.loop(0, 4)
        def _(j):
            at = pl.ds(pl.multiple_of(j * 256, 128), 256)
            slots = pl.ds(j * 8, 8)
            weight = as_matrix(fa[slots, :, p * wide : p * wide + features])
            down = as_matrix(fa[slots, :, p * wide + features : p * wide + features + 128])
            term = transposed_right(arrived_rows[...], weight) + transposed_right(grad_rank, down)
            if p == 0:
                total[:, at] = term
            else:
                total[:, at] += term

        shaped = (devices, share, 128)
        late_terms[p, :, 0:32] = transposed_left(normed[...], grad_rank).astype(narrow_type).reshape(shaped)
        late_terms[p, :, 32:64] = (
            matmul(as_matrix(arrived[p]), rank_ref[p]).astype(narrow_type).reshape(shaped)
        )

    gather_part(0)
    project_back(0)
    late[0].begin()
    early.line()
    late[0].sides()
    gather_part(1)
    project_back(1)
    late[1].begin()
    late[0].corner()
    late[1].sides()
    gather_part(2)
    project_back(2)
    late[2].begin()
    late[0].line()
    late[1].corner()
    late[2].sides()
    gradient_ref[...] = gm_ref[...] + norm_backward(total[...], vectors[0:1], normal, scaling)
    late[1].line()
    late[2].corner()
    early.end(early_ref)
    late[0].end(late_ref.at[0])
    late[2].line()
    late[1].end(late_ref.at[1])
    late[2].end(late_ref.at[2])
    for reduce in [early] + late:
        reduce.drain()

    @pl.loop(0, own)
    def _(k):
        @pl.when(swap.away_block(k))
        def _():
            for p in range(3):
                sent(p, k, dq_ref.at[k]).wait_send()

    over.wait_send()


def last_part(lengths, choice, dq, dkv, tokens, grad_middle, fa, ve, rank, terms, depth, collective):
    heads = dq.shape[0]
    halo = dkv.shape[0] - heads
    rows, features = tokens.shape
    wide = features + 256
    devices, share = fa.shape[0], fa.shape[1]

    def buffers(count, size):
        return [
            pltpu.VMEM(count + (4, depth, size, 128), narrow_type),
            pltpu.VMEM(count + (2, 2, depth, size // 2, 128), narrow_type),
            pltpu.VMEM(count + (2, depth, size // 2, 128), narrow_type),
            pltpu.VMEM(count + (2, depth, size // 2, 128), narrow_type),
        ]

    return pl.pallas_call(
        functools.partial(last_kernel, depth, heads, halo),
        out_shape=(
            jax.ShapeDtypeStruct((rows, features), float_type),
            jax.ShapeDtypeStruct((terms.shape[1], 128), float_type),
            jax.ShapeDtypeStruct((3, 2 * share, 128), float_type),
        ),
        in_specs=[IN_SMEM] * 2 + [IN_VMEM] * 4 + [ANYWHERE] + [IN_VMEM] * 3,
        out_specs=(IN_VMEM, IN_VMEM, IN_VMEM),
        scratch_shapes=[
            pltpu.VMEM((devices, share, 3 * wide), narrow_type),
            pltpu.VMEM((16, features), float_type),
            pltpu.VMEM((rows, features), narrow_type),
            pltpu.VMEM((rows, features), float_type),
            pltpu.VMEM((3, heads, features // heads, rows), narrow_type),
            pltpu.VMEM((rows, features), narrow_type),
            pltpu.VMEM((halo,) + dkv.shape[1:], narrow_type),
            pltpu.VMEM((halo,) + dkv.shape[1:], narrow_type),
            pltpu.VMEM((3, devices, 2 * share, 128), narrow_type),
            buffers((), terms.shape[1]),
            buffers((3,), 2 * share),
            pltpu.VMEM((rows, 128), float_type),
            pltpu.SemaphoreType.DMA((4 * Reduce.COPIES,)),
            pltpu.SemaphoreType.DMA((4 * Reduce.COPIES,)),
            pltpu.SemaphoreType.DMA((1,)),
            pltpu.SemaphoreType.DMA((4, heads)),
            pltpu.SemaphoreType.DMA((4, heads)),
            pltpu.SemaphoreType.DMA((3,)),
        ],
        compiler_params=pltpu.CompilerParams(
            collective_id=collective, has_side_effects=True, vmem_limit_bytes=44 << 20
        ),
    )(lengths, choice, dq, dkv, tokens, grad_middle, fa, ve, rank, terms)


def spread_kernel(result_in, gradient_in, early, late, result, gradient, down, up, exp_down, exp_up, con_down, con_up):
    share = down.shape[1]
    result[...] = result_in[...]
    gradient[...] = gradient_in[...]
    for p in range(4):
        first = late[p, 0:share] if p < 3 else early[0:share]
        second = late[p, share : 2 * share] if p < 3 else early[share : 2 * share]
        down[p] = first
        up[p] = second
    exp_down[...] = early[64:96]
    exp_up[...] = early[96:224]
    con_down[...] = early[224:352].T
    con_up[...] = early[352:384]


def spread(result, gradient, early, late):
    share = late.shape[1] // 2
    shapes = ((4, share, 128), (4, share, 128), (share, 128), (128, 128), (128, 128), (share, 128))
    return pl.pallas_call(
        spread_kernel,
        out_shape=tuple(jax.ShapeDtypeStruct(a.shape, a.dtype) for a in (result, gradient))
        + tuple(jax.ShapeDtypeStruct(shape, float_type) for shape in shapes),
        in_specs=[IN_VMEM] * 4,
        out_specs=(IN_VMEM,) * 8,
        compiler_params=pltpu.CompilerParams(vmem_limit_bytes=24 << 20),
    )(result, gradient, early, late)


BIG = 32768.0


def image_range(lens_ref, first, last):
    low = high = start = jnp.int32(0)
    for image in range(lens_ref.shape[0]):
        end = start + lens_ref[image]
        low = jnp.where((start <= first) & (first < end), start, low)
        high = jnp.where((start <= last) & (last < end), end - 1, high)
        start = end
    return low, high


def image_edges(lens_ref, marks, rows):
    row = lax.broadcasted_iota(jnp.int32, (marks, rows), 0)
    starts = jnp.full((marks, rows), 1 << 30, jnp.int32)
    ends = jnp.zeros((marks, rows), jnp.int32)
    start = jnp.int32(0)
    for image in range(lens_ref.shape[0]):
        end = start + lens_ref[image]
        starts, ends = jnp.where(row == image, start, starts), jnp.where(row == image, end, ends)
        start = end
    return starts, ends


class Blocks:
    def __init__(self, lens_ref, own, halo, rows, marks):
        core = lax.rem(lax.axis_index("seq"), 2)
        self.lens_ref, self.own, self.rows, self.slots = lens_ref, own, rows, own + halo
        self.base = core * (own - halo)
        self.shift = core * halo
        self.starts, self.ends = image_edges(lens_ref, marks, rows)
        self.lane = lax.broadcasted_iota(jnp.int32, (marks, rows), 1)

    def marks(self, slot):
        place = self.lane + (self.base + slot) * self.rows
        return jnp.where((place >= self.starts) & (place < self.ends), 1.0, 0.0).astype(float_type)

    def reach(self, slot):
        first = (self.base + slot) * self.rows
        low, high = image_range(self.lens_ref, first, first + self.rows - 1)
        return lax.div(low, self.rows) - self.base, lax.div(high, self.rows) - self.base


def forward_kernel(
    own, halo, step, lens_ref, x_ref, att_ref, lse_ref, out_ref, keys, queries, values, score, weight, item_row, item_low
):
    slots, _, width, rows = x_ref.shape
    blocks = Blocks(lens_ref, own, halo, rows, keys.shape[1] - width)
    scale = width**-0.5

    @pl.loop(0, slots)
    def _(slot):
        block = jnp.concatenate([x_ref[slot, 1].astype(float_type), (blocks.marks(slot) - 1.0) * BIG], axis=0)
        keys[pl.ds(pl.multiple_of(slot * rows, rows), rows)] = block.T.astype(narrow_type)
        values[slot, 0:width] = x_ref[slot, 2]
        values[slot, width:] = jnp.ones((16, rows), narrow_type)

    def prepare(i, total):
        slot = i + blocks.shift
        queries[i] = jnp.concatenate([x_ref[slot, 0].astype(float_type) * scale, blocks.marks(slot)], axis=0).astype(narrow_type)
        low, high = blocks.reach(slot)
        count = lax.div(high - low + step, step)
        low = jnp.minimum(low, slots - step * count)

        @pl.loop(0, count)
        def _(j):
            item_row[total + j] = i
            item_low[total + j] = low + j * step

        return total + count

    total = lax.fori_loop(0, own, prepare, jnp.int32(0))
    item_row[total] = item_row[total - 1]
    item_low[total] = item_low[total - 1]

    def scored(t, side):
        at = pl.multiple_of(item_low[t] * rows, rows)
        score[side] = matmul(keys[pl.ds(at, step * rows)], queries[item_row[t]])

    def mixed(t):
        low = item_low[t]
        result = matmul(values[low], weight[0:rows])
        for j in range(1, step):
            result += matmul(values[low + j], weight[j * rows : (j + 1) * rows])
        return result

    def soften(fresh, side, highest):
        highest = jnp.where(fresh, -1e30, highest)
        s = score[side]
        higher = jnp.maximum(highest, jnp.max(s, axis=0, keepdims=True))
        fade = jnp.where(fresh, 0.0, jnp.exp(highest - higher))
        return higher, fade, jnp.exp(s - higher).astype(narrow_type)

    def finish(t, out, fade, highest):
        i = item_row[t]
        out = out * fade + mixed(t)
        summed = out[width : width + 1]
        whole = out[0:width] / summed
        att_ref[i] = whole.astype(narrow_type)
        out_ref[i] = whole
        lse_ref[i] = jnp.broadcast_to(highest + jnp.log(summed), (8, rows))
        return out

    def turn(t, side, carry):
        highest, out, fade = carry
        out = finish(t - 1, out, fade, highest)
        scored(t + 1, 1 - side)
        highest, fade, p = soften(item_row[t] != item_row[t - 1], side, highest)
        weight[...] = p
        return highest, out, fade

    scored(0, 0)
    scored(1, 1)
    highest, fade, p = soften(True, 0, jnp.zeros((1, rows), float_type))
    weight[...] = p
    carry = (highest, jnp.zeros((width + 16, rows), float_type), fade)
    pairs = lax.div(total - 1, 2)
    carry = lax.fori_loop(0, pairs, lambda j, c: turn(2 * j + 2, 0, turn(2 * j + 1, 1, c)), carry)
    carry = lax.fori_loop(2 * pairs + 1, total, lambda t, c: turn(t, 1, c), carry)
    highest, out, fade = carry
    finish(total - 1, out, fade, highest)


def attention_forward(lengths, x, own, halo, step=2):
    slots, _, width, rows = x.shape
    marks = -(-lengths.shape[0] // 16) * 16
    most = own * (slots // step + 2) + 8
    return pl.pallas_call(
        functools.partial(forward_kernel, own, halo, step),
        out_shape=(
            jax.ShapeDtypeStruct((own, width, rows), narrow_type),
            jax.ShapeDtypeStruct((own, 8, rows), float_type),
            jax.ShapeDtypeStruct((own, width, rows), float_type),
        ),
        in_specs=[IN_SMEM, IN_VMEM],
        out_specs=(IN_VMEM, IN_VMEM, IN_VMEM),
        scratch_shapes=[
            pltpu.VMEM((slots * rows, width + marks), narrow_type),
            pltpu.VMEM((own, width + marks, rows), narrow_type),
            pltpu.VMEM((slots, width + 16, rows), narrow_type),
            pltpu.VMEM((2, step * rows, rows), float_type),
            pltpu.VMEM((step * rows, rows), narrow_type),
            pltpu.SMEM((most,), jnp.int32),
            pltpu.SMEM((most,), jnp.int32),
        ],
        compiler_params=pltpu.CompilerParams(vmem_limit_bytes=32 << 20),
    )(lengths, x)


def backward_kernel(
    own, halo, step, lens_ref, x_ref, g_ref, lse_ref, out_ref, dq_ref, dkv_ref,
    keys, values, queries, offset, dq, score, grad_prob, weight, grad_score, item_slot, item_low,
):
    slots, _, width, rows = x_ref.shape
    blocks = Blocks(lens_ref, own, halo, rows, keys.shape[2] - width)
    scale = width**-0.5

    def prepare(slot, total):
        block = jnp.concatenate([x_ref[slot, 1].astype(float_type), (blocks.marks(slot) - 1.0) * BIG], axis=0)
        keys[slot] = block.T.astype(narrow_type)
        values[slot] = x_ref[slot, 2].astype(float_type).T.astype(narrow_type)
        dkv_ref[slot] = jnp.zeros((2, width, rows), narrow_type)
        low, high = blocks.reach(slot)
        low = jnp.maximum(low - blocks.shift, 0)
        high = jnp.minimum(high - blocks.shift, own - 1)
        count = jnp.maximum(lax.div(high - low + step, step), 0)
        low = jnp.minimum(low, own - step * count)

        @pl.loop(0, count)
        def _(j):
            item_slot[total + j] = slot
            item_low[total + j] = low + j * step

        return total + count

    total = lax.fori_loop(0, slots, prepare, jnp.int32(0))
    item_slot[total] = item_slot[total - 1]
    item_low[total] = item_low[total - 1]

    @pl.loop(0, own)
    def _(i):
        slot = i + blocks.shift
        q = x_ref[slot, 0].astype(float_type) * scale
        queries[i] = jnp.concatenate([q, blocks.marks(slot)], axis=0).astype(narrow_type)
        g = g_ref[i].astype(float_type)
        offset[i] = jnp.broadcast_to(jnp.sum(g * out_ref[i], axis=0, keepdims=True), (8, rows))
        dq[i] = jnp.zeros((width, rows), float_type)

    def scored(t, side):
        slot, low = item_slot[t], item_low[t]
        for j in range(step):
            score[side, j] = matmul(keys[slot], queries[low + j])
            grad_prob[side, j] = matmul(values[slot], g_ref[low + j])

    def soften(t, side):
        low = item_low[t]
        done = []
        for j in range(step):
            p = jnp.exp(score[side, j] - lse_ref[low + j, 0:1])
            d = p * (grad_prob[side, j] - offset[low + j, 0:1])
            done.append((p.astype(narrow_type), d.astype(narrow_type)))
        return done

    def keep(done):
        for j in range(step):
            weight[j] = done[j][0]
            grad_score[j] = done[j][1]

    def mixed(t, fresh, dk, dv):
        slot, low = item_slot[t], item_low[t]
        dk = jnp.where(fresh, 0.0, dk)
        dv = jnp.where(fresh, 0.0, dv)
        key = x_ref[slot, 1]
        for j in range(step):
            dk += transposed_right(queries[low + j, 0:width], grad_score[j])
            dv += transposed_right(g_ref[low + j], weight[j])
        for j in range(step):
            dq[low + j] += matmul(key, grad_score[j])
        dkv_ref[slot, 0] = dk.astype(narrow_type)
        dkv_ref[slot, 1] = dv.astype(narrow_type)
        return dk, dv

    def turn(t, side, carry):
        fresh = (t == 1) | (item_slot[t - 1] != item_slot[jnp.maximum(t - 2, 0)])
        scored(t + 1, 1 - side)
        done = soften(t, side)
        carry = mixed(t - 1, fresh, *carry)
        keep(done)
        return carry

    scored(0, 0)
    scored(1, 1)
    keep(soften(0, 0))
    zero = jnp.zeros((width, rows), float_type)
    pairs = lax.div(total - 1, 2)
    carry = lax.fori_loop(0, pairs, lambda j, c: turn(2 * j + 2, 0, turn(2 * j + 1, 1, c)), (zero, zero))
    carry = lax.fori_loop(2 * pairs + 1, total, lambda t, c: turn(t, 1, c), carry)
    mixed(total - 1, item_slot[total - 1] != item_slot[jnp.maximum(total - 2, 0)], *carry)

    @pl.loop(0, own)
    def _(i):
        dq_ref[i] = (dq[i] * scale).astype(narrow_type)


def attention_backward(lengths, x, g, lse, out, own, halo, step=1):
    slots, _, width, rows = x.shape
    marks = -(-lengths.shape[0] // 16) * 16
    most = slots * (own // step + 2) + 8
    return pl.pallas_call(
        functools.partial(backward_kernel, own, halo, step),
        out_shape=(
            jax.ShapeDtypeStruct((own, width, rows), narrow_type),
            jax.ShapeDtypeStruct((slots, 2, width, rows), narrow_type),
        ),
        in_specs=[IN_SMEM] + [IN_VMEM] * 4,
        out_specs=(IN_VMEM, IN_VMEM),
        scratch_shapes=[
            pltpu.VMEM((slots, rows, width + marks), narrow_type),
            pltpu.VMEM((slots, rows, width), narrow_type),
            pltpu.VMEM((own, width + marks, rows), narrow_type),
            pltpu.VMEM((own, 8, rows), float_type),
            pltpu.VMEM((own, width, rows), float_type),
            pltpu.VMEM((2, step, rows, rows), float_type),
            pltpu.VMEM((2, step, rows, rows), float_type),
            pltpu.VMEM((step, rows, rows), narrow_type),
            pltpu.VMEM((step, rows, rows), narrow_type),
            pltpu.SMEM((most,), jnp.int32),
            pltpu.SMEM((most,), jnp.int32),
        ],
        compiler_params=pltpu.CompilerParams(vmem_limit_bytes=40 << 20),
    )(lengths, x, g, lse, out)


def layer_on_slice(
    tokens,
    lengths,
    adapter_choice,
    gain_rows,
    bias_rows,
    query_key_value,
    output_weight,
    expand_weight,
    expand_bias,
    contract_weight,
    adapter_in_attention,
    adapter_out_attention,
    adapter_in_expand,
    adapter_out_expand,
    adapter_in_contract,
    adapter_out_contract,
    cotangent,
):
    row_count = tokens.shape[0]
    depth = lax.axis_size("fsdp")
    devices = lax.axis_size(("seq", "fsdp"))
    own = devices // 2
    halo = -(-(LONGEST - 1) // row_count)

    arrays = (
        gain_rows,
        bias_rows,
        expand_bias[None],
        query_key_value,
        output_weight,
        adapter_in_attention,
        adapter_out_attention.transpose(0, 2, 1),
        adapter_in_expand,
        adapter_out_contract.T,
        contract_weight,
        adapter_in_contract,
        adapter_out_expand,
        expand_weight,
    )
    fa, ve, f2, line_a, line_b, on_heads, rank = attention_in(
        lengths, adapter_choice, tokens, arrays, halo, depth, HEADS, devices, 1
    )

    def swapped(line, bit):
        route = [
            (seq * depth + fsdp, (seq ^ bit) * depth + fsdp)
            for seq in range(devices // depth)
            for fsdp in range(depth)
        ]
        return lax.ppermute(line, ("seq", "fsdp"), route)

    lines = (
        line_a,
        line_b,
        swapped(line_a, SIDE_Y),
        swapped(line_b, SIDE_Y),
        swapped(line_a, SIDE_X),
        swapped(line_b, SIDE_X),
    )
    attended, log_totals, attended_wide = attention_forward(lengths, on_heads, own, halo)
    result, grad_middle, terms, grad_on_heads = middle_part(
        lengths, adapter_choice, attended, tokens, cotangent, fa, ve, f2, lines, depth, 2
    )
    grad_queries, grad_key_values = attention_backward(
        lengths, on_heads, grad_on_heads, log_totals, attended_wide, own, halo
    )
    input_gradient, early, late = last_part(
        lengths, adapter_choice, grad_queries, grad_key_values, tokens, grad_middle, fa, ve, rank, terms, depth, 3
    )
    outs = spread(result, input_gradient, early, late)
    return outs[:3] + (outs[3].transpose(0, 2, 1),) + outs[4:7] + (outs[7].T,)


def solution(mesh):
    per_device = layer_on_slice if dict(mesh.shape) == {"seq": 8, "fsdp": 4} else general_layer
    placed = (
        P(("seq", "fsdp"), None),
        P(),
        P(),
        P(None, ("seq", "fsdp")),
        P(None, ("seq", "fsdp")),
        P(("seq", "fsdp"), None),
        P(("seq", "fsdp"), None),
        P(("seq", "fsdp"), None),
        P(("seq", "fsdp")),
        P(("seq", "fsdp"), None),
        P(None, ("seq", "fsdp"), None),
        P(None, None, ("seq", "fsdp")),
        P(("seq", "fsdp"), None),
        P(None, ("seq", "fsdp")),
        P(("seq", "fsdp"), None),
        P(None, ("seq", "fsdp")),
        P(("seq", "fsdp"), None),
    )
    return jax.shard_map(
        per_device,
        mesh=mesh,
        in_specs=placed,
        out_specs=(
            P(("seq", "fsdp"), None),
            P(("seq", "fsdp"), None),
            P(None, ("seq", "fsdp"), None),
            P(None, None, ("seq", "fsdp")),
            P(("seq", "fsdp"), None),
            P(None, ("seq", "fsdp")),
            P(("seq", "fsdp"), None),
            P(None, ("seq", "fsdp")),
        ),
        check_vma=False,
    )
```

```python
import functools
import jax
import jax.numpy as jnp
from jax import lax
from jax.experimental import pallas as pl
from jax.experimental.pallas import tpu as pltpu
from jax.sharding import PartitionSpec as P

HEADS = 16
RANK = 16
HOPS = 6
EDGE = 1408
LONGEST = 1370


epsilon = 1e-06
float_type = jnp.float32
narrow_type = jnp.bfloat16


def passed_along(block, axis, distance):
    devices = range(lax.axis_size(axis))
    route = [(i - distance, i) for i in devices if i - distance in devices]
    return lax.ppermute(block, axis, route)


def layer_norm(inputs_row, gain_row, bias_row):
    center = inputs_row - jnp.mean(inputs_row, axis=-1, keepdims=True)
    scaling = lax.rsqrt(jnp.mean(center * center, axis=-1, keepdims=True) + epsilon)
    normal = center * scaling
    return (normal * gain_row + bias_row, normal, scaling)


def norm_backward(gradient, gain_row, normal, scaling):
    weighted = gradient * gain_row
    return scaling * (
        weighted
        - jnp.mean(weighted, axis=-1, keepdims=True)
        - normal * jnp.mean(weighted * normal, axis=-1, keepdims=True)
    )


def matmul(first_operand, second_operand):
    return jnp.dot(first_operand, second_operand, preferred_element_type=float_type)


def transposed_left(first_operand, second_operand):
    return lax.dot_general(
        first_operand, second_operand, (((0,), (0,)), ((), ())), preferred_element_type=float_type
    )


def transposed_right(first_operand, second_operand):
    return lax.dot_general(
        first_operand, second_operand, (((1,), (1,)), ((), ())), preferred_element_type=float_type
    )


def gelu_slope(hidden_pre):
    cumulative = 0.5 * (1.0 + lax.erf(hidden_pre * 0.7071067811865476))
    density = jnp.exp(-0.5 * hidden_pre * hidden_pre) * 0.3989422804014327
    return cumulative + hidden_pre * density


def general_layer(
    tokens,
    lengths,
    adapter_choice,
    gain_rows,
    bias_rows,
    query_key_value,
    output_weight,
    expand_weight,
    expand_bias,
    contract_weight,
    adapter_in_attention,
    adapter_out_attention,
    adapter_in_expand,
    adapter_out_expand,
    adapter_in_contract,
    adapter_out_contract,
    cotangent,
):
    gathered = (
        lax.all_gather(gain_rows, ("seq", "fsdp"), axis=1, tiled=True),
        lax.all_gather(bias_rows, ("seq", "fsdp"), axis=1, tiled=True),
        lax.all_gather(query_key_value, ("seq", "fsdp"), axis=0, tiled=True),
        lax.all_gather(output_weight, ("seq", "fsdp"), axis=0, tiled=True),
        lax.all_gather(expand_weight, ("seq", "fsdp"), axis=0, tiled=True),
        lax.all_gather(expand_bias, ("seq", "fsdp"), axis=0, tiled=True),
        lax.all_gather(contract_weight, ("seq", "fsdp"), axis=0, tiled=True),
        lax.all_gather(adapter_in_attention, ("seq", "fsdp"), axis=1, tiled=True),
        lax.all_gather(adapter_out_attention, ("seq", "fsdp"), axis=2, tiled=True),
        lax.all_gather(adapter_in_expand, ("seq", "fsdp"), axis=0, tiled=True),
        lax.all_gather(adapter_out_expand, ("seq", "fsdp"), axis=1, tiled=True),
        lax.all_gather(adapter_in_contract, ("seq", "fsdp"), axis=0, tiled=True),
        lax.all_gather(adapter_out_contract, ("seq", "fsdp"), axis=1, tiled=True),
    )
    (
        gains_full,
        biases_full,
        qkv_full,
        output_full,
        expand_full,
        expand_bias_full,
        contract_full,
        attention_down,
        attention_up,
        expand_down,
        expand_up,
        contract_down,
        contract_up,
    ) = gathered
    gains_wide = gains_full.astype(float_type)
    biases_wide = biases_full.astype(float_type)
    row_count, features = tokens.shape
    device_count = lax.axis_size(("seq", "fsdp"))
    position = lax.axis_index(("seq", "fsdp"))
    head_width = features // HEADS
    pair_width = 2 * head_width
    pair_count = HEADS // 2
    scaling_score = head_width ** (-0.5)
    rank_width = attention_down.shape[2]
    window_start = HOPS * row_count - EDGE
    window_rows = row_count + 2 * EDGE
    image_ends = jnp.cumsum(lengths)
    places = (
        position * row_count
        - HOPS * row_count
        + jnp.arange((2 * HOPS + 1) * row_count, dtype=jnp.int32)
    )
    image_of = jnp.sum((places[:, None] >= image_ends[None, :]).astype(jnp.int32), axis=1)
    image_of = jnp.where((places >= 0) & (places < device_count * row_count), image_of, -1)
    own_image = image_of[HOPS * row_count : (HOPS + 1) * row_count]
    key_image = image_of[window_start : window_start + window_rows]
    allowed = own_image[:, None] == key_image[None, :]
    matches = own_image[:, None] == jnp.arange(lengths.shape[0], dtype=jnp.int32)[None, :]
    chosen = jnp.sum(jnp.where(matches, adapter_choice[None, :], 0), axis=1)
    select = (jnp.arange(rank_width, dtype=jnp.int32)[None, :] // RANK == chosen[:, None]).astype(
        float_type
    )
    residual = tokens.astype(float_type)
    normed_first, normal_first, scaling_first = layer_norm(residual, gains_wide[0], biases_wide[0])
    normed_first = normed_first.astype(narrow_type)
    rank_qkv = (
        jnp.einsum(
            "td,pdr->tpr", normed_first, attention_down[:3], preferred_element_type=float_type
        )
        * select[:, None, :]
    ).astype(narrow_type)
    adapted_qkv = jnp.einsum(
        "tpr,prd->tpd", rank_qkv, attention_up[:3], preferred_element_type=float_type
    ).reshape(row_count, 3 * features)
    query_bias = jnp.concatenate([biases_wide[1], jnp.zeros((2 * features,), float_type)])
    projected = (matmul(normed_first, qkv_full) + adapted_qkv + query_bias).astype(narrow_type)
    queries = projected[:, :features]
    key_values = projected[:, features:]
    from_lower = []
    from_higher = []
    for distance in range(1, HOPS + 1):
        from_lower.append(passed_along(key_values, ("seq", "fsdp"), distance))
        from_higher.append(passed_along(key_values, ("seq", "fsdp"), -distance))
    beside_all = jnp.concatenate(from_lower[::-1] + [key_values] + from_higher, axis=0)
    window = beside_all[window_start : window_start + window_rows]

    def pair_slices(pair_index):
        offset = pair_index * pair_width
        query_part = lax.dynamic_slice_in_dim(queries, offset, pair_width, 1).reshape(
            row_count, 2, head_width
        )
        key_part = lax.dynamic_slice_in_dim(window, offset, pair_width, 1).reshape(
            window_rows, 2, head_width
        )
        value_part = lax.dynamic_slice_in_dim(window, features + offset, pair_width, 1).reshape(
            window_rows, 2, head_width
        )
        scores = (
            jnp.einsum("qhd,khd->hqk", query_part, key_part, preferred_element_type=float_type)
            * scaling_score
        )
        scores = jnp.where(allowed[None], scores, -1e30)
        return (query_part, key_part, value_part, scores)

    def pair_forward(pair_index):
        query_part, key_part, value_part, scores = pair_slices(pair_index)
        highest = jnp.max(scores, axis=2, keepdims=True)
        weights = jnp.exp(scores - highest)
        denominator = jnp.sum(weights, axis=2, keepdims=True)
        soft = (weights / denominator).astype(narrow_type)
        mixed_part = jnp.einsum("hqk,khd->qhd", soft, value_part, preferred_element_type=float_type)
        return (
            mixed_part.reshape(row_count, pair_width),
            (highest + jnp.log(denominator))[:, :, 0],
        )

    attended_pairs, log_totals = lax.map(pair_forward, jnp.arange(pair_count))
    attended = attended_pairs.transpose(1, 0, 2).reshape(row_count, features).astype(narrow_type)
    rank_out = (matmul(attended, attention_down[3]) * select).astype(narrow_type)
    mixed = matmul(attended, output_full) + biases_wide[2] + matmul(rank_out, attention_up[3])
    middle = residual + gains_wide[1] * mixed
    normed_second, normal_second, scaling_second = layer_norm(middle, gains_wide[2], biases_wide[3])
    normed_second = normed_second.astype(narrow_type)
    rank_expand = (matmul(normed_second, expand_down) * select).astype(narrow_type)
    hidden_pre = (
        matmul(normed_second, expand_full)
        + expand_bias_full.astype(float_type)
        + matmul(rank_expand, expand_up)
    )
    active = jax.nn.gelu(hidden_pre, approximate=False).astype(narrow_type)
    rank_contract = (matmul(active, contract_down) * select).astype(narrow_type)
    branch = matmul(active, contract_full) + biases_wide[4] + matmul(rank_contract, contract_up)
    result = (middle + gains_wide[3] * branch).astype(narrow_type)
    renewed = lax.optimization_barrier(
        (
            gain_rows,
            bias_rows,
            query_key_value,
            output_weight,
            expand_weight,
            expand_bias,
            contract_weight,
            adapter_in_attention,
            adapter_out_attention,
            adapter_in_expand,
            adapter_out_expand,
            adapter_in_contract,
            adapter_out_contract,
            cotangent,
        )
    )
    gathered = (
        lax.all_gather(renewed[0], ("seq", "fsdp"), axis=1, tiled=True),
        lax.all_gather(renewed[1], ("seq", "fsdp"), axis=1, tiled=True),
        lax.all_gather(renewed[2], ("seq", "fsdp"), axis=0, tiled=True),
        lax.all_gather(renewed[3], ("seq", "fsdp"), axis=0, tiled=True),
        lax.all_gather(renewed[4], ("seq", "fsdp"), axis=0, tiled=True),
        lax.all_gather(renewed[5], ("seq", "fsdp"), axis=0, tiled=True),
        lax.all_gather(renewed[6], ("seq", "fsdp"), axis=0, tiled=True),
        lax.all_gather(renewed[7], ("seq", "fsdp"), axis=1, tiled=True),
        lax.all_gather(renewed[8], ("seq", "fsdp"), axis=2, tiled=True),
        lax.all_gather(renewed[9], ("seq", "fsdp"), axis=0, tiled=True),
        lax.all_gather(renewed[10], ("seq", "fsdp"), axis=1, tiled=True),
        lax.all_gather(renewed[11], ("seq", "fsdp"), axis=0, tiled=True),
        lax.all_gather(renewed[12], ("seq", "fsdp"), axis=1, tiled=True),
    )
    (
        gains_full,
        biases_full,
        qkv_full,
        output_full,
        expand_full,
        expand_bias_full,
        contract_full,
        attention_down,
        attention_up,
        expand_down,
        expand_up,
        contract_down,
        contract_up,
    ) = gathered
    gains_wide = gains_full.astype(float_type)
    gradient_out = cotangent.astype(float_type)
    grad_branch = (gains_wide[3] * gradient_out).astype(narrow_type)
    grad_rank_contract = (transposed_right(grad_branch, contract_up) * select).astype(narrow_type)
    grad_contract_down = transposed_left(active, grad_rank_contract)
    grad_contract_up = transposed_left(rank_contract, grad_branch)
    grad_active = transposed_right(grad_branch, contract_full) + transposed_right(
        grad_rank_contract, contract_down
    )
    grad_hidden = (grad_active * gelu_slope(hidden_pre)).astype(narrow_type)
    grad_rank_expand = (transposed_right(grad_hidden, expand_up) * select).astype(narrow_type)
    grad_expand_down = transposed_left(normed_second, grad_rank_expand)
    grad_expand_up = transposed_left(rank_expand, grad_hidden)
    grad_normed_second = transposed_right(grad_hidden, expand_full) + transposed_right(
        grad_rank_expand, expand_down
    )
    grad_middle = gradient_out + norm_backward(
        grad_normed_second, gains_wide[2], normal_second, scaling_second
    )
    grad_mixed = (gains_wide[1] * grad_middle).astype(narrow_type)
    grad_rank_out = (transposed_right(grad_mixed, attention_up[3]) * select).astype(narrow_type)
    grad_out_down = transposed_left(attended, grad_rank_out)
    grad_out_up = transposed_left(rank_out, grad_mixed)
    grad_attended = (
        transposed_right(grad_mixed, output_full)
        + transposed_right(grad_rank_out, attention_down[3])
    ).astype(narrow_type)

    def pair_backward(pair_index):
        query_part, key_part, value_part, scores = pair_slices(pair_index)
        grad_part = lax.dynamic_slice_in_dim(
            grad_attended, pair_index * pair_width, pair_width, 1
        ).reshape(row_count, 2, head_width)
        log_pair = log_totals[pair_index]
        probable = jnp.exp(scores - log_pair[:, :, None])
        grad_probable = jnp.einsum(
            "qhd,khd->hqk", grad_part, value_part, preferred_element_type=float_type
        )
        grad_scores = probable * (
            grad_probable - jnp.sum(grad_probable * probable, axis=2, keepdims=True)
        )
        grad_scores = grad_scores.astype(narrow_type)
        grad_query = (
            jnp.einsum("hqk,khd->qhd", grad_scores, key_part, preferred_element_type=float_type)
            * scaling_score
        )
        grad_key = (
            jnp.einsum("hqk,qhd->khd", grad_scores, query_part, preferred_element_type=float_type)
            * scaling_score
        )
        grad_value = jnp.einsum(
            "hqk,qhd->khd",
            probable.astype(narrow_type),
            grad_part,
            preferred_element_type=float_type,
        )
        return (
            grad_query.reshape(row_count, pair_width),
            grad_key.reshape(window_rows, pair_width),
            grad_value.reshape(window_rows, pair_width),
        )

    grad_query_pairs, grad_key_pairs, grad_value_pairs = lax.map(
        pair_backward, jnp.arange(pair_count)
    )
    grad_queries = grad_query_pairs.transpose(1, 0, 2).reshape(row_count, features)
    grad_keys = grad_key_pairs.transpose(1, 0, 2).reshape(window_rows, features)
    grad_values = grad_value_pairs.transpose(1, 0, 2).reshape(window_rows, features)
    grad_window = jnp.concatenate([grad_keys, grad_values], axis=1)
    padded_grads = jnp.pad(grad_window, ((window_start, window_start), (0, 0)))
    grad_pairs = padded_grads[HOPS * row_count : (HOPS + 1) * row_count]
    for distance in range(1, HOPS + 1):
        lower_piece = padded_grads[
            (HOPS - distance) * row_count : (HOPS - distance + 1) * row_count
        ]
        higher_piece = padded_grads[
            (HOPS + distance) * row_count : (HOPS + distance + 1) * row_count
        ]
        grad_pairs = grad_pairs + passed_along(
            lower_piece.astype(jnp.bfloat16), ("seq", "fsdp"), -distance
        ).astype(lower_piece.dtype)
        grad_pairs = grad_pairs + passed_along(
            higher_piece.astype(jnp.bfloat16), ("seq", "fsdp"), distance
        ).astype(higher_piece.dtype)
    grad_projected = jnp.concatenate([grad_queries, grad_pairs], axis=1).astype(narrow_type)
    grad_blocks = grad_projected.reshape(row_count, 3, features)
    grad_rank_qkv = (
        jnp.einsum("tpd,prd->tpr", grad_blocks, attention_up[:3], preferred_element_type=float_type)
        * select[:, None, :]
    ).astype(narrow_type)
    grad_qkv_down = jnp.einsum(
        "td,tpr->pdr", normed_first, grad_rank_qkv, preferred_element_type=float_type
    )
    grad_qkv_up = jnp.einsum(
        "tpr,tpd->prd", rank_qkv, grad_blocks, preferred_element_type=float_type
    )
    grad_normed_first = transposed_right(grad_projected, qkv_full) + jnp.einsum(
        "tpr,pdr->td", grad_rank_qkv, attention_down[:3], preferred_element_type=float_type
    )
    input_gradient = grad_middle + norm_backward(
        grad_normed_first, gains_wide[0], normal_first, scaling_first
    )
    grad_attention_down = jnp.concatenate([grad_qkv_down, grad_out_down[None]], axis=0)
    grad_attention_up = jnp.concatenate([grad_qkv_up, grad_out_up[None]], axis=0)
    summed = (
        lax.psum_scatter(grad_attention_down, ("seq", "fsdp"), scatter_dimension=1, tiled=True),
        lax.psum_scatter(grad_attention_up, ("seq", "fsdp"), scatter_dimension=2, tiled=True),
        lax.psum_scatter(grad_expand_down, ("seq", "fsdp"), scatter_dimension=0, tiled=True),
        lax.psum_scatter(grad_expand_up, ("seq", "fsdp"), scatter_dimension=1, tiled=True),
        lax.psum_scatter(grad_contract_down, ("seq", "fsdp"), scatter_dimension=0, tiled=True),
        lax.psum_scatter(grad_contract_up, ("seq", "fsdp"), scatter_dimension=1, tiled=True),
    )
    return (
        result,
        input_gradient,
        summed[0],
        summed[1],
        summed[2],
        summed[3],
        summed[4],
        summed[5],
    )


MESH_ID = pl.DeviceIdType.MESH
CORES, SIDE_X, SIDE_Y = 1, 2, 4
ANYWHERE = pl.BlockSpec(memory_space=pl.ANY)
IN_VMEM = pl.BlockSpec(memory_space=pltpu.VMEM)
IN_SMEM = pl.BlockSpec(memory_space=pltpu.SMEM)


def place_here():
    return lax.axis_index("seq"), lax.axis_index("fsdp")


def remote(source, target, send, receive, seq, fsdp):
    return pltpu.make_async_remote_copy(
        src_ref=source,
        dst_ref=target,
        send_sem=send,
        recv_sem=receive,
        device_id=(seq, fsdp),
        device_id_type=MESH_ID,
    )


def greet(barrier, seq, fsdp):
    pl.semaphore_signal(barrier, 1, device_id=(seq, fsdp), device_id_type=MESH_ID)


def greet_neighbours(barrier, seq, fsdp, depth):
    for bit in (CORES, SIDE_X, SIDE_Y):
        greet(barrier, seq ^ bit, fsdp)
    for step in range(1, depth):
        greet(barrier, seq, lax.rem(fsdp + step, depth))


WHOLE, OPEN, LINE = 0, 1, 2


class Gather:
    STEPS = 10

    def __init__(self, depth, send, receive):
        self.depth, self.send, self.receive = depth, send, receive
        self.seq, self.fsdp = place_here()
        self.me = self.seq * depth + self.fsdp
        self.inside = (self.fsdp == 1) | (self.fsdp == 2)

    def copy(self, index, step, source, target, seq, fsdp):
        at = index * self.STEPS + step
        return remote(source, target, self.send.at[at], self.receive.at[at], seq, fsdp)

    def part(self, chunk, at_seq, first, count):
        full, rows, columns, _, kind, _ = chunk
        base = 0 if kind == LINE else at_seq * self.depth
        return full.at[pl.ds(base + first, count), rows, columns]

    def group(self, chunk, at_seq):
        return self.part(chunk, at_seq, 0, self.depth)

    def sides(self, chunk):
        return (SIDE_X, SIDE_Y) if chunk[3] else (SIDE_Y, SIDE_X)

    def line(self, index, chunk, step):
        pair = lax.div(self.fsdp, 2)
        if step == 0:
            piece, to = self.part(chunk, self.seq, self.fsdp, 1), self.fsdp ^ 1
            if chunk[5] is not None:
                source = chunk[5].at[pl.ds(0, 1), chunk[1], chunk[2]]
                return self.copy(index, step, source, piece, self.seq, to)
        elif step == 1:
            piece, to = self.part(chunk, self.seq, 2 * pair, 2), 3 - self.fsdp
        else:
            piece, to = self.part(chunk, self.seq, 2 - 2 * pair, 2), self.fsdp ^ 1
        return self.copy(index, step, piece, piece, self.seq, to)

    def over(self, index, chunk, step):
        a, b = self.sides(chunk)
        piece = self.group(chunk, self.seq ^ a if step == 2 else self.seq)
        return self.copy(index, 3 + step, piece, piece, self.seq ^ (b if step else a), self.fsdp)

    def across(self, index, chunk, step):
        a, b = self.sides(chunk)
        piece = self.group(chunk, self.seq ^ (0, a, b, a ^ b)[step])
        return self.copy(index, 6 + step, piece, piece, self.seq ^ CORES, self.fsdp)

    def own(self, index, chunk):
        self.line(index, chunk, 0).start()

    def inner(self, index, chunk):
        @pl.when(self.inside)
        def _():
            self.line(index, chunk, 0).wait_recv()
            self.line(index, chunk, 1).start()

    def outer(self, index, chunk):
        @pl.when(self.inside)
        def _():
            self.line(index, chunk, 1).wait_recv()
            self.line(index, chunk, 2).start()

    def arrive(self, index, chunk):
        @pl.when(jnp.logical_not(self.inside))
        def _():
            self.line(index, chunk, 0).wait_recv()
            self.line(index, chunk, 2).wait_recv()

    def first(self, index, chunk):
        self.arrive(index, chunk)
        self.over(index, chunk, 0).start()
        self.over(index, chunk, 1).start()
        self.across(index, chunk, 0).start()

    def second(self, index, chunk):
        self.over(index, chunk, 0).wait_recv()
        if chunk[4] == WHOLE:
            self.over(index, chunk, 2).start()
        self.across(index, chunk, 1).start()

    def third(self, index, chunk):
        self.over(index, chunk, 1).wait_recv()
        self.across(index, chunk, 2).start()
        if chunk[4] == WHOLE:
            self.over(index, chunk, 2).wait_recv()
            self.across(index, chunk, 3).start()

    def finish(self, index, chunk):
        for step in range(4 if chunk[4] == WHOLE else 3):
            self.across(index, chunk, step).wait_recv()

    def drain(self, index, chunk):
        self.line(index, chunk, 0).wait_send()

        @pl.when(self.inside)
        def _():
            self.line(index, chunk, 1).wait_send()
            self.line(index, chunk, 2).wait_send()

        if chunk[4] == LINE:
            return
        for step in range(3 if chunk[4] == WHOLE else 2):
            self.over(index, chunk, step).wait_send()
        for step in range(4 if chunk[4] == WHOLE else 3):
            self.across(index, chunk, step).wait_send()


class Exchange:
    def __init__(self, depth, heads):
        self.depth, self.heads = depth, heads
        self.seq, self.fsdp = place_here()
        self.me = self.seq * depth + self.fsdp
        self.core, self.half = lax.rem(self.seq, 2), lax.div(self.seq, 4)
        self.head = lax.div(self.seq, 2) * depth + self.fsdp
        self.same = (self.half == self.core).astype(jnp.int32)

    def holder(self, k):
        return lax.div(k, self.depth) * 2 + self.half, lax.rem(k, self.depth)

    def owner(self, k):
        block = self.core * self.heads + k
        return lax.div(block, self.depth), lax.rem(block, self.depth)

    def away_head(self, k):
        return (k != self.head) | (self.half != self.core)

    def away_block(self, k):
        return self.core * self.heads + k != self.me

    def greet_holders(self, barrier):
        @pl.loop(0, self.heads)
        def _(k):
            @pl.when(self.away_head(k))
            def _():
                greet(barrier, *self.holder(k))

        return self.heads - self.same

    def greet_owners(self, barrier):
        @pl.loop(0, self.heads)
        def _(k):
            @pl.when(self.away_block(k))
            def _():
                greet(barrier, *self.owner(k))

        return self.heads - self.same


def as_matrix(block):
    return block.reshape(-1, block.shape[-1])


def turned(block, tile=256):
    return block.astype(float_type).T.astype(narrow_type)


def rows_of_vectors(ve, target):
    flat = as_matrix(ve[:, 0:32, :]).astype(float_type)
    target[...] = flat.T[0:16]


def by_feature_wide(block):
    return jnp.concatenate([block, jnp.zeros((112, block.shape[1]), block.dtype)], axis=0)


def selected(lens_ref, choice_ref, block, rows, lanes):
    place = lax.broadcasted_iota(jnp.int32, (rows, lanes), 0) + block * rows
    lane = lax.broadcasted_iota(jnp.int32, (rows, lanes), 1)
    chosen = jnp.zeros((rows, lanes), jnp.int32)
    start = jnp.int32(0)
    for image in range(lens_ref.shape[0]):
        end = start + lens_ref[image]
        chosen = jnp.where((place >= start) & (place < end), choice_ref[image] * RANK, chosen)
        start = end
    return jnp.where((lane >= chosen) & (lane < chosen + RANK), 1.0, 0.0).astype(float_type)


def stood_up(block):
    n, m = block.shape
    block = block.astype(float_type)
    if m < 128:
        block = jnp.concatenate([block, jnp.zeros((n, 128 - m), float_type)], axis=1)
    if n < 128:
        block = jnp.concatenate([block, jnp.zeros((128 - n, 128), float_type)], axis=0)
    return block.T[0:m].astype(narrow_type)


def attention_in_kernel(
    depth,
    halo,
    heads,
    chunks,
    lens_ref,
    choice_ref,
    tok_in,
    gains_in,
    biases_in,
    bias_in,
    wqkv,
    wout,
    a_att,
    b_att,
    a_exp,
    b_con,
    w2,
    a_con,
    b_exp_in,
    w1,
    fa_out,
    ve_out,
    f2,
    line_a,
    line_b,
    y_ref,
    rank_ref,
    fa,
    ve,
    proj,
    normed,
    vectors,
    tok,
    gains,
    biases,
    bias,
    b_exp,
    shard_f2,
    shard_a,
    shard_b,
    select,
    send,
    receive,
    local,
    piece_send,
    piece_receive,
    piece_local,
):
    gather, swap = Gather(depth, send, receive), Exchange(depth, heads)
    me, seq, fsdp = swap.me, swap.seq, swap.fsdp
    core, half, head, own = swap.core, swap.half, swap.head, heads
    features = normed.shape[1]
    wide = features + 256
    barrier = pltpu.get_barrier_semaphore()
    greet_neighbours(barrier, seq, fsdp, depth)
    waits = 3 + depth - 1 + swap.greet_owners(barrier)
    half_columns = line_a.shape[2]
    small = [
        (gains_in, gains.at[0:4]),
        (biases_in, biases.at[0:5]),
        (bias_in, bias),
        (b_exp_in, b_exp),
        (tok_in, tok),
    ]
    places = []
    for p in range(4):
        source = wqkv.at[:, pl.ds(p * features, features)] if p < 3 else wout
        places.append((source, fa.at[me, :, pl.ds(p * wide, features)]))
        places.append((a_att.at[p], fa.at[me, :, pl.ds(p * wide + features, 128)]))
        places.append((b_att.at[p], fa.at[me, :, pl.ds(p * wide + features + 128, 128)]))
    places.append((a_exp, fa.at[me, :, pl.ds(4 * wide, 128)]))
    places.append((b_con, fa.at[me, :, pl.ds(4 * wide + 128, 128)]))
    places.append((w2, shard_f2.at[0, :, pl.ds(0, features)]))
    places.append((a_con, shard_f2.at[0, :, pl.ds(features, 128)]))
    places.append((w1.at[:, pl.ds(0, half_columns)], shard_a.at[0]))
    places.append((w1.at[:, pl.ds(half_columns, half_columns)], shard_b.at[0]))
    placed = [pltpu.make_async_copy(a, b, local.at[i]) for i, (a, b) in enumerate(small + places)]
    for copy in placed:
        copy.start()
    for copy in placed[:3]:
        copy.wait()
    by_feature = jnp.concatenate(
        [gains[0:4].astype(float_type), biases[0:5].astype(float_type), jnp.zeros((7, 32), float_type)], axis=0
    )
    ve[me, 0:32] = stood_up(by_feature_wide(by_feature))
    ve[me, 32:48] = jnp.broadcast_to(bias[...].astype(float_type), (16, 128)).astype(narrow_type)
    for copy in placed[len(small) : len(small) + 14]:
        copy.wait()
    refs = {
        "ve": (ve, WHOLE, None),
        "fa": (fa, WHOLE, None),
        "f2": (f2, OPEN, shard_f2),
        "a": (line_a, LINE, shard_a),
        "b": (line_b, LINE, shard_b),
    }
    chunks = [
        (refs[name][0], rows, columns, flip) + refs[name][1:] for name, rows, columns, flip in chunks
    ]
    first_hidden = [i for i, chunk in enumerate(chunks) if chunk[4] != WHOLE][:1]
    pl.semaphore_wait(barrier, waits)
    early = [i for i, chunk in enumerate(chunks) if chunk[0] is fa or chunk[0] is ve]
    for index in early:
        gather.own(index, chunks[index])
    for copy in placed[3 : len(small)] + placed[len(small) + 14 :]:
        copy.wait()
    shard_f2[0, :, features + 128 : wide] = stood_up(b_exp[...])
    own_shards = [
        pltpu.make_async_copy(shard.at[0], full.at[slot], local.at[i])
        for i, (shard, full, slot) in enumerate(((shard_f2, f2, me), (shard_a, line_a, fsdp), (shard_b, line_b, fsdp)))
    ]
    for copy in own_shards:
        copy.start()
    select[...] = selected(lens_ref, choice_ref, me, *select.shape)
    base = core * (own - halo)
    slot = me - half * (own - halo)

    def piece(p, k):
        return remote(
            proj.at[p, k],
            y_ref.at[slot, p],
            piece_send.at[p, k],
            piece_receive.at[p, lax.rem(me, own)],
            *swap.holder(k),
        )

    def arrival(p, k):
        return remote(
            proj.at[p, 0],
            y_ref.at[core * own + k - base, p],
            piece_send.at[p, k],
            piece_receive.at[p, k],
            seq ^ CORES,
            fsdp,
        )

    def kept(p):
        return pltpu.make_async_copy(proj.at[p, head], y_ref.at[me - base, p], piece_local.at[p])

    def norm():
        rows_of_vectors(ve, vectors)
        rows = tok[...].astype(float_type)
        normed[...] = layer_norm(rows, vectors[0:1], vectors[4:5])[0].astype(narrow_type)

    def project(p):
        down = as_matrix(fa[:, :, p * wide + features : p * wide + features + 128])
        rank = (matmul(normed[...], down) * select[...]).astype(narrow_type)
        rank_ref[p] = rank

        @pl.loop(0, features // 256)
        def _(j):
            weight = as_matrix(fa[:, :, pl.ds(pl.multiple_of(p * wide + j * 256, 128), 256)])
            up = as_matrix(fa[pl.ds(j * 8, 8), :, p * wide + features + 128 : (p + 1) * wide])
            result = matmul(normed[...], weight) + transposed_right(rank, up)
            if p == 0:
                result = result + vectors[5:6, pl.ds(pl.multiple_of(j * 256, 128), 256)]
            proj[p, pl.ds(j * 4, 4)] = result.T.astype(narrow_type).reshape(4, 64, 256)

            @pl.loop(0, 4)
            def _(i):
                k = j * 4 + i

                @pl.when(swap.away_head(k))
                def _():
                    piece(p, k).start()

        @pl.when(half == core)
        def _():
            kept(p).start()

    after = {0: norm, 2: lambda: project(0), 4: lambda: project(1), 6: lambda: project(2)}
    after_attention = [i for i, chunk in enumerate(chunks) if chunk[0] is fa][-1]
    outs = [
        pltpu.make_async_copy(fa, fa_out, local.at[3]),
        pltpu.make_async_copy(ve, ve_out, local.at[4]),
    ]

    def store():
        for copy in outs:
            copy.start()

    def exchanged():
        @pl.loop(0, own)
        def _(k):
            @pl.when(swap.away_block(k))
            def _():
                for p in range(3):
                    arrival(p, k).wait_recv()

        @pl.when(half == core)
        def _():
            for p in range(3):
                kept(p).wait()

        first = jnp.where(core == 0, own - halo, own)
        over = remote(
            y_ref.at[pl.ds(first - base, halo), 1:3],
            y_ref.at[pl.ds(first - (own - halo) * (1 - core), halo), 1:3],
            piece_send.at[3, 0],
            piece_receive.at[3, 0],
            seq ^ CORES,
            fsdp,
        )
        over.start()
        return over

    steps = (gather.own, gather.inner, gather.outer, gather.first, gather.second, gather.third, gather.finish)
    for turn in range(DELAYS[0], len(chunks) + DELAYS[-1]):
        if turn == len(chunks) - 2:
            over = exchanged()
        for delay, step in zip(DELAYS, steps):
            index = turn - delay
            if not 0 <= index < len(chunks) or (delay == DELAYS[0] and index in early):
                continue
            chunk = chunks[index]
            if delay == DELAYS[1] and index in first_hidden:
                for copy in own_shards:
                    copy.wait()
            if chunk[4] == LINE and delay == 0:
                step = gather.arrive
            if chunk[4] == LINE and delay > 0:
                continue
            step(index, chunk)
            if delay == 3:
                after.get(index, lambda: None)()
                if index == after_attention:
                    store()

    over.wait()

    @pl.loop(0, heads)
    def _(k):
        @pl.when(swap.away_head(k))
        def _():
            for p in range(3):
                piece(p, k).wait_send()

    for index, chunk in enumerate(chunks):
        gather.drain(index, chunk)
    for copy in outs:
        copy.wait()


def attention_in(lengths, choice, tokens, arrays, halo, depth, heads, devices, collective):
    rows, features = tokens.shape
    wide = features + 256
    total = 4 * wide + 256
    share, hidden_share, hidden_total = features // devices, arrays[9].shape[0], arrays[12].shape[1]
    chunks = [("ve", slice(0, 48), slice(0, 128), 0)]
    for p in range(3):
        chunks.append(("fa", slice(0, share), slice(p * wide, p * wide + wide // 2), 0))
        chunks.append(("fa", slice(0, share), slice(p * wide + wide // 2, (p + 1) * wide), 1))
    middle = 3 * wide + (total - 3 * wide) // 2
    chunks.append(("fa", slice(0, share), slice(3 * wide, middle), 0))
    chunks.append(("fa", slice(0, share), slice(middle, total), 1))
    for part in range(0, hidden_share, 64):
        chunks.append(("f2", slice(part, part + 64), slice(0, wide // 2), 0))
        chunks.append(("f2", slice(part, part + 64), slice(wide // 2, wide), 1))
    for part in range(0, hidden_total // 2, 2048):
        chunks.append(("a", slice(0, share), slice(part, part + 2048), 0))
        chunks.append(("b", slice(0, share), slice(part, part + 2048), 1))
    copies = Gather.STEPS * len(chunks)
    return pl.pallas_call(
        functools.partial(attention_in_kernel, depth, halo, heads, chunks),
        out_shape=(
            jax.ShapeDtypeStruct((devices, share, total), narrow_type),
            jax.ShapeDtypeStruct((devices, 48, 128), narrow_type),
            jax.ShapeDtypeStruct((devices, hidden_share, wide), narrow_type),
            jax.ShapeDtypeStruct((depth, share, hidden_total // 2), narrow_type),
            jax.ShapeDtypeStruct((depth, share, hidden_total // 2), narrow_type),
            jax.ShapeDtypeStruct((heads + halo, 3, features // heads, rows), narrow_type),
            jax.ShapeDtypeStruct((3, rows, 128), narrow_type),
        ),
        in_specs=[IN_SMEM, IN_SMEM] + [ANYWHERE] * (1 + len(arrays)),
        out_specs=(ANYWHERE,) * 6 + (IN_VMEM,),
        scratch_shapes=[
            pltpu.VMEM((devices, share, total), narrow_type),
            pltpu.VMEM((devices, 48, 128), narrow_type),
            pltpu.VMEM((3, heads, features // heads, rows), narrow_type),
            pltpu.VMEM((rows, features), narrow_type),
            pltpu.VMEM((16, features), float_type),
            pltpu.VMEM((rows, features), narrow_type),
            pltpu.VMEM((4, share), narrow_type),
            pltpu.VMEM((5, share), narrow_type),
            pltpu.VMEM((1, 128), narrow_type),
            pltpu.VMEM((128, 128), narrow_type),
            pltpu.VMEM((1, hidden_share, wide), narrow_type),
            pltpu.VMEM((1, share, hidden_total // 2), narrow_type),
            pltpu.VMEM((1, share, hidden_total // 2), narrow_type),
            pltpu.VMEM((rows, 128), float_type),
            pltpu.SemaphoreType.DMA((copies,)),
            pltpu.SemaphoreType.DMA((copies,)),
            pltpu.SemaphoreType.DMA((24,)),
            pltpu.SemaphoreType.DMA((4, heads)),
            pltpu.SemaphoreType.DMA((4, heads)),
            pltpu.SemaphoreType.DMA((3,)),
        ],
        compiler_params=pltpu.CompilerParams(
            collective_id=collective, has_side_effects=True, vmem_limit_bytes=60 << 20
        ),
    )(lengths, choice, tokens, *arrays)


DELAYS = (-9, -6, -3, 0, 1, 2, 3)
HIDDEN_TILE = 512


def middle_kernel(
    depth,
    heads,
    lens_ref,
    choice_ref,
    att_ref,
    tok_ref,
    cot_ref,
    fa_in,
    ve,
    f2_in,
    line_a,
    line_b,
    ya,
    yb,
    xa,
    xb,
    result_ref,
    gm_ref,
    terms,
    gy_ref,
    fa,
    f2,
    f1,
    att_t,
    att,
    gatt_t,
    vectors,
    hidden_bias,
    middle,
    normal,
    normed,
    branch,
    grad_branch,
    grad_normed,
    ranks,
    rank_sums,
    select,
    send,
    receive,
    local,
    a_send,
    a_receive,
    b_send,
    b_receive,
    own_local,
):
    swap = Exchange(depth, heads)
    me, seq, fsdp = swap.me, swap.seq, swap.fsdp
    core, half, head, own = swap.core, swap.half, swap.head, heads
    devices, share = f1.shape[0], f1.shape[1]
    row_count, features = tok_ref.shape
    wide = features + 256
    tiles = f1.shape[2] // HIDDEN_TILE
    in_tile = HIDDEN_TILE // f2.shape[1]
    barrier = pltpu.get_barrier_semaphore()
    greet_neighbours(barrier, seq, fsdp, depth)
    waits = 3 + depth - 1 + swap.greet_owners(barrier) + swap.greet_holders(barrier)
    half_columns = line_a.shape[2]
    left, right = pl.ds(0, half_columns), pl.ds(half_columns, half_columns)
    lines = [
        (line, f1.at[pl.ds((seq ^ bit) * depth, depth), :, columns])
        for line, bit, columns in (
            (line_a, 0, left),
            (line_b, 0, right),
            (ya, SIDE_Y, left),
            (yb, SIDE_Y, right),
            (xa, SIDE_X, left),
            (xb, SIDE_X, right),
        )
    ]
    groups = [pl.ds((seq ^ k) * depth, depth) for k in range(8)]
    loads = (
        [pltpu.make_async_copy(fa_in.at[:, :, pl.ds(3 * wide, wide + 256)], fa, local.at[0])]
        + [pltpu.make_async_copy(line, place, local.at[1 + i]) for i, (line, place) in enumerate(lines)]
        + [pltpu.make_async_copy(f2_in.at[groups[k]], f2.at[groups[k]], local.at[7 + k]) for k in range(6)]
    )
    for copy in loads:
        copy.start()
    pl.semaphore_wait(barrier, waits)
    quarter = half_columns // 2
    x_side = lax.rem(lax.div(seq, 2), 2)

    def columns_of(start, parity):
        return pl.ds(pl.multiple_of(start + parity * quarter, 128), quarter)

    corners, diagonal = [], []
    for turn in range(2):
        for i, (line, via, to, start, parity) in enumerate(
            ((ya, SIDE_Y, SIDE_X, 0, 1 - x_side), (xb, SIDE_X, SIDE_Y, half_columns, x_side))
        ):
            at = 2 * turn + i
            parity = 1 - parity if turn else parity
            corners.append(
                remote(
                    line.at[:, :, columns_of(0, parity)],
                    f1.at[pl.ds((seq ^ via) * depth, depth), :, columns_of(start, parity)],
                    send.at[at],
                    receive.at[at],
                    seq ^ to,
                    fsdp,
                )
            )
            here = f1.at[
                pl.ds((seq ^ SIDE_X ^ SIDE_Y) * depth, depth),
                :,
                columns_of(start, 1 - x_side if turn else x_side),
            ]
            diagonal.append(remote(here, here, send.at[4 + at], receive.at[4 + at], seq ^ CORES, fsdp))

    tops, tails = pl.ds(0, wide // 2), pl.ds(wide // 2, wide // 2)
    f2_parts = ((SIDE_Y, SIDE_X, tops), (SIDE_X, SIDE_Y, tails))
    rows_over, rows_along = pl.ds(0, 64), pl.ds(64, 64)
    for i, (via, to, columns) in enumerate(f2_parts):
        line = pl.ds((seq ^ via) * depth, depth)
        corners.append(
            remote(
                f2_in.at[line, rows_over, columns],
                f2.at[line, rows_over, columns],
                send.at[8 + i],
                receive.at[8 + i],
                seq ^ to,
                fsdp,
            )
        )
    single = [
        remote(
            f2_in.at[pl.ds((seq ^ via) * depth + fsdp, 1), rows_along, columns],
            f2.at[pl.ds((seq ^ via) * depth + fsdp, 1), rows_along, columns],
            send.at[10 + i],
            receive.at[10 + i],
            seq ^ to,
            fsdp,
        )
        for i, (via, to, columns) in enumerate(f2_parts)
    ]
    far = f2.at[pl.ds((seq ^ SIDE_X ^ SIDE_Y) * depth + fsdp, 1), rows_along]
    along = [
        remote(
            far, far, send.at[11 + step], receive.at[11 + step], seq, lax.rem(fsdp + step, depth)
        )
        for step in range(1, depth)
    ]
    across = [
        remote(line, place, send.at[15 + i], receive.at[15 + i], seq ^ CORES, fsdp)
        for i, (line, place) in enumerate(lines)
    ]
    f2_across = remote(
        f2.at[groups[6]], f2.at[groups[6]], send.at[21], receive.at[21], seq ^ CORES, fsdp
    )

    def attended_piece(k):
        return remote(att_ref.at[k], att_t.at[head], a_send.at[k], a_receive.at[head], *swap.owner(k))

    def attended_arrival(k):
        return remote(att_ref.at[0], att_t.at[k], a_send.at[k], a_receive.at[k], seq ^ CORES, fsdp)

    attended_kept = pltpu.make_async_copy(att_ref.at[me - core * own], att_t.at[head], own_local.at[0])

    @pl.when(half == core)
    def _():
        attended_kept.start()

    @pl.loop(0, own)
    def _(step):
        k = lax.rem(step + me, own)

        @pl.when(swap.away_block(k))
        def _():
            attended_piece(k).start()

    for copy in single + corners[:2] + across:
        copy.start()
    select[...] = selected(lens_ref, choice_ref, me, *select.shape)
    rows_of_vectors(ve, vectors)
    for d in range(devices):
        hidden_bias[:, d * 128 : (d + 1) * 128] = ve[d, 32:48, :].astype(float_type)[0:8]
    grad_branch[...] = (vectors[3:4] * cot_ref[...].astype(float_type)).astype(narrow_type)
    loads[0].wait()
    contract_up = as_matrix(fa[:, :, wide + 128 : wide + 256])
    ranks[1] = (matmul(grad_branch[...], contract_up) * select[...]).astype(narrow_type)
    branch[...] = jnp.zeros_like(branch)
    grad_normed[...] = jnp.zeros_like(grad_normed)
    rank_sums[...] = jnp.zeros_like(rank_sums)

    @pl.loop(0, heads)
    def _(k):
        @pl.when(swap.away_head(k))
        def _():
            attended_arrival(k).wait_recv()

    @pl.when(half == core)
    def _():
        attended_kept.wait()

    for copy in corners[2:]:
        copy.start()
    for copy in single:
        copy.wait_recv()
    for copy in along:
        copy.start()

    for i in range(2):
        corners[i].wait_recv()
        diagonal[i].start()
    for j in range(4):
        att[:, j * 256 : (j + 1) * 256] = turned(as_matrix(att_t[4 * j : 4 * j + 4]))
    out_down = as_matrix(fa[:, :, features : features + 128])
    rank_out = (matmul(att[...], out_down) * select[...]).astype(narrow_type)
    ranks[2] = rank_out

    @pl.loop(0, 4)
    def _(j):
        at = pl.ds(pl.multiple_of(j * 256, 128), 256)
        weight = as_matrix(fa[:, :, at])
        up = as_matrix(fa[pl.ds(j * 8, 8), :, features + 128 : wide])
        mixed = matmul(att[...], weight) + transposed_right(rank_out, up) + vectors[6:7, at]
        middle[:, at] = tok_ref[:, at].astype(float_type) + vectors[1:2, at] * mixed

    shifted, normal_rows, scaling = layer_norm(middle[...], vectors[2:3], vectors[7:8])
    normal[...] = normal_rows
    normed[...] = shifted.astype(narrow_type)
    expand_down = as_matrix(fa[:, :, wide : wide + 128])
    rank_expand = (matmul(normed[...], expand_down) * select[...]).astype(narrow_type)
    ranks[0] = rank_expand
    ranks[3, 0:128] = turned(rank_expand)[:, 0:128]
    ranks[3, 128:256] = turned(rank_expand)[:, 128:256]
    ranks[4, 0:128] = turned(ranks[1])[:, 0:128]
    ranks[4, 128:256] = turned(ranks[1])[:, 128:256]
    for copy in loads[1:]:
        copy.wait()
    for copy in across + diagonal[:2]:
        copy.wait_recv()

    def hidden(k):
        @pl.when(k == 2)
        def _():
            for i in (2, 3):
                corners[i].wait_recv()
                diagonal[i].start()
            for i in (2, 3):
                diagonal[i].wait_recv()

        @pl.when(k == 5)
        def _():
            for copy in corners[4:] + along:
                copy.wait_recv()
            f2_across.start()

        @pl.when(k == 7)
        def _():
            f2_across.wait_recv()

        c = seq ^ k
        at = pl.ds(pl.multiple_of(c * HIDDEN_TILE, 128), HIDDEN_TILE)
        slots = pl.ds(c * in_tile, in_tile)
        expand = as_matrix(f1[:, :, at])
        contract = as_matrix(f2[slots, :, 0:features])
        down = as_matrix(f2[slots, :, features : features + 128])
        up = as_matrix(f2[slots, :, features + 128 : wide])
        before = matmul(normed[...], expand) + transposed_right(ranks[0], up) + hidden_bias[0:1, at]
        total = 0.5 * (1.0 + lax.erf(before * 0.7071067811865476))
        density = jnp.exp(-0.5 * before * before) * 0.3989422804014327
        active = (before * total).astype(narrow_type)
        slope = total + before * density
        branch[...] += matmul(active, contract)
        rank_sums[0] += matmul(active, down)
        grad_active = transposed_right(grad_branch[...], contract) + transposed_right(ranks[1], down)
        grad_hidden = (grad_active * slope).astype(narrow_type)
        rank_sums[1] += matmul(grad_hidden, up)
        grad_normed[...] += transposed_right(grad_hidden, expand)
        turned_expand = jnp.concatenate([ranks[3, 0:128], ranks[3, 128:256]], axis=1)
        turned_contract = jnp.concatenate([ranks[4, 0:128], ranks[4, 128:256]], axis=1)
        grad_up = matmul(turned_expand, grad_hidden).astype(narrow_type)
        grad_down = matmul(turned_contract, active).astype(narrow_type)
        for i in range(in_tile):
            terms[c * in_tile + i, 96:224] = grad_up[:, i * 128 : (i + 1) * 128]
            terms[c * in_tile + i, 224:352] = grad_down[:, i * 128 : (i + 1) * 128]

    pl.loop(0, tiles)(hidden)
    rank_contract = (rank_sums[0] * select[...]).astype(narrow_type)
    grad_rank_expand = (rank_sums[1] * select[...]).astype(narrow_type)
    gradient = grad_normed[...] + transposed_right(grad_rank_expand, expand_down)
    gm_ref[...] = cot_ref[...].astype(float_type) + norm_backward(gradient, vectors[2:3], normal[...], scaling)
    grad_mixed = (vectors[1:2] * gm_ref[...]).astype(narrow_type)
    out_up = as_matrix(fa[:, :, features + 128 : wide])
    grad_rank_out = (matmul(grad_mixed, out_up) * select[...]).astype(narrow_type)

    def gradient_piece(k):
        return remote(
            gatt_t.at[k], gy_ref.at[lax.rem(me, own)], b_send.at[k], b_receive.at[lax.rem(me, own)], *swap.holder(k)
        )

    def gradient_arrival(k):
        return remote(gatt_t.at[0], gy_ref.at[k], b_send.at[k], b_receive.at[k], seq ^ CORES, fsdp)

    gradient_kept = pltpu.make_async_copy(gatt_t.at[head], gy_ref.at[lax.rem(me, own)], own_local.at[1])

    @pl.loop(0, 4)
    def _(j):
        slots = pl.ds(j * 8, 8)
        weight = as_matrix(fa[slots, :, 0:features])
        down = as_matrix(fa[slots, :, features : features + 128])
        rows = transposed_right(grad_mixed, weight) + transposed_right(grad_rank_out, down)
        gatt_t[pl.ds(j * 4, 4)] = rows.T.astype(narrow_type).reshape(4, 64, 256)

        @pl.loop(0, 4)
        def _(i):
            k = j * 4 + i

            @pl.when(swap.away_head(k))
            def _():
                gradient_piece(k).start()

    @pl.when(half == core)
    def _():
        gradient_kept.start()

    up_rows = transposed_right(rank_contract, contract_up)
    result_ref[...] = (
        middle[...] + vectors[3:4] * (branch[...] + vectors[8:9] + up_rows)
    ).astype(narrow_type)
    shaped = (devices, share, 128)
    terms[:, 0:32] = matmul(as_matrix(att_t[...]), grad_rank_out).astype(narrow_type).reshape(shaped)
    terms[:, 32:64] = transposed_left(grad_mixed, rank_out).astype(narrow_type).reshape(shaped)
    terms[:, 64:96] = transposed_left(normed[...], grad_rank_expand).astype(narrow_type).reshape(shaped)
    terms[:, 352:384] = transposed_left(grad_branch[...], rank_contract).astype(narrow_type).reshape(shaped)

    @pl.loop(0, own)
    def _(k):
        @pl.when(swap.away_block(k))
        def _():
            gradient_arrival(k).wait_recv()
            attended_piece(k).wait_send()

    @pl.when(half == core)
    def _():
        gradient_kept.wait()

    @pl.loop(0, heads)
    def _(k):
        @pl.when(swap.away_head(k))
        def _():
            gradient_piece(k).wait_send()

    for copy in single + along + corners + diagonal + across + [f2_across]:
        copy.wait_send()


def middle_part(lengths, choice, att, tokens, cotangent, fa, ve, f2, lines, depth, collective):
    heads, width, rows = att.shape
    features = tokens.shape[1]
    wide = features + 256
    devices, hidden_share = f2.shape[0], f2.shape[1]
    share, hidden_total = features // devices, 2 * lines[0].shape[2]
    copies = 22

    def wide_rows():
        return pltpu.VMEM((rows, features), float_type)

    def narrow_rows():
        return pltpu.VMEM((rows, features), narrow_type)

    return pl.pallas_call(
        functools.partial(middle_kernel, depth, heads),
        out_shape=(
            jax.ShapeDtypeStruct((rows, features), narrow_type),
            jax.ShapeDtypeStruct((rows, features), float_type),
            jax.ShapeDtypeStruct((devices, 384, 128), narrow_type),
            jax.ShapeDtypeStruct((heads, width, rows), narrow_type),
        ),
        in_specs=[IN_SMEM, IN_SMEM, IN_VMEM, IN_VMEM, IN_VMEM, ANYWHERE, IN_VMEM] + [ANYWHERE] * 7,
        out_specs=(IN_VMEM, IN_VMEM, IN_VMEM, ANYWHERE),
        scratch_shapes=[
            pltpu.VMEM((devices, share, wide + 256), narrow_type),
            pltpu.VMEM(f2.shape, narrow_type),
            pltpu.VMEM((devices, share, hidden_total), narrow_type),
            pltpu.VMEM((heads, width, rows), narrow_type),
            narrow_rows(),
            pltpu.VMEM((heads, width, rows), narrow_type),
            pltpu.VMEM((16, features), float_type),
            pltpu.VMEM((8, hidden_total), float_type),
            wide_rows(),
            wide_rows(),
            narrow_rows(),
            wide_rows(),
            narrow_rows(),
            wide_rows(),
            pltpu.VMEM((5, rows, 128), narrow_type),
            pltpu.VMEM((2, rows, 128), float_type),
            pltpu.VMEM((rows, 128), float_type),
            pltpu.SemaphoreType.DMA((copies,)),
            pltpu.SemaphoreType.DMA((copies,)),
            pltpu.SemaphoreType.DMA((13,)),
            pltpu.SemaphoreType.DMA((heads,)),
            pltpu.SemaphoreType.DMA((heads,)),
            pltpu.SemaphoreType.DMA((heads,)),
            pltpu.SemaphoreType.DMA((heads,)),
            pltpu.SemaphoreType.DMA((2,)),
        ],
        compiler_params=pltpu.CompilerParams(
            collective_id=collective, has_side_effects=True, vmem_limit_bytes=54 << 20
        ),
    )(lengths, choice, att, tokens, cotangent, fa, ve, f2, *lines)


class Reduce:
    COPIES = 16

    def __init__(self, depth, base, terms, first, second, third, fourth, send, receive):
        self.depth, self.base, self.terms = depth, base, terms
        self.buffers = first, second, third, fourth
        self.send, self.receive = send, receive
        self.seq, self.fsdp = place_here()
        self.core, self.x, self.y = lax.rem(self.seq, 2), lax.rem(lax.div(self.seq, 2), 2), lax.div(self.seq, 4)
        half = terms.shape[1] // 2
        self.halves = (slice(0, half), slice(half, 2 * half))

    def copy(self, step, source, target, seq, fsdp):
        at = self.base + step
        return remote(source, target, self.send.at[at], self.receive.at[at], seq, fsdp)

    def to_core(self):
        first = self.buffers[0]
        lines = [self.terms.at[pl.ds((2 * t + 1 - self.core) * self.depth, self.depth)] for t in range(4)]
        return [self.copy(t, lines[t], first.at[t], self.seq ^ CORES, self.fsdp) for t in range(4)]

    def to_sides(self):
        first, second = self.buffers[:2]
        x, y = self.x, self.y
        copies = []
        for j in range(2):
            copies.append(
                self.copy(
                    4 + j,
                    first.at[2 * j + 1 - x, :, self.halves[0]],
                    second.at[0, j],
                    self.seq ^ SIDE_X,
                    self.fsdp,
                )
            )
            copies.append(
                self.copy(
                    6 + j,
                    first.at[2 * (1 - y) + j, :, self.halves[1]],
                    second.at[1, j],
                    self.seq ^ SIDE_Y,
                    self.fsdp,
                )
            )
        return copies

    def to_corner(self):
        second, third = self.buffers[1:3]
        return [
            self.copy(8, second.at[0, 1 - self.y], third.at[0], self.seq ^ SIDE_Y, self.fsdp),
            self.copy(9, second.at[1, 1 - self.x], third.at[1], self.seq ^ SIDE_X, self.fsdp),
        ]

    def to_line(self):
        third, fourth = self.buffers[2:]
        copies = []
        for step in range(1, self.depth):
            to = lax.rem(self.fsdp + step, self.depth)
            for j in range(2):
                copies.append(
                    self.copy(8 + 2 * step + j, third.at[j, to], fourth.at[j, step], self.seq, to)
                )
        return copies

    def add(self, target, other):
        @pl.loop(0, self.depth)
        def _(i):
            target[i] = (target[i].astype(float_type) + other[i].astype(float_type)).astype(narrow_type)

    def begin(self):
        for copy in self.to_core():
            copy.start()

    def sides(self):
        first = self.buffers[0]
        for t, copy in enumerate(self.to_core()):
            copy.wait_recv()
            self.add(first.at[t], self.terms.at[pl.ds((2 * t + self.core) * self.depth, self.depth)])
        for copy in self.to_sides():
            copy.start()

    def corner(self):
        first, second = self.buffers[:2]
        copies = self.to_sides()
        for j in range(2):
            copies[2 * j].wait_recv()
            self.add(second.at[0, j], first.at[2 * j + self.x, :, self.halves[0]])
            copies[2 * j + 1].wait_recv()
            self.add(second.at[1, j], first.at[2 * self.y + j, :, self.halves[1]])
        for copy in self.to_corner():
            copy.start()

    def line(self):
        second, third = self.buffers[1:3]
        copies = self.to_corner()
        copies[0].wait_recv()
        self.add(third.at[0], second.at[0, self.y])
        copies[1].wait_recv()
        self.add(third.at[1], second.at[1, self.x])
        for copy in self.to_line():
            copy.start()

    def end(self, out):
        third, fourth = self.buffers[2:]
        for copy in self.to_line():
            copy.wait_recv()
        for j in range(2):
            total = third[j, self.fsdp].astype(float_type)
            for step in range(1, self.depth):
                total = total + fourth[j, step].astype(float_type)
            out[self.halves[j]] = total

    def drain(self):
        for copy in self.to_core() + self.to_sides() + self.to_corner() + self.to_line():
            copy.wait_send()


def last_kernel(
    depth,
    heads,
    halo,
    lens_ref,
    choice_ref,
    dq_ref,
    dkv_ref,
    tok_ref,
    gm_ref,
    fa_in,
    ve,
    rank_ref,
    early_terms,
    gradient_ref,
    early_ref,
    late_ref,
    fa,
    vectors,
    normed_t,
    normal,
    grad_rank,
    total,
    arrived,
    arrived_rows,
    merged,
    other,
    late_terms,
    early_buffers,
    late_buffers,
    select,
    send,
    receive,
    local,
    piece_send,
    piece_receive,
    piece_local,
):
    swap = Exchange(depth, heads)
    me, seq, fsdp = swap.me, swap.seq, swap.fsdp
    core, half, head, own = swap.core, swap.half, swap.head, heads
    row_count, features = tok_ref.shape
    devices, share = fa.shape[0], fa.shape[1]
    wide = features + 256
    barrier = pltpu.get_barrier_semaphore()
    greet_neighbours(barrier, seq, fsdp, depth)
    waits = 3 + depth - 1 + swap.greet_holders(barrier)
    load = pltpu.make_async_copy(fa_in.at[:, :, pl.ds(0, 3 * wide)], fa, local.at[0])
    load.start()
    pl.semaphore_wait(barrier, waits)
    over = remote(
        dkv_ref.at[pl.ds(jnp.where(core == 0, own, 0), halo)],
        other,
        piece_send.at[3, 0], piece_receive.at[3, 0], seq ^ CORES, fsdp)
    over.start()
    early = Reduce(depth, 0, early_terms, *early_buffers, send, receive)
    late = [
        Reduce(
            depth, Reduce.COPIES * (p + 1), late_terms.at[p], *[b.at[p] for b in late_buffers], send, receive
        )
        for p in range(3)
    ]
    shared = jnp.where(core == 0, own - halo, 0)
    shift = core * halo

    def in_shared(k):
        return (k >= shared) & (k < shared + halo)

    def sent(p, k, source):
        return remote(
            source, arrived.at[p, head], piece_send.at[p, k], piece_receive.at[p, head], *swap.owner(k)
        )

    def launch(p, k, source):
        @pl.when(swap.away_block(k))
        def _():
            sent(p, k, source).start()

        @pl.when(core * own + k == me)
        def _():
            pltpu.make_async_copy(source, arrived.at[p, head], piece_local.at[p]).start()

    def arrival(p, k):
        return remote(
            dq_ref.at[0], arrived.at[p, k], piece_send.at[p, k], piece_receive.at[p, k], seq ^ CORES, fsdp
        )

    @pl.loop(0, own)
    def _(step):
        k = lax.rem(step + me, own)
        launch(0, k, dq_ref.at[k])

    over.wait_recv()

    @pl.loop(0, halo)
    def _(i):
        for part in range(2):
            merged[i, part] = (
                dkv_ref[shared + shift + i, part].astype(float_type) + other[i, part].astype(float_type)
            ).astype(narrow_type)

    for p in (1, 2):

        @pl.loop(0, own)
        def _(step, p=p):
            k = lax.rem(step + me, own)

            @pl.when(in_shared(k))
            def _():
                launch(p, k, merged.at[jnp.clip(k - shared, 0, halo - 1), p - 1])

            @pl.when(jnp.logical_not(in_shared(k)))
            def _():
                launch(p, k, dkv_ref.at[k + shift, p - 1])

    early.begin()
    rows_of_vectors(ve, vectors)
    select[...] = selected(lens_ref, choice_ref, me, *select.shape)
    early.sides()
    shifted, normal_rows, scaling = layer_norm(tok_ref[...].astype(float_type), vectors[0:1], vectors[4:5])
    normal[...] = normal_rows
    for j in range(4):
        normed_t[j * 256 : (j + 1) * 256] = turned(shifted[:, j * 256 : (j + 1) * 256])
    early.corner()
    load.wait()

    def gather_part(p):
        @pl.loop(0, heads)
        def _(k):
            @pl.when(swap.away_head(k))
            def _():
                arrival(p, k).wait_recv()

        @pl.when(half == core)
        def _():
            pltpu.make_async_copy(dq_ref.at[0], arrived.at[p, head], piece_local.at[p]).wait()

    def ranks_back(p):
        for j in range(4):
            arrived_rows[:, j * 256 : (j + 1) * 256] = turned(as_matrix(arrived[p, 4 * j : 4 * j + 4]))
        up = as_matrix(fa[:, :, p * wide + features + 128 : (p + 1) * wide])
        grad_rank[...] = (matmul(arrived_rows[...], up) * select[...]).astype(narrow_type)
        shaped = (devices, share, 128)
        late_terms[p, :, 0:32] = matmul(normed_t[...], grad_rank[...]).astype(narrow_type).reshape(shaped)
        late_terms[p, :, 32:64] = (
            matmul(as_matrix(arrived[p]), rank_ref[p]).astype(narrow_type).reshape(shaped)
        )

    def project_back(p, tiles):
        @pl.loop(*tiles)
        def _(j):
            at = pl.ds(pl.multiple_of(j * 256, 128), 256)
            slots = pl.ds(j * 8, 8)
            weight = as_matrix(fa[slots, :, p * wide : p * wide + features])
            down = as_matrix(fa[slots, :, p * wide + features : p * wide + features + 128])
            term = transposed_right(arrived_rows[...], weight) + transposed_right(grad_rank[...], down)
            if p == 0:
                total[:, at] = term
            else:
                total[:, at] += term

    gather_part(0)
    ranks_back(0)
    late[0].begin()
    project_back(0, (0, 4))
    early.line()
    late[0].sides()
    gather_part(1)
    ranks_back(1)
    late[1].begin()
    project_back(1, (0, 4))
    late[0].corner()
    late[1].sides()
    gather_part(2)
    ranks_back(2)
    late[2].begin()
    late[0].line()
    late[1].corner()
    project_back(2, (0, 2))
    late[2].sides()
    project_back(2, (2, 4))
    late[1].line()
    late[2].corner()
    gradient_ref[...] = gm_ref[...] + norm_backward(total[...], vectors[0:1], normal[...], scaling)
    late[2].line()
    early.end(early_ref)
    late[0].end(late_ref.at[0])
    late[1].end(late_ref.at[1])
    late[2].end(late_ref.at[2])
    for reduce in [early] + late:
        reduce.drain()

    @pl.loop(0, own)
    def _(k):
        @pl.when(swap.away_block(k))
        def _():
            for p in range(3):
                sent(p, k, dq_ref.at[k]).wait_send()

    over.wait_send()


def last_part(lengths, choice, dq, dkv, tokens, grad_middle, fa, ve, rank, terms, depth, collective):
    heads = dq.shape[0]
    halo = dkv.shape[0] - heads
    rows, features = tokens.shape
    wide = features + 256
    devices, share = fa.shape[0], fa.shape[1]

    def buffers(count, size):
        return [
            pltpu.VMEM(count + (4, depth, size, 128), narrow_type),
            pltpu.VMEM(count + (2, 2, depth, size // 2, 128), narrow_type),
            pltpu.VMEM(count + (2, depth, size // 2, 128), narrow_type),
            pltpu.VMEM(count + (2, depth, size // 2, 128), narrow_type),
        ]

    return pl.pallas_call(
        functools.partial(last_kernel, depth, heads, halo),
        out_shape=(
            jax.ShapeDtypeStruct((rows, features), float_type),
            jax.ShapeDtypeStruct((terms.shape[1], 128), float_type),
            jax.ShapeDtypeStruct((3, 2 * share, 128), float_type),
        ),
        in_specs=[IN_SMEM] * 2 + [IN_VMEM] * 4 + [ANYWHERE] + [IN_VMEM] * 3,
        out_specs=(IN_VMEM, IN_VMEM, IN_VMEM),
        scratch_shapes=[
            pltpu.VMEM((devices, share, 3 * wide), narrow_type),
            pltpu.VMEM((16, features), float_type),
            pltpu.VMEM((features, rows), narrow_type),
            pltpu.VMEM((rows, features), float_type),
            pltpu.VMEM((rows, 128), narrow_type),
            pltpu.VMEM((rows, features), float_type),
            pltpu.VMEM((3, heads, features // heads, rows), narrow_type),
            pltpu.VMEM((rows, features), narrow_type),
            pltpu.VMEM((halo,) + dkv.shape[1:], narrow_type),
            pltpu.VMEM((halo,) + dkv.shape[1:], narrow_type),
            pltpu.VMEM((3, devices, 2 * share, 128), narrow_type),
            buffers((), terms.shape[1]),
            buffers((3,), 2 * share),
            pltpu.VMEM((rows, 128), float_type),
            pltpu.SemaphoreType.DMA((4 * Reduce.COPIES,)),
            pltpu.SemaphoreType.DMA((4 * Reduce.COPIES,)),
            pltpu.SemaphoreType.DMA((1,)),
            pltpu.SemaphoreType.DMA((4, heads)),
            pltpu.SemaphoreType.DMA((4, heads)),
            pltpu.SemaphoreType.DMA((3,)),
        ],
        compiler_params=pltpu.CompilerParams(
            collective_id=collective, has_side_effects=True, vmem_limit_bytes=44 << 20
        ),
    )(lengths, choice, dq, dkv, tokens, grad_middle, fa, ve, rank, terms)


def spread_kernel(result_in, gradient_in, early, late, result, gradient, down, up, exp_down, exp_up, con_down, con_up):
    share = down.shape[1]
    result[...] = result_in[...]
    gradient[...] = gradient_in[...]
    for p in range(4):
        first = late[p, 0:share] if p < 3 else early[0:share]
        second = late[p, share : 2 * share] if p < 3 else early[share : 2 * share]
        down[p] = first
        up[p] = second
    exp_down[...] = early[64:96]
    exp_up[...] = early[96:224]
    con_down[...] = early[224:352].T
    con_up[...] = early[352:384]


def spread(result, gradient, early, late):
    share = late.shape[1] // 2
    shapes = ((4, share, 128), (4, share, 128), (share, 128), (128, 128), (128, 128), (share, 128))
    return pl.pallas_call(
        spread_kernel,
        out_shape=tuple(jax.ShapeDtypeStruct(a.shape, a.dtype) for a in (result, gradient))
        + tuple(jax.ShapeDtypeStruct(shape, float_type) for shape in shapes),
        in_specs=[IN_VMEM] * 4,
        out_specs=(IN_VMEM,) * 8,
        compiler_params=pltpu.CompilerParams(vmem_limit_bytes=24 << 20),
    )(result, gradient, early, late)


BIG = 32768.0


def image_range(lens_ref, first, last):
    low = high = start = jnp.int32(0)
    for image in range(lens_ref.shape[0]):
        end = start + lens_ref[image]
        low = jnp.where((start <= first) & (first < end), start, low)
        high = jnp.where((start <= last) & (last < end), end - 1, high)
        start = end
    return low, high


def image_edges(lens_ref, marks, rows):
    row = lax.broadcasted_iota(jnp.int32, (marks, rows), 0)
    starts = jnp.full((marks, rows), 1 << 30, jnp.int32)
    ends = jnp.zeros((marks, rows), jnp.int32)
    start = jnp.int32(0)
    for image in range(lens_ref.shape[0]):
        end = start + lens_ref[image]
        starts, ends = jnp.where(row == image, start, starts), jnp.where(row == image, end, ends)
        start = end
    return starts, ends


class Blocks:
    def __init__(self, lens_ref, own, halo, rows, marks):
        core = lax.rem(lax.axis_index("seq"), 2)
        self.lens_ref, self.own, self.rows, self.slots = lens_ref, own, rows, own + halo
        self.base = core * (own - halo)
        self.shift = core * halo
        self.starts, self.ends = image_edges(lens_ref, marks, rows)
        self.lane = lax.broadcasted_iota(jnp.int32, (marks, rows), 1)

    def marks(self, slot):
        place = self.lane + (self.base + slot) * self.rows
        return jnp.where((place >= self.starts) & (place < self.ends), 1.0, 0.0).astype(float_type)

    def reach(self, slot):
        first = (self.base + slot) * self.rows
        low, high = image_range(self.lens_ref, first, first + self.rows - 1)
        return lax.div(low, self.rows) - self.base, lax.div(high, self.rows) - self.base


def forward_kernel(
    own, halo, step, lens_ref, x_ref, att_ref, lse_ref, out_ref, keys, queries, values, score, weight, item_row, item_low
):
    slots, _, width, rows = x_ref.shape
    blocks = Blocks(lens_ref, own, halo, rows, keys.shape[1] - width)
    scale = width**-0.5

    @pl.loop(0, slots)
    def _(slot):
        block = jnp.concatenate([x_ref[slot, 1].astype(float_type), (blocks.marks(slot) - 1.0) * BIG], axis=0)
        keys[pl.ds(pl.multiple_of(slot * rows, rows), rows)] = block.T.astype(narrow_type)
        values[slot, 0:width] = x_ref[slot, 2]
        values[slot, width:] = jnp.ones((16, rows), narrow_type)

    def prepare(i, total):
        slot = i + blocks.shift
        queries[i] = jnp.concatenate([x_ref[slot, 0].astype(float_type) * scale, blocks.marks(slot)], axis=0).astype(narrow_type)
        low, high = blocks.reach(slot)
        count = lax.div(high - low + step, step)
        low = jnp.minimum(low, slots - step * count)

        @pl.loop(0, count)
        def _(j):
            item_row[total + j] = i
            item_low[total + j] = low + j * step

        return total + count

    total = lax.fori_loop(0, own, prepare, jnp.int32(0))
    item_row[total] = item_row[total - 1]
    item_low[total] = item_low[total - 1]

    def scored(t, side):
        at = pl.multiple_of(item_low[t] * rows, rows)
        score[side] = matmul(keys[pl.ds(at, step * rows)], queries[item_row[t]])

    def mixed(t):
        low = item_low[t]
        result = matmul(values[low], weight[0:rows])
        for j in range(1, step):
            result += matmul(values[low + j], weight[j * rows : (j + 1) * rows])
        return result

    def soften(fresh, side, highest):
        highest = jnp.where(fresh, -1e30, highest)
        s = score[side]
        higher = jnp.maximum(highest, jnp.max(s, axis=0, keepdims=True))
        fade = jnp.where(fresh, 0.0, jnp.exp(highest - higher))
        return higher, fade, jnp.exp(s - higher).astype(narrow_type)

    def finish(t, out, fade, highest):
        i = item_row[t]
        out = out * fade + mixed(t)
        summed = out[width : width + 1]
        whole = out[0:width] / summed
        att_ref[i] = whole.astype(narrow_type)
        out_ref[i] = whole
        lse_ref[i] = jnp.broadcast_to(highest + jnp.log(summed), (8, rows))
        return out

    def turn(t, side, carry):
        highest, out, fade = carry
        out = finish(t - 1, out, fade, highest)
        scored(t + 1, 1 - side)
        highest, fade, p = soften(item_row[t] != item_row[t - 1], side, highest)
        weight[...] = p
        return highest, out, fade

    scored(0, 0)
    scored(1, 1)
    highest, fade, p = soften(True, 0, jnp.zeros((1, rows), float_type))
    weight[...] = p
    carry = (highest, jnp.zeros((width + 16, rows), float_type), fade)
    pairs = lax.div(total - 1, 2)
    carry = lax.fori_loop(0, pairs, lambda j, c: turn(2 * j + 2, 0, turn(2 * j + 1, 1, c)), carry)
    carry = lax.fori_loop(2 * pairs + 1, total, lambda t, c: turn(t, 1, c), carry)
    highest, out, fade = carry
    finish(total - 1, out, fade, highest)


def attention_forward(lengths, x, own, halo, step=2):
    slots, _, width, rows = x.shape
    marks = -(-lengths.shape[0] // 16) * 16
    most = own * (slots // step + 2) + 8
    return pl.pallas_call(
        functools.partial(forward_kernel, own, halo, step),
        out_shape=(
            jax.ShapeDtypeStruct((own, width, rows), narrow_type),
            jax.ShapeDtypeStruct((own, 8, rows), float_type),
            jax.ShapeDtypeStruct((own, width, rows), float_type),
        ),
        in_specs=[IN_SMEM, IN_VMEM],
        out_specs=(IN_VMEM, IN_VMEM, IN_VMEM),
        scratch_shapes=[
            pltpu.VMEM((slots * rows, width + marks), narrow_type),
            pltpu.VMEM((own, width + marks, rows), narrow_type),
            pltpu.VMEM((slots, width + 16, rows), narrow_type),
            pltpu.VMEM((2, step * rows, rows), float_type),
            pltpu.VMEM((step * rows, rows), narrow_type),
            pltpu.SMEM((most,), jnp.int32),
            pltpu.SMEM((most,), jnp.int32),
        ],
        compiler_params=pltpu.CompilerParams(vmem_limit_bytes=32 << 20),
    )(lengths, x)


def backward_kernel(
    own, halo, step, lens_ref, x_ref, g_ref, lse_ref, out_ref, dq_ref, dkv_ref,
    keys, values, queries, offset, dq, score, grad_prob, weight, grad_score, item_slot, item_low,
):
    slots, _, width, rows = x_ref.shape
    blocks = Blocks(lens_ref, own, halo, rows, keys.shape[2] - width)
    scale = width**-0.5

    def prepare(slot, total):
        block = jnp.concatenate([x_ref[slot, 1].astype(float_type), (blocks.marks(slot) - 1.0) * BIG], axis=0)
        keys[slot] = block.T.astype(narrow_type)
        values[slot] = x_ref[slot, 2].astype(float_type).T.astype(narrow_type)
        dkv_ref[slot] = jnp.zeros((2, width, rows), narrow_type)
        low, high = blocks.reach(slot)
        low = jnp.maximum(low - blocks.shift, 0)
        high = jnp.minimum(high - blocks.shift, own - 1)
        count = jnp.maximum(lax.div(high - low + step, step), 0)
        low = jnp.minimum(low, own - step * count)

        @pl.loop(0, count)
        def _(j):
            item_slot[total + j] = slot
            item_low[total + j] = low + j * step

        return total + count

    total = lax.fori_loop(0, slots, prepare, jnp.int32(0))
    item_slot[total] = item_slot[total - 1]
    item_low[total] = item_low[total - 1]

    @pl.loop(0, own)
    def _(i):
        slot = i + blocks.shift
        q = x_ref[slot, 0].astype(float_type) * scale
        queries[i] = jnp.concatenate([q, blocks.marks(slot)], axis=0).astype(narrow_type)
        g = g_ref[i].astype(float_type)
        offset[i] = jnp.broadcast_to(jnp.sum(g * out_ref[i], axis=0, keepdims=True), (8, rows))
        dq[i] = jnp.zeros((width, rows), float_type)

    def scored(t, side):
        slot, low = item_slot[t], item_low[t]
        for j in range(step):
            score[side, j] = matmul(keys[slot], queries[low + j])
            grad_prob[side, j] = matmul(values[slot], g_ref[low + j])

    def soften(t, side):
        low = item_low[t]
        done = []
        for j in range(step):
            p = jnp.exp(score[side, j] - lse_ref[low + j, 0:1])
            d = p * (grad_prob[side, j] - offset[low + j, 0:1])
            done.append((p.astype(narrow_type), d.astype(narrow_type)))
        return done

    def keep(done):
        for j in range(step):
            weight[j] = done[j][0]
            grad_score[j] = done[j][1]

    def mixed(t, fresh, dk, dv):
        slot, low = item_slot[t], item_low[t]
        dk = jnp.where(fresh, 0.0, dk)
        dv = jnp.where(fresh, 0.0, dv)
        key = x_ref[slot, 1]
        for j in range(step):
            dk += transposed_right(queries[low + j, 0:width], grad_score[j])
            dv += transposed_right(g_ref[low + j], weight[j])
        for j in range(step):
            dq[low + j] += matmul(key, grad_score[j])
        dkv_ref[slot, 0] = dk.astype(narrow_type)
        dkv_ref[slot, 1] = dv.astype(narrow_type)
        return dk, dv

    def turn(t, side, carry):
        fresh = (t == 1) | (item_slot[t - 1] != item_slot[jnp.maximum(t - 2, 0)])
        scored(t + 1, 1 - side)
        done = soften(t, side)
        carry = mixed(t - 1, fresh, *carry)
        keep(done)
        return carry

    scored(0, 0)
    scored(1, 1)
    keep(soften(0, 0))
    zero = jnp.zeros((width, rows), float_type)
    pairs = lax.div(total - 1, 2)
    carry = lax.fori_loop(0, pairs, lambda j, c: turn(2 * j + 2, 0, turn(2 * j + 1, 1, c)), (zero, zero))
    carry = lax.fori_loop(2 * pairs + 1, total, lambda t, c: turn(t, 1, c), carry)
    mixed(total - 1, item_slot[total - 1] != item_slot[jnp.maximum(total - 2, 0)], *carry)

    @pl.loop(0, own)
    def _(i):
        dq_ref[i] = (dq[i] * scale).astype(narrow_type)


def attention_backward(lengths, x, g, lse, out, own, halo, step=1):
    slots, _, width, rows = x.shape
    marks = -(-lengths.shape[0] // 16) * 16
    most = slots * (own // step + 2) + 8
    return pl.pallas_call(
        functools.partial(backward_kernel, own, halo, step),
        out_shape=(
            jax.ShapeDtypeStruct((own, width, rows), narrow_type),
            jax.ShapeDtypeStruct((slots, 2, width, rows), narrow_type),
        ),
        in_specs=[IN_SMEM] + [IN_VMEM] * 4,
        out_specs=(IN_VMEM, IN_VMEM),
        scratch_shapes=[
            pltpu.VMEM((slots, rows, width + marks), narrow_type),
            pltpu.VMEM((slots, rows, width), narrow_type),
            pltpu.VMEM((own, width + marks, rows), narrow_type),
            pltpu.VMEM((own, 8, rows), float_type),
            pltpu.VMEM((own, width, rows), float_type),
            pltpu.VMEM((2, step, rows, rows), float_type),
            pltpu.VMEM((2, step, rows, rows), float_type),
            pltpu.VMEM((step, rows, rows), narrow_type),
            pltpu.VMEM((step, rows, rows), narrow_type),
            pltpu.SMEM((most,), jnp.int32),
            pltpu.SMEM((most,), jnp.int32),
        ],
        compiler_params=pltpu.CompilerParams(vmem_limit_bytes=40 << 20),
    )(lengths, x, g, lse, out)


def layer_on_slice(
    tokens,
    lengths,
    adapter_choice,
    gain_rows,
    bias_rows,
    query_key_value,
    output_weight,
    expand_weight,
    expand_bias,
    contract_weight,
    adapter_in_attention,
    adapter_out_attention,
    adapter_in_expand,
    adapter_out_expand,
    adapter_in_contract,
    adapter_out_contract,
    cotangent,
):
    row_count = tokens.shape[0]
    depth = lax.axis_size("fsdp")
    devices = lax.axis_size(("seq", "fsdp"))
    own = devices // 2
    halo = -(-(LONGEST - 1) // row_count)

    arrays = (
        gain_rows,
        bias_rows,
        expand_bias[None],
        query_key_value,
        output_weight,
        adapter_in_attention,
        adapter_out_attention.transpose(0, 2, 1),
        adapter_in_expand,
        adapter_out_contract.T,
        contract_weight,
        adapter_in_contract,
        adapter_out_expand,
        expand_weight,
    )
    fa, ve, f2, line_a, line_b, on_heads, rank = attention_in(
        lengths, adapter_choice, tokens, arrays, halo, depth, HEADS, devices, 1
    )

    def swapped(line, bit):
        route = [
            (seq * depth + fsdp, (seq ^ bit) * depth + fsdp)
            for seq in range(devices // depth)
            for fsdp in range(depth)
        ]
        return lax.ppermute(line, ("seq", "fsdp"), route)

    lines = (
        line_a,
        line_b,
        swapped(line_a, SIDE_Y),
        swapped(line_b, SIDE_Y),
        swapped(line_a, SIDE_X),
        swapped(line_b, SIDE_X),
    )
    attended, log_totals, attended_wide = attention_forward(lengths, on_heads, own, halo)
    result, grad_middle, terms, grad_on_heads = middle_part(
        lengths, adapter_choice, attended, tokens, cotangent, fa, ve, f2, lines, depth, 2
    )
    grad_queries, grad_key_values = attention_backward(
        lengths, on_heads, grad_on_heads, log_totals, attended_wide, own, halo
    )
    input_gradient, early, late = last_part(
        lengths, adapter_choice, grad_queries, grad_key_values, tokens, grad_middle, fa, ve, rank, terms, depth, 3
    )
    outs = spread(result, input_gradient, early, late)
    return outs[:3] + (outs[3].transpose(0, 2, 1),) + outs[4:7] + (outs[7].T,)


def solution(mesh):
    per_device = layer_on_slice if dict(mesh.shape) == {"seq": 8, "fsdp": 4} else general_layer
    placed = (
        P(("seq", "fsdp"), None),
        P(),
        P(),
        P(None, ("seq", "fsdp")),
        P(None, ("seq", "fsdp")),
        P(("seq", "fsdp"), None),
        P(("seq", "fsdp"), None),
        P(("seq", "fsdp"), None),
        P(("seq", "fsdp")),
        P(("seq", "fsdp"), None),
        P(None, ("seq", "fsdp"), None),
        P(None, None, ("seq", "fsdp")),
        P(("seq", "fsdp"), None),
        P(None, ("seq", "fsdp")),
        P(("seq", "fsdp"), None),
        P(None, ("seq", "fsdp")),
        P(("seq", "fsdp"), None),
    )
    return jax.shard_map(
        per_device,
        mesh=mesh,
        in_specs=placed,
        out_specs=(
            P(("seq", "fsdp"), None),
            P(("seq", "fsdp"), None),
            P(None, ("seq", "fsdp"), None),
            P(None, None, ("seq", "fsdp")),
            P(("seq", "fsdp"), None),
            P(None, ("seq", "fsdp")),
            P(("seq", "fsdp"), None),
            P(None, ("seq", "fsdp")),
        ),
        check_vma=False,
    )
```

```python
import functools
import jax
import jax.numpy as jnp
from jax import lax
from jax.experimental import pallas as pl
from jax.experimental.pallas import tpu as pltpu
from jax.sharding import PartitionSpec as P

HEADS = 16
RANK = 16
HOPS = 6
EDGE = 1408
LONGEST = 1370


epsilon = 1e-06
float_type = jnp.float32
narrow_type = jnp.bfloat16


def passed_along(block, axis, distance):
    devices = range(lax.axis_size(axis))
    route = [(i - distance, i) for i in devices if i - distance in devices]
    return lax.ppermute(block, axis, route)


def layer_norm(inputs_row, gain_row, bias_row):
    center = inputs_row - jnp.mean(inputs_row, axis=-1, keepdims=True)
    scaling = lax.rsqrt(jnp.mean(center * center, axis=-1, keepdims=True) + epsilon)
    normal = center * scaling
    return (normal * gain_row + bias_row, normal, scaling)


def norm_backward(gradient, gain_row, normal, scaling):
    weighted = gradient * gain_row
    return scaling * (
        weighted
        - jnp.mean(weighted, axis=-1, keepdims=True)
        - normal * jnp.mean(weighted * normal, axis=-1, keepdims=True)
    )


def matmul(first_operand, second_operand):
    return jnp.dot(first_operand, second_operand, preferred_element_type=float_type)


def transposed_left(first_operand, second_operand):
    return lax.dot_general(
        first_operand, second_operand, (((0,), (0,)), ((), ())), preferred_element_type=float_type
    )


def transposed_right(first_operand, second_operand):
    return lax.dot_general(
        first_operand, second_operand, (((1,), (1,)), ((), ())), preferred_element_type=float_type
    )


def gelu_slope(hidden_pre):
    cumulative = 0.5 * (1.0 + lax.erf(hidden_pre * 0.7071067811865476))
    density = jnp.exp(-0.5 * hidden_pre * hidden_pre) * 0.3989422804014327
    return cumulative + hidden_pre * density


def general_layer(
    tokens,
    lengths,
    adapter_choice,
    gain_rows,
    bias_rows,
    query_key_value,
    output_weight,
    expand_weight,
    expand_bias,
    contract_weight,
    adapter_in_attention,
    adapter_out_attention,
    adapter_in_expand,
    adapter_out_expand,
    adapter_in_contract,
    adapter_out_contract,
    cotangent,
):
    gathered = (
        lax.all_gather(gain_rows, ("seq", "fsdp"), axis=1, tiled=True),
        lax.all_gather(bias_rows, ("seq", "fsdp"), axis=1, tiled=True),
        lax.all_gather(query_key_value, ("seq", "fsdp"), axis=0, tiled=True),
        lax.all_gather(output_weight, ("seq", "fsdp"), axis=0, tiled=True),
        lax.all_gather(expand_weight, ("seq", "fsdp"), axis=0, tiled=True),
        lax.all_gather(expand_bias, ("seq", "fsdp"), axis=0, tiled=True),
        lax.all_gather(contract_weight, ("seq", "fsdp"), axis=0, tiled=True),
        lax.all_gather(adapter_in_attention, ("seq", "fsdp"), axis=1, tiled=True),
        lax.all_gather(adapter_out_attention, ("seq", "fsdp"), axis=2, tiled=True),
        lax.all_gather(adapter_in_expand, ("seq", "fsdp"), axis=0, tiled=True),
        lax.all_gather(adapter_out_expand, ("seq", "fsdp"), axis=1, tiled=True),
        lax.all_gather(adapter_in_contract, ("seq", "fsdp"), axis=0, tiled=True),
        lax.all_gather(adapter_out_contract, ("seq", "fsdp"), axis=1, tiled=True),
    )
    (
        gains_full,
        biases_full,
        qkv_full,
        output_full,
        expand_full,
        expand_bias_full,
        contract_full,
        attention_down,
        attention_up,
        expand_down,
        expand_up,
        contract_down,
        contract_up,
    ) = gathered
    gains_wide = gains_full.astype(float_type)
    biases_wide = biases_full.astype(float_type)
    row_count, features = tokens.shape
    device_count = lax.axis_size(("seq", "fsdp"))
    position = lax.axis_index(("seq", "fsdp"))
    head_width = features // HEADS
    pair_width = 2 * head_width
    pair_count = HEADS // 2
    scaling_score = head_width ** (-0.5)
    rank_width = attention_down.shape[2]
    window_start = HOPS * row_count - EDGE
    window_rows = row_count + 2 * EDGE
    image_ends = jnp.cumsum(lengths)
    places = (
        position * row_count
        - HOPS * row_count
        + jnp.arange((2 * HOPS + 1) * row_count, dtype=jnp.int32)
    )
    image_of = jnp.sum((places[:, None] >= image_ends[None, :]).astype(jnp.int32), axis=1)
    image_of = jnp.where((places >= 0) & (places < device_count * row_count), image_of, -1)
    own_image = image_of[HOPS * row_count : (HOPS + 1) * row_count]
    key_image = image_of[window_start : window_start + window_rows]
    allowed = own_image[:, None] == key_image[None, :]
    matches = own_image[:, None] == jnp.arange(lengths.shape[0], dtype=jnp.int32)[None, :]
    chosen = jnp.sum(jnp.where(matches, adapter_choice[None, :], 0), axis=1)
    select = (jnp.arange(rank_width, dtype=jnp.int32)[None, :] // RANK == chosen[:, None]).astype(
        float_type
    )
    residual = tokens.astype(float_type)
    normed_first, normal_first, scaling_first = layer_norm(residual, gains_wide[0], biases_wide[0])
    normed_first = normed_first.astype(narrow_type)
    rank_qkv = (
        jnp.einsum(
            "td,pdr->tpr", normed_first, attention_down[:3], preferred_element_type=float_type
        )
        * select[:, None, :]
    ).astype(narrow_type)
    adapted_qkv = jnp.einsum(
        "tpr,prd->tpd", rank_qkv, attention_up[:3], preferred_element_type=float_type
    ).reshape(row_count, 3 * features)
    query_bias = jnp.concatenate([biases_wide[1], jnp.zeros((2 * features,), float_type)])
    projected = (matmul(normed_first, qkv_full) + adapted_qkv + query_bias).astype(narrow_type)
    queries = projected[:, :features]
    key_values = projected[:, features:]
    from_lower = []
    from_higher = []
    for distance in range(1, HOPS + 1):
        from_lower.append(passed_along(key_values, ("seq", "fsdp"), distance))
        from_higher.append(passed_along(key_values, ("seq", "fsdp"), -distance))
    beside_all = jnp.concatenate(from_lower[::-1] + [key_values] + from_higher, axis=0)
    window = beside_all[window_start : window_start + window_rows]

    def pair_slices(pair_index):
        offset = pair_index * pair_width
        query_part = lax.dynamic_slice_in_dim(queries, offset, pair_width, 1).reshape(
            row_count, 2, head_width
        )
        key_part = lax.dynamic_slice_in_dim(window, offset, pair_width, 1).reshape(
            window_rows, 2, head_width
        )
        value_part = lax.dynamic_slice_in_dim(window, features + offset, pair_width, 1).reshape(
            window_rows, 2, head_width
        )
        scores = (
            jnp.einsum("qhd,khd->hqk", query_part, key_part, preferred_element_type=float_type)
            * scaling_score
        )
        scores = jnp.where(allowed[None], scores, -1e30)
        return (query_part, key_part, value_part, scores)

    def pair_forward(pair_index):
        query_part, key_part, value_part, scores = pair_slices(pair_index)
        highest = jnp.max(scores, axis=2, keepdims=True)
        weights = jnp.exp(scores - highest)
        denominator = jnp.sum(weights, axis=2, keepdims=True)
        soft = (weights / denominator).astype(narrow_type)
        mixed_part = jnp.einsum("hqk,khd->qhd", soft, value_part, preferred_element_type=float_type)
        return (
            mixed_part.reshape(row_count, pair_width),
            (highest + jnp.log(denominator))[:, :, 0],
        )

    attended_pairs, log_totals = lax.map(pair_forward, jnp.arange(pair_count))
    attended = attended_pairs.transpose(1, 0, 2).reshape(row_count, features).astype(narrow_type)
    rank_out = (matmul(attended, attention_down[3]) * select).astype(narrow_type)
    mixed = matmul(attended, output_full) + biases_wide[2] + matmul(rank_out, attention_up[3])
    middle = residual + gains_wide[1] * mixed
    normed_second, normal_second, scaling_second = layer_norm(middle, gains_wide[2], biases_wide[3])
    normed_second = normed_second.astype(narrow_type)
    rank_expand = (matmul(normed_second, expand_down) * select).astype(narrow_type)
    hidden_pre = (
        matmul(normed_second, expand_full)
        + expand_bias_full.astype(float_type)
        + matmul(rank_expand, expand_up)
    )
    active = jax.nn.gelu(hidden_pre, approximate=False).astype(narrow_type)
    rank_contract = (matmul(active, contract_down) * select).astype(narrow_type)
    branch = matmul(active, contract_full) + biases_wide[4] + matmul(rank_contract, contract_up)
    result = (middle + gains_wide[3] * branch).astype(narrow_type)
    renewed = lax.optimization_barrier(
        (
            gain_rows,
            bias_rows,
            query_key_value,
            output_weight,
            expand_weight,
            expand_bias,
            contract_weight,
            adapter_in_attention,
            adapter_out_attention,
            adapter_in_expand,
            adapter_out_expand,
            adapter_in_contract,
            adapter_out_contract,
            cotangent,
        )
    )
    gathered = (
        lax.all_gather(renewed[0], ("seq", "fsdp"), axis=1, tiled=True),
        lax.all_gather(renewed[1], ("seq", "fsdp"), axis=1, tiled=True),
        lax.all_gather(renewed[2], ("seq", "fsdp"), axis=0, tiled=True),
        lax.all_gather(renewed[3], ("seq", "fsdp"), axis=0, tiled=True),
        lax.all_gather(renewed[4], ("seq", "fsdp"), axis=0, tiled=True),
        lax.all_gather(renewed[5], ("seq", "fsdp"), axis=0, tiled=True),
        lax.all_gather(renewed[6], ("seq", "fsdp"), axis=0, tiled=True),
        lax.all_gather(renewed[7], ("seq", "fsdp"), axis=1, tiled=True),
        lax.all_gather(renewed[8], ("seq", "fsdp"), axis=2, tiled=True),
        lax.all_gather(renewed[9], ("seq", "fsdp"), axis=0, tiled=True),
        lax.all_gather(renewed[10], ("seq", "fsdp"), axis=1, tiled=True),
        lax.all_gather(renewed[11], ("seq", "fsdp"), axis=0, tiled=True),
        lax.all_gather(renewed[12], ("seq", "fsdp"), axis=1, tiled=True),
    )
    (
        gains_full,
        biases_full,
        qkv_full,
        output_full,
        expand_full,
        expand_bias_full,
        contract_full,
        attention_down,
        attention_up,
        expand_down,
        expand_up,
        contract_down,
        contract_up,
    ) = gathered
    gains_wide = gains_full.astype(float_type)
    gradient_out = cotangent.astype(float_type)
    grad_branch = (gains_wide[3] * gradient_out).astype(narrow_type)
    grad_rank_contract = (transposed_right(grad_branch, contract_up) * select).astype(narrow_type)
    grad_contract_down = transposed_left(active, grad_rank_contract)
    grad_contract_up = transposed_left(rank_contract, grad_branch)
    grad_active = transposed_right(grad_branch, contract_full) + transposed_right(
        grad_rank_contract, contract_down
    )
    grad_hidden = (grad_active * gelu_slope(hidden_pre)).astype(narrow_type)
    grad_rank_expand = (transposed_right(grad_hidden, expand_up) * select).astype(narrow_type)
    grad_expand_down = transposed_left(normed_second, grad_rank_expand)
    grad_expand_up = transposed_left(rank_expand, grad_hidden)
    grad_normed_second = transposed_right(grad_hidden, expand_full) + transposed_right(
        grad_rank_expand, expand_down
    )
    grad_middle = gradient_out + norm_backward(
        grad_normed_second, gains_wide[2], normal_second, scaling_second
    )
    grad_mixed = (gains_wide[1] * grad_middle).astype(narrow_type)
    grad_rank_out = (transposed_right(grad_mixed, attention_up[3]) * select).astype(narrow_type)
    grad_out_down = transposed_left(attended, grad_rank_out)
    grad_out_up = transposed_left(rank_out, grad_mixed)
    grad_attended = (
        transposed_right(grad_mixed, output_full)
        + transposed_right(grad_rank_out, attention_down[3])
    ).astype(narrow_type)

    def pair_backward(pair_index):
        query_part, key_part, value_part, scores = pair_slices(pair_index)
        grad_part = lax.dynamic_slice_in_dim(
            grad_attended, pair_index * pair_width, pair_width, 1
        ).reshape(row_count, 2, head_width)
        log_pair = log_totals[pair_index]
        probable = jnp.exp(scores - log_pair[:, :, None])
        grad_probable = jnp.einsum(
            "qhd,khd->hqk", grad_part, value_part, preferred_element_type=float_type
        )
        grad_scores = probable * (
            grad_probable - jnp.sum(grad_probable * probable, axis=2, keepdims=True)
        )
        grad_scores = grad_scores.astype(narrow_type)
        grad_query = (
            jnp.einsum("hqk,khd->qhd", grad_scores, key_part, preferred_element_type=float_type)
            * scaling_score
        )
        grad_key = (
            jnp.einsum("hqk,qhd->khd", grad_scores, query_part, preferred_element_type=float_type)
            * scaling_score
        )
        grad_value = jnp.einsum(
            "hqk,qhd->khd",
            probable.astype(narrow_type),
            grad_part,
            preferred_element_type=float_type,
        )
        return (
            grad_query.reshape(row_count, pair_width),
            grad_key.reshape(window_rows, pair_width),
            grad_value.reshape(window_rows, pair_width),
        )

    grad_query_pairs, grad_key_pairs, grad_value_pairs = lax.map(
        pair_backward, jnp.arange(pair_count)
    )
    grad_queries = grad_query_pairs.transpose(1, 0, 2).reshape(row_count, features)
    grad_keys = grad_key_pairs.transpose(1, 0, 2).reshape(window_rows, features)
    grad_values = grad_value_pairs.transpose(1, 0, 2).reshape(window_rows, features)
    grad_window = jnp.concatenate([grad_keys, grad_values], axis=1)
    padded_grads = jnp.pad(grad_window, ((window_start, window_start), (0, 0)))
    grad_pairs = padded_grads[HOPS * row_count : (HOPS + 1) * row_count]
    for distance in range(1, HOPS + 1):
        lower_piece = padded_grads[
            (HOPS - distance) * row_count : (HOPS - distance + 1) * row_count
        ]
        higher_piece = padded_grads[
            (HOPS + distance) * row_count : (HOPS + distance + 1) * row_count
        ]
        grad_pairs = grad_pairs + passed_along(
            lower_piece.astype(jnp.bfloat16), ("seq", "fsdp"), -distance
        ).astype(lower_piece.dtype)
        grad_pairs = grad_pairs + passed_along(
            higher_piece.astype(jnp.bfloat16), ("seq", "fsdp"), distance
        ).astype(higher_piece.dtype)
    grad_projected = jnp.concatenate([grad_queries, grad_pairs], axis=1).astype(narrow_type)
    grad_blocks = grad_projected.reshape(row_count, 3, features)
    grad_rank_qkv = (
        jnp.einsum("tpd,prd->tpr", grad_blocks, attention_up[:3], preferred_element_type=float_type)
        * select[:, None, :]
    ).astype(narrow_type)
    grad_qkv_down = jnp.einsum(
        "td,tpr->pdr", normed_first, grad_rank_qkv, preferred_element_type=float_type
    )
    grad_qkv_up = jnp.einsum(
        "tpr,tpd->prd", rank_qkv, grad_blocks, preferred_element_type=float_type
    )
    grad_normed_first = transposed_right(grad_projected, qkv_full) + jnp.einsum(
        "tpr,pdr->td", grad_rank_qkv, attention_down[:3], preferred_element_type=float_type
    )
    input_gradient = grad_middle + norm_backward(
        grad_normed_first, gains_wide[0], normal_first, scaling_first
    )
    grad_attention_down = jnp.concatenate([grad_qkv_down, grad_out_down[None]], axis=0)
    grad_attention_up = jnp.concatenate([grad_qkv_up, grad_out_up[None]], axis=0)
    summed = (
        lax.psum_scatter(grad_attention_down, ("seq", "fsdp"), scatter_dimension=1, tiled=True),
        lax.psum_scatter(grad_attention_up, ("seq", "fsdp"), scatter_dimension=2, tiled=True),
        lax.psum_scatter(grad_expand_down, ("seq", "fsdp"), scatter_dimension=0, tiled=True),
        lax.psum_scatter(grad_expand_up, ("seq", "fsdp"), scatter_dimension=1, tiled=True),
        lax.psum_scatter(grad_contract_down, ("seq", "fsdp"), scatter_dimension=0, tiled=True),
        lax.psum_scatter(grad_contract_up, ("seq", "fsdp"), scatter_dimension=1, tiled=True),
    )
    return (
        result,
        input_gradient,
        summed[0],
        summed[1],
        summed[2],
        summed[3],
        summed[4],
        summed[5],
    )


MESH_ID = pl.DeviceIdType.MESH
CORES, SIDE_X, SIDE_Y = 1, 2, 4
ANYWHERE = pl.BlockSpec(memory_space=pl.ANY)
IN_VMEM = pl.BlockSpec(memory_space=pltpu.VMEM)
IN_SMEM = pl.BlockSpec(memory_space=pltpu.SMEM)


def place_here():
    return lax.axis_index("seq"), lax.axis_index("fsdp")


def remote(source, target, send, receive, seq, fsdp):
    return pltpu.make_async_remote_copy(
        src_ref=source,
        dst_ref=target,
        send_sem=send,
        recv_sem=receive,
        device_id=(seq, fsdp),
        device_id_type=MESH_ID,
    )


def greet(barrier, seq, fsdp):
    pl.semaphore_signal(barrier, 1, device_id=(seq, fsdp), device_id_type=MESH_ID)


def greet_neighbours(barrier, seq, fsdp, depth):
    for bit in (CORES, SIDE_X, SIDE_Y):
        greet(barrier, seq ^ bit, fsdp)
    for step in range(1, depth):
        greet(barrier, seq, lax.rem(fsdp + step, depth))


WHOLE, OPEN, LINE = 0, 1, 2


class Gather:
    STEPS = 10

    def __init__(self, depth, send, receive):
        self.depth, self.send, self.receive = depth, send, receive
        self.seq, self.fsdp = place_here()
        self.me = self.seq * depth + self.fsdp
        self.inside = (self.fsdp == 1) | (self.fsdp == 2)

    def copy(self, index, step, source, target, seq, fsdp):
        at = index * self.STEPS + step
        return remote(source, target, self.send.at[at], self.receive.at[at], seq, fsdp)

    def part(self, chunk, at_seq, first, count):
        full, rows, columns, _, kind, _ = chunk
        base = 0 if kind == LINE else at_seq * self.depth
        return full.at[pl.ds(base + first, count), rows, columns]

    def group(self, chunk, at_seq):
        return self.part(chunk, at_seq, 0, self.depth)

    def sides(self, chunk):
        return (SIDE_X, SIDE_Y) if chunk[3] else (SIDE_Y, SIDE_X)

    def line(self, index, chunk, step):
        pair = lax.div(self.fsdp, 2)
        if step == 0:
            piece, to = self.part(chunk, self.seq, self.fsdp, 1), self.fsdp ^ 1
            if chunk[5] is not None:
                source = chunk[5].at[pl.ds(0, 1), chunk[1], chunk[2]]
                return self.copy(index, step, source, piece, self.seq, to)
        elif step == 1:
            piece, to = self.part(chunk, self.seq, 2 * pair, 2), 3 - self.fsdp
        else:
            piece, to = self.part(chunk, self.seq, 2 - 2 * pair, 2), self.fsdp ^ 1
        return self.copy(index, step, piece, piece, self.seq, to)

    def over(self, index, chunk, step):
        a, b = self.sides(chunk)
        piece = self.group(chunk, self.seq ^ a if step == 2 else self.seq)
        return self.copy(index, 3 + step, piece, piece, self.seq ^ (b if step else a), self.fsdp)

    def across(self, index, chunk, step):
        a, b = self.sides(chunk)
        piece = self.group(chunk, self.seq ^ (0, a, b, a ^ b)[step])
        return self.copy(index, 6 + step, piece, piece, self.seq ^ CORES, self.fsdp)

    def own(self, index, chunk):
        self.line(index, chunk, 0).start()

    def inner(self, index, chunk):
        @pl.when(self.inside)
        def _():
            self.line(index, chunk, 0).wait_recv()
            self.line(index, chunk, 1).start()

    def outer(self, index, chunk):
        @pl.when(self.inside)
        def _():
            self.line(index, chunk, 1).wait_recv()
            self.line(index, chunk, 2).start()

    def arrive(self, index, chunk):
        @pl.when(jnp.logical_not(self.inside))
        def _():
            self.line(index, chunk, 0).wait_recv()
            self.line(index, chunk, 2).wait_recv()

    def first(self, index, chunk):
        self.arrive(index, chunk)
        self.over(index, chunk, 0).start()
        self.over(index, chunk, 1).start()
        self.across(index, chunk, 0).start()

    def second(self, index, chunk):
        self.over(index, chunk, 0).wait_recv()
        if chunk[4] == WHOLE:
            self.over(index, chunk, 2).start()
        self.across(index, chunk, 1).start()

    def third(self, index, chunk):
        self.over(index, chunk, 1).wait_recv()
        self.across(index, chunk, 2).start()
        if chunk[4] == WHOLE:
            self.over(index, chunk, 2).wait_recv()
            self.across(index, chunk, 3).start()

    def finish(self, index, chunk):
        for step in range(4 if chunk[4] == WHOLE else 3):
            self.across(index, chunk, step).wait_recv()

    def drain(self, index, chunk):
        self.line(index, chunk, 0).wait_send()

        @pl.when(self.inside)
        def _():
            self.line(index, chunk, 1).wait_send()
            self.line(index, chunk, 2).wait_send()

        if chunk[4] == LINE:
            return
        for step in range(3 if chunk[4] == WHOLE else 2):
            self.over(index, chunk, step).wait_send()
        for step in range(4 if chunk[4] == WHOLE else 3):
            self.across(index, chunk, step).wait_send()


class Exchange:
    def __init__(self, depth, heads):
        self.depth, self.heads = depth, heads
        self.seq, self.fsdp = place_here()
        self.me = self.seq * depth + self.fsdp
        self.core, self.half = lax.rem(self.seq, 2), lax.div(self.seq, 4)
        self.head = lax.div(self.seq, 2) * depth + self.fsdp
        self.same = (self.half == self.core).astype(jnp.int32)

    def holder(self, k):
        return lax.div(k, self.depth) * 2 + self.half, lax.rem(k, self.depth)

    def owner(self, k):
        block = self.core * self.heads + k
        return lax.div(block, self.depth), lax.rem(block, self.depth)

    def away_head(self, k):
        return (k != self.head) | (self.half != self.core)

    def away_block(self, k):
        return self.core * self.heads + k != self.me

    def greet_holders(self, barrier):
        @pl.loop(0, self.heads)
        def _(k):
            @pl.when(self.away_head(k))
            def _():
                greet(barrier, *self.holder(k))

        return self.heads - self.same

    def greet_owners(self, barrier):
        @pl.loop(0, self.heads)
        def _(k):
            @pl.when(self.away_block(k))
            def _():
                greet(barrier, *self.owner(k))

        return self.heads - self.same


def as_matrix(block):
    return block.reshape(-1, block.shape[-1])


def turned(block, tile=256):
    return block.astype(float_type).T.astype(narrow_type)


def rows_of_vectors(ve, target):
    flat = as_matrix(ve[:, 0:32, :]).astype(float_type)
    target[...] = flat.T[0:16]


def by_feature_wide(block):
    return jnp.concatenate([block, jnp.zeros((112, block.shape[1]), block.dtype)], axis=0)


def selected(lens_ref, choice_ref, block, rows, lanes):
    place = lax.broadcasted_iota(jnp.int32, (rows, lanes), 0) + block * rows
    lane = lax.broadcasted_iota(jnp.int32, (rows, lanes), 1)
    chosen = jnp.zeros((rows, lanes), jnp.int32)
    start = jnp.int32(0)
    for image in range(lens_ref.shape[0]):
        end = start + lens_ref[image]
        chosen = jnp.where((place >= start) & (place < end), choice_ref[image] * RANK, chosen)
        start = end
    return jnp.where((lane >= chosen) & (lane < chosen + RANK), 1.0, 0.0).astype(float_type)


def stood_up(block):
    n, m = block.shape
    block = block.astype(float_type)
    if m < 128:
        block = jnp.concatenate([block, jnp.zeros((n, 128 - m), float_type)], axis=1)
    if n < 128:
        block = jnp.concatenate([block, jnp.zeros((128 - n, 128), float_type)], axis=0)
    return block.T[0:m].astype(narrow_type)


def attention_in_kernel(
    depth,
    halo,
    heads,
    chunks,
    lens_ref,
    choice_ref,
    tok_in,
    gains_in,
    biases_in,
    bias_in,
    wqkv,
    wout,
    a_att,
    b_att,
    a_exp,
    b_con,
    w2,
    a_con,
    b_exp_in,
    w1,
    fa_out,
    ve_out,
    f2,
    line_a,
    line_b,
    y_ref,
    rank_ref,
    fa,
    ve,
    proj,
    normed,
    vectors,
    tok,
    gains,
    biases,
    bias,
    b_exp,
    shard_f2,
    shard_a,
    shard_b,
    select,
    send,
    receive,
    local,
    piece_send,
    piece_receive,
    piece_local,
):
    gather, swap = Gather(depth, send, receive), Exchange(depth, heads)
    me, seq, fsdp = swap.me, swap.seq, swap.fsdp
    core, half, head, own = swap.core, swap.half, swap.head, heads
    features = normed.shape[1]
    wide = features + 256
    barrier = pltpu.get_barrier_semaphore()
    greet_neighbours(barrier, seq, fsdp, depth)
    waits = 3 + depth - 1 + swap.greet_owners(barrier)
    half_columns = line_a.shape[2]
    small = [
        (gains_in, gains.at[0:4]),
        (biases_in, biases.at[0:5]),
        (bias_in, bias),
        (b_exp_in, b_exp),
        (tok_in, tok),
    ]
    places = []
    for p in range(4):
        source = wqkv.at[:, pl.ds(p * features, features)] if p < 3 else wout
        places.append((source, fa.at[me, :, pl.ds(p * wide, features)]))
        places.append((a_att.at[p], fa.at[me, :, pl.ds(p * wide + features, 128)]))
        places.append((b_att.at[p], fa.at[me, :, pl.ds(p * wide + features + 128, 128)]))
    places.append((a_exp, fa.at[me, :, pl.ds(4 * wide, 128)]))
    places.append((b_con, fa.at[me, :, pl.ds(4 * wide + 128, 128)]))
    places.append((w2, shard_f2.at[0, :, pl.ds(0, features)]))
    places.append((a_con, shard_f2.at[0, :, pl.ds(features, 128)]))
    places.append((w1.at[:, pl.ds(0, half_columns)], shard_a.at[0]))
    places.append((w1.at[:, pl.ds(half_columns, half_columns)], shard_b.at[0]))
    placed = [pltpu.make_async_copy(a, b, local.at[i]) for i, (a, b) in enumerate(small + places)]
    for copy in placed:
        copy.start()
    for copy in placed[:3]:
        copy.wait()
    by_feature = jnp.concatenate(
        [gains[0:4].astype(float_type), biases[0:5].astype(float_type), jnp.zeros((7, 32), float_type)], axis=0
    )
    ve[me, 0:32] = stood_up(by_feature_wide(by_feature))
    ve[me, 32:48] = jnp.broadcast_to(bias[...].astype(float_type), (16, 128)).astype(narrow_type)
    for copy in placed[len(small) : len(small) + 14]:
        copy.wait()
    refs = {
        "ve": (ve, WHOLE, None),
        "fa": (fa, WHOLE, None),
        "f2": (f2, OPEN, shard_f2),
        "a": (line_a, LINE, shard_a),
        "b": (line_b, LINE, shard_b),
    }
    chunks = [
        (refs[name][0], rows, columns, flip) + refs[name][1:] for name, rows, columns, flip in chunks
    ]
    first_hidden = [i for i, chunk in enumerate(chunks) if chunk[4] != WHOLE][:1]
    pl.semaphore_wait(barrier, waits)
    early = [i for i, chunk in enumerate(chunks) if chunk[0] is fa or chunk[0] is ve]
    for index in early:
        gather.own(index, chunks[index])
    for copy in placed[3 : len(small)] + placed[len(small) + 14 :]:
        copy.wait()
    shard_f2[0, :, features + 128 : wide] = stood_up(b_exp[...])
    own_shards = [
        pltpu.make_async_copy(shard.at[0], full.at[slot], local.at[i])
        for i, (shard, full, slot) in enumerate(((shard_f2, f2, me), (shard_a, line_a, fsdp), (shard_b, line_b, fsdp)))
    ]
    for copy in own_shards:
        copy.start()
    select[...] = selected(lens_ref, choice_ref, me, *select.shape)
    base = core * (own - halo)
    slot = me - half * (own - halo)

    def piece(p, k):
        return remote(
            proj.at[p, k],
            y_ref.at[slot, p],
            piece_send.at[p, k],
            piece_receive.at[p, lax.rem(me, own)],
            *swap.holder(k),
        )

    def arrival(p, k):
        return remote(
            proj.at[p, 0],
            y_ref.at[core * own + k - base, p],
            piece_send.at[p, k],
            piece_receive.at[p, k],
            seq ^ CORES,
            fsdp,
        )

    def kept(p):
        return pltpu.make_async_copy(proj.at[p, head], y_ref.at[me - base, p], piece_local.at[p])

    def norm():
        rows_of_vectors(ve, vectors)
        rows = tok[...].astype(float_type)
        normed[...] = layer_norm(rows, vectors[0:1], vectors[4:5])[0].astype(narrow_type)

    def project(p):
        down = as_matrix(fa[:, :, p * wide + features : p * wide + features + 128])
        rank = (matmul(normed[...], down) * select[...]).astype(narrow_type)
        rank_ref[p] = rank

        @pl.loop(0, features // 256)
        def _(j):
            weight = as_matrix(fa[:, :, pl.ds(pl.multiple_of(p * wide + j * 256, 128), 256)])
            up = as_matrix(fa[pl.ds(j * 8, 8), :, p * wide + features + 128 : (p + 1) * wide])
            result = matmul(normed[...], weight) + transposed_right(rank, up)
            if p == 0:
                result = result + vectors[5:6, pl.ds(pl.multiple_of(j * 256, 128), 256)]
            proj[p, pl.ds(j * 4, 4)] = result.T.astype(narrow_type).reshape(4, 64, 256)

            @pl.loop(0, 4)
            def _(i):
                k = j * 4 + i

                @pl.when(swap.away_head(k))
                def _():
                    piece(p, k).start()

        @pl.when(half == core)
        def _():
            kept(p).start()

    after = {0: norm, 2: lambda: project(0), 4: lambda: project(1), 6: lambda: project(2)}
    after_attention = [i for i, chunk in enumerate(chunks) if chunk[0] is fa][-1]
    outs = [
        pltpu.make_async_copy(fa, fa_out, local.at[3]),
        pltpu.make_async_copy(ve, ve_out, local.at[4]),
    ]

    def store():
        for copy in outs:
            copy.start()

    def exchanged():
        @pl.loop(0, own)
        def _(k):
            @pl.when(swap.away_block(k))
            def _():
                for p in range(3):
                    arrival(p, k).wait_recv()

        @pl.when(half == core)
        def _():
            for p in range(3):
                kept(p).wait()

        first = jnp.where(core == 0, own - halo, own)
        over = remote(
            y_ref.at[pl.ds(first - base, halo), 1:3],
            y_ref.at[pl.ds(first - (own - halo) * (1 - core), halo), 1:3],
            piece_send.at[3, 0],
            piece_receive.at[3, 0],
            seq ^ CORES,
            fsdp,
        )
        over.start()
        return over

    steps = (gather.own, gather.inner, gather.outer, gather.first, gather.second, gather.third, gather.finish)
    for turn in range(DELAYS[0], len(chunks) + DELAYS[-1]):
        if turn == len(chunks) - 4:
            over = exchanged()
        for delay, step in zip(DELAYS, steps):
            index = turn - delay
            if not 0 <= index < len(chunks) or (delay == DELAYS[0] and index in early):
                continue
            chunk = chunks[index]
            if delay == DELAYS[1] and index in first_hidden:
                for copy in own_shards:
                    copy.wait()
            if chunk[4] == LINE and delay == 0:
                step = gather.arrive
            if chunk[4] == LINE and delay > 0:
                continue
            step(index, chunk)
            if delay == 3:
                after.get(index, lambda: None)()
                if index == after_attention:
                    store()

    over.wait()

    @pl.loop(0, heads)
    def _(k):
        @pl.when(swap.away_head(k))
        def _():
            for p in range(3):
                piece(p, k).wait_send()

    for index, chunk in enumerate(chunks):
        gather.drain(index, chunk)
    for copy in outs:
        copy.wait()


def attention_in(lengths, choice, tokens, arrays, halo, depth, heads, devices, collective):
    rows, features = tokens.shape
    wide = features + 256
    total = 4 * wide + 256
    share, hidden_share, hidden_total = features // devices, arrays[9].shape[0], arrays[12].shape[1]
    chunks = [("ve", slice(0, 48), slice(0, 128), 0)]
    for p in range(3):
        chunks.append(("fa", slice(0, share), slice(p * wide, p * wide + wide // 2), 0))
        chunks.append(("fa", slice(0, share), slice(p * wide + wide // 2, (p + 1) * wide), 1))
    middle = 3 * wide + (total - 3 * wide) // 2
    chunks.append(("fa", slice(0, share), slice(3 * wide, middle), 0))
    chunks.append(("fa", slice(0, share), slice(middle, total), 1))
    for part in range(0, hidden_share, 64):
        chunks.append(("f2", slice(part, part + 64), slice(0, wide // 2), 0))
        chunks.append(("f2", slice(part, part + 64), slice(wide // 2, wide), 1))
    for part in range(0, hidden_total // 2, 2048):
        chunks.append(("a", slice(0, share), slice(part, part + 2048), 0))
        chunks.append(("b", slice(0, share), slice(part, part + 2048), 1))
    copies = Gather.STEPS * len(chunks)
    return pl.pallas_call(
        functools.partial(attention_in_kernel, depth, halo, heads, chunks),
        out_shape=(
            jax.ShapeDtypeStruct((devices, share, total), narrow_type),
            jax.ShapeDtypeStruct((devices, 48, 128), narrow_type),
            jax.ShapeDtypeStruct((devices, hidden_share, wide), narrow_type),
            jax.ShapeDtypeStruct((depth, share, hidden_total // 2), narrow_type),
            jax.ShapeDtypeStruct((depth, share, hidden_total // 2), narrow_type),
            jax.ShapeDtypeStruct((heads + halo, 3, features // heads, rows), narrow_type),
            jax.ShapeDtypeStruct((3, rows, 128), narrow_type),
        ),
        in_specs=[IN_SMEM, IN_SMEM] + [ANYWHERE] * (1 + len(arrays)),
        out_specs=(ANYWHERE,) * 6 + (IN_VMEM,),
        scratch_shapes=[
            pltpu.VMEM((devices, share, total), narrow_type),
            pltpu.VMEM((devices, 48, 128), narrow_type),
            pltpu.VMEM((3, heads, features // heads, rows), narrow_type),
            pltpu.VMEM((rows, features), narrow_type),
            pltpu.VMEM((16, features), float_type),
            pltpu.VMEM((rows, features), narrow_type),
            pltpu.VMEM((4, share), narrow_type),
            pltpu.VMEM((5, share), narrow_type),
            pltpu.VMEM((1, 128), narrow_type),
            pltpu.VMEM((128, 128), narrow_type),
            pltpu.VMEM((1, hidden_share, wide), narrow_type),
            pltpu.VMEM((1, share, hidden_total // 2), narrow_type),
            pltpu.VMEM((1, share, hidden_total // 2), narrow_type),
            pltpu.VMEM((rows, 128), float_type),
            pltpu.SemaphoreType.DMA((copies,)),
            pltpu.SemaphoreType.DMA((copies,)),
            pltpu.SemaphoreType.DMA((24,)),
            pltpu.SemaphoreType.DMA((4, heads)),
            pltpu.SemaphoreType.DMA((4, heads)),
            pltpu.SemaphoreType.DMA((3,)),
        ],
        compiler_params=pltpu.CompilerParams(
            collective_id=collective, has_side_effects=True, vmem_limit_bytes=60 << 20
        ),
    )(lengths, choice, tokens, *arrays)


DELAYS = (-9, -6, -3, 0, 1, 2, 3)
HIDDEN_TILE = 512


def middle_kernel(
    depth,
    heads,
    lens_ref,
    choice_ref,
    att_ref,
    tok_ref,
    cot_ref,
    fa_in,
    ve,
    f2_in,
    line_a,
    line_b,
    ya,
    yb,
    xa,
    xb,
    result_ref,
    gm_ref,
    terms,
    gy_ref,
    fa,
    f2,
    f1,
    att_t,
    att,
    gatt_t,
    vectors,
    hidden_bias,
    middle,
    normal,
    normed,
    branch,
    grad_branch,
    grad_normed,
    ranks,
    rank_sums,
    select,
    send,
    receive,
    local,
    a_send,
    a_receive,
    b_send,
    b_receive,
    own_local,
):
    swap = Exchange(depth, heads)
    me, seq, fsdp = swap.me, swap.seq, swap.fsdp
    core, half, head, own = swap.core, swap.half, swap.head, heads
    devices, share = f1.shape[0], f1.shape[1]
    row_count, features = tok_ref.shape
    wide = features + 256
    tiles = f1.shape[2] // HIDDEN_TILE
    in_tile = HIDDEN_TILE // f2.shape[1]
    barrier = pltpu.get_barrier_semaphore()
    greet_neighbours(barrier, seq, fsdp, depth)
    waits = 3 + depth - 1 + swap.greet_owners(barrier) + swap.greet_holders(barrier)
    half_columns = line_a.shape[2]
    left, right = pl.ds(0, half_columns), pl.ds(half_columns, half_columns)
    lines = [
        (line, f1.at[pl.ds((seq ^ bit) * depth, depth), :, columns])
        for line, bit, columns in (
            (line_a, 0, left),
            (line_b, 0, right),
            (ya, SIDE_Y, left),
            (yb, SIDE_Y, right),
            (xa, SIDE_X, left),
            (xb, SIDE_X, right),
        )
    ]
    groups = [pl.ds((seq ^ k) * depth, depth) for k in range(8)]
    loads = (
        [pltpu.make_async_copy(fa_in.at[:, :, pl.ds(3 * wide, wide + 256)], fa, local.at[0])]
        + [pltpu.make_async_copy(line, place, local.at[1 + i]) for i, (line, place) in enumerate(lines)]
        + [pltpu.make_async_copy(f2_in.at[groups[k]], f2.at[groups[k]], local.at[7 + k]) for k in range(6)]
    )
    for copy in loads:
        copy.start()
    pl.semaphore_wait(barrier, waits)
    quarter = half_columns // 2
    x_side = lax.rem(lax.div(seq, 2), 2)

    def columns_of(start, parity):
        return pl.ds(pl.multiple_of(start + parity * quarter, 128), quarter)

    corners, diagonal = [], []
    for turn in range(2):
        for i, (line, via, to, start, parity) in enumerate(
            ((ya, SIDE_Y, SIDE_X, 0, 1 - x_side), (xb, SIDE_X, SIDE_Y, half_columns, x_side))
        ):
            at = 2 * turn + i
            parity = 1 - parity if turn else parity
            corners.append(
                remote(
                    line.at[:, :, columns_of(0, parity)],
                    f1.at[pl.ds((seq ^ via) * depth, depth), :, columns_of(start, parity)],
                    send.at[at],
                    receive.at[at],
                    seq ^ to,
                    fsdp,
                )
            )
            here = f1.at[
                pl.ds((seq ^ SIDE_X ^ SIDE_Y) * depth, depth),
                :,
                columns_of(start, 1 - x_side if turn else x_side),
            ]
            diagonal.append(remote(here, here, send.at[4 + at], receive.at[4 + at], seq ^ CORES, fsdp))

    tops, tails = pl.ds(0, wide // 2), pl.ds(wide // 2, wide // 2)
    f2_parts = ((SIDE_Y, SIDE_X, tops), (SIDE_X, SIDE_Y, tails))
    rows_over, rows_along = pl.ds(0, 64), pl.ds(64, 64)
    for i, (via, to, columns) in enumerate(f2_parts):
        line = pl.ds((seq ^ via) * depth, depth)
        corners.append(
            remote(
                f2_in.at[line, rows_over, columns],
                f2.at[line, rows_over, columns],
                send.at[8 + i],
                receive.at[8 + i],
                seq ^ to,
                fsdp,
            )
        )
    single = [
        remote(
            f2_in.at[pl.ds((seq ^ via) * depth + fsdp, 1), rows_along, columns],
            f2.at[pl.ds((seq ^ via) * depth + fsdp, 1), rows_along, columns],
            send.at[10 + i],
            receive.at[10 + i],
            seq ^ to,
            fsdp,
        )
        for i, (via, to, columns) in enumerate(f2_parts)
    ]
    far = f2.at[pl.ds((seq ^ SIDE_X ^ SIDE_Y) * depth + fsdp, 1), rows_along]
    along = [
        remote(
            far, far, send.at[11 + step], receive.at[11 + step], seq, lax.rem(fsdp + step, depth)
        )
        for step in range(1, depth)
    ]
    across = [
        remote(line, place, send.at[15 + i], receive.at[15 + i], seq ^ CORES, fsdp)
        for i, (line, place) in enumerate(lines)
    ]
    f2_across = remote(
        f2.at[groups[6]], f2.at[groups[6]], send.at[21], receive.at[21], seq ^ CORES, fsdp
    )

    def attended_piece(k):
        return remote(att_ref.at[k], att_t.at[head], a_send.at[k], a_receive.at[head], *swap.owner(k))

    def attended_arrival(k):
        return remote(att_ref.at[0], att_t.at[k], a_send.at[k], a_receive.at[k], seq ^ CORES, fsdp)

    attended_kept = pltpu.make_async_copy(att_ref.at[me - core * own], att_t.at[head], own_local.at[0])

    @pl.when(half == core)
    def _():
        attended_kept.start()

    @pl.loop(0, own)
    def _(step):
        k = lax.rem(step + me, own)

        @pl.when(swap.away_block(k))
        def _():
            attended_piece(k).start()

    for copy in single + corners[:2] + across:
        copy.start()
    select[...] = selected(lens_ref, choice_ref, me, *select.shape)
    rows_of_vectors(ve, vectors)
    for d in range(devices):
        hidden_bias[:, d * 128 : (d + 1) * 128] = ve[d, 32:48, :].astype(float_type)[0:8]
    grad_branch[...] = (vectors[3:4] * cot_ref[...].astype(float_type)).astype(narrow_type)
    loads[0].wait()
    contract_up = as_matrix(fa[:, :, wide + 128 : wide + 256])
    ranks[1] = (matmul(grad_branch[...], contract_up) * select[...]).astype(narrow_type)
    branch[...] = jnp.zeros_like(branch)
    grad_normed[...] = jnp.zeros_like(grad_normed)
    rank_sums[...] = jnp.zeros_like(rank_sums)

    @pl.loop(0, heads)
    def _(k):
        @pl.when(swap.away_head(k))
        def _():
            attended_arrival(k).wait_recv()

    @pl.when(half == core)
    def _():
        attended_kept.wait()

    for copy in corners[2:]:
        copy.start()
    for copy in single:
        copy.wait_recv()
    for copy in along:
        copy.start()

    for i in range(2):
        corners[i].wait_recv()
        diagonal[i].start()
    for j in range(4):
        att[:, j * 256 : (j + 1) * 256] = turned(as_matrix(att_t[4 * j : 4 * j + 4]))
    out_down = as_matrix(fa[:, :, features : features + 128])
    rank_out = (matmul(att[...], out_down) * select[...]).astype(narrow_type)
    ranks[2] = rank_out

    @pl.loop(0, 4)
    def _(j):
        at = pl.ds(pl.multiple_of(j * 256, 128), 256)
        weight = as_matrix(fa[:, :, at])
        up = as_matrix(fa[pl.ds(j * 8, 8), :, features + 128 : wide])
        mixed = matmul(att[...], weight) + transposed_right(rank_out, up) + vectors[6:7, at]
        middle[:, at] = tok_ref[:, at].astype(float_type) + vectors[1:2, at] * mixed

    shifted, normal_rows, scaling = layer_norm(middle[...], vectors[2:3], vectors[7:8])
    normal[...] = normal_rows
    normed[...] = shifted.astype(narrow_type)
    expand_down = as_matrix(fa[:, :, wide : wide + 128])
    rank_expand = (matmul(normed[...], expand_down) * select[...]).astype(narrow_type)
    ranks[0] = rank_expand
    ranks[3, 0:128] = turned(rank_expand)[:, 0:128]
    ranks[3, 128:256] = turned(rank_expand)[:, 128:256]
    ranks[4, 0:128] = turned(ranks[1])[:, 0:128]
    ranks[4, 128:256] = turned(ranks[1])[:, 128:256]
    for copy in loads[1:]:
        copy.wait()
    for copy in across + diagonal[:2]:
        copy.wait_recv()

    def hidden(k):
        @pl.when(k == 2)
        def _():
            for i in (2, 3):
                corners[i].wait_recv()
                diagonal[i].start()
            for i in (2, 3):
                diagonal[i].wait_recv()

        @pl.when(k == 5)
        def _():
            for copy in corners[4:] + along:
                copy.wait_recv()
            f2_across.start()

        @pl.when(k == 7)
        def _():
            f2_across.wait_recv()

        c = seq ^ k
        at = pl.ds(pl.multiple_of(c * HIDDEN_TILE, 128), HIDDEN_TILE)
        slots = pl.ds(c * in_tile, in_tile)
        expand = as_matrix(f1[:, :, at])
        contract = as_matrix(f2[slots, :, 0:features])
        down = as_matrix(f2[slots, :, features : features + 128])
        up = as_matrix(f2[slots, :, features + 128 : wide])
        before = matmul(normed[...], expand) + transposed_right(ranks[0], up) + hidden_bias[0:1, at]
        total = 0.5 * (1.0 + lax.erf(before * 0.7071067811865476))
        density = jnp.exp(-0.5 * before * before) * 0.3989422804014327
        active = (before * total).astype(narrow_type)
        slope = total + before * density
        branch[...] += matmul(active, contract)
        rank_sums[0] += matmul(active, down)
        grad_active = transposed_right(grad_branch[...], contract) + transposed_right(ranks[1], down)
        grad_hidden = (grad_active * slope).astype(narrow_type)
        rank_sums[1] += matmul(grad_hidden, up)
        grad_normed[...] += transposed_right(grad_hidden, expand)
        turned_expand = jnp.concatenate([ranks[3, 0:128], ranks[3, 128:256]], axis=1)
        turned_contract = jnp.concatenate([ranks[4, 0:128], ranks[4, 128:256]], axis=1)
        grad_up = matmul(turned_expand, grad_hidden).astype(narrow_type)
        grad_down = matmul(turned_contract, active).astype(narrow_type)
        for i in range(in_tile):
            terms[c * in_tile + i, 96:224] = grad_up[:, i * 128 : (i + 1) * 128]
            terms[c * in_tile + i, 224:352] = grad_down[:, i * 128 : (i + 1) * 128]

    pl.loop(0, tiles)(hidden)
    rank_contract = (rank_sums[0] * select[...]).astype(narrow_type)
    grad_rank_expand = (rank_sums[1] * select[...]).astype(narrow_type)
    gradient = grad_normed[...] + transposed_right(grad_rank_expand, expand_down)
    gm_ref[...] = cot_ref[...].astype(float_type) + norm_backward(gradient, vectors[2:3], normal[...], scaling)
    grad_mixed = (vectors[1:2] * gm_ref[...]).astype(narrow_type)
    out_up = as_matrix(fa[:, :, features + 128 : wide])
    grad_rank_out = (matmul(grad_mixed, out_up) * select[...]).astype(narrow_type)

    def gradient_piece(k):
        return remote(
            gatt_t.at[k], gy_ref.at[lax.rem(me, own)], b_send.at[k], b_receive.at[lax.rem(me, own)], *swap.holder(k)
        )

    def gradient_arrival(k):
        return remote(gatt_t.at[0], gy_ref.at[k], b_send.at[k], b_receive.at[k], seq ^ CORES, fsdp)

    gradient_kept = pltpu.make_async_copy(gatt_t.at[head], gy_ref.at[lax.rem(me, own)], own_local.at[1])

    @pl.loop(0, 4)
    def _(j):
        slots = pl.ds(j * 8, 8)
        weight = as_matrix(fa[slots, :, 0:features])
        down = as_matrix(fa[slots, :, features : features + 128])
        rows = transposed_right(grad_mixed, weight) + transposed_right(grad_rank_out, down)
        gatt_t[pl.ds(j * 4, 4)] = rows.T.astype(narrow_type).reshape(4, 64, 256)

        @pl.loop(0, 4)
        def _(i):
            k = j * 4 + i

            @pl.when(swap.away_head(k))
            def _():
                gradient_piece(k).start()

    @pl.when(half == core)
    def _():
        gradient_kept.start()

    up_rows = transposed_right(rank_contract, contract_up)
    result_ref[...] = (
        middle[...] + vectors[3:4] * (branch[...] + vectors[8:9] + up_rows)
    ).astype(narrow_type)
    shaped = (devices, share, 128)
    terms[:, 0:32] = matmul(as_matrix(att_t[...]), grad_rank_out).astype(narrow_type).reshape(shaped)
    terms[:, 32:64] = transposed_left(grad_mixed, rank_out).astype(narrow_type).reshape(shaped)
    terms[:, 64:96] = transposed_left(normed[...], grad_rank_expand).astype(narrow_type).reshape(shaped)
    terms[:, 352:384] = transposed_left(grad_branch[...], rank_contract).astype(narrow_type).reshape(shaped)

    @pl.loop(0, own)
    def _(k):
        @pl.when(swap.away_block(k))
        def _():
            gradient_arrival(k).wait_recv()
            attended_piece(k).wait_send()

    @pl.when(half == core)
    def _():
        gradient_kept.wait()

    @pl.loop(0, heads)
    def _(k):
        @pl.when(swap.away_head(k))
        def _():
            gradient_piece(k).wait_send()

    for copy in single + along + corners + diagonal + across + [f2_across]:
        copy.wait_send()


def middle_part(lengths, choice, att, tokens, cotangent, fa, ve, f2, lines, depth, collective):
    heads, width, rows = att.shape
    features = tokens.shape[1]
    wide = features + 256
    devices, hidden_share = f2.shape[0], f2.shape[1]
    share, hidden_total = features // devices, 2 * lines[0].shape[2]
    copies = 22

    def wide_rows():
        return pltpu.VMEM((rows, features), float_type)

    def narrow_rows():
        return pltpu.VMEM((rows, features), narrow_type)

    return pl.pallas_call(
        functools.partial(middle_kernel, depth, heads),
        out_shape=(
            jax.ShapeDtypeStruct((rows, features), narrow_type),
            jax.ShapeDtypeStruct((rows, features), float_type),
            jax.ShapeDtypeStruct((devices, 384, 128), narrow_type),
            jax.ShapeDtypeStruct((heads, width, rows), narrow_type),
        ),
        in_specs=[IN_SMEM, IN_SMEM, IN_VMEM, IN_VMEM, IN_VMEM, ANYWHERE, IN_VMEM] + [ANYWHERE] * 7,
        out_specs=(IN_VMEM, IN_VMEM, IN_VMEM, ANYWHERE),
        scratch_shapes=[
            pltpu.VMEM((devices, share, wide + 256), narrow_type),
            pltpu.VMEM(f2.shape, narrow_type),
            pltpu.VMEM((devices, share, hidden_total), narrow_type),
            pltpu.VMEM((heads, width, rows), narrow_type),
            narrow_rows(),
            pltpu.VMEM((heads, width, rows), narrow_type),
            pltpu.VMEM((16, features), float_type),
            pltpu.VMEM((8, hidden_total), float_type),
            wide_rows(),
            wide_rows(),
            narrow_rows(),
            wide_rows(),
            narrow_rows(),
            wide_rows(),
            pltpu.VMEM((5, rows, 128), narrow_type),
            pltpu.VMEM((2, rows, 128), float_type),
            pltpu.VMEM((rows, 128), float_type),
            pltpu.SemaphoreType.DMA((copies,)),
            pltpu.SemaphoreType.DMA((copies,)),
            pltpu.SemaphoreType.DMA((13,)),
            pltpu.SemaphoreType.DMA((heads,)),
            pltpu.SemaphoreType.DMA((heads,)),
            pltpu.SemaphoreType.DMA((heads,)),
            pltpu.SemaphoreType.DMA((heads,)),
            pltpu.SemaphoreType.DMA((2,)),
        ],
        compiler_params=pltpu.CompilerParams(
            collective_id=collective, has_side_effects=True, vmem_limit_bytes=54 << 20
        ),
    )(lengths, choice, att, tokens, cotangent, fa, ve, f2, *lines)


class Reduce:
    COPIES = 16

    def __init__(self, depth, base, terms, first, second, third, fourth, send, receive):
        self.depth, self.base, self.terms = depth, base, terms
        self.buffers = first, second, third, fourth
        self.send, self.receive = send, receive
        self.seq, self.fsdp = place_here()
        self.core, self.x, self.y = lax.rem(self.seq, 2), lax.rem(lax.div(self.seq, 2), 2), lax.div(self.seq, 4)
        half = terms.shape[1] // 2
        self.halves = (slice(0, half), slice(half, 2 * half))

    def copy(self, step, source, target, seq, fsdp):
        at = self.base + step
        return remote(source, target, self.send.at[at], self.receive.at[at], seq, fsdp)

    def to_core(self):
        first = self.buffers[0]
        lines = [self.terms.at[pl.ds((2 * t + 1 - self.core) * self.depth, self.depth)] for t in range(4)]
        return [self.copy(t, lines[t], first.at[t], self.seq ^ CORES, self.fsdp) for t in range(4)]

    def to_sides(self):
        first, second = self.buffers[:2]
        x, y = self.x, self.y
        copies = []
        for j in range(2):
            copies.append(
                self.copy(
                    4 + j,
                    first.at[2 * j + 1 - x, :, self.halves[0]],
                    second.at[0, j],
                    self.seq ^ SIDE_X,
                    self.fsdp,
                )
            )
            copies.append(
                self.copy(
                    6 + j,
                    first.at[2 * (1 - y) + j, :, self.halves[1]],
                    second.at[1, j],
                    self.seq ^ SIDE_Y,
                    self.fsdp,
                )
            )
        return copies

    def to_corner(self):
        second, third = self.buffers[1:3]
        return [
            self.copy(8, second.at[0, 1 - self.y], third.at[0], self.seq ^ SIDE_Y, self.fsdp),
            self.copy(9, second.at[1, 1 - self.x], third.at[1], self.seq ^ SIDE_X, self.fsdp),
        ]

    def to_line(self):
        third, fourth = self.buffers[2:]
        copies = []
        for step in range(1, self.depth):
            to = lax.rem(self.fsdp + step, self.depth)
            for j in range(2):
                copies.append(
                    self.copy(8 + 2 * step + j, third.at[j, to], fourth.at[j, step], self.seq, to)
                )
        return copies

    def add(self, target, other):
        @pl.loop(0, self.depth)
        def _(i):
            target[i] = (target[i].astype(float_type) + other[i].astype(float_type)).astype(narrow_type)

    def begin(self):
        for copy in self.to_core():
            copy.start()

    def sides(self):
        first = self.buffers[0]
        for t, copy in enumerate(self.to_core()):
            copy.wait_recv()
            self.add(first.at[t], self.terms.at[pl.ds((2 * t + self.core) * self.depth, self.depth)])
        for copy in self.to_sides():
            copy.start()

    def corner(self):
        first, second = self.buffers[:2]
        copies = self.to_sides()
        for j in range(2):
            copies[2 * j].wait_recv()
            self.add(second.at[0, j], first.at[2 * j + self.x, :, self.halves[0]])
            copies[2 * j + 1].wait_recv()
            self.add(second.at[1, j], first.at[2 * self.y + j, :, self.halves[1]])
        for copy in self.to_corner():
            copy.start()

    def line(self):
        second, third = self.buffers[1:3]
        copies = self.to_corner()
        copies[0].wait_recv()
        self.add(third.at[0], second.at[0, self.y])
        copies[1].wait_recv()
        self.add(third.at[1], second.at[1, self.x])
        for copy in self.to_line():
            copy.start()

    def end(self, out):
        third, fourth = self.buffers[2:]
        for copy in self.to_line():
            copy.wait_recv()
        for j in range(2):
            total = third[j, self.fsdp].astype(float_type)
            for step in range(1, self.depth):
                total = total + fourth[j, step].astype(float_type)
            out[self.halves[j]] = total

    def drain(self):
        for copy in self.to_core() + self.to_sides() + self.to_corner() + self.to_line():
            copy.wait_send()


def last_kernel(
    depth,
    heads,
    halo,
    lens_ref,
    choice_ref,
    dq_ref,
    dkv_ref,
    tok_ref,
    gm_ref,
    fa_in,
    ve,
    rank_ref,
    early_terms,
    gradient_ref,
    early_ref,
    late_ref,
    fa,
    vectors,
    normed_t,
    normal,
    grad_rank,
    total,
    arrived,
    arrived_rows,
    merged,
    other,
    late_terms,
    early_buffers,
    late_buffers,
    select,
    send,
    receive,
    local,
    piece_send,
    piece_receive,
    piece_local,
):
    swap = Exchange(depth, heads)
    me, seq, fsdp = swap.me, swap.seq, swap.fsdp
    core, half, head, own = swap.core, swap.half, swap.head, heads
    row_count, features = tok_ref.shape
    devices, share = fa.shape[0], fa.shape[1]
    wide = features + 256
    barrier = pltpu.get_barrier_semaphore()
    greet_neighbours(barrier, seq, fsdp, depth)
    waits = 3 + depth - 1 + swap.greet_holders(barrier)
    load = pltpu.make_async_copy(fa_in.at[:, :, pl.ds(0, 3 * wide)], fa, local.at[0])
    load.start()
    pl.semaphore_wait(barrier, waits)
    over = remote(
        dkv_ref.at[pl.ds(jnp.where(core == 0, own, 0), halo)],
        other,
        piece_send.at[3, 0], piece_receive.at[3, 0], seq ^ CORES, fsdp)
    over.start()
    early = Reduce(depth, 0, early_terms, *early_buffers, send, receive)
    late = [
        Reduce(
            depth, Reduce.COPIES * (p + 1), late_terms.at[p], *[b.at[p] for b in late_buffers], send, receive
        )
        for p in range(3)
    ]
    shared = jnp.where(core == 0, own - halo, 0)
    shift = core * halo

    def in_shared(k):
        return (k >= shared) & (k < shared + halo)

    def sent(p, k, source):
        return remote(
            source, arrived.at[p, head], piece_send.at[p, k], piece_receive.at[p, head], *swap.owner(k)
        )

    def launch(p, k, source):
        @pl.when(swap.away_block(k))
        def _():
            sent(p, k, source).start()

        @pl.when(core * own + k == me)
        def _():
            pltpu.make_async_copy(source, arrived.at[p, head], piece_local.at[p]).start()

    def arrival(p, k):
        return remote(
            dq_ref.at[0], arrived.at[p, k], piece_send.at[p, k], piece_receive.at[p, k], seq ^ CORES, fsdp
        )

    @pl.loop(0, own)
    def _(step):
        k = lax.rem(step + me, own)
        launch(0, k, dq_ref.at[k])

    over.wait_recv()

    @pl.loop(0, halo)
    def _(i):
        for part in range(2):
            merged[i, part] = (
                dkv_ref[shared + shift + i, part].astype(float_type) + other[i, part].astype(float_type)
            ).astype(narrow_type)

    for p in (1, 2):

        @pl.loop(0, own)
        def _(step, p=p):
            k = lax.rem(step + me, own)

            @pl.when(in_shared(k))
            def _():
                launch(p, k, merged.at[jnp.clip(k - shared, 0, halo - 1), p - 1])

            @pl.when(jnp.logical_not(in_shared(k)))
            def _():
                launch(p, k, dkv_ref.at[k + shift, p - 1])

    early.begin()
    rows_of_vectors(ve, vectors)
    select[...] = selected(lens_ref, choice_ref, me, *select.shape)
    early.sides()
    shifted, normal_rows, scaling = layer_norm(tok_ref[...].astype(float_type), vectors[0:1], vectors[4:5])
    normal[...] = normal_rows
    for j in range(4):
        normed_t[j * 256 : (j + 1) * 256] = turned(shifted[:, j * 256 : (j + 1) * 256])
    early.corner()
    load.wait()

    def gather_part(p):
        @pl.loop(0, heads)
        def _(k):
            @pl.when(swap.away_head(k))
            def _():
                arrival(p, k).wait_recv()

        @pl.when(half == core)
        def _():
            pltpu.make_async_copy(dq_ref.at[0], arrived.at[p, head], piece_local.at[p]).wait()

    def ranks_back(p):
        for j in range(4):
            arrived_rows[:, j * 256 : (j + 1) * 256] = turned(as_matrix(arrived[p, 4 * j : 4 * j + 4]))
        up = as_matrix(fa[:, :, p * wide + features + 128 : (p + 1) * wide])
        grad_rank[...] = (matmul(arrived_rows[...], up) * select[...]).astype(narrow_type)
        shaped = (devices, share, 128)
        late_terms[p, :, 0:32] = matmul(normed_t[...], grad_rank[...]).astype(narrow_type).reshape(shaped)
        late_terms[p, :, 32:64] = (
            matmul(as_matrix(arrived[p]), rank_ref[p]).astype(narrow_type).reshape(shaped)
        )

    def project_back(p, tiles):
        @pl.loop(*tiles)
        def _(j):
            at = pl.ds(pl.multiple_of(j * 256, 128), 256)
            slots = pl.ds(j * 8, 8)
            weight = as_matrix(fa[slots, :, p * wide : p * wide + features])
            down = as_matrix(fa[slots, :, p * wide + features : p * wide + features + 128])
            term = transposed_right(arrived_rows[...], weight) + transposed_right(grad_rank[...], down)
            if p == 0:
                total[:, at] = term
            else:
                total[:, at] += term

    gather_part(0)
    ranks_back(0)
    late[0].begin()
    project_back(0, (0, 4))
    late[0].sides()
    gather_part(1)
    ranks_back(1)
    late[1].begin()
    project_back(1, (0, 4))
    late[0].corner()
    early.line()
    late[1].sides()
    gather_part(2)
    ranks_back(2)
    late[2].begin()
    late[0].line()
    late[1].corner()
    project_back(2, (0, 2))
    late[2].sides()
    project_back(2, (2, 4))
    late[1].line()
    late[2].corner()
    gradient_ref[...] = gm_ref[...] + norm_backward(total[...], vectors[0:1], normal[...], scaling)
    late[2].line()
    early.end(early_ref)
    late[0].end(late_ref.at[0])
    late[1].end(late_ref.at[1])
    late[2].end(late_ref.at[2])
    for reduce in [early] + late:
        reduce.drain()

    @pl.loop(0, own)
    def _(k):
        @pl.when(swap.away_block(k))
        def _():
            for p in range(3):
                sent(p, k, dq_ref.at[k]).wait_send()

    over.wait_send()


def last_part(lengths, choice, dq, dkv, tokens, grad_middle, fa, ve, rank, terms, depth, collective):
    heads = dq.shape[0]
    halo = dkv.shape[0] - heads
    rows, features = tokens.shape
    wide = features + 256
    devices, share = fa.shape[0], fa.shape[1]

    def buffers(count, size):
        return [
            pltpu.VMEM(count + (4, depth, size, 128), narrow_type),
            pltpu.VMEM(count + (2, 2, depth, size // 2, 128), narrow_type),
            pltpu.VMEM(count + (2, depth, size // 2, 128), narrow_type),
            pltpu.VMEM(count + (2, depth, size // 2, 128), narrow_type),
        ]

    return pl.pallas_call(
        functools.partial(last_kernel, depth, heads, halo),
        out_shape=(
            jax.ShapeDtypeStruct((rows, features), float_type),
            jax.ShapeDtypeStruct((terms.shape[1], 128), float_type),
            jax.ShapeDtypeStruct((3, 2 * share, 128), float_type),
        ),
        in_specs=[IN_SMEM] * 2 + [IN_VMEM] * 4 + [ANYWHERE] + [IN_VMEM] * 3,
        out_specs=(IN_VMEM, IN_VMEM, IN_VMEM),
        scratch_shapes=[
            pltpu.VMEM((devices, share, 3 * wide), narrow_type),
            pltpu.VMEM((16, features), float_type),
            pltpu.VMEM((features, rows), narrow_type),
            pltpu.VMEM((rows, features), float_type),
            pltpu.VMEM((rows, 128), narrow_type),
            pltpu.VMEM((rows, features), float_type),
            pltpu.VMEM((3, heads, features // heads, rows), narrow_type),
            pltpu.VMEM((rows, features), narrow_type),
            pltpu.VMEM((halo,) + dkv.shape[1:], narrow_type),
            pltpu.VMEM((halo,) + dkv.shape[1:], narrow_type),
            pltpu.VMEM((3, devices, 2 * share, 128), narrow_type),
            buffers((), terms.shape[1]),
            buffers((3,), 2 * share),
            pltpu.VMEM((rows, 128), float_type),
            pltpu.SemaphoreType.DMA((4 * Reduce.COPIES,)),
            pltpu.SemaphoreType.DMA((4 * Reduce.COPIES,)),
            pltpu.SemaphoreType.DMA((1,)),
            pltpu.SemaphoreType.DMA((4, heads)),
            pltpu.SemaphoreType.DMA((4, heads)),
            pltpu.SemaphoreType.DMA((3,)),
        ],
        compiler_params=pltpu.CompilerParams(
            collective_id=collective, has_side_effects=True, vmem_limit_bytes=44 << 20
        ),
    )(lengths, choice, dq, dkv, tokens, grad_middle, fa, ve, rank, terms)


def spread_kernel(result_in, gradient_in, early, late, result, gradient, down, up, exp_down, exp_up, con_down, con_up):
    share = down.shape[1]
    result[...] = result_in[...]
    gradient[...] = gradient_in[...]
    for p in range(4):
        first = late[p, 0:share] if p < 3 else early[0:share]
        second = late[p, share : 2 * share] if p < 3 else early[share : 2 * share]
        down[p] = first
        up[p] = second
    exp_down[...] = early[64:96]
    exp_up[...] = early[96:224]
    con_down[...] = early[224:352].T
    con_up[...] = early[352:384]


def spread(result, gradient, early, late):
    share = late.shape[1] // 2
    shapes = ((4, share, 128), (4, share, 128), (share, 128), (128, 128), (128, 128), (share, 128))
    return pl.pallas_call(
        spread_kernel,
        out_shape=tuple(jax.ShapeDtypeStruct(a.shape, a.dtype) for a in (result, gradient))
        + tuple(jax.ShapeDtypeStruct(shape, float_type) for shape in shapes),
        in_specs=[IN_VMEM] * 4,
        out_specs=(IN_VMEM,) * 8,
        compiler_params=pltpu.CompilerParams(vmem_limit_bytes=24 << 20),
    )(result, gradient, early, late)


BIG = 32768.0


def image_range(lens_ref, first, last):
    low = high = start = jnp.int32(0)
    for image in range(lens_ref.shape[0]):
        end = start + lens_ref[image]
        low = jnp.where((start <= first) & (first < end), start, low)
        high = jnp.where((start <= last) & (last < end), end - 1, high)
        start = end
    return low, high


def image_edges(lens_ref, marks, rows):
    row = lax.broadcasted_iota(jnp.int32, (marks, rows), 0)
    starts = jnp.full((marks, rows), 1 << 30, jnp.int32)
    ends = jnp.zeros((marks, rows), jnp.int32)
    start = jnp.int32(0)
    for image in range(lens_ref.shape[0]):
        end = start + lens_ref[image]
        starts, ends = jnp.where(row == image, start, starts), jnp.where(row == image, end, ends)
        start = end
    return starts, ends


class Blocks:
    def __init__(self, lens_ref, own, halo, rows, marks):
        core = lax.rem(lax.axis_index("seq"), 2)
        self.lens_ref, self.own, self.rows, self.slots = lens_ref, own, rows, own + halo
        self.base = core * (own - halo)
        self.shift = core * halo
        self.starts, self.ends = image_edges(lens_ref, marks, rows)
        self.lane = lax.broadcasted_iota(jnp.int32, (marks, rows), 1)

    def marks(self, slot):
        place = self.lane + (self.base + slot) * self.rows
        return jnp.where((place >= self.starts) & (place < self.ends), 1.0, 0.0).astype(float_type)

    def reach(self, slot):
        first = (self.base + slot) * self.rows
        low, high = image_range(self.lens_ref, first, first + self.rows - 1)
        return lax.div(low, self.rows) - self.base, lax.div(high, self.rows) - self.base


def forward_kernel(
    own, halo, step, lens_ref, x_ref, att_ref, lse_ref, out_ref, keys, queries, values, score, weight, item_row, item_low
):
    slots, _, width, rows = x_ref.shape
    blocks = Blocks(lens_ref, own, halo, rows, keys.shape[1] - width)
    scale = width**-0.5

    @pl.loop(0, slots)
    def _(slot):
        block = jnp.concatenate([x_ref[slot, 1].astype(float_type), (blocks.marks(slot) - 1.0) * BIG], axis=0)
        keys[pl.ds(pl.multiple_of(slot * rows, rows), rows)] = block.T.astype(narrow_type)
        values[slot, 0:width] = x_ref[slot, 2]
        values[slot, width:] = jnp.ones((16, rows), narrow_type)

    def prepare(i, total):
        slot = i + blocks.shift
        queries[i] = jnp.concatenate([x_ref[slot, 0].astype(float_type) * scale, blocks.marks(slot)], axis=0).astype(narrow_type)
        low, high = blocks.reach(slot)
        count = lax.div(high - low + step, step)
        low = jnp.minimum(low, slots - step * count)

        @pl.loop(0, count)
        def _(j):
            item_row[total + j] = i
            item_low[total + j] = low + j * step

        return total + count

    total = lax.fori_loop(0, own, prepare, jnp.int32(0))
    item_row[total] = item_row[total - 1]
    item_low[total] = item_low[total - 1]

    def scored(t, side):
        at = pl.multiple_of(item_low[t] * rows, rows)
        score[side] = matmul(keys[pl.ds(at, step * rows)], queries[item_row[t]])

    def mixed(t):
        low = item_low[t]
        result = matmul(values[low], weight[0:rows])
        for j in range(1, step):
            result += matmul(values[low + j], weight[j * rows : (j + 1) * rows])
        return result

    def soften(fresh, side, highest):
        highest = jnp.where(fresh, -1e30, highest)
        s = score[side]
        higher = jnp.maximum(highest, jnp.max(s, axis=0, keepdims=True))
        fade = jnp.where(fresh, 0.0, jnp.exp(highest - higher))
        return higher, fade, jnp.exp(s - higher).astype(narrow_type)

    def finish(t, out, fade, highest):
        i = item_row[t]
        out = out * fade + mixed(t)
        summed = out[width : width + 1]
        whole = out[0:width] / summed
        att_ref[i] = whole.astype(narrow_type)
        out_ref[i] = whole
        lse_ref[i] = jnp.broadcast_to(highest + jnp.log(summed), (8, rows))
        return out

    def turn(t, side, carry):
        highest, out, fade = carry
        out = finish(t - 1, out, fade, highest)
        scored(t + 1, 1 - side)
        highest, fade, p = soften(item_row[t] != item_row[t - 1], side, highest)
        weight[...] = p
        return highest, out, fade

    scored(0, 0)
    scored(1, 1)
    highest, fade, p = soften(True, 0, jnp.zeros((1, rows), float_type))
    weight[...] = p
    carry = (highest, jnp.zeros((width + 16, rows), float_type), fade)
    pairs = lax.div(total - 1, 2)
    carry = lax.fori_loop(0, pairs, lambda j, c: turn(2 * j + 2, 0, turn(2 * j + 1, 1, c)), carry)
    carry = lax.fori_loop(2 * pairs + 1, total, lambda t, c: turn(t, 1, c), carry)
    highest, out, fade = carry
    finish(total - 1, out, fade, highest)


def attention_forward(lengths, x, own, halo, step=2):
    slots, _, width, rows = x.shape
    marks = -(-lengths.shape[0] // 16) * 16
    most = own * (slots // step + 2) + 8
    return pl.pallas_call(
        functools.partial(forward_kernel, own, halo, step),
        out_shape=(
            jax.ShapeDtypeStruct((own, width, rows), narrow_type),
            jax.ShapeDtypeStruct((own, 8, rows), float_type),
            jax.ShapeDtypeStruct((own, width, rows), float_type),
        ),
        in_specs=[IN_SMEM, IN_VMEM],
        out_specs=(IN_VMEM, IN_VMEM, IN_VMEM),
        scratch_shapes=[
            pltpu.VMEM((slots * rows, width + marks), narrow_type),
            pltpu.VMEM((own, width + marks, rows), narrow_type),
            pltpu.VMEM((slots, width + 16, rows), narrow_type),
            pltpu.VMEM((2, step * rows, rows), float_type),
            pltpu.VMEM((step * rows, rows), narrow_type),
            pltpu.SMEM((most,), jnp.int32),
            pltpu.SMEM((most,), jnp.int32),
        ],
        compiler_params=pltpu.CompilerParams(vmem_limit_bytes=32 << 20),
    )(lengths, x)


def backward_kernel(
    own, halo, step, lens_ref, x_ref, g_ref, lse_ref, out_ref, dq_ref, dkv_ref,
    keys, values, queries, offset, dq, score, grad_prob, weight, grad_score, item_slot, item_low,
):
    slots, _, width, rows = x_ref.shape
    blocks = Blocks(lens_ref, own, halo, rows, keys.shape[2] - width)
    scale = width**-0.5

    def prepare(slot, total):
        block = jnp.concatenate([x_ref[slot, 1].astype(float_type), (blocks.marks(slot) - 1.0) * BIG], axis=0)
        keys[slot] = block.T.astype(narrow_type)
        values[slot] = x_ref[slot, 2].astype(float_type).T.astype(narrow_type)
        dkv_ref[slot] = jnp.zeros((2, width, rows), narrow_type)
        low, high = blocks.reach(slot)
        low = jnp.maximum(low - blocks.shift, 0)
        high = jnp.minimum(high - blocks.shift, own - 1)
        count = jnp.maximum(lax.div(high - low + step, step), 0)
        low = jnp.minimum(low, own - step * count)

        @pl.loop(0, count)
        def _(j):
            item_slot[total + j] = slot
            item_low[total + j] = low + j * step

        return total + count

    total = lax.fori_loop(0, slots, prepare, jnp.int32(0))
    item_slot[total] = item_slot[total - 1]
    item_low[total] = item_low[total - 1]

    @pl.loop(0, own)
    def _(i):
        slot = i + blocks.shift
        q = x_ref[slot, 0].astype(float_type) * scale
        queries[i] = jnp.concatenate([q, blocks.marks(slot)], axis=0).astype(narrow_type)
        g = g_ref[i].astype(float_type)
        offset[i] = jnp.broadcast_to(jnp.sum(g * out_ref[i], axis=0, keepdims=True), (8, rows))
        dq[i] = jnp.zeros((width, rows), float_type)

    def scored(t, side):
        slot, low = item_slot[t], item_low[t]
        for j in range(step):
            score[side, j] = matmul(keys[slot], queries[low + j])
            grad_prob[side, j] = matmul(values[slot], g_ref[low + j])

    def soften(t, side):
        low = item_low[t]
        done = []
        for j in range(step):
            p = jnp.exp(score[side, j] - lse_ref[low + j, 0:1])
            d = p * (grad_prob[side, j] - offset[low + j, 0:1])
            done.append((p.astype(narrow_type), d.astype(narrow_type)))
        return done

    def keep(done):
        for j in range(step):
            weight[j] = done[j][0]
            grad_score[j] = done[j][1]

    def mixed(t, fresh, dk, dv):
        slot, low = item_slot[t], item_low[t]
        dk = jnp.where(fresh, 0.0, dk)
        dv = jnp.where(fresh, 0.0, dv)
        key = x_ref[slot, 1]
        for j in range(step):
            dk += transposed_right(queries[low + j, 0:width], grad_score[j])
            dv += transposed_right(g_ref[low + j], weight[j])
        for j in range(step):
            dq[low + j] += matmul(key, grad_score[j])
        dkv_ref[slot, 0] = dk.astype(narrow_type)
        dkv_ref[slot, 1] = dv.astype(narrow_type)
        return dk, dv

    def turn(t, side, carry):
        fresh = (t == 1) | (item_slot[t - 1] != item_slot[jnp.maximum(t - 2, 0)])
        scored(t + 1, 1 - side)
        done = soften(t, side)
        carry = mixed(t - 1, fresh, *carry)
        keep(done)
        return carry

    scored(0, 0)
    scored(1, 1)
    keep(soften(0, 0))
    zero = jnp.zeros((width, rows), float_type)
    pairs = lax.div(total - 1, 2)
    carry = lax.fori_loop(0, pairs, lambda j, c: turn(2 * j + 2, 0, turn(2 * j + 1, 1, c)), (zero, zero))
    carry = lax.fori_loop(2 * pairs + 1, total, lambda t, c: turn(t, 1, c), carry)
    mixed(total - 1, item_slot[total - 1] != item_slot[jnp.maximum(total - 2, 0)], *carry)

    @pl.loop(0, own)
    def _(i):
        dq_ref[i] = (dq[i] * scale).astype(narrow_type)


def attention_backward(lengths, x, g, lse, out, own, halo, step=1):
    slots, _, width, rows = x.shape
    marks = -(-lengths.shape[0] // 16) * 16
    most = slots * (own // step + 2) + 8
    return pl.pallas_call(
        functools.partial(backward_kernel, own, halo, step),
        out_shape=(
            jax.ShapeDtypeStruct((own, width, rows), narrow_type),
            jax.ShapeDtypeStruct((slots, 2, width, rows), narrow_type),
        ),
        in_specs=[IN_SMEM] + [IN_VMEM] * 4,
        out_specs=(IN_VMEM, IN_VMEM),
        scratch_shapes=[
            pltpu.VMEM((slots, rows, width + marks), narrow_type),
            pltpu.VMEM((slots, rows, width), narrow_type),
            pltpu.VMEM((own, width + marks, rows), narrow_type),
            pltpu.VMEM((own, 8, rows), float_type),
            pltpu.VMEM((own, width, rows), float_type),
            pltpu.VMEM((2, step, rows, rows), float_type),
            pltpu.VMEM((2, step, rows, rows), float_type),
            pltpu.VMEM((step, rows, rows), narrow_type),
            pltpu.VMEM((step, rows, rows), narrow_type),
            pltpu.SMEM((most,), jnp.int32),
            pltpu.SMEM((most,), jnp.int32),
        ],
        compiler_params=pltpu.CompilerParams(vmem_limit_bytes=40 << 20),
    )(lengths, x, g, lse, out)


def layer_on_slice(
    tokens,
    lengths,
    adapter_choice,
    gain_rows,
    bias_rows,
    query_key_value,
    output_weight,
    expand_weight,
    expand_bias,
    contract_weight,
    adapter_in_attention,
    adapter_out_attention,
    adapter_in_expand,
    adapter_out_expand,
    adapter_in_contract,
    adapter_out_contract,
    cotangent,
):
    row_count = tokens.shape[0]
    depth = lax.axis_size("fsdp")
    devices = lax.axis_size(("seq", "fsdp"))
    own = devices // 2
    halo = -(-(LONGEST - 1) // row_count)

    arrays = (
        gain_rows,
        bias_rows,
        expand_bias[None],
        query_key_value,
        output_weight,
        adapter_in_attention,
        adapter_out_attention.transpose(0, 2, 1),
        adapter_in_expand,
        adapter_out_contract.T,
        contract_weight,
        adapter_in_contract,
        adapter_out_expand,
        expand_weight,
    )
    fa, ve, f2, line_a, line_b, on_heads, rank = attention_in(
        lengths, adapter_choice, tokens, arrays, halo, depth, HEADS, devices, 1
    )

    def swapped(line, bit):
        route = [
            (seq * depth + fsdp, (seq ^ bit) * depth + fsdp)
            for seq in range(devices // depth)
            for fsdp in range(depth)
        ]
        return lax.ppermute(line, ("seq", "fsdp"), route)

    lines = (
        line_a,
        line_b,
        swapped(line_a, SIDE_Y),
        swapped(line_b, SIDE_Y),
        swapped(line_a, SIDE_X),
        swapped(line_b, SIDE_X),
    )
    attended, log_totals, attended_wide = attention_forward(lengths, on_heads, own, halo)
    result, grad_middle, terms, grad_on_heads = middle_part(
        lengths, adapter_choice, attended, tokens, cotangent, fa, ve, f2, lines, depth, 2
    )
    grad_queries, grad_key_values = attention_backward(
        lengths, on_heads, grad_on_heads, log_totals, attended_wide, own, halo
    )
    input_gradient, early, late = last_part(
        lengths, adapter_choice, grad_queries, grad_key_values, tokens, grad_middle, fa, ve, rank, terms, depth, 3
    )
    outs = spread(result, input_gradient, early, late)
    return outs[:3] + (outs[3].transpose(0, 2, 1),) + outs[4:7] + (outs[7].T,)


def solution(mesh):
    per_device = layer_on_slice if dict(mesh.shape) == {"seq": 8, "fsdp": 4} else general_layer
    placed = (
        P(("seq", "fsdp"), None),
        P(),
        P(),
        P(None, ("seq", "fsdp")),
        P(None, ("seq", "fsdp")),
        P(("seq", "fsdp"), None),
        P(("seq", "fsdp"), None),
        P(("seq", "fsdp"), None),
        P(("seq", "fsdp")),
        P(("seq", "fsdp"), None),
        P(None, ("seq", "fsdp"), None),
        P(None, None, ("seq", "fsdp")),
        P(("seq", "fsdp"), None),
        P(None, ("seq", "fsdp")),
        P(("seq", "fsdp"), None),
        P(None, ("seq", "fsdp")),
        P(("seq", "fsdp"), None),
    )
    return jax.shard_map(
        per_device,
        mesh=mesh,
        in_specs=placed,
        out_specs=(
            P(("seq", "fsdp"), None),
            P(("seq", "fsdp"), None),
            P(None, ("seq", "fsdp"), None),
            P(None, None, ("seq", "fsdp")),
            P(("seq", "fsdp"), None),
            P(None, ("seq", "fsdp")),
            P(("seq", "fsdp"), None),
            P(None, ("seq", "fsdp")),
        ),
        check_vma=False,
    )
```

```python
import functools
import jax
import jax.numpy as jnp
from jax import lax
from jax.experimental import pallas as pl
from jax.experimental.pallas import tpu as pltpu
from jax.sharding import PartitionSpec as P

HEADS = 16
RANK = 16
HOPS = 6
EDGE = 1408
LONGEST = 1370


epsilon = 1e-06
float_type = jnp.float32
narrow_type = jnp.bfloat16


def passed_along(block, axis, distance):
    devices = range(lax.axis_size(axis))
    route = [(i - distance, i) for i in devices if i - distance in devices]
    return lax.ppermute(block, axis, route)


def layer_norm(inputs_row, gain_row, bias_row):
    center = inputs_row - jnp.mean(inputs_row, axis=-1, keepdims=True)
    scaling = lax.rsqrt(jnp.mean(center * center, axis=-1, keepdims=True) + epsilon)
    normal = center * scaling
    return (normal * gain_row + bias_row, normal, scaling)


def norm_backward(gradient, gain_row, normal, scaling):
    weighted = gradient * gain_row
    return scaling * (
        weighted
        - jnp.mean(weighted, axis=-1, keepdims=True)
        - normal * jnp.mean(weighted * normal, axis=-1, keepdims=True)
    )


def matmul(first_operand, second_operand):
    return jnp.dot(first_operand, second_operand, preferred_element_type=float_type)


def transposed_left(first_operand, second_operand):
    return lax.dot_general(
        first_operand, second_operand, (((0,), (0,)), ((), ())), preferred_element_type=float_type
    )


def transposed_right(first_operand, second_operand):
    return lax.dot_general(
        first_operand, second_operand, (((1,), (1,)), ((), ())), preferred_element_type=float_type
    )


def gelu_slope(hidden_pre):
    cumulative = 0.5 * (1.0 + lax.erf(hidden_pre * 0.7071067811865476))
    density = jnp.exp(-0.5 * hidden_pre * hidden_pre) * 0.3989422804014327
    return cumulative + hidden_pre * density


def general_layer(
    tokens,
    lengths,
    adapter_choice,
    gain_rows,
    bias_rows,
    query_key_value,
    output_weight,
    expand_weight,
    expand_bias,
    contract_weight,
    adapter_in_attention,
    adapter_out_attention,
    adapter_in_expand,
    adapter_out_expand,
    adapter_in_contract,
    adapter_out_contract,
    cotangent,
):
    gathered = (
        lax.all_gather(gain_rows, ("seq", "fsdp"), axis=1, tiled=True),
        lax.all_gather(bias_rows, ("seq", "fsdp"), axis=1, tiled=True),
        lax.all_gather(query_key_value, ("seq", "fsdp"), axis=0, tiled=True),
        lax.all_gather(output_weight, ("seq", "fsdp"), axis=0, tiled=True),
        lax.all_gather(expand_weight, ("seq", "fsdp"), axis=0, tiled=True),
        lax.all_gather(expand_bias, ("seq", "fsdp"), axis=0, tiled=True),
        lax.all_gather(contract_weight, ("seq", "fsdp"), axis=0, tiled=True),
        lax.all_gather(adapter_in_attention, ("seq", "fsdp"), axis=1, tiled=True),
        lax.all_gather(adapter_out_attention, ("seq", "fsdp"), axis=2, tiled=True),
        lax.all_gather(adapter_in_expand, ("seq", "fsdp"), axis=0, tiled=True),
        lax.all_gather(adapter_out_expand, ("seq", "fsdp"), axis=1, tiled=True),
        lax.all_gather(adapter_in_contract, ("seq", "fsdp"), axis=0, tiled=True),
        lax.all_gather(adapter_out_contract, ("seq", "fsdp"), axis=1, tiled=True),
    )
    (
        gains_full,
        biases_full,
        qkv_full,
        output_full,
        expand_full,
        expand_bias_full,
        contract_full,
        attention_down,
        attention_up,
        expand_down,
        expand_up,
        contract_down,
        contract_up,
    ) = gathered
    gains_wide = gains_full.astype(float_type)
    biases_wide = biases_full.astype(float_type)
    row_count, features = tokens.shape
    device_count = lax.axis_size(("seq", "fsdp"))
    position = lax.axis_index(("seq", "fsdp"))
    head_width = features // HEADS
    pair_width = 2 * head_width
    pair_count = HEADS // 2
    scaling_score = head_width ** (-0.5)
    rank_width = attention_down.shape[2]
    window_start = HOPS * row_count - EDGE
    window_rows = row_count + 2 * EDGE
    image_ends = jnp.cumsum(lengths)
    places = (
        position * row_count
        - HOPS * row_count
        + jnp.arange((2 * HOPS + 1) * row_count, dtype=jnp.int32)
    )
    image_of = jnp.sum((places[:, None] >= image_ends[None, :]).astype(jnp.int32), axis=1)
    image_of = jnp.where((places >= 0) & (places < device_count * row_count), image_of, -1)
    own_image = image_of[HOPS * row_count : (HOPS + 1) * row_count]
    key_image = image_of[window_start : window_start + window_rows]
    allowed = own_image[:, None] == key_image[None, :]
    matches = own_image[:, None] == jnp.arange(lengths.shape[0], dtype=jnp.int32)[None, :]
    chosen = jnp.sum(jnp.where(matches, adapter_choice[None, :], 0), axis=1)
    select = (jnp.arange(rank_width, dtype=jnp.int32)[None, :] // RANK == chosen[:, None]).astype(
        float_type
    )
    residual = tokens.astype(float_type)
    normed_first, normal_first, scaling_first = layer_norm(residual, gains_wide[0], biases_wide[0])
    normed_first = normed_first.astype(narrow_type)
    rank_qkv = (
        jnp.einsum(
            "td,pdr->tpr", normed_first, attention_down[:3], preferred_element_type=float_type
        )
        * select[:, None, :]
    ).astype(narrow_type)
    adapted_qkv = jnp.einsum(
        "tpr,prd->tpd", rank_qkv, attention_up[:3], preferred_element_type=float_type
    ).reshape(row_count, 3 * features)
    query_bias = jnp.concatenate([biases_wide[1], jnp.zeros((2 * features,), float_type)])
    projected = (matmul(normed_first, qkv_full) + adapted_qkv + query_bias).astype(narrow_type)
    queries = projected[:, :features]
    key_values = projected[:, features:]
    from_lower = []
    from_higher = []
    for distance in range(1, HOPS + 1):
        from_lower.append(passed_along(key_values, ("seq", "fsdp"), distance))
        from_higher.append(passed_along(key_values, ("seq", "fsdp"), -distance))
    beside_all = jnp.concatenate(from_lower[::-1] + [key_values] + from_higher, axis=0)
    window = beside_all[window_start : window_start + window_rows]

    def pair_slices(pair_index):
        offset = pair_index * pair_width
        query_part = lax.dynamic_slice_in_dim(queries, offset, pair_width, 1).reshape(
            row_count, 2, head_width
        )
        key_part = lax.dynamic_slice_in_dim(window, offset, pair_width, 1).reshape(
            window_rows, 2, head_width
        )
        value_part = lax.dynamic_slice_in_dim(window, features + offset, pair_width, 1).reshape(
            window_rows, 2, head_width
        )
        scores = (
            jnp.einsum("qhd,khd->hqk", query_part, key_part, preferred_element_type=float_type)
            * scaling_score
        )
        scores = jnp.where(allowed[None], scores, -1e30)
        return (query_part, key_part, value_part, scores)

    def pair_forward(pair_index):
        query_part, key_part, value_part, scores = pair_slices(pair_index)
        highest = jnp.max(scores, axis=2, keepdims=True)
        weights = jnp.exp(scores - highest)
        denominator = jnp.sum(weights, axis=2, keepdims=True)
        soft = (weights / denominator).astype(narrow_type)
        mixed_part = jnp.einsum("hqk,khd->qhd", soft, value_part, preferred_element_type=float_type)
        return (
            mixed_part.reshape(row_count, pair_width),
            (highest + jnp.log(denominator))[:, :, 0],
        )

    attended_pairs, log_totals = lax.map(pair_forward, jnp.arange(pair_count))
    attended = attended_pairs.transpose(1, 0, 2).reshape(row_count, features).astype(narrow_type)
    rank_out = (matmul(attended, attention_down[3]) * select).astype(narrow_type)
    mixed = matmul(attended, output_full) + biases_wide[2] + matmul(rank_out, attention_up[3])
    middle = residual + gains_wide[1] * mixed
    normed_second, normal_second, scaling_second = layer_norm(middle, gains_wide[2], biases_wide[3])
    normed_second = normed_second.astype(narrow_type)
    rank_expand = (matmul(normed_second, expand_down) * select).astype(narrow_type)
    hidden_pre = (
        matmul(normed_second, expand_full)
        + expand_bias_full.astype(float_type)
        + matmul(rank_expand, expand_up)
    )
    active = jax.nn.gelu(hidden_pre, approximate=False).astype(narrow_type)
    rank_contract = (matmul(active, contract_down) * select).astype(narrow_type)
    branch = matmul(active, contract_full) + biases_wide[4] + matmul(rank_contract, contract_up)
    result = (middle + gains_wide[3] * branch).astype(narrow_type)
    renewed = lax.optimization_barrier(
        (
            gain_rows,
            bias_rows,
            query_key_value,
            output_weight,
            expand_weight,
            expand_bias,
            contract_weight,
            adapter_in_attention,
            adapter_out_attention,
            adapter_in_expand,
            adapter_out_expand,
            adapter_in_contract,
            adapter_out_contract,
            cotangent,
        )
    )
    gathered = (
        lax.all_gather(renewed[0], ("seq", "fsdp"), axis=1, tiled=True),
        lax.all_gather(renewed[1], ("seq", "fsdp"), axis=1, tiled=True),
        lax.all_gather(renewed[2], ("seq", "fsdp"), axis=0, tiled=True),
        lax.all_gather(renewed[3], ("seq", "fsdp"), axis=0, tiled=True),
        lax.all_gather(renewed[4], ("seq", "fsdp"), axis=0, tiled=True),
        lax.all_gather(renewed[5], ("seq", "fsdp"), axis=0, tiled=True),
        lax.all_gather(renewed[6], ("seq", "fsdp"), axis=0, tiled=True),
        lax.all_gather(renewed[7], ("seq", "fsdp"), axis=1, tiled=True),
        lax.all_gather(renewed[8], ("seq", "fsdp"), axis=2, tiled=True),
        lax.all_gather(renewed[9], ("seq", "fsdp"), axis=0, tiled=True),
        lax.all_gather(renewed[10], ("seq", "fsdp"), axis=1, tiled=True),
        lax.all_gather(renewed[11], ("seq", "fsdp"), axis=0, tiled=True),
        lax.all_gather(renewed[12], ("seq", "fsdp"), axis=1, tiled=True),
    )
    (
        gains_full,
        biases_full,
        qkv_full,
        output_full,
        expand_full,
        expand_bias_full,
        contract_full,
        attention_down,
        attention_up,
        expand_down,
        expand_up,
        contract_down,
        contract_up,
    ) = gathered
    gains_wide = gains_full.astype(float_type)
    gradient_out = cotangent.astype(float_type)
    grad_branch = (gains_wide[3] * gradient_out).astype(narrow_type)
    grad_rank_contract = (transposed_right(grad_branch, contract_up) * select).astype(narrow_type)
    grad_contract_down = transposed_left(active, grad_rank_contract)
    grad_contract_up = transposed_left(rank_contract, grad_branch)
    grad_active = transposed_right(grad_branch, contract_full) + transposed_right(
        grad_rank_contract, contract_down
    )
    grad_hidden = (grad_active * gelu_slope(hidden_pre)).astype(narrow_type)
    grad_rank_expand = (transposed_right(grad_hidden, expand_up) * select).astype(narrow_type)
    grad_expand_down = transposed_left(normed_second, grad_rank_expand)
    grad_expand_up = transposed_left(rank_expand, grad_hidden)
    grad_normed_second = transposed_right(grad_hidden, expand_full) + transposed_right(
        grad_rank_expand, expand_down
    )
    grad_middle = gradient_out + norm_backward(
        grad_normed_second, gains_wide[2], normal_second, scaling_second
    )
    grad_mixed = (gains_wide[1] * grad_middle).astype(narrow_type)
    grad_rank_out = (transposed_right(grad_mixed, attention_up[3]) * select).astype(narrow_type)
    grad_out_down = transposed_left(attended, grad_rank_out)
    grad_out_up = transposed_left(rank_out, grad_mixed)
    grad_attended = (
        transposed_right(grad_mixed, output_full)
        + transposed_right(grad_rank_out, attention_down[3])
    ).astype(narrow_type)

    def pair_backward(pair_index):
        query_part, key_part, value_part, scores = pair_slices(pair_index)
        grad_part = lax.dynamic_slice_in_dim(
            grad_attended, pair_index * pair_width, pair_width, 1
        ).reshape(row_count, 2, head_width)
        log_pair = log_totals[pair_index]
        probable = jnp.exp(scores - log_pair[:, :, None])
        grad_probable = jnp.einsum(
            "qhd,khd->hqk", grad_part, value_part, preferred_element_type=float_type
        )
        grad_scores = probable * (
            grad_probable - jnp.sum(grad_probable * probable, axis=2, keepdims=True)
        )
        grad_scores = grad_scores.astype(narrow_type)
        grad_query = (
            jnp.einsum("hqk,khd->qhd", grad_scores, key_part, preferred_element_type=float_type)
            * scaling_score
        )
        grad_key = (
            jnp.einsum("hqk,qhd->khd", grad_scores, query_part, preferred_element_type=float_type)
            * scaling_score
        )
        grad_value = jnp.einsum(
            "hqk,qhd->khd",
            probable.astype(narrow_type),
            grad_part,
            preferred_element_type=float_type,
        )
        return (
            grad_query.reshape(row_count, pair_width),
            grad_key.reshape(window_rows, pair_width),
            grad_value.reshape(window_rows, pair_width),
        )

    grad_query_pairs, grad_key_pairs, grad_value_pairs = lax.map(
        pair_backward, jnp.arange(pair_count)
    )
    grad_queries = grad_query_pairs.transpose(1, 0, 2).reshape(row_count, features)
    grad_keys = grad_key_pairs.transpose(1, 0, 2).reshape(window_rows, features)
    grad_values = grad_value_pairs.transpose(1, 0, 2).reshape(window_rows, features)
    grad_window = jnp.concatenate([grad_keys, grad_values], axis=1)
    padded_grads = jnp.pad(grad_window, ((window_start, window_start), (0, 0)))
    grad_pairs = padded_grads[HOPS * row_count : (HOPS + 1) * row_count]
    for distance in range(1, HOPS + 1):
        lower_piece = padded_grads[
            (HOPS - distance) * row_count : (HOPS - distance + 1) * row_count
        ]
        higher_piece = padded_grads[
            (HOPS + distance) * row_count : (HOPS + distance + 1) * row_count
        ]
        grad_pairs = grad_pairs + passed_along(
            lower_piece.astype(jnp.bfloat16), ("seq", "fsdp"), -distance
        ).astype(lower_piece.dtype)
        grad_pairs = grad_pairs + passed_along(
            higher_piece.astype(jnp.bfloat16), ("seq", "fsdp"), distance
        ).astype(higher_piece.dtype)
    grad_projected = jnp.concatenate([grad_queries, grad_pairs], axis=1).astype(narrow_type)
    grad_blocks = grad_projected.reshape(row_count, 3, features)
    grad_rank_qkv = (
        jnp.einsum("tpd,prd->tpr", grad_blocks, attention_up[:3], preferred_element_type=float_type)
        * select[:, None, :]
    ).astype(narrow_type)
    grad_qkv_down = jnp.einsum(
        "td,tpr->pdr", normed_first, grad_rank_qkv, preferred_element_type=float_type
    )
    grad_qkv_up = jnp.einsum(
        "tpr,tpd->prd", rank_qkv, grad_blocks, preferred_element_type=float_type
    )
    grad_normed_first = transposed_right(grad_projected, qkv_full) + jnp.einsum(
        "tpr,pdr->td", grad_rank_qkv, attention_down[:3], preferred_element_type=float_type
    )
    input_gradient = grad_middle + norm_backward(
        grad_normed_first, gains_wide[0], normal_first, scaling_first
    )
    grad_attention_down = jnp.concatenate([grad_qkv_down, grad_out_down[None]], axis=0)
    grad_attention_up = jnp.concatenate([grad_qkv_up, grad_out_up[None]], axis=0)
    summed = (
        lax.psum_scatter(grad_attention_down, ("seq", "fsdp"), scatter_dimension=1, tiled=True),
        lax.psum_scatter(grad_attention_up, ("seq", "fsdp"), scatter_dimension=2, tiled=True),
        lax.psum_scatter(grad_expand_down, ("seq", "fsdp"), scatter_dimension=0, tiled=True),
        lax.psum_scatter(grad_expand_up, ("seq", "fsdp"), scatter_dimension=1, tiled=True),
        lax.psum_scatter(grad_contract_down, ("seq", "fsdp"), scatter_dimension=0, tiled=True),
        lax.psum_scatter(grad_contract_up, ("seq", "fsdp"), scatter_dimension=1, tiled=True),
    )
    return (
        result,
        input_gradient,
        summed[0],
        summed[1],
        summed[2],
        summed[3],
        summed[4],
        summed[5],
    )


MESH_ID = pl.DeviceIdType.MESH
CORES, SIDE_X, SIDE_Y = 1, 2, 4
ANYWHERE = pl.BlockSpec(memory_space=pl.ANY)
IN_VMEM = pl.BlockSpec(memory_space=pltpu.VMEM)
IN_SMEM = pl.BlockSpec(memory_space=pltpu.SMEM)


def place_here():
    return lax.axis_index("seq"), lax.axis_index("fsdp")


def remote(source, target, send, receive, seq, fsdp):
    return pltpu.make_async_remote_copy(
        src_ref=source,
        dst_ref=target,
        send_sem=send,
        recv_sem=receive,
        device_id=(seq, fsdp),
        device_id_type=MESH_ID,
    )


def greet(barrier, seq, fsdp):
    pl.semaphore_signal(barrier, 1, device_id=(seq, fsdp), device_id_type=MESH_ID)


def greet_neighbours(barrier, seq, fsdp, depth):
    for bit in (CORES, SIDE_X, SIDE_Y):
        greet(barrier, seq ^ bit, fsdp)
    for step in range(1, depth):
        greet(barrier, seq, lax.rem(fsdp + step, depth))


WHOLE, OPEN, LINE = 0, 1, 2


class Gather:
    STEPS = 10

    def __init__(self, depth, send, receive):
        self.depth, self.send, self.receive = depth, send, receive
        self.seq, self.fsdp = place_here()
        self.me = self.seq * depth + self.fsdp
        self.inside = (self.fsdp == 1) | (self.fsdp == 2)

    def copy(self, index, step, source, target, seq, fsdp):
        at = index * self.STEPS + step
        return remote(source, target, self.send.at[at], self.receive.at[at], seq, fsdp)

    def part(self, chunk, at_seq, first, count):
        full, rows, columns, _, kind, _ = chunk
        base = 0 if kind == LINE else at_seq * self.depth
        return full.at[pl.ds(base + first, count), rows, columns]

    def group(self, chunk, at_seq):
        return self.part(chunk, at_seq, 0, self.depth)

    def sides(self, chunk):
        return (SIDE_X, SIDE_Y) if chunk[3] else (SIDE_Y, SIDE_X)

    def line(self, index, chunk, step):
        pair = lax.div(self.fsdp, 2)
        if step == 0:
            piece, to = self.part(chunk, self.seq, self.fsdp, 1), self.fsdp ^ 1
            if chunk[5] is not None:
                source = chunk[5].at[pl.ds(0, 1), chunk[1], chunk[2]]
                return self.copy(index, step, source, piece, self.seq, to)
        elif step == 1:
            piece, to = self.part(chunk, self.seq, 2 * pair, 2), 3 - self.fsdp
        else:
            piece, to = self.part(chunk, self.seq, 2 - 2 * pair, 2), self.fsdp ^ 1
        return self.copy(index, step, piece, piece, self.seq, to)

    def over(self, index, chunk, step):
        a, b = self.sides(chunk)
        piece = self.group(chunk, self.seq ^ a if step == 2 else self.seq)
        return self.copy(index, 3 + step, piece, piece, self.seq ^ (b if step else a), self.fsdp)

    def across(self, index, chunk, step):
        a, b = self.sides(chunk)
        piece = self.group(chunk, self.seq ^ (0, a, b, a ^ b)[step])
        return self.copy(index, 6 + step, piece, piece, self.seq ^ CORES, self.fsdp)

    def own(self, index, chunk):
        self.line(index, chunk, 0).start()

    def inner(self, index, chunk):
        @pl.when(self.inside)
        def _():
            self.line(index, chunk, 0).wait_recv()
            self.line(index, chunk, 1).start()

    def outer(self, index, chunk):
        @pl.when(self.inside)
        def _():
            self.line(index, chunk, 1).wait_recv()
            self.line(index, chunk, 2).start()

    def arrive(self, index, chunk):
        @pl.when(jnp.logical_not(self.inside))
        def _():
            self.line(index, chunk, 0).wait_recv()
            self.line(index, chunk, 2).wait_recv()

    def first(self, index, chunk):
        self.arrive(index, chunk)
        self.over(index, chunk, 0).start()
        self.over(index, chunk, 1).start()
        self.across(index, chunk, 0).start()

    def second(self, index, chunk):
        self.over(index, chunk, 0).wait_recv()
        if chunk[4] == WHOLE:
            self.over(index, chunk, 2).start()
        self.across(index, chunk, 1).start()

    def third(self, index, chunk):
        self.over(index, chunk, 1).wait_recv()
        self.across(index, chunk, 2).start()
        if chunk[4] == WHOLE:
            self.over(index, chunk, 2).wait_recv()
            self.across(index, chunk, 3).start()

    def finish(self, index, chunk):
        for step in range(4 if chunk[4] == WHOLE else 3):
            self.across(index, chunk, step).wait_recv()

    def drain(self, index, chunk):
        self.line(index, chunk, 0).wait_send()

        @pl.when(self.inside)
        def _():
            self.line(index, chunk, 1).wait_send()
            self.line(index, chunk, 2).wait_send()

        if chunk[4] == LINE:
            return
        for step in range(3 if chunk[4] == WHOLE else 2):
            self.over(index, chunk, step).wait_send()
        for step in range(4 if chunk[4] == WHOLE else 3):
            self.across(index, chunk, step).wait_send()


class Exchange:
    def __init__(self, depth, heads):
        self.depth, self.heads = depth, heads
        self.seq, self.fsdp = place_here()
        self.me = self.seq * depth + self.fsdp
        self.core, self.half = lax.rem(self.seq, 2), lax.div(self.seq, 4)
        self.head = lax.div(self.seq, 2) * depth + self.fsdp
        self.same = (self.half == self.core).astype(jnp.int32)

    def holder(self, k):
        return lax.div(k, self.depth) * 2 + self.half, lax.rem(k, self.depth)

    def owner(self, k):
        block = self.core * self.heads + k
        return lax.div(block, self.depth), lax.rem(block, self.depth)

    def away_head(self, k):
        return (k != self.head) | (self.half != self.core)

    def away_block(self, k):
        return self.core * self.heads + k != self.me

    def greet_holders(self, barrier):
        @pl.loop(0, self.heads)
        def _(k):
            @pl.when(self.away_head(k))
            def _():
                greet(barrier, *self.holder(k))

        return self.heads - self.same

    def greet_owners(self, barrier):
        @pl.loop(0, self.heads)
        def _(k):
            @pl.when(self.away_block(k))
            def _():
                greet(barrier, *self.owner(k))

        return self.heads - self.same


def as_matrix(block):
    return block.reshape(-1, block.shape[-1])


def turned(block, tile=256):
    return block.astype(float_type).T.astype(narrow_type)


def rows_of_vectors(ve, target):
    flat = as_matrix(ve[:, 0:32, :]).astype(float_type)
    target[...] = flat.T[0:16]


def by_feature_wide(block):
    return jnp.concatenate([block, jnp.zeros((112, block.shape[1]), block.dtype)], axis=0)


def selected(lens_ref, choice_ref, block, rows, lanes):
    place = lax.broadcasted_iota(jnp.int32, (rows, lanes), 0) + block * rows
    lane = lax.broadcasted_iota(jnp.int32, (rows, lanes), 1)
    chosen = jnp.zeros((rows, lanes), jnp.int32)
    start = jnp.int32(0)
    for image in range(lens_ref.shape[0]):
        end = start + lens_ref[image]
        chosen = jnp.where((place >= start) & (place < end), choice_ref[image] * RANK, chosen)
        start = end
    return jnp.where((lane >= chosen) & (lane < chosen + RANK), 1.0, 0.0).astype(float_type)


def stood_up(block):
    n, m = block.shape
    block = block.astype(float_type)
    if m < 128:
        block = jnp.concatenate([block, jnp.zeros((n, 128 - m), float_type)], axis=1)
    if n < 128:
        block = jnp.concatenate([block, jnp.zeros((128 - n, 128), float_type)], axis=0)
    return block.T[0:m].astype(narrow_type)


def attention_in_kernel(
    depth,
    halo,
    heads,
    chunks,
    lens_ref,
    choice_ref,
    tok_in,
    gains_in,
    biases_in,
    bias_in,
    wqkv,
    wout,
    a_att,
    b_att,
    a_exp,
    b_con,
    w2,
    a_con,
    b_exp_in,
    w1,
    fa_out,
    ve_out,
    f2,
    line_a,
    line_b,
    y_ref,
    rank_ref,
    fa,
    ve,
    proj,
    normed,
    vectors,
    tok,
    gains,
    biases,
    bias,
    b_exp,
    shard_f2,
    shard_a,
    shard_b,
    select,
    send,
    receive,
    local,
    piece_send,
    piece_receive,
    piece_local,
):
    gather, swap = Gather(depth, send, receive), Exchange(depth, heads)
    me, seq, fsdp = swap.me, swap.seq, swap.fsdp
    core, half, head, own = swap.core, swap.half, swap.head, heads
    features = normed.shape[1]
    wide = features + 256
    barrier = pltpu.get_barrier_semaphore()
    greet_neighbours(barrier, seq, fsdp, depth)
    waits = 3 + depth - 1 + swap.greet_owners(barrier)
    half_columns = line_a.shape[2]
    small = [
        (gains_in, gains.at[0:4]),
        (biases_in, biases.at[0:5]),
        (bias_in, bias),
        (b_exp_in, b_exp),
        (tok_in, tok),
    ]
    places = []
    for p in range(4):
        source = wqkv.at[:, pl.ds(p * features, features)] if p < 3 else wout
        places.append((source, fa.at[me, :, pl.ds(p * wide, features)]))
        places.append((a_att.at[p], fa.at[me, :, pl.ds(p * wide + features, 128)]))
        places.append((b_att.at[p], fa.at[me, :, pl.ds(p * wide + features + 128, 128)]))
    places.append((a_exp, fa.at[me, :, pl.ds(4 * wide, 128)]))
    places.append((b_con, fa.at[me, :, pl.ds(4 * wide + 128, 128)]))
    places.append((w2, shard_f2.at[0, :, pl.ds(0, features)]))
    places.append((a_con, shard_f2.at[0, :, pl.ds(features, 128)]))
    places.append((w1.at[:, pl.ds(0, half_columns)], shard_a.at[0]))
    places.append((w1.at[:, pl.ds(half_columns, half_columns)], shard_b.at[0]))
    placed = [pltpu.make_async_copy(a, b, local.at[i]) for i, (a, b) in enumerate(small + places)]
    for copy in placed:
        copy.start()
    for copy in placed[:3]:
        copy.wait()
    by_feature = jnp.concatenate(
        [gains[0:4].astype(float_type), biases[0:5].astype(float_type), jnp.zeros((7, 32), float_type)], axis=0
    )
    ve[me, 0:32] = stood_up(by_feature_wide(by_feature))
    ve[me, 32:48] = jnp.broadcast_to(bias[...].astype(float_type), (16, 128)).astype(narrow_type)
    for copy in placed[len(small) : len(small) + 14]:
        copy.wait()
    refs = {
        "ve": (ve, WHOLE, None),
        "fa": (fa, WHOLE, None),
        "f2": (f2, OPEN, shard_f2),
        "a": (line_a, LINE, shard_a),
        "b": (line_b, LINE, shard_b),
    }
    chunks = [
        (refs[name][0], rows, columns, flip) + refs[name][1:] for name, rows, columns, flip in chunks
    ]
    first_hidden = [i for i, chunk in enumerate(chunks) if chunk[4] != WHOLE][:1]
    pl.semaphore_wait(barrier, waits)
    early = [i for i, chunk in enumerate(chunks) if chunk[0] is fa or chunk[0] is ve]
    for index in early:
        gather.own(index, chunks[index])
    for copy in placed[3 : len(small)] + placed[len(small) + 14 :]:
        copy.wait()
    shard_f2[0, :, features + 128 : wide] = stood_up(b_exp[...])
    own_shards = [
        pltpu.make_async_copy(shard.at[0], full.at[slot], local.at[i])
        for i, (shard, full, slot) in enumerate(((shard_f2, f2, me), (shard_a, line_a, fsdp), (shard_b, line_b, fsdp)))
    ]
    for copy in own_shards:
        copy.start()
    select[...] = selected(lens_ref, choice_ref, me, *select.shape)
    base = core * (own - halo)
    slot = me - half * (own - halo)

    def piece(p, k):
        return remote(
            proj.at[p, k],
            y_ref.at[slot, p],
            piece_send.at[p, k],
            piece_receive.at[p, lax.rem(me, own)],
            *swap.holder(k),
        )

    def arrival(p, k):
        return remote(
            proj.at[p, 0],
            y_ref.at[core * own + k - base, p],
            piece_send.at[p, k],
            piece_receive.at[p, k],
            seq ^ CORES,
            fsdp,
        )

    def kept(p):
        return pltpu.make_async_copy(proj.at[p, head], y_ref.at[me - base, p], piece_local.at[p])

    def norm():
        rows_of_vectors(ve, vectors)
        rows = tok[...].astype(float_type)
        normed[...] = layer_norm(rows, vectors[0:1], vectors[4:5])[0].astype(narrow_type)

    def project(p):
        down = as_matrix(fa[:, :, p * wide + features : p * wide + features + 128])
        rank = (matmul(normed[...], down) * select[...]).astype(narrow_type)
        rank_ref[p] = rank

        @pl.loop(0, features // 256)
        def _(j):
            weight = as_matrix(fa[:, :, pl.ds(pl.multiple_of(p * wide + j * 256, 128), 256)])
            up = as_matrix(fa[pl.ds(j * 8, 8), :, p * wide + features + 128 : (p + 1) * wide])
            result = matmul(normed[...], weight) + transposed_right(rank, up)
            if p == 0:
                result = result + vectors[5:6, pl.ds(pl.multiple_of(j * 256, 128), 256)]
            proj[p, pl.ds(j * 4, 4)] = result.T.astype(narrow_type).reshape(4, 64, 256)

            @pl.loop(0, 4)
            def _(i):
                k = j * 4 + i

                @pl.when(swap.away_head(k))
                def _():
                    piece(p, k).start()

        @pl.when(half == core)
        def _():
            kept(p).start()

    after = {0: norm, 2: lambda: project(0), 4: lambda: project(1), 6: lambda: project(2)}
    after_attention = [i for i, chunk in enumerate(chunks) if chunk[0] is fa][-1]
    outs = [
        pltpu.make_async_copy(fa, fa_out, local.at[3]),
        pltpu.make_async_copy(ve, ve_out, local.at[4]),
    ]

    def store():
        for copy in outs:
            copy.start()

    def exchanged():
        @pl.loop(0, own)
        def _(k):
            @pl.when(swap.away_block(k))
            def _():
                for p in range(3):
                    arrival(p, k).wait_recv()

        @pl.when(half == core)
        def _():
            for p in range(3):
                kept(p).wait()

        first = jnp.where(core == 0, own - halo, own)
        over = remote(
            y_ref.at[pl.ds(first - base, halo), 1:3],
            y_ref.at[pl.ds(first - (own - halo) * (1 - core), halo), 1:3],
            piece_send.at[3, 0],
            piece_receive.at[3, 0],
            seq ^ CORES,
            fsdp,
        )
        over.start()
        return over

    steps = (gather.own, gather.inner, gather.outer, gather.first, gather.second, gather.third, gather.finish)
    for turn in range(DELAYS[0], len(chunks) + DELAYS[-1]):
        if turn == len(chunks) - 2:
            over = exchanged()
        for delay, step in zip(DELAYS, steps):
            index = turn - delay
            if not 0 <= index < len(chunks) or (delay == DELAYS[0] and index in early):
                continue
            chunk = chunks[index]
            if delay == DELAYS[1] and index in first_hidden:
                for copy in own_shards:
                    copy.wait()
            if chunk[4] == LINE and delay == 0:
                step = gather.arrive
            if chunk[4] == LINE and delay > 0:
                continue
            step(index, chunk)
            if delay == 3:
                after.get(index, lambda: None)()
                if index == after_attention:
                    store()

    over.wait()

    @pl.loop(0, heads)
    def _(k):
        @pl.when(swap.away_head(k))
        def _():
            for p in range(3):
                piece(p, k).wait_send()

    for index, chunk in enumerate(chunks):
        gather.drain(index, chunk)
    for copy in outs:
        copy.wait()


def attention_in(lengths, choice, tokens, arrays, halo, depth, heads, devices, collective):
    rows, features = tokens.shape
    wide = features + 256
    total = 4 * wide + 256
    share, hidden_share, hidden_total = features // devices, arrays[9].shape[0], arrays[12].shape[1]
    chunks = [("ve", slice(0, 48), slice(0, 128), 0)]
    for p in range(3):
        chunks.append(("fa", slice(0, share), slice(p * wide, p * wide + wide // 2), 0))
        chunks.append(("fa", slice(0, share), slice(p * wide + wide // 2, (p + 1) * wide), 1))
    middle = 3 * wide + (total - 3 * wide) // 2
    chunks.append(("fa", slice(0, share), slice(3 * wide, middle), 0))
    chunks.append(("fa", slice(0, share), slice(middle, total), 1))
    for part in range(0, hidden_share, 64):
        chunks.append(("f2", slice(part, part + 64), slice(0, wide // 2), 0))
        chunks.append(("f2", slice(part, part + 64), slice(wide // 2, wide), 1))
    for part in range(0, hidden_total // 2, 2048):
        chunks.append(("a", slice(0, share), slice(part, part + 2048), 0))
        chunks.append(("b", slice(0, share), slice(part, part + 2048), 1))
    copies = Gather.STEPS * len(chunks)
    return pl.pallas_call(
        functools.partial(attention_in_kernel, depth, halo, heads, chunks),
        out_shape=(
            jax.ShapeDtypeStruct((devices, share, total), narrow_type),
            jax.ShapeDtypeStruct((devices, 48, 128), narrow_type),
            jax.ShapeDtypeStruct((devices, hidden_share, wide), narrow_type),
            jax.ShapeDtypeStruct((depth, share, hidden_total // 2), narrow_type),
            jax.ShapeDtypeStruct((depth, share, hidden_total // 2), narrow_type),
            jax.ShapeDtypeStruct((heads + halo, 3, features // heads, rows), narrow_type),
            jax.ShapeDtypeStruct((3, rows, 128), narrow_type),
        ),
        in_specs=[IN_SMEM, IN_SMEM] + [ANYWHERE] * (1 + len(arrays)),
        out_specs=(ANYWHERE,) * 6 + (IN_VMEM,),
        scratch_shapes=[
            pltpu.VMEM((devices, share, total), narrow_type),
            pltpu.VMEM((devices, 48, 128), narrow_type),
            pltpu.VMEM((3, heads, features // heads, rows), narrow_type),
            pltpu.VMEM((rows, features), narrow_type),
            pltpu.VMEM((16, features), float_type),
            pltpu.VMEM((rows, features), narrow_type),
            pltpu.VMEM((4, share), narrow_type),
            pltpu.VMEM((5, share), narrow_type),
            pltpu.VMEM((1, 128), narrow_type),
            pltpu.VMEM((128, 128), narrow_type),
            pltpu.VMEM((1, hidden_share, wide), narrow_type),
            pltpu.VMEM((1, share, hidden_total // 2), narrow_type),
            pltpu.VMEM((1, share, hidden_total // 2), narrow_type),
            pltpu.VMEM((rows, 128), float_type),
            pltpu.SemaphoreType.DMA((copies,)),
            pltpu.SemaphoreType.DMA((copies,)),
            pltpu.SemaphoreType.DMA((24,)),
            pltpu.SemaphoreType.DMA((4, heads)),
            pltpu.SemaphoreType.DMA((4, heads)),
            pltpu.SemaphoreType.DMA((3,)),
        ],
        compiler_params=pltpu.CompilerParams(
            collective_id=collective, has_side_effects=True, vmem_limit_bytes=60 << 20
        ),
    )(lengths, choice, tokens, *arrays)


DELAYS = (-8, -4, -2, 0, 1, 2, 3)
HIDDEN_TILE = 512


def middle_kernel(
    depth,
    heads,
    lens_ref,
    choice_ref,
    att_ref,
    tok_ref,
    cot_ref,
    fa_in,
    ve,
    f2_in,
    line_a,
    line_b,
    ya,
    yb,
    xa,
    xb,
    result_ref,
    gm_ref,
    terms,
    gy_ref,
    fa,
    f2,
    f1,
    att_t,
    att,
    gatt_t,
    vectors,
    hidden_bias,
    middle,
    normal,
    normed,
    branch,
    grad_branch,
    grad_normed,
    ranks,
    rank_sums,
    select,
    send,
    receive,
    local,
    a_send,
    a_receive,
    b_send,
    b_receive,
    own_local,
):
    swap = Exchange(depth, heads)
    me, seq, fsdp = swap.me, swap.seq, swap.fsdp
    core, half, head, own = swap.core, swap.half, swap.head, heads
    devices, share = f1.shape[0], f1.shape[1]
    row_count, features = tok_ref.shape
    wide = features + 256
    tiles = f1.shape[2] // HIDDEN_TILE
    in_tile = HIDDEN_TILE // f2.shape[1]
    barrier = pltpu.get_barrier_semaphore()
    greet_neighbours(barrier, seq, fsdp, depth)
    waits = 3 + depth - 1 + swap.greet_owners(barrier) + swap.greet_holders(barrier)
    half_columns = line_a.shape[2]
    left, right = pl.ds(0, half_columns), pl.ds(half_columns, half_columns)
    lines = [
        (line, f1.at[pl.ds((seq ^ bit) * depth, depth), :, columns])
        for line, bit, columns in (
            (line_a, 0, left),
            (line_b, 0, right),
            (ya, SIDE_Y, left),
            (yb, SIDE_Y, right),
            (xa, SIDE_X, left),
            (xb, SIDE_X, right),
        )
    ]
    groups = [pl.ds((seq ^ k) * depth, depth) for k in range(8)]
    loads = (
        [pltpu.make_async_copy(fa_in.at[:, :, pl.ds(3 * wide, wide + 256)], fa, local.at[0])]
        + [pltpu.make_async_copy(line, place, local.at[1 + i]) for i, (line, place) in enumerate(lines)]
        + [pltpu.make_async_copy(f2_in.at[groups[k]], f2.at[groups[k]], local.at[7 + k]) for k in range(6)]
    )
    for copy in loads:
        copy.start()
    pl.semaphore_wait(barrier, waits)
    quarter = half_columns // 2
    x_side = lax.rem(lax.div(seq, 2), 2)

    def columns_of(start, parity):
        return pl.ds(pl.multiple_of(start + parity * quarter, 128), quarter)

    corners, diagonal = [], []
    for turn in range(2):
        for i, (line, via, to, start, parity) in enumerate(
            ((ya, SIDE_Y, SIDE_X, 0, 1 - x_side), (xb, SIDE_X, SIDE_Y, half_columns, x_side))
        ):
            at = 2 * turn + i
            parity = 1 - parity if turn else parity
            corners.append(
                remote(
                    line.at[:, :, columns_of(0, parity)],
                    f1.at[pl.ds((seq ^ via) * depth, depth), :, columns_of(start, parity)],
                    send.at[at],
                    receive.at[at],
                    seq ^ to,
                    fsdp,
                )
            )
            here = f1.at[
                pl.ds((seq ^ SIDE_X ^ SIDE_Y) * depth, depth),
                :,
                columns_of(start, 1 - x_side if turn else x_side),
            ]
            diagonal.append(remote(here, here, send.at[4 + at], receive.at[4 + at], seq ^ CORES, fsdp))

    tops, tails = pl.ds(0, wide // 2), pl.ds(wide // 2, wide // 2)
    f2_parts = ((SIDE_Y, SIDE_X, tops), (SIDE_X, SIDE_Y, tails))
    rows_over, rows_along = pl.ds(0, 64), pl.ds(64, 64)
    for i, (via, to, columns) in enumerate(f2_parts):
        line = pl.ds((seq ^ via) * depth, depth)
        corners.append(
            remote(
                f2_in.at[line, rows_over, columns],
                f2.at[line, rows_over, columns],
                send.at[8 + i],
                receive.at[8 + i],
                seq ^ to,
                fsdp,
            )
        )
    single = [
        remote(
            f2_in.at[pl.ds((seq ^ via) * depth + fsdp, 1), rows_along, columns],
            f2.at[pl.ds((seq ^ via) * depth + fsdp, 1), rows_along, columns],
            send.at[10 + i],
            receive.at[10 + i],
            seq ^ to,
            fsdp,
        )
        for i, (via, to, columns) in enumerate(f2_parts)
    ]
    far = f2.at[pl.ds((seq ^ SIDE_X ^ SIDE_Y) * depth + fsdp, 1), rows_along]
    along = [
        remote(
            far, far, send.at[11 + step], receive.at[11 + step], seq, lax.rem(fsdp + step, depth)
        )
        for step in range(1, depth)
    ]
    across = [
        remote(line, place, send.at[15 + i], receive.at[15 + i], seq ^ CORES, fsdp)
        for i, (line, place) in enumerate(lines)
    ]
    f2_across = remote(
        f2.at[groups[6]], f2.at[groups[6]], send.at[21], receive.at[21], seq ^ CORES, fsdp
    )

    def attended_piece(k):
        return remote(att_ref.at[k], att_t.at[head], a_send.at[k], a_receive.at[head], *swap.owner(k))

    def attended_arrival(k):
        return remote(att_ref.at[0], att_t.at[k], a_send.at[k], a_receive.at[k], seq ^ CORES, fsdp)

    attended_kept = pltpu.make_async_copy(att_ref.at[me - core * own], att_t.at[head], own_local.at[0])

    @pl.when(half == core)
    def _():
        attended_kept.start()

    @pl.loop(0, own)
    def _(step):
        k = lax.rem(step + me, own)

        @pl.when(swap.away_block(k))
        def _():
            attended_piece(k).start()

    for copy in single + corners[:2] + across:
        copy.start()
    select[...] = selected(lens_ref, choice_ref, me, *select.shape)
    rows_of_vectors(ve, vectors)
    for d in range(devices):
        hidden_bias[:, d * 128 : (d + 1) * 128] = ve[d, 32:48, :].astype(float_type)[0:8]
    grad_branch[...] = (vectors[3:4] * cot_ref[...].astype(float_type)).astype(narrow_type)
    loads[0].wait()
    contract_up = as_matrix(fa[:, :, wide + 128 : wide + 256])
    ranks[1] = (matmul(grad_branch[...], contract_up) * select[...]).astype(narrow_type)
    branch[...] = jnp.zeros_like(branch)
    grad_normed[...] = jnp.zeros_like(grad_normed)
    rank_sums[...] = jnp.zeros_like(rank_sums)

    @pl.loop(0, heads)
    def _(k):
        @pl.when(swap.away_head(k))
        def _():
            attended_arrival(k).wait_recv()

    @pl.when(half == core)
    def _():
        attended_kept.wait()

    for copy in corners[2:]:
        copy.start()
    for copy in single:
        copy.wait_recv()
    for copy in along:
        copy.start()

    for i in range(2):
        corners[i].wait_recv()
        diagonal[i].start()
    for j in range(4):
        att[:, j * 256 : (j + 1) * 256] = turned(as_matrix(att_t[4 * j : 4 * j + 4]))
    out_down = as_matrix(fa[:, :, features : features + 128])
    rank_out = (matmul(att[...], out_down) * select[...]).astype(narrow_type)
    ranks[2] = rank_out

    @pl.loop(0, 4)
    def _(j):
        at = pl.ds(pl.multiple_of(j * 256, 128), 256)
        weight = as_matrix(fa[:, :, at])
        up = as_matrix(fa[pl.ds(j * 8, 8), :, features + 128 : wide])
        mixed = matmul(att[...], weight) + transposed_right(rank_out, up) + vectors[6:7, at]
        middle[:, at] = tok_ref[:, at].astype(float_type) + vectors[1:2, at] * mixed

    shifted, normal_rows, scaling = layer_norm(middle[...], vectors[2:3], vectors[7:8])
    normal[...] = normal_rows
    normed[...] = shifted.astype(narrow_type)
    expand_down = as_matrix(fa[:, :, wide : wide + 128])
    rank_expand = (matmul(normed[...], expand_down) * select[...]).astype(narrow_type)
    ranks[0] = rank_expand
    ranks[3, 0:128] = turned(rank_expand)[:, 0:128]
    ranks[3, 128:256] = turned(rank_expand)[:, 128:256]
    ranks[4, 0:128] = turned(ranks[1])[:, 0:128]
    ranks[4, 128:256] = turned(ranks[1])[:, 128:256]
    for copy in loads[1:]:
        copy.wait()
    for copy in across + diagonal[:2]:
        copy.wait_recv()

    def hidden(k):
        @pl.when(k == 2)
        def _():
            for i in (2, 3):
                corners[i].wait_recv()
                diagonal[i].start()
            for i in (2, 3):
                diagonal[i].wait_recv()

        @pl.when(k == 5)
        def _():
            for copy in corners[4:] + along:
                copy.wait_recv()
            f2_across.start()

        @pl.when(k == 7)
        def _():
            f2_across.wait_recv()

        c = seq ^ k
        at = pl.ds(pl.multiple_of(c * HIDDEN_TILE, 128), HIDDEN_TILE)
        slots = pl.ds(c * in_tile, in_tile)
        expand = as_matrix(f1[:, :, at])
        contract = as_matrix(f2[slots, :, 0:features])
        down = as_matrix(f2[slots, :, features : features + 128])
        up = as_matrix(f2[slots, :, features + 128 : wide])
        before = matmul(normed[...], expand) + transposed_right(ranks[0], up) + hidden_bias[0:1, at]
        total = 0.5 * (1.0 + lax.erf(before * 0.7071067811865476))
        density = jnp.exp(-0.5 * before * before) * 0.3989422804014327
        active = (before * total).astype(narrow_type)
        slope = total + before * density
        branch[...] += matmul(active, contract)
        rank_sums[0] += matmul(active, down)
        grad_active = transposed_right(grad_branch[...], contract) + transposed_right(ranks[1], down)
        grad_hidden = (grad_active * slope).astype(narrow_type)
        rank_sums[1] += matmul(grad_hidden, up)
        grad_normed[...] += transposed_right(grad_hidden, expand)
        turned_expand = jnp.concatenate([ranks[3, 0:128], ranks[3, 128:256]], axis=1)
        turned_contract = jnp.concatenate([ranks[4, 0:128], ranks[4, 128:256]], axis=1)
        grad_up = matmul(turned_expand, grad_hidden).astype(narrow_type)
        grad_down = matmul(turned_contract, active).astype(narrow_type)
        for i in range(in_tile):
            terms[c * in_tile + i, 96:224] = grad_up[:, i * 128 : (i + 1) * 128]
            terms[c * in_tile + i, 224:352] = grad_down[:, i * 128 : (i + 1) * 128]

    pl.loop(0, tiles)(hidden)
    rank_contract = (rank_sums[0] * select[...]).astype(narrow_type)
    grad_rank_expand = (rank_sums[1] * select[...]).astype(narrow_type)
    gradient = grad_normed[...] + transposed_right(grad_rank_expand, expand_down)
    gm_ref[...] = cot_ref[...].astype(float_type) + norm_backward(gradient, vectors[2:3], normal[...], scaling)
    grad_mixed = (vectors[1:2] * gm_ref[...]).astype(narrow_type)
    out_up = as_matrix(fa[:, :, features + 128 : wide])
    grad_rank_out = (matmul(grad_mixed, out_up) * select[...]).astype(narrow_type)

    def gradient_piece(k):
        return remote(
            gatt_t.at[k], gy_ref.at[lax.rem(me, own)], b_send.at[k], b_receive.at[lax.rem(me, own)], *swap.holder(k)
        )

    def gradient_arrival(k):
        return remote(gatt_t.at[0], gy_ref.at[k], b_send.at[k], b_receive.at[k], seq ^ CORES, fsdp)

    gradient_kept = pltpu.make_async_copy(gatt_t.at[head], gy_ref.at[lax.rem(me, own)], own_local.at[1])

    @pl.loop(0, 4)
    def _(j):
        slots = pl.ds(j * 8, 8)
        weight = as_matrix(fa[slots, :, 0:features])
        down = as_matrix(fa[slots, :, features : features + 128])
        rows = transposed_right(grad_mixed, weight) + transposed_right(grad_rank_out, down)
        gatt_t[pl.ds(j * 4, 4)] = rows.T.astype(narrow_type).reshape(4, 64, 256)

        @pl.loop(0, 4)
        def _(i):
            k = j * 4 + i

            @pl.when(swap.away_head(k))
            def _():
                gradient_piece(k).start()

    @pl.when(half == core)
    def _():
        gradient_kept.start()

    up_rows = transposed_right(rank_contract, contract_up)
    result_ref[...] = (
        middle[...] + vectors[3:4] * (branch[...] + vectors[8:9] + up_rows)
    ).astype(narrow_type)
    shaped = (devices, share, 128)
    terms[:, 0:32] = matmul(as_matrix(att_t[...]), grad_rank_out).astype(narrow_type).reshape(shaped)
    terms[:, 32:64] = transposed_left(grad_mixed, rank_out).astype(narrow_type).reshape(shaped)
    terms[:, 64:96] = transposed_left(normed[...], grad_rank_expand).astype(narrow_type).reshape(shaped)
    terms[:, 352:384] = transposed_left(grad_branch[...], rank_contract).astype(narrow_type).reshape(shaped)

    @pl.loop(0, own)
    def _(k):
        @pl.when(swap.away_block(k))
        def _():
            gradient_arrival(k).wait_recv()
            attended_piece(k).wait_send()

    @pl.when(half == core)
    def _():
        gradient_kept.wait()

    @pl.loop(0, heads)
    def _(k):
        @pl.when(swap.away_head(k))
        def _():
            gradient_piece(k).wait_send()

    for copy in single + along + corners + diagonal + across + [f2_across]:
        copy.wait_send()


def middle_part(lengths, choice, att, tokens, cotangent, fa, ve, f2, lines, depth, collective):
    heads, width, rows = att.shape
    features = tokens.shape[1]
    wide = features + 256
    devices, hidden_share = f2.shape[0], f2.shape[1]
    share, hidden_total = features // devices, 2 * lines[0].shape[2]
    copies = 22

    def wide_rows():
        return pltpu.VMEM((rows, features), float_type)

    def narrow_rows():
        return pltpu.VMEM((rows, features), narrow_type)

    return pl.pallas_call(
        functools.partial(middle_kernel, depth, heads),
        out_shape=(
            jax.ShapeDtypeStruct((rows, features), narrow_type),
            jax.ShapeDtypeStruct((rows, features), float_type),
            jax.ShapeDtypeStruct((devices, 384, 128), narrow_type),
            jax.ShapeDtypeStruct((heads, width, rows), narrow_type),
        ),
        in_specs=[IN_SMEM, IN_SMEM, IN_VMEM, IN_VMEM, IN_VMEM, ANYWHERE, IN_VMEM] + [ANYWHERE] * 7,
        out_specs=(IN_VMEM, IN_VMEM, IN_VMEM, ANYWHERE),
        scratch_shapes=[
            pltpu.VMEM((devices, share, wide + 256), narrow_type),
            pltpu.VMEM(f2.shape, narrow_type),
            pltpu.VMEM((devices, share, hidden_total), narrow_type),
            pltpu.VMEM((heads, width, rows), narrow_type),
            narrow_rows(),
            pltpu.VMEM((heads, width, rows), narrow_type),
            pltpu.VMEM((16, features), float_type),
            pltpu.VMEM((8, hidden_total), float_type),
            wide_rows(),
            wide_rows(),
            narrow_rows(),
            wide_rows(),
            narrow_rows(),
            wide_rows(),
            pltpu.VMEM((5, rows, 128), narrow_type),
            pltpu.VMEM((2, rows, 128), float_type),
            pltpu.VMEM((rows, 128), float_type),
            pltpu.SemaphoreType.DMA((copies,)),
            pltpu.SemaphoreType.DMA((copies,)),
            pltpu.SemaphoreType.DMA((13,)),
            pltpu.SemaphoreType.DMA((heads,)),
            pltpu.SemaphoreType.DMA((heads,)),
            pltpu.SemaphoreType.DMA((heads,)),
            pltpu.SemaphoreType.DMA((heads,)),
            pltpu.SemaphoreType.DMA((2,)),
        ],
        compiler_params=pltpu.CompilerParams(
            collective_id=collective, has_side_effects=True, vmem_limit_bytes=54 << 20
        ),
    )(lengths, choice, att, tokens, cotangent, fa, ve, f2, *lines)


class Reduce:
    COPIES = 16

    def __init__(self, depth, base, terms, first, second, third, fourth, send, receive):
        self.depth, self.base, self.terms = depth, base, terms
        self.buffers = first, second, third, fourth
        self.send, self.receive = send, receive
        self.seq, self.fsdp = place_here()
        self.core, self.x, self.y = lax.rem(self.seq, 2), lax.rem(lax.div(self.seq, 2), 2), lax.div(self.seq, 4)
        half = terms.shape[1] // 2
        self.halves = (slice(0, half), slice(half, 2 * half))

    def copy(self, step, source, target, seq, fsdp):
        at = self.base + step
        return remote(source, target, self.send.at[at], self.receive.at[at], seq, fsdp)

    def to_core(self):
        first = self.buffers[0]
        lines = [self.terms.at[pl.ds((2 * t + 1 - self.core) * self.depth, self.depth)] for t in range(4)]
        return [self.copy(t, lines[t], first.at[t], self.seq ^ CORES, self.fsdp) for t in range(4)]

    def to_sides(self):
        first, second = self.buffers[:2]
        x, y = self.x, self.y
        copies = []
        for j in range(2):
            copies.append(
                self.copy(
                    4 + j,
                    first.at[2 * j + 1 - x, :, self.halves[0]],
                    second.at[0, j],
                    self.seq ^ SIDE_X,
                    self.fsdp,
                )
            )
            copies.append(
                self.copy(
                    6 + j,
                    first.at[2 * (1 - y) + j, :, self.halves[1]],
                    second.at[1, j],
                    self.seq ^ SIDE_Y,
                    self.fsdp,
                )
            )
        return copies

    def to_corner(self):
        second, third = self.buffers[1:3]
        return [
            self.copy(8, second.at[0, 1 - self.y], third.at[0], self.seq ^ SIDE_Y, self.fsdp),
            self.copy(9, second.at[1, 1 - self.x], third.at[1], self.seq ^ SIDE_X, self.fsdp),
        ]

    def to_line(self):
        third, fourth = self.buffers[2:]
        copies = []
        for step in range(1, self.depth):
            to = lax.rem(self.fsdp + step, self.depth)
            for j in range(2):
                copies.append(
                    self.copy(8 + 2 * step + j, third.at[j, to], fourth.at[j, step], self.seq, to)
                )
        return copies

    def add(self, target, other):
        @pl.loop(0, self.depth)
        def _(i):
            target[i] = (target[i].astype(float_type) + other[i].astype(float_type)).astype(narrow_type)

    def begin(self):
        for copy in self.to_core():
            copy.start()

    def sides(self):
        first = self.buffers[0]
        for t, copy in enumerate(self.to_core()):
            copy.wait_recv()
            self.add(first.at[t], self.terms.at[pl.ds((2 * t + self.core) * self.depth, self.depth)])
        for copy in self.to_sides():
            copy.start()

    def corner(self):
        first, second = self.buffers[:2]
        copies = self.to_sides()
        for j in range(2):
            copies[2 * j].wait_recv()
            self.add(second.at[0, j], first.at[2 * j + self.x, :, self.halves[0]])
            copies[2 * j + 1].wait_recv()
            self.add(second.at[1, j], first.at[2 * self.y + j, :, self.halves[1]])
        for copy in self.to_corner():
            copy.start()

    def line(self):
        second, third = self.buffers[1:3]
        copies = self.to_corner()
        copies[0].wait_recv()
        self.add(third.at[0], second.at[0, self.y])
        copies[1].wait_recv()
        self.add(third.at[1], second.at[1, self.x])
        for copy in self.to_line():
            copy.start()

    def end(self, out):
        third, fourth = self.buffers[2:]
        for copy in self.to_line():
            copy.wait_recv()
        for j in range(2):
            total = third[j, self.fsdp].astype(float_type)
            for step in range(1, self.depth):
                total = total + fourth[j, step].astype(float_type)
            out[self.halves[j]] = total

    def drain(self):
        for copy in self.to_core() + self.to_sides() + self.to_corner() + self.to_line():
            copy.wait_send()


def last_kernel(
    depth,
    heads,
    halo,
    lens_ref,
    choice_ref,
    dq_ref,
    dkv_ref,
    tok_ref,
    gm_ref,
    fa_in,
    ve,
    rank_ref,
    early_terms,
    gradient_ref,
    early_ref,
    late_ref,
    fa,
    vectors,
    normed_t,
    normal,
    grad_rank,
    total,
    arrived,
    arrived_rows,
    merged,
    other,
    late_terms,
    early_buffers,
    late_buffers,
    select,
    send,
    receive,
    local,
    piece_send,
    piece_receive,
    piece_local,
):
    swap = Exchange(depth, heads)
    me, seq, fsdp = swap.me, swap.seq, swap.fsdp
    core, half, head, own = swap.core, swap.half, swap.head, heads
    row_count, features = tok_ref.shape
    devices, share = fa.shape[0], fa.shape[1]
    wide = features + 256
    barrier = pltpu.get_barrier_semaphore()
    greet_neighbours(barrier, seq, fsdp, depth)
    waits = 3 + depth - 1 + swap.greet_holders(barrier)
    load = pltpu.make_async_copy(fa_in.at[:, :, pl.ds(0, 3 * wide)], fa, local.at[0])
    load.start()
    pl.semaphore_wait(barrier, waits)
    over = remote(
        dkv_ref.at[pl.ds(jnp.where(core == 0, own, 0), halo)],
        other,
        piece_send.at[3, 0], piece_receive.at[3, 0], seq ^ CORES, fsdp)
    over.start()
    early = Reduce(depth, 0, early_terms, *early_buffers, send, receive)
    late = [
        Reduce(
            depth, Reduce.COPIES * (p + 1), late_terms.at[p], *[b.at[p] for b in late_buffers], send, receive
        )
        for p in range(3)
    ]
    shared = jnp.where(core == 0, own - halo, 0)
    shift = core * halo

    def in_shared(k):
        return (k >= shared) & (k < shared + halo)

    def sent(p, k, source):
        return remote(
            source, arrived.at[p, head], piece_send.at[p, k], piece_receive.at[p, head], *swap.owner(k)
        )

    def launch(p, k, source):
        @pl.when(swap.away_block(k))
        def _():
            sent(p, k, source).start()

        @pl.when(core * own + k == me)
        def _():
            pltpu.make_async_copy(source, arrived.at[p, head], piece_local.at[p]).start()

    def arrival(p, k):
        return remote(
            dq_ref.at[0], arrived.at[p, k], piece_send.at[p, k], piece_receive.at[p, k], seq ^ CORES, fsdp
        )

    @pl.loop(0, own)
    def _(step):
        k = lax.rem(step + me, own)
        launch(0, k, dq_ref.at[k])

    over.wait_recv()

    @pl.loop(0, halo)
    def _(i):
        for part in range(2):
            merged[i, part] = (
                dkv_ref[shared + shift + i, part].astype(float_type) + other[i, part].astype(float_type)
            ).astype(narrow_type)

    for p in (1, 2):

        @pl.loop(0, own)
        def _(step, p=p):
            k = lax.rem(step + me, own)

            @pl.when(in_shared(k))
            def _():
                launch(p, k, merged.at[jnp.clip(k - shared, 0, halo - 1), p - 1])

            @pl.when(jnp.logical_not(in_shared(k)))
            def _():
                launch(p, k, dkv_ref.at[k + shift, p - 1])

    early.begin()
    rows_of_vectors(ve, vectors)
    select[...] = selected(lens_ref, choice_ref, me, *select.shape)
    early.sides()
    shifted, normal_rows, scaling = layer_norm(tok_ref[...].astype(float_type), vectors[0:1], vectors[4:5])
    normal[...] = normal_rows
    for j in range(4):
        normed_t[j * 256 : (j + 1) * 256] = turned(shifted[:, j * 256 : (j + 1) * 256])
    early.corner()
    load.wait()

    def gather_part(p):
        @pl.loop(0, heads)
        def _(k):
            @pl.when(swap.away_head(k))
            def _():
                arrival(p, k).wait_recv()

        @pl.when(half == core)
        def _():
            pltpu.make_async_copy(dq_ref.at[0], arrived.at[p, head], piece_local.at[p]).wait()

    def ranks_back(p):
        for j in range(4):
            arrived_rows[:, j * 256 : (j + 1) * 256] = turned(as_matrix(arrived[p, 4 * j : 4 * j + 4]))
        up = as_matrix(fa[:, :, p * wide + features + 128 : (p + 1) * wide])
        grad_rank[...] = (matmul(arrived_rows[...], up) * select[...]).astype(narrow_type)
        shaped = (devices, share, 128)
        late_terms[p, :, 0:32] = matmul(normed_t[...], grad_rank[...]).astype(narrow_type).reshape(shaped)
        late_terms[p, :, 32:64] = (
            matmul(as_matrix(arrived[p]), rank_ref[p]).astype(narrow_type).reshape(shaped)
        )

    def project_back(p, tiles):
        @pl.loop(*tiles)
        def _(j):
            at = pl.ds(pl.multiple_of(j * 256, 128), 256)
            slots = pl.ds(j * 8, 8)
            weight = as_matrix(fa[slots, :, p * wide : p * wide + features])
            down = as_matrix(fa[slots, :, p * wide + features : p * wide + features + 128])
            term = transposed_right(arrived_rows[...], weight) + transposed_right(grad_rank[...], down)
            if p == 0:
                total[:, at] = term
            else:
                total[:, at] += term

    gather_part(0)
    ranks_back(0)
    late[0].begin()
    project_back(0, (0, 4))
    early.line()
    late[0].sides()
    gather_part(1)
    ranks_back(1)
    late[1].begin()
    project_back(1, (0, 4))
    late[0].corner()
    late[1].sides()
    gather_part(2)
    ranks_back(2)
    late[2].begin()
    late[0].line()
    late[1].corner()
    project_back(2, (0, 2))
    late[2].sides()
    project_back(2, (2, 4))
    late[1].line()
    late[2].corner()
    gradient_ref[...] = gm_ref[...] + norm_backward(total[...], vectors[0:1], normal[...], scaling)
    late[2].line()
    early.end(early_ref)
    late[0].end(late_ref.at[0])
    late[1].end(late_ref.at[1])
    late[2].end(late_ref.at[2])
    for reduce in [early] + late:
        reduce.drain()

    @pl.loop(0, own)
    def _(k):
        @pl.when(swap.away_block(k))
        def _():
            for p in range(3):
                sent(p, k, dq_ref.at[k]).wait_send()

    over.wait_send()


def last_part(lengths, choice, dq, dkv, tokens, grad_middle, fa, ve, rank, terms, depth, collective):
    heads = dq.shape[0]
    halo = dkv.shape[0] - heads
    rows, features = tokens.shape
    wide = features + 256
    devices, share = fa.shape[0], fa.shape[1]

    def buffers(count, size):
        return [
            pltpu.VMEM(count + (4, depth, size, 128), narrow_type),
            pltpu.VMEM(count + (2, 2, depth, size // 2, 128), narrow_type),
            pltpu.VMEM(count + (2, depth, size // 2, 128), narrow_type),
            pltpu.VMEM(count + (2, depth, size // 2, 128), narrow_type),
        ]

    return pl.pallas_call(
        functools.partial(last_kernel, depth, heads, halo),
        out_shape=(
            jax.ShapeDtypeStruct((rows, features), float_type),
            jax.ShapeDtypeStruct((terms.shape[1], 128), float_type),
            jax.ShapeDtypeStruct((3, 2 * share, 128), float_type),
        ),
        in_specs=[IN_SMEM] * 2 + [IN_VMEM] * 4 + [ANYWHERE] + [IN_VMEM] * 3,
        out_specs=(IN_VMEM, IN_VMEM, IN_VMEM),
        scratch_shapes=[
            pltpu.VMEM((devices, share, 3 * wide), narrow_type),
            pltpu.VMEM((16, features), float_type),
            pltpu.VMEM((features, rows), narrow_type),
            pltpu.VMEM((rows, features), float_type),
            pltpu.VMEM((rows, 128), narrow_type),
            pltpu.VMEM((rows, features), float_type),
            pltpu.VMEM((3, heads, features // heads, rows), narrow_type),
            pltpu.VMEM((rows, features), narrow_type),
            pltpu.VMEM((halo,) + dkv.shape[1:], narrow_type),
            pltpu.VMEM((halo,) + dkv.shape[1:], narrow_type),
            pltpu.VMEM((3, devices, 2 * share, 128), narrow_type),
            buffers((), terms.shape[1]),
            buffers((3,), 2 * share),
            pltpu.VMEM((rows, 128), float_type),
            pltpu.SemaphoreType.DMA((4 * Reduce.COPIES,)),
            pltpu.SemaphoreType.DMA((4 * Reduce.COPIES,)),
            pltpu.SemaphoreType.DMA((1,)),
            pltpu.SemaphoreType.DMA((4, heads)),
            pltpu.SemaphoreType.DMA((4, heads)),
            pltpu.SemaphoreType.DMA((3,)),
        ],
        compiler_params=pltpu.CompilerParams(
            collective_id=collective, has_side_effects=True, vmem_limit_bytes=44 << 20
        ),
    )(lengths, choice, dq, dkv, tokens, grad_middle, fa, ve, rank, terms)


def spread_kernel(result_in, gradient_in, early, late, result, gradient, down, up, exp_down, exp_up, con_down, con_up):
    share = down.shape[1]
    result[...] = result_in[...]
    gradient[...] = gradient_in[...]
    for p in range(4):
        first = late[p, 0:share] if p < 3 else early[0:share]
        second = late[p, share : 2 * share] if p < 3 else early[share : 2 * share]
        down[p] = first
        up[p] = second
    exp_down[...] = early[64:96]
    exp_up[...] = early[96:224]
    con_down[...] = early[224:352].T
    con_up[...] = early[352:384]


def spread(result, gradient, early, late):
    share = late.shape[1] // 2
    shapes = ((4, share, 128), (4, share, 128), (share, 128), (128, 128), (128, 128), (share, 128))
    return pl.pallas_call(
        spread_kernel,
        out_shape=tuple(jax.ShapeDtypeStruct(a.shape, a.dtype) for a in (result, gradient))
        + tuple(jax.ShapeDtypeStruct(shape, float_type) for shape in shapes),
        in_specs=[IN_VMEM] * 4,
        out_specs=(IN_VMEM,) * 8,
        compiler_params=pltpu.CompilerParams(vmem_limit_bytes=24 << 20),
    )(result, gradient, early, late)


BIG = 32768.0


def image_range(lens_ref, first, last):
    low = high = start = jnp.int32(0)
    for image in range(lens_ref.shape[0]):
        end = start + lens_ref[image]
        low = jnp.where((start <= first) & (first < end), start, low)
        high = jnp.where((start <= last) & (last < end), end - 1, high)
        start = end
    return low, high


def image_edges(lens_ref, marks, rows):
    row = lax.broadcasted_iota(jnp.int32, (marks, rows), 0)
    starts = jnp.full((marks, rows), 1 << 30, jnp.int32)
    ends = jnp.zeros((marks, rows), jnp.int32)
    start = jnp.int32(0)
    for image in range(lens_ref.shape[0]):
        end = start + lens_ref[image]
        starts, ends = jnp.where(row == image, start, starts), jnp.where(row == image, end, ends)
        start = end
    return starts, ends


class Blocks:
    def __init__(self, lens_ref, own, halo, rows, marks):
        core = lax.rem(lax.axis_index("seq"), 2)
        self.lens_ref, self.own, self.rows, self.slots = lens_ref, own, rows, own + halo
        self.base = core * (own - halo)
        self.shift = core * halo
        self.starts, self.ends = image_edges(lens_ref, marks, rows)
        self.lane = lax.broadcasted_iota(jnp.int32, (marks, rows), 1)

    def marks(self, slot):
        place = self.lane + (self.base + slot) * self.rows
        return jnp.where((place >= self.starts) & (place < self.ends), 1.0, 0.0).astype(float_type)

    def reach(self, slot):
        first = (self.base + slot) * self.rows
        low, high = image_range(self.lens_ref, first, first + self.rows - 1)
        return lax.div(low, self.rows) - self.base, lax.div(high, self.rows) - self.base


def forward_kernel(
    own, halo, step, lens_ref, x_ref, att_ref, lse_ref, out_ref, keys, queries, values, score, weight, item_row, item_low
):
    slots, _, width, rows = x_ref.shape
    blocks = Blocks(lens_ref, own, halo, rows, keys.shape[1] - width)
    scale = width**-0.5

    @pl.loop(0, slots)
    def _(slot):
        block = jnp.concatenate([x_ref[slot, 1].astype(float_type), (blocks.marks(slot) - 1.0) * BIG], axis=0)
        keys[pl.ds(pl.multiple_of(slot * rows, rows), rows)] = block.T.astype(narrow_type)
        values[slot, 0:width] = x_ref[slot, 2]
        values[slot, width:] = jnp.ones((16, rows), narrow_type)

    def prepare(i, total):
        slot = i + blocks.shift
        queries[i] = jnp.concatenate([x_ref[slot, 0].astype(float_type) * scale, blocks.marks(slot)], axis=0).astype(narrow_type)
        low, high = blocks.reach(slot)
        count = lax.div(high - low + step, step)
        low = jnp.minimum(low, slots - step * count)

        @pl.loop(0, count)
        def _(j):
            item_row[total + j] = i
            item_low[total + j] = low + j * step

        return total + count

    total = lax.fori_loop(0, own, prepare, jnp.int32(0))
    item_row[total] = item_row[total - 1]
    item_low[total] = item_low[total - 1]

    def scored(t, side):
        at = pl.multiple_of(item_low[t] * rows, rows)
        score[side] = matmul(keys[pl.ds(at, step * rows)], queries[item_row[t]])

    def mixed(t):
        low = item_low[t]
        result = matmul(values[low], weight[0:rows])
        for j in range(1, step):
            result += matmul(values[low + j], weight[j * rows : (j + 1) * rows])
        return result

    def soften(fresh, side, highest):
        highest = jnp.where(fresh, -1e30, highest)
        s = score[side]
        higher = jnp.maximum(highest, jnp.max(s, axis=0, keepdims=True))
        fade = jnp.where(fresh, 0.0, jnp.exp(highest - higher))
        return higher, fade, jnp.exp(s - higher).astype(narrow_type)

    def finish(t, out, fade, highest):
        i = item_row[t]
        out = out * fade + mixed(t)
        summed = out[width : width + 1]
        whole = out[0:width] / summed
        att_ref[i] = whole.astype(narrow_type)
        out_ref[i] = whole
        lse_ref[i] = jnp.broadcast_to(highest + jnp.log(summed), (8, rows))
        return out

    def turn(t, side, carry):
        highest, out, fade = carry
        out = finish(t - 1, out, fade, highest)
        scored(t + 1, 1 - side)
        highest, fade, p = soften(item_row[t] != item_row[t - 1], side, highest)
        weight[...] = p
        return highest, out, fade

    scored(0, 0)
    scored(1, 1)
    highest, fade, p = soften(True, 0, jnp.zeros((1, rows), float_type))
    weight[...] = p
    carry = (highest, jnp.zeros((width + 16, rows), float_type), fade)
    pairs = lax.div(total - 1, 2)
    carry = lax.fori_loop(0, pairs, lambda j, c: turn(2 * j + 2, 0, turn(2 * j + 1, 1, c)), carry)
    carry = lax.fori_loop(2 * pairs + 1, total, lambda t, c: turn(t, 1, c), carry)
    highest, out, fade = carry
    finish(total - 1, out, fade, highest)


def attention_forward(lengths, x, own, halo, step=2):
    slots, _, width, rows = x.shape
    marks = -(-lengths.shape[0] // 16) * 16
    most = own * (slots // step + 2) + 8
    return pl.pallas_call(
        functools.partial(forward_kernel, own, halo, step),
        out_shape=(
            jax.ShapeDtypeStruct((own, width, rows), narrow_type),
            jax.ShapeDtypeStruct((own, 8, rows), float_type),
            jax.ShapeDtypeStruct((own, width, rows), float_type),
        ),
        in_specs=[IN_SMEM, IN_VMEM],
        out_specs=(IN_VMEM, IN_VMEM, IN_VMEM),
        scratch_shapes=[
            pltpu.VMEM((slots * rows, width + marks), narrow_type),
            pltpu.VMEM((own, width + marks, rows), narrow_type),
            pltpu.VMEM((slots, width + 16, rows), narrow_type),
            pltpu.VMEM((2, step * rows, rows), float_type),
            pltpu.VMEM((step * rows, rows), narrow_type),
            pltpu.SMEM((most,), jnp.int32),
            pltpu.SMEM((most,), jnp.int32),
        ],
        compiler_params=pltpu.CompilerParams(vmem_limit_bytes=32 << 20),
    )(lengths, x)


def backward_kernel(
    own, halo, step, lens_ref, x_ref, g_ref, lse_ref, out_ref, dq_ref, dkv_ref,
    keys, values, queries, offset, dq, score, grad_prob, weight, grad_score, item_slot, item_low,
):
    slots, _, width, rows = x_ref.shape
    blocks = Blocks(lens_ref, own, halo, rows, keys.shape[2] - width)
    scale = width**-0.5

    def prepare(slot, total):
        block = jnp.concatenate([x_ref[slot, 1].astype(float_type), (blocks.marks(slot) - 1.0) * BIG], axis=0)
        keys[slot] = block.T.astype(narrow_type)
        values[slot] = x_ref[slot, 2].astype(float_type).T.astype(narrow_type)
        dkv_ref[slot] = jnp.zeros((2, width, rows), narrow_type)
        low, high = blocks.reach(slot)
        low = jnp.maximum(low - blocks.shift, 0)
        high = jnp.minimum(high - blocks.shift, own - 1)
        count = jnp.maximum(lax.div(high - low + step, step), 0)
        low = jnp.minimum(low, own - step * count)

        @pl.loop(0, count)
        def _(j):
            item_slot[total + j] = slot
            item_low[total + j] = low + j * step

        return total + count

    total = lax.fori_loop(0, slots, prepare, jnp.int32(0))
    item_slot[total] = item_slot[total - 1]
    item_low[total] = item_low[total - 1]

    @pl.loop(0, own)
    def _(i):
        slot = i + blocks.shift
        q = x_ref[slot, 0].astype(float_type) * scale
        queries[i] = jnp.concatenate([q, blocks.marks(slot)], axis=0).astype(narrow_type)
        g = g_ref[i].astype(float_type)
        offset[i] = jnp.broadcast_to(jnp.sum(g * out_ref[i], axis=0, keepdims=True), (8, rows))
        dq[i] = jnp.zeros((width, rows), float_type)

    def scored(t, side):
        slot, low = item_slot[t], item_low[t]
        for j in range(step):
            score[side, j] = matmul(keys[slot], queries[low + j])
            grad_prob[side, j] = matmul(values[slot], g_ref[low + j])

    def soften(t, side):
        low = item_low[t]
        done = []
        for j in range(step):
            p = jnp.exp(score[side, j] - lse_ref[low + j, 0:1])
            d = p * (grad_prob[side, j] - offset[low + j, 0:1])
            done.append((p.astype(narrow_type), d.astype(narrow_type)))
        return done

    def keep(done):
        for j in range(step):
            weight[j] = done[j][0]
            grad_score[j] = done[j][1]

    def mixed(t, fresh, dk, dv):
        slot, low = item_slot[t], item_low[t]
        dk = jnp.where(fresh, 0.0, dk)
        dv = jnp.where(fresh, 0.0, dv)
        key = x_ref[slot, 1]
        for j in range(step):
            dk += transposed_right(queries[low + j, 0:width], grad_score[j])
            dv += transposed_right(g_ref[low + j], weight[j])
        for j in range(step):
            dq[low + j] += matmul(key, grad_score[j])
        dkv_ref[slot, 0] = dk.astype(narrow_type)
        dkv_ref[slot, 1] = dv.astype(narrow_type)
        return dk, dv

    def turn(t, side, carry):
        fresh = (t == 1) | (item_slot[t - 1] != item_slot[jnp.maximum(t - 2, 0)])
        scored(t + 1, 1 - side)
        done = soften(t, side)
        carry = mixed(t - 1, fresh, *carry)
        keep(done)
        return carry

    scored(0, 0)
    scored(1, 1)
    keep(soften(0, 0))
    zero = jnp.zeros((width, rows), float_type)
    pairs = lax.div(total - 1, 2)
    carry = lax.fori_loop(0, pairs, lambda j, c: turn(2 * j + 2, 0, turn(2 * j + 1, 1, c)), (zero, zero))
    carry = lax.fori_loop(2 * pairs + 1, total, lambda t, c: turn(t, 1, c), carry)
    mixed(total - 1, item_slot[total - 1] != item_slot[jnp.maximum(total - 2, 0)], *carry)

    @pl.loop(0, own)
    def _(i):
        dq_ref[i] = (dq[i] * scale).astype(narrow_type)


def attention_backward(lengths, x, g, lse, out, own, halo, step=1):
    slots, _, width, rows = x.shape
    marks = -(-lengths.shape[0] // 16) * 16
    most = slots * (own // step + 2) + 8
    return pl.pallas_call(
        functools.partial(backward_kernel, own, halo, step),
        out_shape=(
            jax.ShapeDtypeStruct((own, width, rows), narrow_type),
            jax.ShapeDtypeStruct((slots, 2, width, rows), narrow_type),
        ),
        in_specs=[IN_SMEM] + [IN_VMEM] * 4,
        out_specs=(IN_VMEM, IN_VMEM),
        scratch_shapes=[
            pltpu.VMEM((slots, rows, width + marks), narrow_type),
            pltpu.VMEM((slots, rows, width), narrow_type),
            pltpu.VMEM((own, width + marks, rows), narrow_type),
            pltpu.VMEM((own, 8, rows), float_type),
            pltpu.VMEM((own, width, rows), float_type),
            pltpu.VMEM((2, step, rows, rows), float_type),
            pltpu.VMEM((2, step, rows, rows), float_type),
            pltpu.VMEM((step, rows, rows), narrow_type),
            pltpu.VMEM((step, rows, rows), narrow_type),
            pltpu.SMEM((most,), jnp.int32),
            pltpu.SMEM((most,), jnp.int32),
        ],
        compiler_params=pltpu.CompilerParams(vmem_limit_bytes=40 << 20),
    )(lengths, x, g, lse, out)


def layer_on_slice(
    tokens,
    lengths,
    adapter_choice,
    gain_rows,
    bias_rows,
    query_key_value,
    output_weight,
    expand_weight,
    expand_bias,
    contract_weight,
    adapter_in_attention,
    adapter_out_attention,
    adapter_in_expand,
    adapter_out_expand,
    adapter_in_contract,
    adapter_out_contract,
    cotangent,
):
    row_count = tokens.shape[0]
    depth = lax.axis_size("fsdp")
    devices = lax.axis_size(("seq", "fsdp"))
    own = devices // 2
    halo = -(-(LONGEST - 1) // row_count)

    arrays = (
        gain_rows,
        bias_rows,
        expand_bias[None],
        query_key_value,
        output_weight,
        adapter_in_attention,
        adapter_out_attention.transpose(0, 2, 1),
        adapter_in_expand,
        adapter_out_contract.T,
        contract_weight,
        adapter_in_contract,
        adapter_out_expand,
        expand_weight,
    )
    fa, ve, f2, line_a, line_b, on_heads, rank = attention_in(
        lengths, adapter_choice, tokens, arrays, halo, depth, HEADS, devices, 1
    )

    def swapped(line, bit):
        route = [
            (seq * depth + fsdp, (seq ^ bit) * depth + fsdp)
            for seq in range(devices // depth)
            for fsdp in range(depth)
        ]
        return lax.ppermute(line, ("seq", "fsdp"), route)

    lines = (
        line_a,
        line_b,
        swapped(line_a, SIDE_Y),
        swapped(line_b, SIDE_Y),
        swapped(line_a, SIDE_X),
        swapped(line_b, SIDE_X),
    )
    attended, log_totals, attended_wide = attention_forward(lengths, on_heads, own, halo)
    result, grad_middle, terms, grad_on_heads = middle_part(
        lengths, adapter_choice, attended, tokens, cotangent, fa, ve, f2, lines, depth, 2
    )
    grad_queries, grad_key_values = attention_backward(
        lengths, on_heads, grad_on_heads, log_totals, attended_wide, own, halo
    )
    input_gradient, early, late = last_part(
        lengths, adapter_choice, grad_queries, grad_key_values, tokens, grad_middle, fa, ve, rank, terms, depth, 3
    )
    outs = spread(result, input_gradient, early, late)
    return outs[:3] + (outs[3].transpose(0, 2, 1),) + outs[4:7] + (outs[7].T,)


def solution(mesh):
    per_device = layer_on_slice if dict(mesh.shape) == {"seq": 8, "fsdp": 4} else general_layer
    placed = (
        P(("seq", "fsdp"), None),
        P(),
        P(),
        P(None, ("seq", "fsdp")),
        P(None, ("seq", "fsdp")),
        P(("seq", "fsdp"), None),
        P(("seq", "fsdp"), None),
        P(("seq", "fsdp"), None),
        P(("seq", "fsdp")),
        P(("seq", "fsdp"), None),
        P(None, ("seq", "fsdp"), None),
        P(None, None, ("seq", "fsdp")),
        P(("seq", "fsdp"), None),
        P(None, ("seq", "fsdp")),
        P(("seq", "fsdp"), None),
        P(None, ("seq", "fsdp")),
        P(("seq", "fsdp"), None),
    )
    return jax.shard_map(
        per_device,
        mesh=mesh,
        in_specs=placed,
        out_specs=(
            P(("seq", "fsdp"), None),
            P(("seq", "fsdp"), None),
            P(None, ("seq", "fsdp"), None),
            P(None, None, ("seq", "fsdp")),
            P(("seq", "fsdp"), None),
            P(None, ("seq", "fsdp")),
            P(("seq", "fsdp"), None),
            P(None, ("seq", "fsdp")),
        ),
        check_vma=False,
    )
```
